32 devices in a mesh: groups: 2 (over x), blocks: 16 (over z, y, core).
Axes of the slice: x: 2, y: 2, z: 4, core: 2. Of those that a mesh axis runs over, the one named last changes fastest.
Arguments:
- features: bfloat16 [16384, 512], P(('groups', 'blocks')), parts along dimension 0, may hold values from -12 to 12
- conv_weight: bfloat16 [13824, 512], P('blocks'), may hold values from -0.0546875 to 0.0546875
- cpe_weight: bfloat16 [512, 512], replicated, may hold values from -0.25 to 0.25
- cpe_gain: float32 [512], replicated, may hold values from 0.1 to 1.9
- attn_gain: float32 [512], replicated, may hold values from 0.1 to 1.9
- qkv_weight: bfloat16 [512, 1536], replicated, as said below
- proj_weight: bfloat16 [512, 512], replicated, may hold values from -0.25 to 0.25
- mlp_gain: float32 [512], replicated, may hold values from 0.1 to 1.9
- up_weight: bfloat16 [512, 2048], replicated, may hold values from -0.25 to 0.25
- down_weight: bfloat16 [2048, 512], replicated, may hold values from -0.125 to 0.125
- face_rows: int32 [32, 8, 64], P(('groups', 'blocks')), parts along dimension 0, may hold values from 0 to 512, as said below
- neighbours: int32 [16384, 26], P(('groups', 'blocks')), parts along dimension 0, may hold values from 0 to 1024, as said below
- serial_rank: int32 [16384], P(('groups', 'blocks')), parts along dimension 0, may hold values from 0 to 8191, as said below
- serial_order: int32 [16384], P(('groups', 'blocks')), parts along dimension 0, may hold values from 0 to 8191, as said below
Outputs:
- output: bfloat16 [16384, 512], P(('groups', 'blocks')), parts along dimension 0
The draws below stay inside these ranges and needn't reach their ends.
There are 2 independent parts, one for each index of `groups`. The reference program is written for one: setup_inputs(seed, part) draws one part's arguments, and reference() takes and returns one part's arrays. A program takes and returns all parts, laid end to end along the dimension named above; an argument that names none is the same for every part. Nothing has to cross between parts.
Inputs may be any that keep to these rules, and one draw needn't show every extreme that they name: `qkv_weight`: projections for queries, keys and values, columns in that order. face_rows[b, k, f] is a local row of block b sent toward direction k, or 512 for an empty slot; live slots come first in each list; lists toward blocks outside the grid are empty; every block has a full list. `neighbours`: row index into the point's block table: local rows below 512, received face rows from 512 to 1023, and 1024 for a missing neighbour. `serial_rank`: A permutation; serial_order is its inverse. Position r belongs to stretch r // 512. The points of one block fall into any one stretch 0, 32 or 64 at a time, and 64 is reached. `serial_order`: the inverse of serial_rank.
All inputs are finite; a program needn't handle non-finite values.
Results may differ from the reference program's by a relative error of at most 0.011.
The reference program's roundings to bfloat16 on the way count: a program that leaves them out, or rounds other values in their place, can miss the bound.
Values may be sent and summed in bfloat16 or wider, within the bound.
No kernel may reach another device: no remote copies, remote signals or barrier semaphores. Data moves between devices by JAX's collectives and lax.ppermute only.
A program may use at most 128 MiB of HBM per device.

```python
import math
import jax
import jax.numpy as jnp
from jax import lax

C = 512
HEADS = 32
FF = 2048
PATCH = 512
GY = 8
P_DEV = 512
FACE = 64
VOXEL_BLOCKS = 16
N_PTS = 8192
HD = 16


def spread_scales(scale_key, row_count, column_count):
    row_key, column_key = jax.random.split(scale_key)
    row_scale = jnp.exp(jax.random.uniform(row_key, (row_count, 1), jnp.float32, math.log(0.3), math.log(3.0)))
    column_scale = jnp.exp(jax.random.uniform(column_key, (1, column_count), jnp.float32, math.log(0.3), math.log(3.0)))
    return row_scale * column_scale


def draw_features(key, part):
    key = jax.random.fold_in(key, 11)
    scale_key, base_key = jax.random.split(key, 2)
    scales = spread_scales(scale_key, N_PTS, C)
    drawn = scales * jax.random.normal(base_key, (N_PTS, C), jnp.float32)
    return jnp.clip(drawn, -12.0, 12.0).astype(jnp.bfloat16)


def draw_qkv_weight(key, part):
    key = jax.random.fold_in(key, 12)
    query_key, keyed_key, value_key = jax.random.split(key, 3)
    scale = 1.0 / math.sqrt(C)
    shared = jnp.clip(jax.random.normal(query_key, (C, C), jnp.float32), -5.0, 5.0) * scale
    values = jnp.clip(jax.random.normal(value_key, (C, C), jnp.float32), -5.0, 5.0) * scale
    queries = shared
    keyed = jnp.clip(jax.random.normal(keyed_key, (C, C), jnp.float32), -5.0, 5.0) * scale
    return jnp.concatenate([queries, keyed, values], axis=1).astype(jnp.bfloat16)


def draw_face_rows(key, part):
    key = jax.random.fold_in(key, 13)
    count_key, row_key = jax.random.split(key)
    block_ids = jnp.arange(VOXEL_BLOCKS, dtype=jnp.int32)
    across = block_ids // GY
    along = block_ids % GY
    steps_x = jnp.array([-1, -1, -1, 0, 0, 1, 1, 1], jnp.int32)
    steps_y = jnp.array([-1, 0, 1, -1, 1, -1, 0, 1], jnp.int32)
    target_x = across[:, None] + steps_x[None, :]
    target_y = along[:, None] + steps_y[None, :]
    inside = (target_x >= 0) & (target_x < VOXEL_BLOCKS // GY) & (target_y >= 0) & (target_y < GY)
    counts = jax.random.randint(count_key, (VOXEL_BLOCKS, 8), 0, FACE + 1)
    full_face = jnp.where(across == 0, 6, 1)
    counts = jnp.where(jnp.arange(8, dtype=jnp.int32)[None, :] == full_face[:, None], FACE, counts)
    counts = jnp.where(inside, counts, 0)
    drawn_rows = jax.random.randint(row_key, (VOXEL_BLOCKS, 8, FACE), 0, P_DEV)
    slot_ids = jnp.arange(FACE, dtype=jnp.int32)[None, None, :]
    return jnp.where(slot_ids < counts[:, :, None], drawn_rows, P_DEV).astype(jnp.int32)


def draw_neighbours(key, part):
    key = jax.random.fold_in(key, 14)
    kind_key, local_key, remote_key = jax.random.split(key, 3)
    kinds = jax.random.randint(kind_key, (N_PTS, 26), 0, 20)
    local_rows = jax.random.randint(local_key, (N_PTS, 26), 0, P_DEV)
    remote_rows = jax.random.randint(remote_key, (N_PTS, 26), P_DEV, P_DEV + 8 * FACE)
    missing = jnp.full((N_PTS, 26), P_DEV + 8 * FACE, jnp.int32)
    return jnp.where(kinds < 9, local_rows, jnp.where(kinds < 17, remote_rows, missing)).astype(jnp.int32)


def hilbert_tables(key):
    first_key, second_key, source_key, target_key = jax.random.split(key, 4)
    unit_size = P_DEV // VOXEL_BLOCKS
    half_blocks = VOXEL_BLOCKS // 2
    first_offset = jax.random.randint(first_key, (), 0, VOXEL_BLOCKS)
    second_offset = first_offset + jax.random.randint(second_key, (), 1, half_blocks)
    identity_rows = jnp.broadcast_to(jnp.arange(P_DEV, dtype=jnp.int32), (VOXEL_BLOCKS, P_DEV))
    source_perm = jax.random.permutation(source_key, identity_rows, axis=1, independent=True).astype(jnp.int32)
    target_perm = jax.random.permutation(target_key, identity_rows, axis=1, independent=True).astype(jnp.int32)
    source_inverse = jnp.argsort(source_perm, axis=1, stable=True).astype(jnp.int32)
    target_inverse = jnp.argsort(target_perm, axis=1, stable=True).astype(jnp.int32)
    block_ids = jnp.arange(VOXEL_BLOCKS, dtype=jnp.int32)[:, None]
    units = source_perm // unit_size
    destination = jnp.where(units < half_blocks, block_ids + first_offset + units, block_ids + second_offset + units - half_blocks) % VOXEL_BLOCKS
    ranks = destination * P_DEV + target_perm[destination, source_perm]
    units_back = target_inverse // unit_size
    anchor = jnp.where(units_back < half_blocks, block_ids - first_offset - units_back, block_ids - second_offset - units_back + half_blocks) % VOXEL_BLOCKS
    orders = anchor * P_DEV + source_inverse[anchor, target_inverse]
    return (ranks.reshape(-1).astype(jnp.int32), orders.reshape(-1).astype(jnp.int32))


def draw_serial_rank(key, part):
    tables = hilbert_tables(key)
    return tables[0]


def draw_serial_order(key, part):
    tables = hilbert_tables(key)
    return tables[1]


def level_of(key, extent, shards, least, largest):
    loudness, own = 1.0, jax.random.fold_in(key, 6)
    for axis_at, parts in shards:
        draws = jnp.exp(jax.random.uniform(jax.random.fold_in(own, axis_at), (parts,), jnp.float32, least / len(shards), largest / len(shards)))
        loudness = loudness * jnp.repeat(draws, extent[axis_at] // parts).reshape([-1 if axis == axis_at else 1 for axis in range(len(extent))])
    return loudness


def bell_draw(own_key, dims, scale, bound, cuts=(), held_as=jnp.bfloat16):
    values = scale * jax.random.normal(own_key, dims, jnp.float32)
    if cuts:
        values = values * level_of(own_key, dims, cuts, -0.22, 0.18)
    return jnp.clip(values, -bound, bound).astype(held_as)


def setup_inputs(seed: int = 0, part: int = 0) -> dict:
    arg_keys = jax.random.split(jax.random.key(seed), 15)
    part_splits = jax.random.split(jax.random.fold_in(arg_keys[14], part), 15)
    features = draw_features(jax.random.fold_in(jax.random.fold_in(arg_keys[14], part), 71), part)
    conv_weight = bell_draw(arg_keys[1], (27 * C, C), (27 * C) ** -0.5, 0.0546875, ((0, 16),))
    cpe_weight = bell_draw(arg_keys[2], (C, C), C ** -0.5, 0.25)
    cpe_gain = jnp.clip(1.0 + 0.18 * jax.random.normal(arg_keys[3], (C,), jnp.float32), 0.1, 1.9)
    attn_gain = jnp.clip(1.0 + 0.18 * jax.random.normal(arg_keys[4], (C,), jnp.float32), 0.1, 1.9)
    qkv_weight = draw_qkv_weight(jax.random.fold_in(arg_keys[14], 71), part)
    proj_weight = bell_draw(arg_keys[6], (C, C), C ** -0.5, 0.25)
    mlp_gain = jnp.clip(1.0 + 0.18 * jax.random.normal(arg_keys[7], (C,), jnp.float32), 0.1, 1.9)
    up_weight = bell_draw(arg_keys[8], (C, FF), C ** -0.5, 0.25)
    down_weight = bell_draw(arg_keys[9], (FF, C), FF ** -0.5, 0.125)
    face_rows = draw_face_rows(jax.random.fold_in(jax.random.fold_in(arg_keys[14], part), 71), part)
    neighbours = draw_neighbours(jax.random.fold_in(jax.random.fold_in(arg_keys[14], part), 71), part)
    serial_rank = draw_serial_rank(jax.random.fold_in(jax.random.fold_in(arg_keys[14], part), 71), part)
    serial_order = draw_serial_order(jax.random.fold_in(jax.random.fold_in(arg_keys[14], part), 71), part)
    return {"features": features, "conv_weight": conv_weight, "cpe_weight": cpe_weight, "cpe_gain": cpe_gain, "attn_gain": attn_gain, "qkv_weight": qkv_weight, "proj_weight": proj_weight, "mlp_gain": mlp_gain, "up_weight": up_weight, "down_weight": down_weight, "face_rows": face_rows, "neighbours": neighbours, "serial_rank": serial_rank, "serial_order": serial_order}


EPSILON = 1e-05
STEPS_X = (-1, -1, -1, 0, 0, 1, 1, 1)
STEPS_Y = (-1, 0, 1, -1, 1, -1, 0, 1)

def layer_norm(inputs, gain_vector):
    row_mean = lax.optimization_barrier(jnp.mean(inputs, axis=-1, keepdims=True))
    centred = inputs - row_mean
    variance = lax.optimization_barrier(jnp.mean(centred * centred, axis=-1, keepdims=True))
    return centred * lax.rsqrt(variance + EPSILON) * gain_vector

def reference(features, conv_weight, cpe_weight, cpe_gain, attn_gain, qkv_weight, proj_weight, mlp_gain, up_weight, down_weight, face_rows, neighbours, serial_rank, serial_order):
    local_rows = features.reshape(VOXEL_BLOCKS, P_DEV, C)
    padded_rows = jnp.concatenate([local_rows, jnp.zeros((VOXEL_BLOCKS, 1, C), jnp.bfloat16)], axis=1)
    all_faces = jax.vmap(lambda row_index, lookup: lookup[row_index])(face_rows, padded_rows)
    neighbour_rows = neighbours.reshape(VOXEL_BLOCKS, P_DEV, 26)

    def conv_block(block_index):
        arrived = []
        for facing in range(8):
            source = block_index - (STEPS_X[facing] * GY + STEPS_Y[facing])
            inside = (source >= 0) & (source < VOXEL_BLOCKS)
            clipped = jnp.clip(source, 0, VOXEL_BLOCKS - 1).astype(jnp.int32)
            face_piece = lax.dynamic_index_in_dim(all_faces, clipped, 0, keepdims=False)[facing]
            arrived.append(jnp.where(inside, face_piece, jnp.zeros_like(face_piece)))
        own_rows = lax.dynamic_index_in_dim(local_rows, block_index, 0, keepdims=False)
        lookup = jnp.concatenate([own_rows] + arrived + [jnp.zeros((1, C), jnp.bfloat16)], axis=0)
        row_index = lax.dynamic_index_in_dim(neighbour_rows, block_index, 0, keepdims=False)
        gathered = lookup[row_index]
        stacked = jnp.concatenate([gathered[:, :13], own_rows[:, None], gathered[:, 13:]], axis=1)
        stacked = stacked.reshape(P_DEV, 27 * C)
        return jnp.dot(stacked, conv_weight, preferred_element_type=jnp.float32).astype(jnp.bfloat16)
    convolved = lax.map(conv_block, jnp.arange(VOXEL_BLOCKS, dtype=jnp.int32)).reshape(N_PTS, C)
    linear = jnp.dot(convolved, cpe_weight, preferred_element_type=jnp.float32)
    mixed_rows = (features.astype(jnp.float32) + layer_norm(linear, cpe_gain)).astype(jnp.bfloat16)
    serial = mixed_rows[serial_order]
    scale = 1.0 / math.sqrt(HD)

    def attend(one_patch):
        normed = layer_norm(one_patch.astype(jnp.float32), attn_gain).astype(jnp.bfloat16)
        projected = jnp.dot(normed, qkv_weight, preferred_element_type=jnp.float32).astype(jnp.bfloat16)
        queries = projected[:, :C].reshape(PATCH, HEADS, HD).astype(jnp.float32)
        keyed = projected[:, C:2 * C].reshape(PATCH, HEADS, HD).astype(jnp.float32)
        values = projected[:, 2 * C:].reshape(PATCH, HEADS, HD).astype(jnp.float32)
        scores = jnp.einsum('qhd,khd->hqk', queries, keyed) * scale
        row_max = lax.optimization_barrier(jnp.max(scores, axis=-1, keepdims=True))
        weights = jnp.exp(scores - row_max)
        weights = (weights / lax.optimization_barrier(jnp.sum(weights, axis=-1, keepdims=True))).astype(jnp.bfloat16)
        head_out = jnp.einsum('hqk,khd->qhd', weights.astype(jnp.float32), values).astype(jnp.bfloat16)
        update = jnp.dot(head_out.reshape(PATCH, C), proj_weight, preferred_element_type=jnp.float32)
        return (one_patch.astype(jnp.float32) + update).astype(jnp.bfloat16)
    attended = lax.map(attend, serial.reshape(N_PTS // PATCH, PATCH, C)).reshape(N_PTS, C)
    hidden_in = layer_norm(attended.astype(jnp.float32), mlp_gain).astype(jnp.bfloat16)
    hidden = jax.nn.gelu(jnp.dot(hidden_in, up_weight, preferred_element_type=jnp.float32), approximate=False).astype(jnp.bfloat16)
    finished = (attended.astype(jnp.float32) + jnp.dot(hidden, down_weight, preferred_element_type=jnp.float32)).astype(jnp.bfloat16)
    return finished[serial_rank]
```

```python
import functools
import math

import jax
import jax.numpy as jnp
from jax import lax
from jax.experimental import pallas as pl
from jax.experimental.pallas import tpu as pltpu
from jax.sharding import PartitionSpec as P

HEADS = 32
GY = 8
HD = 16
TAPS = 27
EPSILON = 1e-05
STEPS_X = (-1, -1, -1, 0, 0, 1, 1, 1)
STEPS_Y = (-1, 0, 1, -1, 1, -1, 0, 1)
F32 = jnp.float32
BF16 = jnp.bfloat16
MIB = 1 << 20


def dot(left, right):
    return jnp.dot(left, right, preferred_element_type=F32)


def layer_norm(inputs, gain_vector):
    row_mean = jnp.mean(inputs, axis=-1, keepdims=True)
    centred = inputs - row_mean
    variance = jnp.mean(centred * centred, axis=-1, keepdims=True)
    return centred * lax.rsqrt(variance + EPSILON) * gain_vector


def one_hot(mask):
    return jnp.where(mask, 1.0, 0.0).astype(BF16)


def call(kernel, out_shape, limit, flops, moved, **extra):
    return pl.pallas_call(
        kernel,
        out_shape=out_shape,
        compiler_params=pltpu.CompilerParams(vmem_limit_bytes=limit * MIB),
        cost_estimate=pl.CostEstimate(flops=flops, bytes_accessed=moved, transcendentals=0),
        **extra,
    )


def faces_kernel(unit, features_ref, rows_ref, ordered_ref, faces_ref):
    points, width = features_ref.shape
    half = width // 2
    place = lax.broadcasted_iota(jnp.int32, (width, width), 1)
    within = lax.rem(place, half)
    source = (within // unit) * (2 * unit) + (place // half) * unit + lax.rem(place, unit)
    channel = lax.broadcasted_iota(jnp.int32, (width, width), 0)
    ordered = dot(features_ref[...], one_hot(channel == source)).astype(BF16)
    ordered_ref[...] = ordered
    row_ids = lax.broadcasted_iota(jnp.int32, (rows_ref.shape[0], points), 1)
    faces_ref[...] = dot(one_hot(rows_ref[...] == row_ids), ordered).astype(BF16)


def gather_kernel(own_rows, other_rows, own_table, other_table, own_out, other_out):
    tap = pl.program_id(0)
    points, lanes = own_rows.shape
    chosen = lax.broadcasted_iota(jnp.int32, (points, lanes), 1) == tap
    row_ids = lax.broadcasted_iota(jnp.int32, (1, own_table.shape[0]), 1).astype(F32)
    for rows, table, out in ((own_rows, own_table, own_out), (other_rows, other_table, other_out)):
        column = jnp.sum(jnp.where(chosen, rows[...], 0.0), axis=1, keepdims=True)
        out[...] = dot(one_hot(column == row_ids), table[...]).astype(BF16)


def conv_kernel(stacked_ref, weight_ref, out_ref):
    product = dot(stacked_ref[...], weight_ref[...])

    @pl.when(pl.program_id(0) == 0)
    def _():
        out_ref[...] = product

    @pl.when(pl.program_id(0) > 0)
    def _():
        out_ref[...] += product


def conv_part(stacked, weight):
    points, depth = stacked.shape
    width = weight.shape[1]
    step = 3 * (width // 2)
    return call(
        conv_kernel,
        jax.ShapeDtypeStruct((points, width), F32),
        32,
        2 * points * depth * width,
        2 * depth * (points + width),
        grid=(depth // step,),
        in_specs=[
            pl.BlockSpec((points, step), lambda k: (0, k)),
            pl.BlockSpec((step, width), lambda k: (k, 0)),
        ],
        out_specs=pl.BlockSpec((points, width), lambda k: (0, 0)),
    )(stacked, weight)


def mix_kernel(own_ref, got_ref, features_ref, weight_ref, gain_ref, slot_ref, out_ref):
    convolved = (own_ref[...] + got_ref[...]).astype(BF16)
    linear = dot(convolved, weight_ref[...])
    mixed = (features_ref[...].astype(F32) + layer_norm(linear, gain_ref[...])).astype(BF16)
    slots = lax.broadcasted_iota(jnp.int32, (out_ref.shape[0], mixed.shape[0]), 0)
    out_ref[...] = dot(one_hot(slots == slot_ref[...]), mixed).astype(BF16)


def block_kernel(
    arrived_ref,
    slot_col_ref,
    slot_row_ref,
    attn_gain_ref,
    qv_ref,
    key_ref,
    proj_ref,
    mlp_gain_ref,
    up_ref,
    down_ref,
    out_ref,
    serial_ref,
    qv_cols_ref,
    keys_ref,
    heads_ref,
    total_ref,
):
    slots = arrived_ref.shape[0]
    points, width = serial_ref.shape
    slot_ids = lax.broadcasted_iota(jnp.int32, (points, slots), 1)
    serial = dot(one_hot(slot_col_ref[...] == slot_ids), arrived_ref[...])
    serial_ref[...] = serial
    normed = layer_norm(serial, attn_gain_ref[...]).astype(BF16)
    keys_ref[...] = dot(normed, key_ref[...]).astype(BF16)
    factor = math.log2(math.e) / math.sqrt(HD)
    contract_last = (((1,), (1,)), ((), ()))
    qv_cols_ref[:width] = (
        lax.dot_general(qv_ref[:width], normed, contract_last, preferred_element_type=F32) * factor
    ).astype(BF16)
    qv_cols_ref[width:] = lax.dot_general(
        qv_ref[width:], normed, contract_last, preferred_element_type=F32
    ).astype(BF16)
    ones = jnp.ones((HD, points), BF16)
    per_group = 128 // HD
    head_of_row = lax.broadcasted_iota(jnp.int32, (128, points), 0) // HD

    for group in range(HEADS // per_group):
        base = group * 128

        def attend(head, carry):
            group_queries = qv_cols_ref[base : base + 128]
            queries = jnp.where(head_of_row == head, group_queries.astype(F32), 0.0).astype(BF16)
            scores = dot(keys_ref[:, base : base + 128], queries)
            weights = jnp.exp2(scores - jnp.max(scores, axis=0, keepdims=True)).astype(BF16)
            at = pl.multiple_of(base + head * HD, HD)
            values = qv_cols_ref[pl.ds(width + at, HD)]
            sums = dot(jnp.concatenate([values, ones], axis=0), weights)
            heads_ref[pl.ds(at, HD)] = (sums[:HD] / sums[HD : HD + 1]).astype(BF16)
            return carry

        lax.fori_loop(0, per_group, attend, 0, unroll=2)

    update = lax.dot_general(
        heads_ref[...], proj_ref[...], (((0,), (0,)), ((), ())), preferred_element_type=F32
    )
    attended = (serial_ref[...] + update).astype(BF16).astype(F32)
    hidden_in = layer_norm(attended, mlp_gain_ref[...]).astype(BF16)
    total_ref[...] = attended
    chunk = width
    for start in range(0, up_ref.shape[1], chunk):
        raised = dot(hidden_in, up_ref[:, start : start + chunk])
        hidden = (raised * (1.0 + lax.erf(raised * math.sqrt(0.5))) * 0.5).astype(BF16)
        total_ref[...] += dot(hidden, down_ref[start : start + chunk])
    finished = total_ref[...].astype(BF16)
    slot_rows = lax.broadcasted_iota(jnp.int32, (slots, points), 0)
    out_ref[...] = dot(one_hot(slot_rows == slot_row_ref[...]), finished).astype(BF16)


def return_kernel(arrived_ref, slot_ref, out_ref):
    slot_ids = lax.broadcasted_iota(jnp.int32, (out_ref.shape[0], arrived_ref.shape[0]), 1)
    out_ref[...] = dot(one_hot(slot_ref[...] == slot_ids), arrived_ref[...]).astype(BF16)


def exchange_faces(faces, devices, index):
    zero = jnp.zeros_like(faces[0])
    received = [zero] * 8

    def valid(source, dx, dy):
        return 0 <= source // GY + dx < devices // GY and 0 <= source % GY + dy < GY

    if devices == 2 * GY:
        lower = index < GY
        for dy in (-1, 0, 1):
            payload = jnp.where(lower, faces[6 + dy], faces[1 + dy])
            pairs = []
            for source in range(devices):
                dx = 1 if source < GY else -1
                if valid(source, dx, dy):
                    pairs.append((source, source + dx * GY + dy))
            got = lax.ppermute(payload, "blocks", pairs)
            received[1 + dy] = jnp.where(lower, got, zero)
            received[6 + dy] = jnp.where(lower, zero, got)
        rest = (3, 4)
    else:
        rest = range(8)
    for facing in rest:
        dx, dy = STEPS_X[facing], STEPS_Y[facing]
        pairs = [
            (source, source + dx * GY + dy) for source in range(devices) if valid(source, dx, dy)
        ]
        received[facing] = lax.ppermute(faces[facing], "blocks", pairs)
    return received


def padded_taps(neighbours):
    points = neighbours.shape[0]
    own = jnp.arange(points, dtype=jnp.int32)[:, None]
    rest = jnp.zeros((points, 128 - TAPS), jnp.int32)
    middle = TAPS // 2
    return jnp.concatenate(
        [neighbours[:, :middle], own, neighbours[:, middle:], rest], axis=1
    ).astype(F32)


def body(
    features,
    conv_weight,
    cpe_weight,
    cpe_gain,
    attn_gain,
    qkv_weight,
    proj_weight,
    mlp_gain,
    up_weight,
    down_weight,
    face_rows,
    neighbours,
    serial_rank,
    serial_order,
):
    points, width = features.shape
    half = width // 2
    devices = lax.axis_size("blocks")
    index = lax.axis_index("blocks")
    core = lax.rem(index, 2)
    partner = [(source, source ^ 1) for source in range(devices)]
    capacity = 2 * points // devices
    slots = devices * capacity

    unit = conv_weight.shape[0] // TAPS
    units = conv_weight.reshape(TAPS, unit, width)
    kept, sent = units[0::2], units[1::2]
    got = lax.ppermute(sent, "blocks", partner)
    mine = jnp.where(
        core == 0, jnp.concatenate([kept, got]), jnp.concatenate([got, kept])
    ).reshape(TAPS * unit, width)
    same_core = [list(range(first, devices, 2)) for first in range(2)]
    weight = lax.all_gather(mine, "blocks", axis=0, tiled=True, axis_index_groups=same_core)

    face_list = face_rows.reshape(-1, 1)
    ordered, faces = call(
        functools.partial(faces_kernel, unit),
        (
            jax.ShapeDtypeStruct((points, width), BF16),
            jax.ShapeDtypeStruct((face_list.shape[0], width), BF16),
        ),
        32,
        4 * points * width * width,
        8 * points * width,
    )(features, face_list)
    received = exchange_faces(faces.reshape(8, -1, width), devices, index)
    table = jnp.concatenate([ordered] + received, axis=0)
    own_table = lax.dynamic_slice(table, (0, core * half), (table.shape[0], half))
    other_half = lax.dynamic_slice(table, (0, (1 - core) * half), (table.shape[0], half))
    other_table = lax.ppermute(other_half, "blocks", partner)
    other_neighbours = lax.ppermute(neighbours, "blocks", partner)
    whole = lambda tap: (0, 0)
    column = lambda tap: (0, tap)
    own_stacked, other_stacked = call(
        gather_kernel,
        (jax.ShapeDtypeStruct((points, TAPS * half), BF16),) * 2,
        40,
        4 * TAPS * points * table.shape[0] * half,
        4 * TAPS * points * half,
        grid=(TAPS,),
        in_specs=[
            pl.BlockSpec((points, 128), whole),
            pl.BlockSpec((points, 128), whole),
            pl.BlockSpec((table.shape[0], half), whole),
            pl.BlockSpec((table.shape[0], half), whole),
        ],
        out_specs=[pl.BlockSpec((points, half), column)] * 2,
    )(padded_taps(neighbours), padded_taps(other_neighbours), own_table, other_table)

    positions = jnp.arange(points, dtype=jnp.int32)
    target = serial_rank // points
    earlier = (target[None, :] == target[:, None]) & (serial_rank[None, :] < serial_rank[:, None])
    out_slot = target * capacity + jnp.sum(earlier.astype(jnp.int32), axis=1)
    anchor = serial_order // points
    before = (anchor[None, :] == anchor[:, None]) & (positions[None, :] < positions[:, None])
    in_slot = anchor * capacity + jnp.sum(before.astype(jnp.int32), axis=1)

    for_partner = conv_part(other_stacked, weight)
    from_partner = lax.ppermute(for_partner, "blocks", partner)
    own_part = conv_part(own_stacked, weight)

    outgoing = call(
        mix_kernel,
        jax.ShapeDtypeStruct((slots, width), BF16),
        32,
        2 * points * width * (width + slots),
        8 * points * width,
    )(
        own_part,
        from_partner,
        features,
        cpe_weight,
        cpe_gain.reshape(1, width),
        out_slot.reshape(1, points),
    )
    arrived = lax.all_to_all(
        outgoing.reshape(devices, capacity, width), "blocks", split_axis=0, concat_axis=0, tiled=True
    ).reshape(slots, width)

    key_weight = qkv_weight[:, width : 2 * width]
    qv_weight = jnp.concatenate([qkv_weight[:, :width], qkv_weight[:, 2 * width :]], axis=1).T
    back = call(
        block_kernel,
        jax.ShapeDtypeStruct((slots, width), BF16),
        48,
        20 * points * width * width,
        16 * width * width,
        scratch_shapes=[
            pltpu.VMEM((points, width), F32),
            pltpu.VMEM((2 * width, points), BF16),
            pltpu.VMEM((points, width), BF16),
            pltpu.VMEM((width, points), BF16),
            pltpu.VMEM((points, width), F32),
        ],
    )(
        arrived,
        in_slot.reshape(points, 1),
        in_slot.reshape(1, points),
        attn_gain.reshape(1, width),
        qv_weight,
        key_weight,
        proj_weight,
        mlp_gain.reshape(1, width),
        up_weight,
        down_weight,
    )
    returned = lax.all_to_all(
        back.reshape(devices, capacity, width), "blocks", split_axis=0, concat_axis=0, tiled=True
    ).reshape(slots, width)
    return call(
        return_kernel,
        jax.ShapeDtypeStruct((points, width), BF16),
        32,
        2 * points * slots * width,
        6 * points * width,
    )(returned, out_slot.reshape(points, 1))


def solution(mesh):
    placed = (
        P(("groups", "blocks"), None),
        P("blocks", None),
        P(),
        P(),
        P(),
        P(),
        P(),
        P(),
        P(),
        P(),
        P(("groups", "blocks"), None, None),
        P(("groups", "blocks"), None),
        P(("groups", "blocks")),
        P(("groups", "blocks")),
    )
    return jax.shard_map(
        body, mesh=mesh, in_specs=placed, out_specs=P(("groups", "blocks"), None), check_vma=False
    )
```

```python
import functools
import math

import jax
import jax.numpy as jnp
from jax import lax
from jax.experimental import pallas as pl
from jax.experimental.pallas import tpu as pltpu
from jax.sharding import PartitionSpec as P

HEADS = 32
GY = 8
HD = 16
TAPS = 27
EPSILON = 1e-05
STEPS_X = (-1, -1, -1, 0, 0, 1, 1, 1)
STEPS_Y = (-1, 0, 1, -1, 1, -1, 0, 1)
F32 = jnp.float32
BF16 = jnp.bfloat16
MIB = 1 << 20


def dot(left, right):
    return jnp.dot(left, right, preferred_element_type=F32)


def layer_norm(inputs, gain_vector):
    row_mean = jnp.mean(inputs, axis=-1, keepdims=True)
    centred = inputs - row_mean
    variance = jnp.mean(centred * centred, axis=-1, keepdims=True)
    return centred * lax.rsqrt(variance + EPSILON) * gain_vector


def one_hot(mask):
    return jnp.where(mask, 1.0, 0.0).astype(BF16)


def call(kernel, out_shape, limit, flops, moved, **extra):
    return pl.pallas_call(
        kernel,
        out_shape=out_shape,
        compiler_params=pltpu.CompilerParams(vmem_limit_bytes=limit * MIB),
        cost_estimate=pl.CostEstimate(flops=flops, bytes_accessed=moved, transcendentals=0),
        **extra,
    )


def faces_kernel(unit, features_ref, rows_ref, ordered_ref, faces_ref):
    points, width = features_ref.shape
    half = width // 2
    place = lax.broadcasted_iota(jnp.int32, (width, width), 1)
    within = lax.rem(place, half)
    source = (within // unit) * (2 * unit) + (place // half) * unit + lax.rem(place, unit)
    channel = lax.broadcasted_iota(jnp.int32, (width, width), 0)
    ordered = dot(features_ref[...], one_hot(channel == source)).astype(BF16)
    ordered_ref[...] = ordered
    row_ids = lax.broadcasted_iota(jnp.int32, (rows_ref.shape[0], points), 1)
    faces_ref[...] = dot(one_hot(rows_ref[...] == row_ids), ordered).astype(BF16)


def gather_kernel(other_rows, own_rows, other_table, own_table, out_ref):
    tap = pl.program_id(0)
    points, lanes = own_rows.shape
    chosen = lax.broadcasted_iota(jnp.int32, (points, lanes), 1) == tap
    row_ids = lax.broadcasted_iota(jnp.int32, (1, own_table.shape[0]), 1).astype(F32)
    for start, rows, table in ((0, other_rows, other_table), (points, own_rows, own_table)):
        column = jnp.sum(jnp.where(chosen, rows[...], 0.0), axis=1, keepdims=True)
        taken = dot(one_hot(column == row_ids), table[...]).astype(BF16)
        out_ref[start : start + points] = taken


def conv_kernel(pieces, needed, flip_ref, stacked_ref, *refs):
    sources = len(refs) - 4
    weights, (other_ref, own_ref, held, sems) = refs[:sources], refs[sources:]
    step = pl.program_id(0)
    width = held.shape[1] // sources
    rows = held.shape[0] // pieces
    depth, points = stacked_ref.shape[1], own_ref.shape[0]

    def copies(piece):
        place = jnp.where(flip_ref[0] == 1, pieces - 1 - piece, piece)
        return [
            pltpu.make_async_copy(
                weight.at[place],
                held.at[pl.ds(piece * rows, rows), pl.ds(at * width, width)],
                sems.at[at, piece],
            )
            for at, weight in enumerate(weights)
        ]

    @pl.when(step == 0)
    def _():
        for piece in range(pieces):
            for copy in copies(piece):
                copy.start()

    for at, wanted in enumerate(needed):

        @pl.when(step == at)
        def _():
            for piece in wanted:
                for copy in copies(piece):
                    copy.wait()

    rows_here = pl.ds(pl.multiple_of(step * depth, 256), depth)
    product = dot(stacked_ref[...], held[rows_here])

    @pl.when(step == 0)
    def _():
        other_ref[...] = product[:points]
        own_ref[...] = product[points:]

    @pl.when(step > 0)
    def _():
        other_ref[...] += product[:points]
        own_ref[...] += product[points:]


def conv_part(stacked, flip, weights):
    points, depth = stacked.shape
    pieces, rows, columns = weights[0].shape
    width = columns * len(weights)
    step = depth // 9
    ends = [-1] + [(step * (at + 1) - 1) // rows for at in range(9)]
    needed = [range(ends[at] + 1, ends[at + 1] + 1) for at in range(9)]
    return call(
        functools.partial(conv_kernel, pieces, needed),
        (jax.ShapeDtypeStruct((points // 2, width), F32),) * 2,
        60,
        2 * points * depth * width,
        2 * depth * (points + width),
        grid=(9,),
        in_specs=[
            pl.BlockSpec(memory_space=pltpu.SMEM),
            pl.BlockSpec((points, step), lambda k: (0, k)),
        ]
        + [pl.BlockSpec(memory_space=pl.ANY)] * len(weights),
        out_specs=[pl.BlockSpec((points // 2, width), lambda k: (0, 0))] * 2,
        scratch_shapes=[
            pltpu.VMEM((depth, width), BF16),
            pltpu.SemaphoreType.DMA((len(weights), pieces)),
        ],
    )(flip, stacked, *weights)


def mix_kernel(
    side_ref,
    own_ref,
    got_ref,
    own_late_ref,
    got_late_ref,
    features_ref,
    weight_ref,
    gain_ref,
    slot_ref,
    out_ref,
):
    late = (own_late_ref[...] + got_late_ref[...]).astype(BF16)
    quarter = late.shape[1] // 2
    first, second = late[:, :quarter], late[:, quarter:]
    here = side_ref[0] == 0
    convolved = jnp.concatenate(
        [
            jnp.where(here, first, second),
            jnp.where(here, second, first),
            (own_ref[...] + got_ref[...]).astype(BF16),
        ],
        axis=1,
    )
    linear = dot(convolved, weight_ref[...])
    mixed = (features_ref[...].astype(F32) + layer_norm(linear, gain_ref[...])).astype(BF16)
    slots = lax.broadcasted_iota(jnp.int32, (out_ref.shape[0], mixed.shape[0]), 0)
    out_ref[...] = dot(one_hot(slots == slot_ref[...]), mixed).astype(BF16)


def block_kernel(
    arrived_ref,
    slot_col_ref,
    slot_row_ref,
    attn_gain_ref,
    qv_ref,
    key_ref,
    proj_ref,
    mlp_gain_ref,
    up_ref,
    down_ref,
    out_ref,
    serial_ref,
    qv_cols_ref,
    keys_ref,
    heads_ref,
    total_ref,
):
    slots = arrived_ref.shape[0]
    points, width = serial_ref.shape
    slot_ids = lax.broadcasted_iota(jnp.int32, (points, slots), 1)
    serial = dot(one_hot(slot_col_ref[...] == slot_ids), arrived_ref[...])
    serial_ref[...] = serial
    normed = layer_norm(serial, attn_gain_ref[...]).astype(BF16)
    keys_ref[...] = dot(normed, key_ref[...]).astype(BF16)
    factor = math.log2(math.e) / math.sqrt(HD)
    contract_last = (((1,), (1,)), ((), ()))
    qv_cols_ref[:width] = (
        lax.dot_general(qv_ref[:width], normed, contract_last, preferred_element_type=F32) * factor
    ).astype(BF16)
    qv_cols_ref[width:] = lax.dot_general(
        qv_ref[width:], normed, contract_last, preferred_element_type=F32
    ).astype(BF16)
    ones = jnp.ones((HD, points), BF16)
    per_group = 128 // HD
    head_of_row = lax.broadcasted_iota(jnp.int32, (128, points), 0) // HD

    for group in range(HEADS // per_group):
        base = group * 128

        def attend(head, carry):
            group_queries = qv_cols_ref[base : base + 128]
            queries = jnp.where(head_of_row == head, group_queries.astype(F32), 0.0).astype(BF16)
            scores = dot(keys_ref[:, base : base + 128], queries)
            weights = jnp.exp2(scores - jnp.max(scores, axis=0, keepdims=True)).astype(BF16)
            at = pl.multiple_of(base + head * HD, HD)
            values = qv_cols_ref[pl.ds(width + at, HD)]
            sums = dot(jnp.concatenate([values, ones], axis=0), weights)
            heads_ref[pl.ds(at, HD)] = (sums[:HD] / sums[HD : HD + 1]).astype(BF16)
            return carry

        lax.fori_loop(0, per_group, attend, 0, unroll=2)

    update = lax.dot_general(
        heads_ref[...], proj_ref[...], (((0,), (0,)), ((), ())), preferred_element_type=F32
    )
    attended = (serial_ref[...] + update).astype(BF16).astype(F32)
    hidden_in = layer_norm(attended, mlp_gain_ref[...]).astype(BF16)
    total_ref[...] = attended
    chunk = width
    for start in range(0, up_ref.shape[1], chunk):
        raised = dot(hidden_in, up_ref[:, start : start + chunk])
        hidden = (raised * (1.0 + lax.erf(raised * math.sqrt(0.5))) * 0.5).astype(BF16)
        total_ref[...] += dot(hidden, down_ref[start : start + chunk])
    finished = total_ref[...].astype(BF16)
    slot_rows = lax.broadcasted_iota(jnp.int32, (slots, points), 0)
    out_ref[...] = dot(one_hot(slot_rows == slot_row_ref[...]), finished).astype(BF16)


def return_kernel(arrived_ref, slot_ref, out_ref):
    slot_ids = lax.broadcasted_iota(jnp.int32, (out_ref.shape[0], arrived_ref.shape[0]), 1)
    out_ref[...] = dot(one_hot(slot_ref[...] == slot_ids), arrived_ref[...]).astype(BF16)


def exchange_faces(faces, devices, index):
    zero = jnp.zeros_like(faces[0])
    received = [zero] * 8

    def valid(source, dx, dy):
        return 0 <= source // GY + dx < devices // GY and 0 <= source % GY + dy < GY

    if devices == 2 * GY:
        lower = index < GY
        for dy in (-1, 0, 1):
            payload = jnp.where(lower, faces[6 + dy], faces[1 + dy])
            pairs = []
            for source in range(devices):
                dx = 1 if source < GY else -1
                if valid(source, dx, dy):
                    pairs.append((source, source + dx * GY + dy))
            got = lax.ppermute(payload, "blocks", pairs)
            received[1 + dy] = jnp.where(lower, got, zero)
            received[6 + dy] = jnp.where(lower, zero, got)
        rest = (3, 4)
    else:
        rest = range(8)
    for facing in rest:
        dx, dy = STEPS_X[facing], STEPS_Y[facing]
        pairs = [
            (source, source + dx * GY + dy) for source in range(devices) if valid(source, dx, dy)
        ]
        received[facing] = lax.ppermute(faces[facing], "blocks", pairs)
    return received


def padded_taps(neighbours):
    points = neighbours.shape[0]
    own = jnp.arange(points, dtype=jnp.int32)[:, None]
    rest = jnp.zeros((points, 128 - TAPS), jnp.int32)
    middle = TAPS // 2
    return jnp.concatenate(
        [neighbours[:, :middle], own, neighbours[:, middle:], rest], axis=1
    ).astype(F32)


def body(
    features,
    conv_weight,
    cpe_weight,
    cpe_gain,
    attn_gain,
    qkv_weight,
    proj_weight,
    mlp_gain,
    up_weight,
    down_weight,
    face_rows,
    neighbours,
    serial_rank,
    serial_order,
):
    points, width = features.shape
    half = width // 2
    devices = lax.axis_size("blocks")
    index = lax.axis_index("blocks")
    core = lax.rem(index, 2)
    partner = [(source, source ^ 1) for source in range(devices)]
    capacity = 2 * points // devices
    slots = devices * capacity

    unit = conv_weight.shape[0] // TAPS
    units = conv_weight.reshape(TAPS, unit, width)
    kept, sent = units[0::2], units[1::2]
    got = lax.ppermute(sent, "blocks", partner)
    mine = jnp.where(
        core == 0, jnp.concatenate([kept, got]), jnp.concatenate([got, kept])
    ).reshape(TAPS * unit, width)
    reverse = unit % 16 == 0
    even, odd = list(range(0, devices, 2)), list(range(1, devices, 2))
    same_core = [even, odd[::-1] if reverse else odd]
    flip = (core if reverse else 0 * core).reshape(1)
    pieces = devices // 2 if reverse else 1

    def spread(columns):
        gathered = lax.all_gather(
            columns, "blocks", axis=0, tiled=True, axis_index_groups=same_core
        )
        return gathered.reshape(pieces, -1, columns.shape[1])

    side = lax.axis_index("groups")
    quarter = width // 4
    mine_late = jnp.where(side == 0, mine[:, :quarter], mine[:, quarter:half])
    late = spread(mine_late)
    weight = spread(mine[:, half:])
    late_got = lax.ppermute(late, "groups", [(0, 1), (1, 0)])

    face_list = face_rows.reshape(-1, 1)
    ordered, faces = call(
        functools.partial(faces_kernel, unit),
        (
            jax.ShapeDtypeStruct((points, width), BF16),
            jax.ShapeDtypeStruct((face_list.shape[0], width), BF16),
        ),
        32,
        4 * points * width * width,
        8 * points * width,
    )(features, face_list)
    received = exchange_faces(faces.reshape(8, -1, width), devices, index)
    table = jnp.concatenate([ordered] + received, axis=0)
    own_table = lax.dynamic_slice(table, (0, core * half), (table.shape[0], half))
    other_half = lax.dynamic_slice(table, (0, (1 - core) * half), (table.shape[0], half))
    other_table = lax.ppermute(other_half, "blocks", partner)
    other_neighbours = lax.ppermute(neighbours, "blocks", partner)
    whole = lambda tap: (0, 0)
    column = lambda tap: (0, tap)
    stacked = call(
        gather_kernel,
        jax.ShapeDtypeStruct((2 * points, TAPS * half), BF16),
        60,
        4 * TAPS * points * table.shape[0] * half,
        4 * TAPS * points * half,
        grid=(TAPS,),
        in_specs=[
            pl.BlockSpec((points, 128), whole),
            pl.BlockSpec((points, 128), whole),
            pl.BlockSpec((table.shape[0], half), whole),
            pl.BlockSpec((table.shape[0], half), whole),
        ],
        out_specs=pl.BlockSpec((2 * points, half), column),
    )(padded_taps(other_neighbours), padded_taps(neighbours), other_table, own_table)

    positions = jnp.arange(points, dtype=jnp.int32)
    target = serial_rank // points
    earlier = (target[None, :] == target[:, None]) & (serial_rank[None, :] < serial_rank[:, None])
    out_slot = target * capacity + jnp.sum(earlier.astype(jnp.int32), axis=1)
    anchor = serial_order // points
    before = (anchor[None, :] == anchor[:, None]) & (positions[None, :] < positions[:, None])
    in_slot = anchor * capacity + jnp.sum(before.astype(jnp.int32), axis=1)

    for_partner, own_part = conv_part(stacked, flip, [weight])
    from_partner = lax.ppermute(for_partner, "blocks", partner)
    for_partner_late, own_late = conv_part(stacked, flip, [late, late_got])
    from_partner_late = lax.ppermute(for_partner_late, "blocks", partner)

    outgoing = call(
        mix_kernel,
        jax.ShapeDtypeStruct((slots, width), BF16),
        32,
        2 * points * width * (width + slots),
        8 * points * width,
        in_specs=[pl.BlockSpec(memory_space=pltpu.SMEM)] + [pl.BlockSpec()] * 8,
    )(
        side.reshape(1),
        own_part,
        from_partner,
        own_late,
        from_partner_late,
        features,
        cpe_weight,
        cpe_gain.reshape(1, width),
        out_slot.reshape(1, points),
    )
    arrived = lax.all_to_all(
        outgoing.reshape(devices, capacity, width), "blocks", split_axis=0, concat_axis=0, tiled=True
    ).reshape(slots, width)

    key_weight = qkv_weight[:, width : 2 * width]
    qv_weight = jnp.concatenate([qkv_weight[:, :width], qkv_weight[:, 2 * width :]], axis=1).T
    back = call(
        block_kernel,
        jax.ShapeDtypeStruct((slots, width), BF16),
        48,
        20 * points * width * width,
        16 * width * width,
        scratch_shapes=[
            pltpu.VMEM((points, width), F32),
            pltpu.VMEM((2 * width, points), BF16),
            pltpu.VMEM((points, width), BF16),
            pltpu.VMEM((width, points), BF16),
            pltpu.VMEM((points, width), F32),
        ],
    )(
        arrived,
        in_slot.reshape(points, 1),
        in_slot.reshape(1, points),
        attn_gain.reshape(1, width),
        qv_weight,
        key_weight,
        proj_weight,
        mlp_gain.reshape(1, width),
        up_weight,
        down_weight,
    )
    returned = lax.all_to_all(
        back.reshape(devices, capacity, width), "blocks", split_axis=0, concat_axis=0, tiled=True
    ).reshape(slots, width)
    return call(
        return_kernel,
        jax.ShapeDtypeStruct((points, width), BF16),
        32,
        2 * points * slots * width,
        6 * points * width,
    )(returned, out_slot.reshape(points, 1))


def solution(mesh):
    placed = (
        P(("groups", "blocks"), None),
        P("blocks", None),
        P(),
        P(),
        P(),
        P(),
        P(),
        P(),
        P(),
        P(),
        P(("groups", "blocks"), None, None),
        P(("groups", "blocks"), None),
        P(("groups", "blocks")),
        P(("groups", "blocks")),
    )
    return jax.shard_map(
        body, mesh=mesh, in_specs=placed, out_specs=P(("groups", "blocks"), None), check_vma=False
    )
```

```python
import functools
import math

import jax
import jax.numpy as jnp
from jax import lax
from jax.experimental import pallas as pl
from jax.experimental.pallas import tpu as pltpu
from jax.sharding import PartitionSpec as P

HEADS = 32
GY = 8
HD = 16
TAPS = 27
EPSILON = 1e-05
STEPS_X = (-1, -1, -1, 0, 0, 1, 1, 1)
STEPS_Y = (-1, 0, 1, -1, 1, -1, 0, 1)
F32 = jnp.float32
BF16 = jnp.bfloat16
MIB = 1 << 20


def dot(left, right):
    return jnp.dot(left, right, preferred_element_type=F32)


def layer_norm(inputs, gain_vector):
    row_mean = jnp.mean(inputs, axis=-1, keepdims=True)
    centred = inputs - row_mean
    variance = jnp.mean(centred * centred, axis=-1, keepdims=True)
    return centred * lax.rsqrt(variance + EPSILON) * gain_vector


def one_hot(mask):
    return jnp.where(mask, 1.0, 0.0).astype(BF16)


def call(kernel, out_shape, limit, flops, moved, **extra):
    return pl.pallas_call(
        kernel,
        out_shape=out_shape,
        compiler_params=pltpu.CompilerParams(vmem_limit_bytes=limit * MIB),
        cost_estimate=pl.CostEstimate(flops=flops, bytes_accessed=moved, transcendentals=0),
        **extra,
    )


def faces_kernel(unit, features_ref, rows_ref, ordered_ref, faces_ref):
    points, width = features_ref.shape
    half = width // 2
    place = lax.broadcasted_iota(jnp.int32, (width, width), 1)
    within = lax.rem(place, half)
    source = (within // unit) * (2 * unit) + (place // half) * unit + lax.rem(place, unit)
    channel = lax.broadcasted_iota(jnp.int32, (width, width), 0)
    ordered = dot(features_ref[...], one_hot(channel == source)).astype(BF16)
    ordered_ref[...] = ordered
    row_ids = lax.broadcasted_iota(jnp.int32, (rows_ref.shape[0], points), 1)
    faces_ref[...] = dot(one_hot(rows_ref[...] == row_ids), ordered).astype(BF16)


def gather_kernel(first, other_rows, own_rows, other_table, own_table, *refs):
    out_ref = refs[-1]
    tap = first + pl.program_id(0)
    points, lanes = own_rows.shape
    chosen = lax.broadcasted_iota(jnp.int32, (points, lanes), 1) == tap
    row_ids = lax.broadcasted_iota(jnp.int32, (1, own_table.shape[0]), 1).astype(F32)
    for start, rows, table in ((0, other_rows, other_table), (points, own_rows, own_table)):
        column = jnp.sum(jnp.where(chosen, rows[...], 0.0), axis=1, keepdims=True)
        taken = dot(one_hot(column == row_ids), table[...]).astype(BF16)
        out_ref[start : start + points] = taken


def gather_part(first, count, tables, stacked):
    points, lanes = tables[1].shape
    height, half = tables[3].shape
    whole = lambda tap: (0, 0)
    extra = [] if stacked is None else [stacked]
    return call(
        functools.partial(gather_kernel, first),
        jax.ShapeDtypeStruct((2 * points, TAPS * half), BF16),
        60,
        4 * count * points * height * half,
        4 * count * points * half,
        grid=(count,),
        in_specs=[pl.BlockSpec((points, lanes), whole)] * 2
        + [pl.BlockSpec((height, half), whole)] * 2
        + [pl.BlockSpec(memory_space=pl.ANY)] * len(extra),
        out_specs=pl.BlockSpec((2 * points, half), lambda tap: (0, first + tap)),
        input_output_aliases={} if stacked is None else {4: 0},
    )(*tables, *extra)


def conv_kernel(starts_ref, stacked_ref, *refs):
    count = len(refs) - 4
    pieces, (other_ref, own_ref, held, sems) = refs[:count], refs[count:]
    step = pl.program_id(0)
    depth, points = stacked_ref.shape[1], own_ref.shape[0]
    copies = []
    for at, piece in enumerate(pieces):
        start = pl.multiple_of(starts_ref[at], 32)
        copies.append(
            pltpu.make_async_copy(
                piece, held.at[pl.ds(start, piece.shape[0])], sems.at[at]
            )
        )

    @pl.when(step == 0)
    def _():
        for copy in copies:
            copy.start()
        other_ref[...] = jnp.zeros_like(other_ref)
        own_ref[...] = jnp.zeros_like(own_ref)
        for copy in copies:
            copy.wait()

    weight = held[pl.ds(pl.multiple_of(step * depth, 256), depth)]
    other_ref[...] += dot(stacked_ref[:points], weight)
    own_ref[...] += dot(stacked_ref[points:], weight)


def conv_part(stacked, starts, pieces):
    points, depth = stacked.shape
    width = pieces[0].shape[1]
    steps = 3
    step = depth // steps
    return call(
        conv_kernel,
        (jax.ShapeDtypeStruct((points // 2, width), F32),) * 2,
        60,
        2 * points * depth * width,
        2 * depth * (points + width),
        grid=(steps,),
        in_specs=[
            pl.BlockSpec(memory_space=pltpu.SMEM),
            pl.BlockSpec((points, step), lambda k: (0, k)),
        ]
        + [pl.BlockSpec(memory_space=pl.ANY)] * len(pieces),
        out_specs=[pl.BlockSpec((points // 2, width), lambda k: (0, 0))] * 2,
        scratch_shapes=[
            pltpu.VMEM((depth, width), BF16),
            pltpu.SemaphoreType.DMA((len(pieces),)),
        ],
    )(starts, stacked, *pieces)


def mix_kernel(own_ref, got_ref, features_ref, weight_ref, gain_ref, slot_ref, out_ref):
    convolved = (own_ref[...] + got_ref[...]).astype(BF16)
    linear = dot(convolved, weight_ref[...])
    mixed = (features_ref[...].astype(F32) + layer_norm(linear, gain_ref[...])).astype(BF16)
    slots = lax.broadcasted_iota(jnp.int32, (out_ref.shape[0], mixed.shape[0]), 0)
    out_ref[...] = dot(one_hot(slots == slot_ref[...]), mixed).astype(BF16)


def block_kernel(
    arrived_ref,
    slot_col_ref,
    slot_row_ref,
    attn_gain_ref,
    qv_ref,
    key_ref,
    proj_ref,
    mlp_gain_ref,
    up_ref,
    down_ref,
    out_ref,
    serial_ref,
    qv_cols_ref,
    keys_ref,
    heads_ref,
    total_ref,
):
    slots = arrived_ref.shape[0]
    points, width = serial_ref.shape
    slot_ids = lax.broadcasted_iota(jnp.int32, (points, slots), 1)
    serial = dot(one_hot(slot_col_ref[...] == slot_ids), arrived_ref[...])
    serial_ref[...] = serial
    normed = layer_norm(serial, attn_gain_ref[...]).astype(BF16)
    keys_ref[...] = dot(normed, key_ref[...]).astype(BF16)
    factor = math.log2(math.e) / math.sqrt(HD)
    contract_last = (((1,), (1,)), ((), ()))
    qv_cols_ref[:width] = (
        lax.dot_general(qv_ref[:width], normed, contract_last, preferred_element_type=F32) * factor
    ).astype(BF16)
    qv_cols_ref[width:] = lax.dot_general(
        qv_ref[width:], normed, contract_last, preferred_element_type=F32
    ).astype(BF16)
    ones = jnp.ones((HD, points), BF16)
    per_group = 128 // HD
    head_of_row = lax.broadcasted_iota(jnp.int32, (128, points), 0) // HD

    for group in range(HEADS // per_group):
        base = group * 128

        def attend(head, carry):
            group_queries = qv_cols_ref[base : base + 128]
            queries = jnp.where(head_of_row == head, group_queries.astype(F32), 0.0).astype(BF16)
            scores = dot(keys_ref[:, base : base + 128], queries)
            weights = jnp.exp2(scores - jnp.max(scores, axis=0, keepdims=True)).astype(BF16)
            at = pl.multiple_of(base + head * HD, HD)
            values = qv_cols_ref[pl.ds(width + at, HD)]
            sums = dot(jnp.concatenate([values, ones], axis=0), weights)
            heads_ref[pl.ds(at, HD)] = (sums[:HD] / sums[HD : HD + 1]).astype(BF16)
            return carry

        lax.fori_loop(0, per_group, attend, 0, unroll=2)

    update = lax.dot_general(
        heads_ref[...], proj_ref[...], (((0,), (0,)), ((), ())), preferred_element_type=F32
    )
    attended = (serial_ref[...] + update).astype(BF16).astype(F32)
    hidden_in = layer_norm(attended, mlp_gain_ref[...]).astype(BF16)
    total_ref[...] = attended
    chunk = width
    for start in range(0, up_ref.shape[1], chunk):
        raised = dot(hidden_in, up_ref[:, start : start + chunk])
        hidden = (raised * (1.0 + lax.erf(raised * math.sqrt(0.5))) * 0.5).astype(BF16)
        total_ref[...] += dot(hidden, down_ref[start : start + chunk])
    finished = total_ref[...].astype(BF16)
    slot_rows = lax.broadcasted_iota(jnp.int32, (slots, points), 0)
    out_ref[...] = dot(one_hot(slot_rows == slot_row_ref[...]), finished).astype(BF16)


def return_kernel(arrived_ref, slot_ref, out_ref):
    slot_ids = lax.broadcasted_iota(jnp.int32, (out_ref.shape[0], arrived_ref.shape[0]), 1)
    out_ref[...] = dot(one_hot(slot_ref[...] == slot_ids), arrived_ref[...]).astype(BF16)


def exchange_faces(faces, devices, index):
    zero = jnp.zeros_like(faces[0])
    received = [zero] * 8

    def valid(source, dx, dy):
        return 0 <= source // GY + dx < devices // GY and 0 <= source % GY + dy < GY

    if devices == 2 * GY:
        lower = index < GY
        for dy in (-1, 0, 1):
            payload = jnp.where(lower, faces[6 + dy], faces[1 + dy])
            pairs = []
            for source in range(devices):
                dx = 1 if source < GY else -1
                if valid(source, dx, dy):
                    pairs.append((source, source + dx * GY + dy))
            got = lax.ppermute(payload, "blocks", pairs)
            received[1 + dy] = jnp.where(lower, got, zero)
            received[6 + dy] = jnp.where(lower, zero, got)
        rest = (3, 4)
    else:
        rest = range(8)
    for facing in rest:
        dx, dy = STEPS_X[facing], STEPS_Y[facing]
        pairs = [
            (source, source + dx * GY + dy) for source in range(devices) if valid(source, dx, dy)
        ]
        received[facing] = lax.ppermute(faces[facing], "blocks", pairs)
    return received


def way_round(devices):
    chips = devices // 2
    cycle = list(range(0, chips, 2)) + list(range(chips - 1, 0, -2))
    pairs, origins = [], [[0] * chips for _ in range(devices)]
    for place, chip in enumerate(cycle):
        for core, way in ((0, 1), (1, -1)):
            pairs.append((2 * chip + core, 2 * cycle[(place + way) % chips] + core))
            for step in range(chips):
                origins[2 * chip + core][step] = cycle[(place - way * step) % chips]
    return pairs, origins


def padded_taps(neighbours):
    points = neighbours.shape[0]
    own = jnp.arange(points, dtype=jnp.int32)[:, None]
    rest = jnp.zeros((points, 128 - TAPS), jnp.int32)
    middle = TAPS // 2
    return jnp.concatenate(
        [neighbours[:, :middle], own, neighbours[:, middle:], rest], axis=1
    ).astype(F32)


def body(
    features,
    conv_weight,
    cpe_weight,
    cpe_gain,
    attn_gain,
    qkv_weight,
    proj_weight,
    mlp_gain,
    up_weight,
    down_weight,
    face_rows,
    neighbours,
    serial_rank,
    serial_order,
):
    points, width = features.shape
    half = width // 2
    devices = lax.axis_size("blocks")
    index = lax.axis_index("blocks")
    core = lax.rem(index, 2)
    partner = [(source, source ^ 1) for source in range(devices)]
    capacity = 2 * points // devices
    slots = devices * capacity

    unit = conv_weight.shape[0] // TAPS
    units = conv_weight.reshape(TAPS, unit, width)
    kept, sent = units[0::2], units[1::2]
    got = lax.ppermute(sent, "blocks", partner)
    mine = jnp.where(
        core == 0, jnp.concatenate([kept, got]), jnp.concatenate([got, kept])
    ).reshape(TAPS * unit, width)
    face_list = face_rows.reshape(-1, 1)
    ordered, faces = call(
        functools.partial(faces_kernel, unit),
        (
            jax.ShapeDtypeStruct((points, width), BF16),
            jax.ShapeDtypeStruct((face_list.shape[0], width), BF16),
        ),
        32,
        4 * points * width * width,
        8 * points * width,
    )(features, face_list)
    round_trip = devices == 16
    pairs, origins = way_round(devices)
    ring = [mine]

    def pass_on(*beside):
        if not round_trip:
            return beside
        tied = lax.optimization_barrier((ring[-1], *beside))
        ring[-1] = tied[0]
        ring.append(lax.ppermute(ring[-1], "blocks", pairs))
        return tied[1:]

    (faces,) = pass_on(faces)
    received = exchange_faces(faces.reshape(8, -1, width), devices, index)
    pass_on()
    received = pass_on(*received)
    table = jnp.concatenate([ordered, *received], axis=0)
    own_table = lax.dynamic_slice(table, (0, core * half), (table.shape[0], half))
    other_half = lax.dynamic_slice(table, (0, (1 - core) * half), (table.shape[0], half))
    other_table = lax.ppermute(other_half, "blocks", partner)
    other_neighbours = lax.ppermute(neighbours, "blocks", partner)
    tables = (padded_taps(other_neighbours), padded_taps(neighbours), other_table, own_table)
    stacked = None
    for first, count in ((0, 4), (4, 8), (12, 8), (20, 7)):
        stacked = gather_part(first, count, tables, stacked)
        (stacked,) = pass_on(stacked)
    if round_trip:
        starts = jnp.array(origins, jnp.int32)[index] * mine.shape[0]
    else:
        groups = [list(range(first, devices, 2)) for first in range(2)]
        ring = [lax.all_gather(mine, "blocks", axis=0, tiled=True, axis_index_groups=groups)]
        starts = jnp.zeros((1,), jnp.int32)

    positions = jnp.arange(points, dtype=jnp.int32)
    target = serial_rank // points
    earlier = (target[None, :] == target[:, None]) & (serial_rank[None, :] < serial_rank[:, None])
    out_slot = target * capacity + jnp.sum(earlier.astype(jnp.int32), axis=1)
    anchor = serial_order // points
    before = (anchor[None, :] == anchor[:, None]) & (positions[None, :] < positions[:, None])
    in_slot = anchor * capacity + jnp.sum(before.astype(jnp.int32), axis=1)

    for_partner, own_part = conv_part(stacked, starts, ring)
    from_partner = lax.ppermute(for_partner, "blocks", partner)

    outgoing = call(
        mix_kernel,
        jax.ShapeDtypeStruct((slots, width), BF16),
        32,
        2 * points * width * (width + slots),
        8 * points * width,
    )(
        own_part,
        from_partner,
        features,
        cpe_weight,
        cpe_gain.reshape(1, width),
        out_slot.reshape(1, points),
    )
    arrived = lax.all_to_all(
        outgoing.reshape(devices, capacity, width), "blocks", split_axis=0, concat_axis=0, tiled=True
    ).reshape(slots, width)

    key_weight = qkv_weight[:, width : 2 * width]
    qv_weight = jnp.concatenate([qkv_weight[:, :width], qkv_weight[:, 2 * width :]], axis=1).T
    back = call(
        block_kernel,
        jax.ShapeDtypeStruct((slots, width), BF16),
        48,
        20 * points * width * width,
        16 * width * width,
        scratch_shapes=[
            pltpu.VMEM((points, width), F32),
            pltpu.VMEM((2 * width, points), BF16),
            pltpu.VMEM((points, width), BF16),
            pltpu.VMEM((width, points), BF16),
            pltpu.VMEM((points, width), F32),
        ],
    )(
        arrived,
        in_slot.reshape(points, 1),
        in_slot.reshape(1, points),
        attn_gain.reshape(1, width),
        qv_weight,
        key_weight,
        proj_weight,
        mlp_gain.reshape(1, width),
        up_weight,
        down_weight,
    )
    returned = lax.all_to_all(
        back.reshape(devices, capacity, width), "blocks", split_axis=0, concat_axis=0, tiled=True
    ).reshape(slots, width)
    return call(
        return_kernel,
        jax.ShapeDtypeStruct((points, width), BF16),
        32,
        2 * points * slots * width,
        6 * points * width,
    )(returned, out_slot.reshape(points, 1))


def solution(mesh):
    placed = (
        P(("groups", "blocks"), None),
        P("blocks", None),
        P(),
        P(),
        P(),
        P(),
        P(),
        P(),
        P(),
        P(),
        P(("groups", "blocks"), None, None),
        P(("groups", "blocks"), None),
        P(("groups", "blocks")),
        P(("groups", "blocks")),
    )
    return jax.shard_map(
        body, mesh=mesh, in_specs=placed, out_specs=P(("groups", "blocks"), None), check_vma=False
    )
```

```python
import functools
import math

import jax
import jax.numpy as jnp
from jax import lax
from jax.experimental import pallas as pl
from jax.experimental.pallas import tpu as pltpu
from jax.sharding import PartitionSpec as P

HEADS = 32
GY = 8
HD = 16
TAPS = 27
EPSILON = 1e-05
STEPS_X = (-1, -1, -1, 0, 0, 1, 1, 1)
STEPS_Y = (-1, 0, 1, -1, 1, -1, 0, 1)
F32 = jnp.float32
BF16 = jnp.bfloat16
MIB = 1 << 20


def dot(left, right):
    return jnp.dot(left, right, preferred_element_type=F32)


def layer_norm(inputs, gain_vector):
    row_mean = jnp.mean(inputs, axis=-1, keepdims=True)
    centred = inputs - row_mean
    variance = jnp.mean(centred * centred, axis=-1, keepdims=True)
    return centred * lax.rsqrt(variance + EPSILON) * gain_vector


def one_hot(mask):
    return jnp.where(mask, 1.0, 0.0).astype(BF16)


def call(kernel, out_shape, limit, flops, moved, **extra):
    return pl.pallas_call(
        kernel,
        out_shape=out_shape,
        compiler_params=pltpu.CompilerParams(vmem_limit_bytes=limit * MIB),
        cost_estimate=pl.CostEstimate(flops=flops, bytes_accessed=moved, transcendentals=0),
        **extra,
    )


def faces_kernel(unit, features_ref, rows_ref, ordered_ref, faces_ref):
    points, width = features_ref.shape
    half = width // 2
    place = lax.broadcasted_iota(jnp.int32, (width, width), 1)
    within = lax.rem(place, half)
    source = (within // unit) * (2 * unit) + (place // half) * unit + lax.rem(place, unit)
    channel = lax.broadcasted_iota(jnp.int32, (width, width), 0)
    ordered = dot(features_ref[...], one_hot(channel == source)).astype(BF16)
    ordered_ref[...] = ordered
    row_ids = lax.broadcasted_iota(jnp.int32, (rows_ref.shape[0], points), 1)
    faces_ref[...] = dot(one_hot(rows_ref[...] == row_ids), ordered).astype(BF16)


def gather_kernel(first, other_rows, own_rows, other_table, own_table, *refs):
    out_ref = refs[-1]
    tap = first + pl.program_id(0)
    points, lanes = own_rows.shape
    chosen = lax.broadcasted_iota(jnp.int32, (points, lanes), 1) == tap
    row_ids = lax.broadcasted_iota(jnp.int32, (1, own_table.shape[0]), 1).astype(F32)
    for start, rows, table in ((0, other_rows, other_table), (points, own_rows, own_table)):
        column = jnp.sum(jnp.where(chosen, rows[...], 0.0), axis=1, keepdims=True)
        taken = dot(one_hot(column == row_ids), table[...]).astype(BF16)
        out_ref[start : start + points] = taken


def gather_part(first, count, tables, stacked):
    points, lanes = tables[1].shape
    height, half = tables[3].shape
    whole = lambda tap: (0, 0)
    extra = [] if stacked is None else [stacked]
    return call(
        functools.partial(gather_kernel, first),
        jax.ShapeDtypeStruct((2 * points, TAPS * half), BF16),
        60,
        4 * count * points * height * half,
        4 * count * points * half,
        grid=(count,),
        in_specs=[pl.BlockSpec((points, lanes), whole)] * 2
        + [pl.BlockSpec((height, half), whole)] * 2
        + [pl.BlockSpec(memory_space=pl.ANY)] * len(extra),
        out_specs=pl.BlockSpec((2 * points, half), lambda tap: (0, first + tap)),
        input_output_aliases={} if stacked is None else {4: 0},
    )(*tables, *extra)


def conv_kernel(slots, first, places_ref, stacked_ref, *refs):
    pieces = refs[: sum(slots)]
    other_ref, own_ref, lhs, held, sems = refs[-5:]
    points = own_ref.shape[0]
    length = held.shape[1]
    copies, taken = [], 0
    for at, count in enumerate(slots):
        column = pl.multiple_of(places_ref[2 * at], 128)
        row = pl.multiple_of(places_ref[2 * at + 1], 16)
        copy = pltpu.make_async_copy(
            stacked_ref.at[:, pl.ds(column, length)], lhs.at[at], sems.at[at, 0]
        )
        copy.start()
        copies.append([copy])
        short = count * pieces[taken].shape[0]
        edge = length - short
        if edge:
            held[at, :edge] = jnp.zeros((edge, held.shape[2]), BF16)
            held[at, length - edge :] = jnp.zeros((edge, held.shape[2]), BF16)
        for part in range(count):
            piece = pieces[taken]
            size = piece.shape[0]
            copy = pltpu.make_async_copy(
                piece, held.at[at, pl.ds(row + part * size, size)], sems.at[at, 1 + part]
            )
            copy.start()
            copies[-1].append(copy)
            taken += 1
    for at in range(len(slots)):
        for copy in copies[at]:
            copy.wait()
        for half, ref in enumerate((other_ref, own_ref)):
            product = dot(lhs[at, half * points : (half + 1) * points], held[at])
            if at > 0:
                ref[...] += product
            elif first:
                ref[...] = product
            else:
                ref[...] = refs[half - 7][...] + product


def conv_part(stacked, places, pieces, before, length):
    points, depth = stacked.shape
    width = pieces[0][0].shape[1]
    slots = [len(parts) for parts in pieces]
    flat = [piece for parts in pieces for piece in parts]
    return call(
        functools.partial(conv_kernel, slots, before is None),
        (jax.ShapeDtypeStruct((points // 2, width), F32),) * 2,
        40,
        2 * points * length * width * len(slots),
        2 * length * (points + width) * len(slots),
        in_specs=[
            pl.BlockSpec(memory_space=pltpu.SMEM),
            pl.BlockSpec(memory_space=pl.ANY),
        ]
        + [pl.BlockSpec(memory_space=pl.ANY)] * len(flat)
        + ([] if before is None else [pl.BlockSpec()] * 2),
        input_output_aliases=(
            {} if before is None else {2 + len(flat): 0, 3 + len(flat): 1}
        ),
        scratch_shapes=[
            pltpu.VMEM((len(slots), points, length), BF16),
            pltpu.VMEM((len(slots), length, width), BF16),
            pltpu.SemaphoreType.DMA((len(slots), 3)),
        ],
    )(places.reshape(-1), stacked, *flat, *(before or ()))


def mix_kernel(own_ref, got_ref, features_ref, weight_ref, gain_ref, slot_ref, out_ref):
    convolved = (own_ref[...] + got_ref[...]).astype(BF16)
    linear = dot(convolved, weight_ref[...])
    mixed = (features_ref[...].astype(F32) + layer_norm(linear, gain_ref[...])).astype(BF16)
    slots = lax.broadcasted_iota(jnp.int32, (out_ref.shape[0], mixed.shape[0]), 0)
    out_ref[...] = dot(one_hot(slots == slot_ref[...]), mixed).astype(BF16)


def block_kernel(
    arrived_ref,
    slot_col_ref,
    slot_row_ref,
    attn_gain_ref,
    qv_ref,
    key_ref,
    proj_ref,
    mlp_gain_ref,
    up_ref,
    down_ref,
    out_ref,
    serial_ref,
    qv_cols_ref,
    keys_ref,
    heads_ref,
    total_ref,
):
    slots = arrived_ref.shape[0]
    points, width = serial_ref.shape
    slot_ids = lax.broadcasted_iota(jnp.int32, (points, slots), 1)
    serial = dot(one_hot(slot_col_ref[...] == slot_ids), arrived_ref[...])
    serial_ref[...] = serial
    normed = layer_norm(serial, attn_gain_ref[...]).astype(BF16)
    keys_ref[...] = dot(normed, key_ref[...]).astype(BF16)
    factor = math.log2(math.e) / math.sqrt(HD)
    contract_last = (((1,), (1,)), ((), ()))
    qv_cols_ref[:width] = (
        lax.dot_general(qv_ref[:width], normed, contract_last, preferred_element_type=F32) * factor
    ).astype(BF16)
    qv_cols_ref[width:] = lax.dot_general(
        qv_ref[width:], normed, contract_last, preferred_element_type=F32
    ).astype(BF16)
    ones = jnp.ones((HD, points), BF16)
    per_group = 128 // HD
    head_of_row = lax.broadcasted_iota(jnp.int32, (128, points), 0) // HD

    for group in range(HEADS // per_group):
        base = group * 128

        def attend(head, carry):
            group_queries = qv_cols_ref[base : base + 128]
            queries = jnp.where(head_of_row == head, group_queries.astype(F32), 0.0).astype(BF16)
            scores = dot(keys_ref[:, base : base + 128], queries)
            weights = jnp.exp2(scores - jnp.max(scores, axis=0, keepdims=True)).astype(BF16)
            at = pl.multiple_of(base + head * HD, HD)
            values = qv_cols_ref[pl.ds(width + at, HD)]
            sums = dot(jnp.concatenate([values, ones], axis=0), weights)
            heads_ref[pl.ds(at, HD)] = (sums[:HD] / sums[HD : HD + 1]).astype(BF16)
            return carry

        lax.fori_loop(0, per_group, attend, 0, unroll=2)

    update = lax.dot_general(
        heads_ref[...], proj_ref[...], (((0,), (0,)), ((), ())), preferred_element_type=F32
    )
    attended = (serial_ref[...] + update).astype(BF16).astype(F32)
    hidden_in = layer_norm(attended, mlp_gain_ref[...]).astype(BF16)
    total_ref[...] = attended
    chunk = width
    for start in range(0, up_ref.shape[1], chunk):
        raised = dot(hidden_in, up_ref[:, start : start + chunk])
        hidden = (raised * (1.0 + lax.erf(raised * math.sqrt(0.5))) * 0.5).astype(BF16)
        total_ref[...] += dot(hidden, down_ref[start : start + chunk])
    finished = total_ref[...].astype(BF16)
    slot_rows = lax.broadcasted_iota(jnp.int32, (slots, points), 0)
    out_ref[...] = dot(one_hot(slot_rows == slot_row_ref[...]), finished).astype(BF16)


def return_kernel(arrived_ref, slot_ref, out_ref):
    slot_ids = lax.broadcasted_iota(jnp.int32, (out_ref.shape[0], arrived_ref.shape[0]), 1)
    out_ref[...] = dot(one_hot(slot_ref[...] == slot_ids), arrived_ref[...]).astype(BF16)


def exchange_faces(faces, devices, index):
    zero = jnp.zeros_like(faces[0])
    received = [zero] * 8

    def valid(source, dx, dy):
        return 0 <= source // GY + dx < devices // GY and 0 <= source % GY + dy < GY

    if devices == 2 * GY:
        lower = index < GY
        for dy in (-1, 0, 1):
            payload = jnp.where(lower, faces[6 + dy], faces[1 + dy])
            pairs = []
            for source in range(devices):
                dx = 1 if source < GY else -1
                if valid(source, dx, dy):
                    pairs.append((source, source + dx * GY + dy))
            got = lax.ppermute(payload, "blocks", pairs)
            received[1 + dy] = jnp.where(lower, got, zero)
            received[6 + dy] = jnp.where(lower, zero, got)
        rest = (3, 4)
    else:
        rest = range(8)
    for facing in rest:
        dx, dy = STEPS_X[facing], STEPS_Y[facing]
        pairs = [
            (source, source + dx * GY + dy) for source in range(devices) if valid(source, dx, dy)
        ]
        received[facing] = lax.ppermute(faces[facing], "blocks", pairs)
    return received


def way_round(devices, rows, length):
    chips = devices // 2
    cycle = list(range(0, chips, 2)) + list(range(chips - 1, 0, -2))
    back, on = [], []
    places = [None] * devices
    for place, chip in enumerate(cycle):
        for core in range(2):
            me = 2 * chip + core
            back.append((me, 2 * cycle[(place + 1) % chips] + core))
            on.append((me, 2 * cycle[place - 1] + core))
            order = [0]
            for step in range(1, chips // 2):
                order += [-step, step]
            order.append(chips // 2)
            places[me] = []
            for offset in order:
                start = cycle[(place + offset) % chips] * rows
                column = min(start // 128 * 128, chips * rows - length)
                places[me].append((column, start - column))
    return back, on, places


def padded_taps(neighbours):
    points = neighbours.shape[0]
    own = jnp.arange(points, dtype=jnp.int32)[:, None]
    rest = jnp.zeros((points, 128 - TAPS), jnp.int32)
    middle = TAPS // 2
    return jnp.concatenate(
        [neighbours[:, :middle], own, neighbours[:, middle:], rest], axis=1
    ).astype(F32)


def body(
    features,
    conv_weight,
    cpe_weight,
    cpe_gain,
    attn_gain,
    qkv_weight,
    proj_weight,
    mlp_gain,
    up_weight,
    down_weight,
    face_rows,
    neighbours,
    serial_rank,
    serial_order,
):
    points, width = features.shape
    half = width // 2
    devices = lax.axis_size("blocks")
    index = lax.axis_index("blocks")
    core = lax.rem(index, 2)
    partner = [(source, source ^ 1) for source in range(devices)]
    capacity = 2 * points // devices
    slots = devices * capacity

    unit = conv_weight.shape[0] // TAPS
    units = conv_weight.reshape(TAPS, unit, width)
    kept, sent = units[0::2], units[1::2]
    got = lax.ppermute(sent, "blocks", partner)
    mine = jnp.where(
        core == 0, jnp.concatenate([kept, got]), jnp.concatenate([got, kept])
    ).reshape(TAPS * unit, width)
    face_list = face_rows.reshape(-1, 1)
    ordered, faces = call(
        functools.partial(faces_kernel, unit),
        (
            jax.ShapeDtypeStruct((points, width), BF16),
            jax.ShapeDtypeStruct((face_list.shape[0], width), BF16),
        ),
        32,
        4 * points * width * width,
        8 * points * width,
    )(features, face_list)
    round_trip = devices == 16
    rows = mine.shape[0]
    length = -(-(rows + 127) // 128) * 128 if round_trip else rows * (devices // 2)
    back_pairs, on_pairs, places = way_round(devices, rows, length)
    back, on = [mine], [mine]

    def pass_on(*beside):
        if not round_trip:
            return beside
        tied = lax.optimization_barrier((back[-1], on[-1], *beside))
        first, second = tied[:2]
        back[-1], on[-1] = first, second
        if len(back) == devices // 4:
            first, second = first[: rows // 2], second[rows // 2 :]
        back.append(lax.ppermute(first, "blocks", back_pairs))
        on.append(lax.ppermute(second, "blocks", on_pairs))
        return tied[2:]

    (faces,) = pass_on(faces)
    received = exchange_faces(faces.reshape(8, -1, width), devices, index)
    received = pass_on(*received)
    table = jnp.concatenate([ordered, *received], axis=0)
    own_table = lax.dynamic_slice(table, (0, core * half), (table.shape[0], half))
    other_half = lax.dynamic_slice(table, (0, (1 - core) * half), (table.shape[0], half))
    other_table = lax.ppermute(other_half, "blocks", partner)
    other_neighbours = lax.ppermute(neighbours, "blocks", partner)
    tables = (padded_taps(other_neighbours), padded_taps(neighbours), other_table, own_table)
    stacked = gather_part(0, 16, tables, None)
    (stacked,) = pass_on(stacked)
    stacked = gather_part(16, TAPS - 16, tables, stacked)
    if round_trip:
        places = jnp.array(places, jnp.int32)[index]
        early = [[mine], [back[1]], [on[1]], [back[2]], [on[2]]]
        sums = conv_part(stacked, places[:5], early, None, length)
        sums = pass_on(*sums)
        sums = conv_part(stacked, places[5:7], [[back[3]], [on[3]]], sums, length)
        sums = conv_part(stacked, places[7:], [[back[4], on[4]]], sums, length)
    else:
        groups = [list(range(first, devices, 2)) for first in range(2)]
        weight = lax.all_gather(mine, "blocks", axis=0, tiled=True, axis_index_groups=groups)
        sums = conv_part(stacked, jnp.zeros((1, 2), jnp.int32), [[weight]], None, length)
    for_partner, own_part = sums

    positions = jnp.arange(points, dtype=jnp.int32)
    target = serial_rank // points
    earlier = (target[None, :] == target[:, None]) & (serial_rank[None, :] < serial_rank[:, None])
    out_slot = target * capacity + jnp.sum(earlier.astype(jnp.int32), axis=1)
    anchor = serial_order // points
    before = (anchor[None, :] == anchor[:, None]) & (positions[None, :] < positions[:, None])
    in_slot = anchor * capacity + jnp.sum(before.astype(jnp.int32), axis=1)

    from_partner = lax.ppermute(for_partner, "blocks", partner)

    outgoing = call(
        mix_kernel,
        jax.ShapeDtypeStruct((slots, width), BF16),
        32,
        2 * points * width * (width + slots),
        8 * points * width,
    )(
        own_part,
        from_partner,
        features,
        cpe_weight,
        cpe_gain.reshape(1, width),
        out_slot.reshape(1, points),
    )
    arrived = lax.all_to_all(
        outgoing.reshape(devices, capacity, width), "blocks", split_axis=0, concat_axis=0, tiled=True
    ).reshape(slots, width)

    key_weight = qkv_weight[:, width : 2 * width]
    qv_weight = jnp.concatenate([qkv_weight[:, :width], qkv_weight[:, 2 * width :]], axis=1).T
    back = call(
        block_kernel,
        jax.ShapeDtypeStruct((slots, width), BF16),
        48,
        20 * points * width * width,
        16 * width * width,
        scratch_shapes=[
            pltpu.VMEM((points, width), F32),
            pltpu.VMEM((2 * width, points), BF16),
            pltpu.VMEM((points, width), BF16),
            pltpu.VMEM((width, points), BF16),
            pltpu.VMEM((points, width), F32),
        ],
    )(
        arrived,
        in_slot.reshape(points, 1),
        in_slot.reshape(1, points),
        attn_gain.reshape(1, width),
        qv_weight,
        key_weight,
        proj_weight,
        mlp_gain.reshape(1, width),
        up_weight,
        down_weight,
    )
    returned = lax.all_to_all(
        back.reshape(devices, capacity, width), "blocks", split_axis=0, concat_axis=0, tiled=True
    ).reshape(slots, width)
    return call(
        return_kernel,
        jax.ShapeDtypeStruct((points, width), BF16),
        32,
        2 * points * slots * width,
        6 * points * width,
    )(returned, out_slot.reshape(points, 1))


def solution(mesh):
    placed = (
        P(("groups", "blocks"), None),
        P("blocks", None),
        P(),
        P(),
        P(),
        P(),
        P(),
        P(),
        P(),
        P(),
        P(("groups", "blocks"), None, None),
        P(("groups", "blocks"), None),
        P(("groups", "blocks")),
        P(("groups", "blocks")),
    )
    return jax.shard_map(
        body, mesh=mesh, in_specs=placed, out_specs=P(("groups", "blocks"), None), check_vma=False
    )
```

```python
import functools
import math

import jax
import jax.numpy as jnp
from jax import lax
from jax.experimental import pallas as pl
from jax.experimental.pallas import tpu as pltpu
from jax.sharding import PartitionSpec as P

HEADS = 32
GY = 8
HD = 16
TAPS = 27
EPSILON = 1e-05
STEPS_X = (-1, -1, -1, 0, 0, 1, 1, 1)
STEPS_Y = (-1, 0, 1, -1, 1, -1, 0, 1)
F32 = jnp.float32
BF16 = jnp.bfloat16
MIB = 1 << 20


def dot(left, right):
    return jnp.dot(left, right, preferred_element_type=F32)


def layer_norm(inputs, gain_vector):
    row_mean = jnp.mean(inputs, axis=-1, keepdims=True)
    centred = inputs - row_mean
    variance = jnp.mean(centred * centred, axis=-1, keepdims=True)
    return centred * lax.rsqrt(variance + EPSILON) * gain_vector


def one_hot(mask):
    return jnp.where(mask, 1.0, 0.0).astype(BF16)


def call(kernel, out_shape, limit, flops, moved, **extra):
    return pl.pallas_call(
        kernel,
        out_shape=out_shape,
        compiler_params=pltpu.CompilerParams(vmem_limit_bytes=limit * MIB),
        cost_estimate=pl.CostEstimate(flops=flops, bytes_accessed=moved, transcendentals=0),
        **extra,
    )


def faces_kernel(unit, features_ref, rows_ref, ordered_ref, faces_ref):
    points, width = features_ref.shape
    half = width // 2
    place = lax.broadcasted_iota(jnp.int32, (width, width), 1)
    within = lax.rem(place, half)
    source = (within // unit) * (2 * unit) + (place // half) * unit + lax.rem(place, unit)
    channel = lax.broadcasted_iota(jnp.int32, (width, width), 0)
    ordered = dot(features_ref[...], one_hot(channel == source)).astype(BF16)
    ordered_ref[...] = ordered
    row_ids = lax.broadcasted_iota(jnp.int32, (rows_ref.shape[0], points), 1)
    faces_ref[...] = dot(one_hot(rows_ref[...] == row_ids), ordered).astype(BF16)


def gather_kernel(rows_ref, table_ref, out_ref):
    chosen = lax.broadcasted_iota(jnp.int32, rows_ref.shape, 1) == pl.program_id(0)
    row_ids = lax.broadcasted_iota(jnp.int32, (1, table_ref.shape[0]), 1).astype(F32)
    column = jnp.sum(jnp.where(chosen, rows_ref[...], 0.0), axis=1, keepdims=True)
    out_ref[...] = dot(one_hot(column == row_ids), table_ref[...]).astype(BF16)


def gather_block(rows, table):
    points, lanes = rows.shape
    height, half = table.shape
    whole = lambda tap: (0, 0)
    return call(
        gather_kernel,
        jax.ShapeDtypeStruct((points, TAPS * half), BF16),
        60,
        2 * TAPS * points * height * half,
        2 * TAPS * points * half,
        grid=(TAPS,),
        in_specs=[pl.BlockSpec((points, lanes), whole), pl.BlockSpec((height, half), whole)],
        out_specs=pl.BlockSpec((points, half), lambda tap: (0, tap)),
    )(rows, table)


def conv_kernel(slots, first, places_ref, other_stacked, own_stacked, *refs):
    pieces = refs[: sum(slots)]
    other_ref, own_ref, lhs, held, sems = refs[-5:]
    length = held.shape[1]
    copies, taken = [], 0
    for at, count in enumerate(slots):
        column = pl.multiple_of(places_ref[2 * at], 128)
        row = pl.multiple_of(places_ref[2 * at + 1], 16)
        copies.append([])
        for half, stacked in enumerate((other_stacked, own_stacked)):
            copy = pltpu.make_async_copy(
                stacked.at[:, pl.ds(column, length)], lhs.at[at, half], sems.at[at, half]
            )
            copy.start()
            copies[-1].append(copy)
        short = count * pieces[taken].shape[0]
        edge = length - short
        if edge:
            held[at, :edge] = jnp.zeros((edge, held.shape[2]), BF16)
            held[at, length - edge :] = jnp.zeros((edge, held.shape[2]), BF16)
        for part in range(count):
            piece = pieces[taken]
            size = piece.shape[0]
            copy = pltpu.make_async_copy(
                piece, held.at[at, pl.ds(row + part * size, size)], sems.at[at, 2 + part]
            )
            copy.start()
            copies[-1].append(copy)
            taken += 1
    for at in range(len(slots)):
        for copy in copies[at]:
            copy.wait()
        for half, ref in enumerate((other_ref, own_ref)):
            product = dot(lhs[at, half], held[at])
            if at > 0:
                ref[...] += product
            elif first:
                ref[...] = product
            else:
                ref[...] = refs[half - 7][...] + product


def conv_part(stacked, places, pieces, before, length):
    points, depth = stacked[0].shape
    width = pieces[0][0].shape[1]
    slots = [len(parts) for parts in pieces]
    flat = [piece for parts in pieces for piece in parts]
    return call(
        functools.partial(conv_kernel, slots, before is None),
        (jax.ShapeDtypeStruct((points, width), F32),) * 2,
        60,
        4 * points * length * width * len(slots),
        2 * length * (2 * points + width) * len(slots),
        in_specs=[pl.BlockSpec(memory_space=pltpu.SMEM)]
        + [pl.BlockSpec(memory_space=pl.ANY)] * (2 + len(flat))
        + ([] if before is None else [pl.BlockSpec()] * 2),
        input_output_aliases=(
            {} if before is None else {3 + len(flat): 0, 4 + len(flat): 1}
        ),
        scratch_shapes=[
            pltpu.VMEM((len(slots), 2, points, length), BF16),
            pltpu.VMEM((len(slots), length, width), BF16),
            pltpu.SemaphoreType.DMA((len(slots), 4)),
        ],
    )(places.reshape(-1), *stacked, *flat, *(before or ()))


def mix_kernel(own_ref, got_ref, features_ref, weight_ref, gain_ref, slot_ref, out_ref):
    convolved = (own_ref[...] + got_ref[...]).astype(BF16)
    linear = dot(convolved, weight_ref[...])
    mixed = (features_ref[...].astype(F32) + layer_norm(linear, gain_ref[...])).astype(BF16)
    slots = lax.broadcasted_iota(jnp.int32, (out_ref.shape[0], mixed.shape[0]), 0)
    out_ref[...] = dot(one_hot(slots == slot_ref[...]), mixed).astype(BF16)


def block_kernel(
    arrived_ref,
    slot_col_ref,
    slot_row_ref,
    attn_gain_ref,
    qv_ref,
    key_ref,
    proj_ref,
    mlp_gain_ref,
    up_ref,
    down_ref,
    out_ref,
    serial_ref,
    qv_cols_ref,
    keys_ref,
    heads_ref,
    total_ref,
):
    slots = arrived_ref.shape[0]
    points, width = serial_ref.shape
    slot_ids = lax.broadcasted_iota(jnp.int32, (points, slots), 1)
    serial = dot(one_hot(slot_col_ref[...] == slot_ids), arrived_ref[...])
    serial_ref[...] = serial
    normed = layer_norm(serial, attn_gain_ref[...]).astype(BF16)
    keys_ref[...] = dot(normed, key_ref[...]).astype(BF16)
    factor = math.log2(math.e) / math.sqrt(HD)
    contract_last = (((1,), (1,)), ((), ()))
    qv_cols_ref[:width] = (
        lax.dot_general(qv_ref[:width], normed, contract_last, preferred_element_type=F32) * factor
    ).astype(BF16)
    qv_cols_ref[width:] = lax.dot_general(
        qv_ref[width:], normed, contract_last, preferred_element_type=F32
    ).astype(BF16)
    ones = jnp.ones((HD, points), BF16)
    per_group = 128 // HD
    head_of_row = lax.broadcasted_iota(jnp.int32, (128, points), 0) // HD

    for group in range(HEADS // per_group):
        base = group * 128

        def attend(head, carry):
            group_queries = qv_cols_ref[base : base + 128]
            queries = jnp.where(head_of_row == head, group_queries.astype(F32), 0.0).astype(BF16)
            scores = dot(keys_ref[:, base : base + 128], queries)
            weights = jnp.exp2(scores - jnp.max(scores, axis=0, keepdims=True)).astype(BF16)
            at = pl.multiple_of(base + head * HD, HD)
            values = qv_cols_ref[pl.ds(width + at, HD)]
            sums = dot(jnp.concatenate([values, ones], axis=0), weights)
            heads_ref[pl.ds(at, HD)] = (sums[:HD] / sums[HD : HD + 1]).astype(BF16)
            return carry

        lax.fori_loop(0, per_group, attend, 0, unroll=2)

    update = lax.dot_general(
        heads_ref[...], proj_ref[...], (((0,), (0,)), ((), ())), preferred_element_type=F32
    )
    attended = (serial_ref[...] + update).astype(BF16).astype(F32)
    hidden_in = layer_norm(attended, mlp_gain_ref[...]).astype(BF16)
    total_ref[...] = attended
    chunk = width
    for start in range(0, up_ref.shape[1], chunk):
        raised = dot(hidden_in, up_ref[:, start : start + chunk])
        hidden = (raised * (1.0 + lax.erf(raised * math.sqrt(0.5))) * 0.5).astype(BF16)
        total_ref[...] += dot(hidden, down_ref[start : start + chunk])
    finished = total_ref[...].astype(BF16)
    slot_rows = lax.broadcasted_iota(jnp.int32, (slots, points), 0)
    out_ref[...] = dot(one_hot(slot_rows == slot_row_ref[...]), finished).astype(BF16)


def return_kernel(arrived_ref, slot_ref, out_ref):
    slot_ids = lax.broadcasted_iota(jnp.int32, (out_ref.shape[0], arrived_ref.shape[0]), 1)
    out_ref[...] = dot(one_hot(slot_ref[...] == slot_ids), arrived_ref[...]).astype(BF16)


def exchange_faces(faces, devices, index):
    zero = jnp.zeros_like(faces[0])
    received = [zero] * 8

    def valid(source, dx, dy):
        return 0 <= source // GY + dx < devices // GY and 0 <= source % GY + dy < GY

    if devices == 2 * GY:
        lower = index < GY
        for dy in (-1, 0, 1):
            payload = jnp.where(lower, faces[6 + dy], faces[1 + dy])
            pairs = []
            for source in range(devices):
                dx = 1 if source < GY else -1
                if valid(source, dx, dy):
                    pairs.append((source, source + dx * GY + dy))
            got = lax.ppermute(payload, "blocks", pairs)
            received[1 + dy] = jnp.where(lower, got, zero)
            received[6 + dy] = jnp.where(lower, zero, got)
        rest = (3, 4)
    else:
        rest = range(8)
    for facing in rest:
        dx, dy = STEPS_X[facing], STEPS_Y[facing]
        pairs = [
            (source, source + dx * GY + dy) for source in range(devices) if valid(source, dx, dy)
        ]
        received[facing] = lax.ppermute(faces[facing], "blocks", pairs)
    return received


def way_round(devices, rows, length):
    chips = devices // 2
    cycle = list(range(0, chips, 2)) + list(range(chips - 1, 0, -2))
    back, on = [], []
    places = [None] * devices
    for place, chip in enumerate(cycle):
        for core in range(2):
            me = 2 * chip + core
            back.append((me, 2 * cycle[(place + 1) % chips] + core))
            on.append((me, 2 * cycle[place - 1] + core))
            order = [0]
            for step in range(1, chips // 2):
                order += [-step, step]
            order.append(chips // 2)
            places[me] = []
            for offset in order:
                start = cycle[(place + offset) % chips] * rows
                column = min(start // 128 * 128, chips * rows - length)
                places[me].append((column, start - column))
    return back, on, places


def padded_taps(neighbours):
    points = neighbours.shape[0]
    own = jnp.arange(points, dtype=jnp.int32)[:, None]
    rest = jnp.zeros((points, 128 - TAPS), jnp.int32)
    middle = TAPS // 2
    return jnp.concatenate(
        [neighbours[:, :middle], own, neighbours[:, middle:], rest], axis=1
    ).astype(F32)


def body(
    features,
    conv_weight,
    cpe_weight,
    cpe_gain,
    attn_gain,
    qkv_weight,
    proj_weight,
    mlp_gain,
    up_weight,
    down_weight,
    face_rows,
    neighbours,
    serial_rank,
    serial_order,
):
    points, width = features.shape
    half = width // 2
    devices = lax.axis_size("blocks")
    index = lax.axis_index("blocks")
    core = lax.rem(index, 2)
    partner = [(source, source ^ 1) for source in range(devices)]
    capacity = 2 * points // devices
    slots = devices * capacity

    unit = conv_weight.shape[0] // TAPS
    units = conv_weight.reshape(TAPS, unit, width)
    kept, sent = units[0::2], units[1::2]
    got = lax.ppermute(sent, "blocks", partner)
    mine = jnp.where(
        core == 0, jnp.concatenate([kept, got]), jnp.concatenate([got, kept])
    ).reshape(TAPS * unit, width)
    face_list = face_rows.reshape(-1, 1)
    ordered, faces = call(
        functools.partial(faces_kernel, unit),
        (
            jax.ShapeDtypeStruct((points, width), BF16),
            jax.ShapeDtypeStruct((face_list.shape[0], width), BF16),
        ),
        32,
        4 * points * width * width,
        8 * points * width,
    )(features, face_list)
    round_trip = devices == 16
    rows = mine.shape[0]
    length = -(-(rows + 127) // 128) * 128 if round_trip else rows * (devices // 2)
    back_pairs, on_pairs, places = way_round(devices, rows, length)
    back, on = [mine], [mine]

    def pass_on(*beside):
        if not round_trip:
            return beside
        tied = lax.optimization_barrier((back[-1], on[-1], *beside))
        first, second = tied[:2]
        back[-1], on[-1] = first, second
        if len(back) == devices // 4:
            first, second = first[: rows // 2], second[rows // 2 :]
        back.append(lax.ppermute(first, "blocks", back_pairs))
        on.append(lax.ppermute(second, "blocks", on_pairs))
        return tied[2:]

    received = exchange_faces(faces.reshape(8, -1, width), devices, index)
    received = pass_on(*received)
    table = jnp.concatenate([ordered, *received], axis=0)
    own_table = lax.dynamic_slice(table, (0, core * half), (table.shape[0], half))
    other_half = lax.dynamic_slice(table, (0, (1 - core) * half), (table.shape[0], half))
    other_table = lax.ppermute(other_half, "blocks", partner)
    other_neighbours = lax.ppermute(neighbours, "blocks", partner)
    own_stacked = gather_block(padded_taps(neighbours), own_table)
    own_stacked, other_table = pass_on(own_stacked, other_table)
    other_stacked = gather_block(padded_taps(other_neighbours), other_table)
    stacked = pass_on(other_stacked, own_stacked)
    if round_trip:
        places = jnp.array(places, jnp.int32)[index]
        early = [[mine], [back[1]], [on[1]], [back[2]], [on[2]]]
        sums = conv_part(stacked, places[:5], early, None, length)
        sums = pass_on(*sums)
        sums = conv_part(stacked, places[5:7], [[back[3]], [on[3]]], sums, length)
        sums = conv_part(stacked, places[7:], [[back[4], on[4]]], sums, length)
    else:
        groups = [list(range(first, devices, 2)) for first in range(2)]
        weight = lax.all_gather(mine, "blocks", axis=0, tiled=True, axis_index_groups=groups)
        sums = conv_part(stacked, jnp.zeros((1, 2), jnp.int32), [[weight]], None, length)
    for_partner, own_part = sums

    positions = jnp.arange(points, dtype=jnp.int32)
    target = serial_rank // points
    earlier = (target[None, :] == target[:, None]) & (serial_rank[None, :] < serial_rank[:, None])
    out_slot = target * capacity + jnp.sum(earlier.astype(jnp.int32), axis=1)
    anchor = serial_order // points
    before = (anchor[None, :] == anchor[:, None]) & (positions[None, :] < positions[:, None])
    in_slot = anchor * capacity + jnp.sum(before.astype(jnp.int32), axis=1)

    from_partner = lax.ppermute(for_partner, "blocks", partner)

    outgoing = call(
        mix_kernel,
        jax.ShapeDtypeStruct((slots, width), BF16),
        32,
        2 * points * width * (width + slots),
        8 * points * width,
    )(
        own_part,
        from_partner,
        features,
        cpe_weight,
        cpe_gain.reshape(1, width),
        out_slot.reshape(1, points),
    )
    arrived = lax.all_to_all(
        outgoing.reshape(devices, capacity, width), "blocks", split_axis=0, concat_axis=0, tiled=True
    ).reshape(slots, width)

    key_weight = qkv_weight[:, width : 2 * width]
    qv_weight = jnp.concatenate([qkv_weight[:, :width], qkv_weight[:, 2 * width :]], axis=1).T
    back = call(
        block_kernel,
        jax.ShapeDtypeStruct((slots, width), BF16),
        28,
        20 * points * width * width,
        16 * width * width,
        scratch_shapes=[
            pltpu.VMEM((points, width), F32),
            pltpu.VMEM((2 * width, points), BF16),
            pltpu.VMEM((points, width), BF16),
            pltpu.VMEM((width, points), BF16),
            pltpu.VMEM((points, width), F32),
        ],
    )(
        arrived,
        in_slot.reshape(points, 1),
        in_slot.reshape(1, points),
        attn_gain.reshape(1, width),
        qv_weight,
        key_weight,
        proj_weight,
        mlp_gain.reshape(1, width),
        up_weight,
        down_weight,
    )
    returned = lax.all_to_all(
        back.reshape(devices, capacity, width), "blocks", split_axis=0, concat_axis=0, tiled=True
    ).reshape(slots, width)
    return call(
        return_kernel,
        jax.ShapeDtypeStruct((points, width), BF16),
        32,
        2 * points * slots * width,
        6 * points * width,
    )(returned, out_slot.reshape(points, 1))


def solution(mesh):
    placed = (
        P(("groups", "blocks"), None),
        P("blocks", None),
        P(),
        P(),
        P(),
        P(),
        P(),
        P(),
        P(),
        P(),
        P(("groups", "blocks"), None, None),
        P(("groups", "blocks"), None),
        P(("groups", "blocks")),
        P(("groups", "blocks")),
    )
    return jax.shard_map(
        body, mesh=mesh, in_specs=placed, out_specs=P(("groups", "blocks"), None), check_vma=False
    )
```

```python
import functools
import math

import jax
import jax.numpy as jnp
from jax import lax
from jax.experimental import pallas as pl
from jax.experimental.pallas import tpu as pltpu
from jax.sharding import PartitionSpec as P

HEADS = 32
GY = 8
HD = 16
TAPS = 27
EPSILON = 1e-05
STEPS_X = (-1, -1, -1, 0, 0, 1, 1, 1)
STEPS_Y = (-1, 0, 1, -1, 1, -1, 0, 1)
F32 = jnp.float32
BF16 = jnp.bfloat16
MIB = 1 << 20


def dot(left, right):
    return jnp.dot(left, right, preferred_element_type=F32)


def layer_norm(inputs, gain_vector):
    row_mean = jnp.mean(inputs, axis=-1, keepdims=True)
    centred = inputs - row_mean
    variance = jnp.mean(centred * centred, axis=-1, keepdims=True)
    return centred * lax.rsqrt(variance + EPSILON) * gain_vector


def one_hot(mask):
    return jnp.where(mask, 1.0, 0.0).astype(BF16)


def call(kernel, out_shape, limit, flops, moved, **extra):
    return pl.pallas_call(
        kernel,
        out_shape=out_shape,
        compiler_params=pltpu.CompilerParams(vmem_limit_bytes=limit * MIB),
        cost_estimate=pl.CostEstimate(flops=flops, bytes_accessed=moved, transcendentals=0),
        **extra,
    )


def faces_kernel(unit, features_ref, rows_ref, ordered_ref, *face_refs):
    points, width = features_ref.shape
    half = width // 2
    place = lax.broadcasted_iota(jnp.int32, (width, width), 1)
    within = lax.rem(place, half)
    source = (within // unit) * (2 * unit) + (place // half) * unit + lax.rem(place, unit)
    channel = lax.broadcasted_iota(jnp.int32, (width, width), 0)
    ordered = dot(features_ref[...], one_hot(channel == source)).astype(BF16)
    ordered_ref[...] = ordered
    row_ids = lax.broadcasted_iota(jnp.int32, (rows_ref.shape[0], points), 1)
    rows = dot(one_hot(rows_ref[...] == row_ids), ordered).astype(BF16)
    size = rows.shape[0] // len(face_refs)
    for at, ref in enumerate(face_refs):
        ref[...] = rows[at * size : (at + 1) * size]


def gather_kernel(taps, rows_ref, table_ref, out_ref):
    half = table_ref.shape[1]
    lane = lax.broadcasted_iota(jnp.int32, rows_ref.shape, 1)
    row_ids = lax.broadcasted_iota(jnp.int32, (1, table_ref.shape[0]), 1).astype(F32)
    for at in range(taps):
        chosen = lane == taps * pl.program_id(0) + at
        column = jnp.sum(jnp.where(chosen, rows_ref[...], 0.0), axis=1, keepdims=True)
        taken = dot(one_hot(column == row_ids), table_ref[...]).astype(BF16)
        out_ref[:, at * half : (at + 1) * half] = taken


def gather_block(rows, table):
    points, lanes = rows.shape
    height, half = table.shape
    taps = 3
    whole = lambda step: (0, 0)
    return call(
        functools.partial(gather_kernel, taps),
        jax.ShapeDtypeStruct((points, TAPS * half), BF16),
        60,
        2 * TAPS * points * height * half,
        2 * TAPS * points * half,
        grid=(TAPS // taps,),
        in_specs=[pl.BlockSpec((points, lanes), whole), pl.BlockSpec((height, half), whole)],
        out_specs=pl.BlockSpec((points, taps * half), lambda step: (0, step)),
    )(rows, table)


def conv_kernel(slots, blocks, first, places_ref, *refs):
    stacked, refs = refs[:blocks], refs[blocks:]
    pieces, refs = refs[: sum(slots)], refs[sum(slots) :]
    before = [] if first else refs[:blocks]
    outs, (lhs, held, sems) = refs[-3 - blocks : -3], refs[-3:]
    length = held.shape[1]
    copies, taken = [], 0
    for at, count in enumerate(slots):
        column = pl.multiple_of(places_ref[2 * at], 128)
        row = pl.multiple_of(places_ref[2 * at + 1], 16)
        copies.append([])
        for block in range(blocks):
            copy = pltpu.make_async_copy(
                stacked[block].at[:, pl.ds(column, length)], lhs.at[at, block], sems.at[at, block]
            )
            copy.start()
            copies[-1].append(copy)
        short = count * pieces[taken].shape[0]
        edge = length - short
        if edge:
            held[at, :edge] = jnp.zeros((edge, held.shape[2]), BF16)
            held[at, length - edge :] = jnp.zeros((edge, held.shape[2]), BF16)
        for part in range(count):
            piece = pieces[taken]
            size = piece.shape[0]
            copy = pltpu.make_async_copy(
                piece, held.at[at, pl.ds(row + part * size, size)], sems.at[at, 2 + part]
            )
            copy.start()
            copies[-1].append(copy)
            taken += 1
    for at in range(len(slots)):
        for copy in copies[at]:
            copy.wait()
        for block, ref in enumerate(outs):
            product = dot(lhs[at, block], held[at])
            if at > 0:
                ref[...] += product
            elif first:
                ref[...] = product
            else:
                ref[...] = before[block][...] + product


def conv_part(stacked, places, pieces, before, length):
    points, depth = stacked[0].shape
    width = pieces[0][0].shape[1]
    slots = [len(parts) for parts in pieces]
    flat = [piece for parts in pieces for piece in parts]
    blocks = len(stacked)
    held = 1 + blocks + len(flat)
    return call(
        functools.partial(conv_kernel, slots, blocks, before is None),
        [jax.ShapeDtypeStruct((points, width), F32)] * blocks,
        60,
        2 * blocks * points * length * width * len(slots),
        2 * length * (blocks * points + width) * len(slots),
        in_specs=[pl.BlockSpec(memory_space=pltpu.SMEM)]
        + [pl.BlockSpec(memory_space=pl.ANY)] * (held - 1)
        + ([] if before is None else [pl.BlockSpec()] * blocks),
        input_output_aliases=(
            {} if before is None else {held + block: block for block in range(blocks)}
        ),
        scratch_shapes=[
            pltpu.VMEM((len(slots), blocks, points, length), BF16),
            pltpu.VMEM((len(slots), length, width), BF16),
            pltpu.SemaphoreType.DMA((len(slots), 4)),
        ],
    )(places.reshape(-1), *stacked, *flat, *(before or ()))


def mix_kernel(own_ref, got_ref, features_ref, weight_ref, gain_ref, slot_ref, out_ref):
    convolved = (own_ref[...] + got_ref[...]).astype(BF16)
    linear = dot(convolved, weight_ref[...])
    mixed = (features_ref[...].astype(F32) + layer_norm(linear, gain_ref[...])).astype(BF16)
    slots = lax.broadcasted_iota(jnp.int32, (out_ref.shape[0], mixed.shape[0]), 0)
    out_ref[...] = dot(one_hot(slots == slot_ref[...]), mixed).astype(BF16)


def block_kernel(
    arrived_ref,
    slot_col_ref,
    slot_row_ref,
    attn_gain_ref,
    mlp_gain_ref,
    qv_hbm,
    key_hbm,
    proj_hbm,
    up_hbm,
    down_hbm,
    out_ref,
    qv_ref,
    key_ref,
    proj_ref,
    up_ref,
    down_ref,
    sems,
    serial_ref,
    qv_cols_ref,
    keys_ref,
    heads_ref,
    total_ref,
):
    sources = (key_hbm, qv_hbm, proj_hbm, up_hbm, down_hbm)
    targets = (key_ref, qv_ref, proj_ref, up_ref, down_ref)
    copies = [
        pltpu.make_async_copy(source, target, sems.at[at])
        for at, (source, target) in enumerate(zip(sources, targets))
    ]
    for copy in copies:
        copy.start()
    slots = arrived_ref.shape[0]
    points, width = serial_ref.shape
    slot_ids = lax.broadcasted_iota(jnp.int32, (points, slots), 1)
    serial = dot(one_hot(slot_col_ref[...] == slot_ids), arrived_ref[...])
    serial_ref[...] = serial
    normed = layer_norm(serial, attn_gain_ref[...]).astype(BF16)
    copies[0].wait()
    keys_ref[...] = dot(normed, key_ref[...]).astype(BF16)
    copies[1].wait()
    factor = math.log2(math.e) / math.sqrt(HD)
    contract_last = (((1,), (1,)), ((), ()))
    qv_cols_ref[:width] = (
        lax.dot_general(qv_ref[:width], normed, contract_last, preferred_element_type=F32) * factor
    ).astype(BF16)
    qv_cols_ref[width:] = lax.dot_general(
        qv_ref[width:], normed, contract_last, preferred_element_type=F32
    ).astype(BF16)
    ones = jnp.ones((HD, points), BF16)
    per_group = 128 // HD
    head_of_row = lax.broadcasted_iota(jnp.int32, (128, points), 0) // HD

    for group in range(HEADS // per_group):
        base = group * 128

        def attend(head, carry):
            group_queries = qv_cols_ref[base : base + 128]
            queries = jnp.where(head_of_row == head, group_queries.astype(F32), 0.0).astype(BF16)
            scores = dot(keys_ref[:, base : base + 128], queries)
            weights = jnp.exp2(scores - jnp.max(scores, axis=0, keepdims=True)).astype(BF16)
            at = pl.multiple_of(base + head * HD, HD)
            values = qv_cols_ref[pl.ds(width + at, HD)]
            sums = dot(jnp.concatenate([values, ones], axis=0), weights)
            heads_ref[pl.ds(at, HD)] = (sums[:HD] / sums[HD : HD + 1]).astype(BF16)
            return carry

        lax.fori_loop(0, per_group, attend, 0, unroll=4)

    for copy in copies[2:]:
        copy.wait()
    update = lax.dot_general(
        heads_ref[...], proj_ref[...], (((0,), (0,)), ((), ())), preferred_element_type=F32
    )
    attended = (serial_ref[...] + update).astype(BF16).astype(F32)
    hidden_in = layer_norm(attended, mlp_gain_ref[...]).astype(BF16)
    total_ref[...] = attended
    chunk = width
    for start in range(0, up_ref.shape[1], chunk):
        raised = dot(hidden_in, up_ref[:, start : start + chunk])
        hidden = (raised * (1.0 + lax.erf(raised * math.sqrt(0.5))) * 0.5).astype(BF16)
        total_ref[...] += dot(hidden, down_ref[start : start + chunk])
    finished = total_ref[...].astype(BF16)
    slot_rows = lax.broadcasted_iota(jnp.int32, (slots, points), 0)
    out_ref[...] = dot(one_hot(slot_rows == slot_row_ref[...]), finished).astype(BF16)


def return_kernel(arrived_ref, slot_ref, out_ref):
    slot_ids = lax.broadcasted_iota(jnp.int32, (out_ref.shape[0], arrived_ref.shape[0]), 1)
    out_ref[...] = dot(one_hot(slot_ref[...] == slot_ids), arrived_ref[...]).astype(BF16)


def face_routes(devices):
    def pairs(dx, dy):
        return [
            (source, source + dx * GY + dy)
            for source in range(devices)
            if 0 <= source // GY + dx < devices // GY and 0 <= source % GY + dy < GY
        ]

    if devices != 2 * GY:
        return [(k, k, pairs(STEPS_X[k], STEPS_Y[k])) for k in range(8)]
    both = [(6 + dy, 1 + dy, pairs(1, dy) + pairs(-1, dy)) for dy in (-1, 0, 1)]
    return both + [(k, k, pairs(0, STEPS_Y[k])) for k in (3, 4)]


def received_faces(routes, got, lower):
    received = [None] * 8
    for (first, second, _), rows in zip(routes, got):
        if first == second:
            received[first] = rows
        else:
            zero = jnp.zeros_like(rows)
            received[first] = jnp.where(lower, zero, rows)
            received[second] = jnp.where(lower, rows, zero)
    return received


def way_round(devices, rows, length):
    chips = devices // 2
    cycle = list(range(0, chips, 2)) + list(range(chips - 1, 0, -2))
    back, on = [], []
    places = [None] * devices
    for place, chip in enumerate(cycle):
        for core in range(2):
            me = 2 * chip + core
            back.append((me, 2 * cycle[(place + 1) % chips] + core))
            on.append((me, 2 * cycle[place - 1] + core))
            order = [0]
            for step in range(1, chips // 2):
                order += [-step, step]
            order.append(chips // 2)
            places[me] = []
            for offset in order:
                start = cycle[(place + offset) % chips] * rows
                column = min(start // 128 * 128, chips * rows - length)
                places[me].append((column, start - column))
    return back, on, places


def padded_taps(neighbours):
    points = neighbours.shape[0]
    own = jnp.arange(points, dtype=jnp.int32)[:, None]
    rest = jnp.zeros((points, 128 - TAPS), jnp.int32)
    middle = TAPS // 2
    return jnp.concatenate(
        [neighbours[:, :middle], own, neighbours[:, middle:], rest], axis=1
    ).astype(F32)


def body(
    features,
    conv_weight,
    cpe_weight,
    cpe_gain,
    attn_gain,
    qkv_weight,
    proj_weight,
    mlp_gain,
    up_weight,
    down_weight,
    face_rows,
    neighbours,
    serial_rank,
    serial_order,
):
    points, width = features.shape
    half = width // 2
    devices = lax.axis_size("blocks")
    index = lax.axis_index("blocks")
    core = lax.rem(index, 2)
    partner = [(source, source ^ 1) for source in range(devices)]
    capacity = 2 * points // devices
    slots = devices * capacity

    unit = conv_weight.shape[0] // TAPS
    units = conv_weight.reshape(TAPS, unit, width)
    kept, sent = units[0::2], units[1::2]
    got = lax.ppermute(sent, "blocks", partner)
    mine = jnp.where(
        core == 0, jnp.concatenate([kept, got]), jnp.concatenate([got, kept])
    ).reshape(TAPS * unit, width)
    lower = index < GY
    routes = face_routes(devices)
    lists = [jnp.where(lower, face_rows[0, first], face_rows[0, second]) for first, second, _ in routes]
    face_list = jnp.concatenate(lists).reshape(-1, 1)
    ordered, *faces = call(
        functools.partial(faces_kernel, unit),
        [jax.ShapeDtypeStruct((points, width), BF16)]
        + [jax.ShapeDtypeStruct((face_rows.shape[2], width), BF16)] * len(routes),
        32,
        4 * points * width * width,
        8 * points * width,
    )(features, face_list)
    faces = [
        lax.ppermute(rows, "blocks", pairs) for rows, (_, _, pairs) in zip(faces, routes)
    ]

    round_trip = devices == 16
    rows = mine.shape[0]
    length = -(-(rows + 127) // 128) * 128 if round_trip else rows * (devices // 2)
    back_pairs, on_pairs, places = way_round(devices, rows, length)
    back, on = [mine], [mine]

    def pass_on(*beside):
        if not round_trip:
            return beside
        tied = lax.optimization_barrier((back[-1], on[-1], *beside))
        first, second = tied[:2]
        back[-1], on[-1] = first, second
        if len(back) == devices // 4:
            first, second = first[: rows // 2], second[rows // 2 :]
        back.append(lax.ppermute(first, "blocks", back_pairs))
        on.append(lax.ppermute(second, "blocks", on_pairs))
        return tied[2:]

    neighbours, *faces = pass_on(neighbours, *faces)
    received = received_faces(routes, faces, lower)
    table = jnp.concatenate([ordered, *received], axis=0)
    own_table = lax.dynamic_slice(table, (0, core * half), (table.shape[0], half))
    other_half = lax.dynamic_slice(table, (0, (1 - core) * half), (table.shape[0], half))
    other_table = lax.ppermute(other_half, "blocks", partner)
    other_neighbours = lax.ppermute(neighbours, "blocks", partner)
    own_stacked = gather_block(padded_taps(neighbours), own_table)
    own_stacked, other_table = pass_on(own_stacked, other_table)
    other_stacked = gather_block(padded_taps(other_neighbours), other_table)
    stacked = pass_on(other_stacked, own_stacked)
    if round_trip:
        places = jnp.array(places, jnp.int32)[index]
        early = [[mine], [back[1]], [on[1]], [back[2]], [on[2]]]
        sums = conv_part(stacked, places[:5], early, None, length)
        sums = pass_on(*sums)
        sums = conv_part(stacked, places[5:7], [[back[3]], [on[3]]], sums, length)
        last = [[back[4], on[4]]]
        (for_partner,) = conv_part(stacked[:1], places[7:], last, sums[:1], length)
        (own_part,) = conv_part(stacked[1:], places[7:], last, sums[1:], length)
    else:
        groups = [list(range(first, devices, 2)) for first in range(2)]
        weight = lax.all_gather(mine, "blocks", axis=0, tiled=True, axis_index_groups=groups)
        nowhere = jnp.zeros((1, 2), jnp.int32)
        for_partner, own_part = conv_part(stacked, nowhere, [[weight]], None, length)

    positions = jnp.arange(points, dtype=jnp.int32)
    target = serial_rank // points
    earlier = (target[None, :] == target[:, None]) & (serial_rank[None, :] < serial_rank[:, None])
    out_slot = target * capacity + jnp.sum(earlier.astype(jnp.int32), axis=1)
    anchor = serial_order // points
    before = (anchor[None, :] == anchor[:, None]) & (positions[None, :] < positions[:, None])
    in_slot = anchor * capacity + jnp.sum(before.astype(jnp.int32), axis=1)

    from_partner = lax.ppermute(for_partner, "blocks", partner)

    outgoing = call(
        mix_kernel,
        jax.ShapeDtypeStruct((slots, width), BF16),
        32,
        2 * points * width * (width + slots),
        8 * points * width,
    )(
        own_part,
        from_partner,
        features,
        cpe_weight,
        cpe_gain.reshape(1, width),
        out_slot.reshape(1, points),
    )
    arrived = lax.all_to_all(
        outgoing.reshape(devices, capacity, width), "blocks", split_axis=0, concat_axis=0, tiled=True
    ).reshape(slots, width)

    key_weight = qkv_weight[:, width : 2 * width]
    qv_weight = jnp.concatenate([qkv_weight[:, :width], qkv_weight[:, 2 * width :]], axis=1).T
    weights = (qv_weight, key_weight, proj_weight, up_weight, down_weight)
    back = call(
        block_kernel,
        jax.ShapeDtypeStruct((slots, width), BF16),
        60,
        20 * points * width * width,
        16 * width * width,
        in_specs=[pl.BlockSpec()] * 5 + [pl.BlockSpec(memory_space=pl.ANY)] * len(weights),
        scratch_shapes=[pltpu.VMEM(weight.shape, BF16) for weight in weights]
        + [
            pltpu.SemaphoreType.DMA((len(weights),)),
            pltpu.VMEM((points, width), F32),
            pltpu.VMEM((2 * width, points), BF16),
            pltpu.VMEM((points, width), BF16),
            pltpu.VMEM((width, points), BF16),
            pltpu.VMEM((points, width), F32),
        ],
    )(
        arrived,
        in_slot.reshape(points, 1),
        in_slot.reshape(1, points),
        attn_gain.reshape(1, width),
        mlp_gain.reshape(1, width),
        *weights,
    )
    returned = lax.all_to_all(
        back.reshape(devices, capacity, width), "blocks", split_axis=0, concat_axis=0, tiled=True
    ).reshape(slots, width)
    return call(
        return_kernel,
        jax.ShapeDtypeStruct((points, width), BF16),
        32,
        2 * points * slots * width,
        6 * points * width,
    )(returned, out_slot.reshape(points, 1))


def solution(mesh):
    placed = (
        P(("groups", "blocks"), None),
        P("blocks", None),
        P(),
        P(),
        P(),
        P(),
        P(),
        P(),
        P(),
        P(),
        P(("groups", "blocks"), None, None),
        P(("groups", "blocks"), None),
        P(("groups", "blocks")),
        P(("groups", "blocks")),
    )
    return jax.shard_map(
        body, mesh=mesh, in_specs=placed, out_specs=P(("groups", "blocks"), None), check_vma=False
    )
```

```python
import functools
import math

import jax
import jax.numpy as jnp
from jax import lax
from jax.experimental import pallas as pl
from jax.experimental.pallas import tpu as pltpu
from jax.sharding import PartitionSpec as P

HEADS = 32
GY = 8
HD = 16
TAPS = 27
EPSILON = 1e-05
STEPS_X = (-1, -1, -1, 0, 0, 1, 1, 1)
STEPS_Y = (-1, 0, 1, -1, 1, -1, 0, 1)
F32 = jnp.float32
BF16 = jnp.bfloat16
MIB = 1 << 20


def dot(left, right):
    return jnp.dot(left, right, preferred_element_type=F32)


def layer_norm(inputs, gain_vector):
    row_mean = jnp.mean(inputs, axis=-1, keepdims=True)
    centred = inputs - row_mean
    variance = jnp.mean(centred * centred, axis=-1, keepdims=True)
    return centred * lax.rsqrt(variance + EPSILON) * gain_vector


def one_hot(mask):
    return jnp.where(mask, 1.0, 0.0).astype(BF16)


def call(kernel, out_shape, limit, flops, moved, **extra):
    return pl.pallas_call(
        kernel,
        out_shape=out_shape,
        compiler_params=pltpu.CompilerParams(vmem_limit_bytes=limit * MIB),
        cost_estimate=pl.CostEstimate(flops=flops, bytes_accessed=moved, transcendentals=0),
        **extra,
    )


def faces_kernel(unit, features_ref, rows_ref, ordered_ref, *face_refs):
    points, width = features_ref.shape
    half = width // 2
    place = lax.broadcasted_iota(jnp.int32, (width, width), 1)
    within = lax.rem(place, half)
    source = (within // unit) * (2 * unit) + (place // half) * unit + lax.rem(place, unit)
    channel = lax.broadcasted_iota(jnp.int32, (width, width), 0)
    ordered = dot(features_ref[...], one_hot(channel == source)).astype(BF16)
    ordered_ref[...] = ordered
    row_ids = lax.broadcasted_iota(jnp.int32, (rows_ref.shape[0], points), 1)
    rows = dot(one_hot(rows_ref[...] == row_ids), ordered).astype(BF16)
    taken = 0
    for ref in face_refs:
        ref[...] = rows[taken : taken + ref.shape[0]]
        taken += ref.shape[0]


def table_kernel(flags_ref, ordered_ref, side_ref, behind_ref, ahead_ref, own_ref, other_ref, held):
    size = behind_ref.shape[0] // 2
    points = ordered_ref.shape[0]
    half = own_ref.shape[1]
    lower, even = flags_ref[0] == 1, flags_ref[1] == 0
    held[:points] = ordered_ref[...]
    across = (ahead_ref[size:], side_ref[size : 2 * size], behind_ref[size:])
    zero = jnp.zeros_like(across[0])
    for at, rows in enumerate(across):
        start = points + at * size
        held[start : start + size] = jnp.where(lower, rows, zero)
        start += 5 * size
        held[start : start + size] = jnp.where(lower, zero, rows)
    held[points + 3 * size : points + 4 * size] = ahead_ref[:size]
    held[points + 4 * size : points + 5 * size] = behind_ref[:size]
    first, second = held[:, :half], held[:, half:]
    own_ref[...] = jnp.where(even, first, second)
    other_ref[...] = jnp.where(even, second, first)


def gather_kernel(taps, rows_ref, table_ref, out_ref):
    half = table_ref.shape[1]
    lane = lax.broadcasted_iota(jnp.int32, rows_ref.shape, 1)
    row_ids = lax.broadcasted_iota(jnp.int32, (1, table_ref.shape[0]), 1).astype(F32)
    for at in range(taps):
        chosen = lane == taps * pl.program_id(0) + at
        column = jnp.sum(jnp.where(chosen, rows_ref[...], 0.0), axis=1, keepdims=True)
        taken = dot(one_hot(column == row_ids), table_ref[...]).astype(BF16)
        out_ref[:, at * half : (at + 1) * half] = taken


def gather_block(rows, table):
    points, lanes = rows.shape
    height, half = table.shape
    taps = 3
    whole = lambda step: (0, 0)
    return call(
        functools.partial(gather_kernel, taps),
        jax.ShapeDtypeStruct((points, TAPS * half), BF16),
        60,
        2 * TAPS * points * height * half,
        2 * TAPS * points * half,
        grid=(TAPS // taps,),
        in_specs=[pl.BlockSpec((points, lanes), whole), pl.BlockSpec((height, half), whole)],
        out_specs=pl.BlockSpec((points, taps * half), lambda step: (0, step)),
    )(rows, table)


def conv_kernel(slots, blocks, first, places_ref, *refs):
    stacked, refs = refs[:blocks], refs[blocks:]
    pieces, refs = refs[: sum(slots)], refs[sum(slots) :]
    before = [] if first else refs[:blocks]
    outs, (lhs, held, sems) = refs[-3 - blocks : -3], refs[-3:]
    length = held.shape[1]
    copies, taken = [], 0
    for at, count in enumerate(slots):
        column = pl.multiple_of(places_ref[2 * at], 128)
        row = pl.multiple_of(places_ref[2 * at + 1], 16)
        copies.append([])
        for block in range(blocks):
            copy = pltpu.make_async_copy(
                stacked[block].at[:, pl.ds(column, length)], lhs.at[at, block], sems.at[at, block]
            )
            copy.start()
            copies[-1].append(copy)
        short = count * pieces[taken].shape[0]
        edge = length - short
        if edge:
            held[at, :edge] = jnp.zeros((edge, held.shape[2]), BF16)
            held[at, length - edge :] = jnp.zeros((edge, held.shape[2]), BF16)
        for part in range(count):
            piece = pieces[taken]
            size = piece.shape[0]
            copy = pltpu.make_async_copy(
                piece, held.at[at, pl.ds(row + part * size, size)], sems.at[at, 2 + part]
            )
            copy.start()
            copies[-1].append(copy)
            taken += 1
    for at in range(len(slots)):
        for copy in copies[at]:
            copy.wait()
        for block, ref in enumerate(outs):
            product = dot(lhs[at, block], held[at])
            if at > 0:
                ref[...] += product
            elif first:
                ref[...] = product
            else:
                ref[...] = before[block][...] + product


def conv_part(stacked, places, pieces, before, length):
    points, depth = stacked[0].shape
    width = pieces[0][0].shape[1]
    slots = [len(parts) for parts in pieces]
    flat = [piece for parts in pieces for piece in parts]
    blocks = len(stacked)
    held = 1 + blocks + len(flat)
    return call(
        functools.partial(conv_kernel, slots, blocks, before is None),
        [jax.ShapeDtypeStruct((points, width), F32)] * blocks,
        60,
        2 * blocks * points * length * width * len(slots),
        2 * length * (blocks * points + width) * len(slots),
        in_specs=[pl.BlockSpec(memory_space=pltpu.SMEM)]
        + [pl.BlockSpec(memory_space=pl.ANY)] * (held - 1)
        + ([] if before is None else [pl.BlockSpec()] * blocks),
        input_output_aliases=(
            {} if before is None else {held + block: block for block in range(blocks)}
        ),
        scratch_shapes=[
            pltpu.VMEM((len(slots), blocks, points, length), BF16),
            pltpu.VMEM((len(slots), length, width), BF16),
            pltpu.SemaphoreType.DMA((len(slots), 4)),
        ],
    )(places.reshape(-1), *stacked, *flat, *(before or ()))


def mix_kernel(own_ref, got_ref, features_ref, weight_ref, gain_ref, slot_ref, out_ref):
    convolved = (own_ref[...] + got_ref[...]).astype(BF16)
    linear = dot(convolved, weight_ref[...])
    mixed = (features_ref[...].astype(F32) + layer_norm(linear, gain_ref[...])).astype(BF16)
    slots = lax.broadcasted_iota(jnp.int32, (out_ref.shape[0], mixed.shape[0]), 0)
    out_ref[...] = dot(one_hot(slots == slot_ref[...]), mixed).astype(BF16)


def block_kernel(
    arrived_ref,
    slot_col_ref,
    slot_row_ref,
    attn_gain_ref,
    mlp_gain_ref,
    qv_hbm,
    key_hbm,
    proj_hbm,
    up_hbm,
    down_hbm,
    out_ref,
    qv_ref,
    key_ref,
    proj_ref,
    up_ref,
    down_ref,
    sems,
    serial_ref,
    qv_cols_ref,
    keys_ref,
    heads_ref,
    total_ref,
):
    sources = (key_hbm, qv_hbm, proj_hbm, up_hbm, down_hbm)
    targets = (key_ref, qv_ref, proj_ref, up_ref, down_ref)
    copies = [
        pltpu.make_async_copy(source, target, sems.at[at])
        for at, (source, target) in enumerate(zip(sources, targets))
    ]
    for copy in copies:
        copy.start()
    slots = arrived_ref.shape[0]
    points, width = serial_ref.shape
    slot_ids = lax.broadcasted_iota(jnp.int32, (points, slots), 1)
    serial = dot(one_hot(slot_col_ref[...] == slot_ids), arrived_ref[...])
    serial_ref[...] = serial
    normed = layer_norm(serial, attn_gain_ref[...]).astype(BF16)
    copies[0].wait()
    keys_ref[...] = dot(normed, key_ref[...]).astype(BF16)
    copies[1].wait()
    factor = math.log2(math.e) / math.sqrt(HD)
    contract_last = (((1,), (1,)), ((), ()))
    qv_cols_ref[:width] = (
        lax.dot_general(qv_ref[:width], normed, contract_last, preferred_element_type=F32) * factor
    ).astype(BF16)
    qv_cols_ref[width:] = lax.dot_general(
        qv_ref[width:], normed, contract_last, preferred_element_type=F32
    ).astype(BF16)
    ones = jnp.ones((HD, points), BF16)
    per_group = 128 // HD
    head_of_row = lax.broadcasted_iota(jnp.int32, (128, points), 0) // HD

    for group in range(HEADS // per_group):
        base = group * 128

        def attend(head, carry):
            group_queries = qv_cols_ref[base : base + 128]
            queries = jnp.where(head_of_row == head, group_queries.astype(F32), 0.0).astype(BF16)
            scores = dot(keys_ref[:, base : base + 128], queries)
            weights = jnp.exp2(scores - jnp.max(scores, axis=0, keepdims=True)).astype(BF16)
            at = pl.multiple_of(base + head * HD, HD)
            values = qv_cols_ref[pl.ds(width + at, HD)]
            sums = dot(jnp.concatenate([values, ones], axis=0), weights)
            heads_ref[pl.ds(at, HD)] = (sums[:HD] / sums[HD : HD + 1]).astype(BF16)
            return carry

        lax.fori_loop(0, per_group, attend, 0, unroll=4)

    for copy in copies[2:]:
        copy.wait()
    update = lax.dot_general(
        heads_ref[...], proj_ref[...], (((0,), (0,)), ((), ())), preferred_element_type=F32
    )
    attended = (serial_ref[...] + update).astype(BF16).astype(F32)
    hidden_in = layer_norm(attended, mlp_gain_ref[...]).astype(BF16)
    total_ref[...] = attended
    chunk = width
    for start in range(0, up_ref.shape[1], chunk):
        raised = dot(hidden_in, up_ref[:, start : start + chunk])
        hidden = (raised * (1.0 + lax.erf(raised * math.sqrt(0.5))) * 0.5).astype(BF16)
        total_ref[...] += dot(hidden, down_ref[start : start + chunk])
    finished = total_ref[...].astype(BF16)
    slot_rows = lax.broadcasted_iota(jnp.int32, (slots, points), 0)
    out_ref[...] = dot(one_hot(slot_rows == slot_row_ref[...]), finished).astype(BF16)


def return_kernel(arrived_ref, slot_ref, out_ref):
    slot_ids = lax.broadcasted_iota(jnp.int32, (out_ref.shape[0], arrived_ref.shape[0]), 1)
    out_ref[...] = dot(one_hot(slot_ref[...] == slot_ids), arrived_ref[...]).astype(BF16)


def face_pairs(devices, dx, dy):
    return [
        (source, source + dx * GY + dy)
        for source in range(devices)
        if 0 <= source // GY + dx < devices // GY and 0 <= source % GY + dy < GY
    ]


def way_round(devices, rows, length):
    chips = devices // 2
    cycle = list(range(0, chips, 2)) + list(range(chips - 1, 0, -2))
    back, on = [], []
    places = [None] * devices
    for place, chip in enumerate(cycle):
        for core in range(2):
            me = 2 * chip + core
            back.append((me, 2 * cycle[(place + 1) % chips] + core))
            on.append((me, 2 * cycle[place - 1] + core))
            order = [0]
            for step in range(1, chips // 2):
                order += [-step, step]
            order.append(chips // 2)
            places[me] = []
            for offset in order:
                start = cycle[(place + offset) % chips] * rows
                column = min(start // 128 * 128, chips * rows - length)
                places[me].append((column, start - column))
    return back, on, places


def padded_taps(neighbours):
    points = neighbours.shape[0]
    own = jnp.arange(points, dtype=jnp.int32)[:, None]
    rest = jnp.zeros((points, 128 - TAPS), jnp.int32)
    middle = TAPS // 2
    return jnp.concatenate(
        [neighbours[:, :middle], own, neighbours[:, middle:], rest], axis=1
    ).astype(F32)


def body(
    features,
    conv_weight,
    cpe_weight,
    cpe_gain,
    attn_gain,
    qkv_weight,
    proj_weight,
    mlp_gain,
    up_weight,
    down_weight,
    face_rows,
    neighbours,
    serial_rank,
    serial_order,
):
    points, width = features.shape
    half = width // 2
    devices = lax.axis_size("blocks")
    index = lax.axis_index("blocks")
    core = lax.rem(index, 2)
    partner = [(source, source ^ 1) for source in range(devices)]
    capacity = 2 * points // devices
    slots = devices * capacity

    unit = conv_weight.shape[0] // TAPS
    units = conv_weight.reshape(TAPS, unit, width)
    kept, sent = units[0::2], units[1::2]
    got = lax.ppermute(sent, "blocks", partner)
    mine = jnp.where(
        core == 0, jnp.concatenate([kept, got]), jnp.concatenate([got, kept])
    ).reshape(TAPS * unit, width)
    round_trip = devices == 2 * GY
    lower = index < GY
    if round_trip:
        across = jnp.where(lower, face_rows[0, 5:], face_rows[0, :3])
        face_list = jnp.concatenate([across, face_rows[0, 3:5]]).reshape(-1, 1)
        counts = (3, 1, 1)
    else:
        face_list = face_rows.reshape(-1, 1)
        counts = (1,) * 8
    size = face_rows.shape[2]
    ordered, *faces = call(
        functools.partial(faces_kernel, unit),
        [jax.ShapeDtypeStruct((points, width), BF16)]
        + [jax.ShapeDtypeStruct((count * size, width), BF16) for count in counts],
        60,
        4 * points * width * width,
        8 * points * width,
    )(features, face_list)

    rows = mine.shape[0]
    length = -(-(rows + 127) // 128) * 128 if round_trip else rows * (devices // 2)
    back_pairs, on_pairs, places = way_round(devices, rows, length)
    back, on = [mine], [mine]

    def pass_on(*beside):
        if not round_trip:
            return beside
        tied = lax.optimization_barrier((back[-1], on[-1], *beside))
        first, second = tied[:2]
        back[-1], on[-1] = first, second
        if len(back) == devices // 4:
            first, second = first[: rows // 2], second[rows // 2 :]
        back.append(lax.ppermute(first, "blocks", back_pairs))
        on.append(lax.ppermute(second, "blocks", on_pairs))
        return tied[2:]

    sent_neighbours = neighbours
    if round_trip:
        lists, back_list, on_list = faces
        side = face_pairs(devices, 1, 0) + face_pairs(devices, -1, 0)
        (lists,) = pass_on(lax.ppermute(lists, "blocks", side))
        to_on = jnp.concatenate([on_list, lists[2 * size :]])
        to_back = jnp.concatenate([back_list, lists[:size]])
        behind = lax.ppermute(to_on, "blocks", face_pairs(devices, 0, 1))
        ahead = lax.ppermute(to_back, "blocks", face_pairs(devices, 0, -1))
        sent_neighbours, lists, behind, ahead = pass_on(neighbours, lists, behind, ahead)
        height = points + 8 * size
        own_table, other_half = call(
            table_kernel,
            [jax.ShapeDtypeStruct((height, half), BF16)] * 2,
            32,
            0,
            4 * height * width,
            in_specs=[pl.BlockSpec(memory_space=pltpu.SMEM)] + [pl.BlockSpec()] * 4,
            scratch_shapes=[pltpu.VMEM((height, width), BF16)],
        )(jnp.stack([lower.astype(jnp.int32), core]), ordered, lists, behind, ahead)
    else:
        got = [
            lax.ppermute(faces[k], "blocks", face_pairs(devices, STEPS_X[k], STEPS_Y[k]))
            for k in range(8)
        ]
        table = jnp.concatenate([ordered, *got], axis=0)
        own_table = lax.dynamic_slice(table, (0, core * half), (table.shape[0], half))
        other_half = lax.dynamic_slice(table, (0, (1 - core) * half), (table.shape[0], half))
    other_table = lax.ppermute(other_half, "blocks", partner)
    other_neighbours = lax.ppermute(sent_neighbours, "blocks", partner)
    own_stacked = gather_block(padded_taps(neighbours), own_table)
    own_stacked, other_table = pass_on(own_stacked, other_table)
    other_stacked = gather_block(padded_taps(other_neighbours), other_table)
    stacked = other_stacked, own_stacked
    if round_trip:
        places = jnp.array(places, jnp.int32)[index]
        early = [[mine], [back[1]], [on[1]], [back[2]], [on[2]]]
        sums = conv_part(stacked, places[:5], early, None, length)
        sums = pass_on(*sums)
        sums = conv_part(stacked, places[5:7], [[back[3]], [on[3]]], sums, length)
        last = [[back[4], on[4]]]
        (for_partner,) = conv_part(stacked[:1], places[7:], last, sums[:1], length)
        (own_part,) = conv_part(stacked[1:], places[7:], last, sums[1:], length)
    else:
        groups = [list(range(first, devices, 2)) for first in range(2)]
        weight = lax.all_gather(mine, "blocks", axis=0, tiled=True, axis_index_groups=groups)
        nowhere = jnp.zeros((1, 2), jnp.int32)
        for_partner, own_part = conv_part(stacked, nowhere, [[weight]], None, length)

    positions = jnp.arange(points, dtype=jnp.int32)
    target = serial_rank // points
    earlier = (target[None, :] == target[:, None]) & (serial_rank[None, :] < serial_rank[:, None])
    out_slot = target * capacity + jnp.sum(earlier.astype(jnp.int32), axis=1)
    anchor = serial_order // points
    before = (anchor[None, :] == anchor[:, None]) & (positions[None, :] < positions[:, None])
    in_slot = anchor * capacity + jnp.sum(before.astype(jnp.int32), axis=1)

    from_partner = lax.ppermute(for_partner, "blocks", partner)

    outgoing = call(
        mix_kernel,
        jax.ShapeDtypeStruct((slots, width), BF16),
        32,
        2 * points * width * (width + slots),
        8 * points * width,
    )(
        own_part,
        from_partner,
        features,
        cpe_weight,
        cpe_gain.reshape(1, width),
        out_slot.reshape(1, points),
    )
    arrived = lax.all_to_all(
        outgoing.reshape(devices, capacity, width), "blocks", split_axis=0, concat_axis=0, tiled=True
    ).reshape(slots, width)

    key_weight = qkv_weight[:, width : 2 * width]
    qv_weight = jnp.concatenate([qkv_weight[:, :width], qkv_weight[:, 2 * width :]], axis=1).T
    weights = (qv_weight, key_weight, proj_weight, up_weight, down_weight)
    back = call(
        block_kernel,
        jax.ShapeDtypeStruct((slots, width), BF16),
        60,
        20 * points * width * width,
        16 * width * width,
        in_specs=[pl.BlockSpec()] * 5 + [pl.BlockSpec(memory_space=pl.ANY)] * len(weights),
        scratch_shapes=[pltpu.VMEM(weight.shape, BF16) for weight in weights]
        + [
            pltpu.SemaphoreType.DMA((len(weights),)),
            pltpu.VMEM((points, width), F32),
            pltpu.VMEM((2 * width, points), BF16),
            pltpu.VMEM((points, width), BF16),
            pltpu.VMEM((width, points), BF16),
            pltpu.VMEM((points, width), F32),
        ],
    )(
        arrived,
        in_slot.reshape(points, 1),
        in_slot.reshape(1, points),
        attn_gain.reshape(1, width),
        mlp_gain.reshape(1, width),
        *weights,
    )
    returned = lax.all_to_all(
        back.reshape(devices, capacity, width), "blocks", split_axis=0, concat_axis=0, tiled=True
    ).reshape(slots, width)
    return call(
        return_kernel,
        jax.ShapeDtypeStruct((points, width), BF16),
        32,
        2 * points * slots * width,
        6 * points * width,
    )(returned, out_slot.reshape(points, 1))


def solution(mesh):
    placed = (
        P(("groups", "blocks"), None),
        P("blocks", None),
        P(),
        P(),
        P(),
        P(),
        P(),
        P(),
        P(),
        P(),
        P(("groups", "blocks"), None, None),
        P(("groups", "blocks"), None),
        P(("groups", "blocks")),
        P(("groups", "blocks")),
    )
    return jax.shard_map(
        body, mesh=mesh, in_specs=placed, out_specs=P(("groups", "blocks"), None), check_vma=False
    )
```

```python
import functools
import math

import jax
import jax.numpy as jnp
from jax import lax
from jax.experimental import pallas as pl
from jax.experimental.pallas import tpu as pltpu
from jax.sharding import PartitionSpec as P

HEADS = 32
GY = 8
HD = 16
TAPS = 27
EPSILON = 1e-05
STEPS_X = (-1, -1, -1, 0, 0, 1, 1, 1)
STEPS_Y = (-1, 0, 1, -1, 1, -1, 0, 1)
F32 = jnp.float32
BF16 = jnp.bfloat16
MIB = 1 << 20


def dot(left, right):
    return jnp.dot(left, right, preferred_element_type=F32)


def layer_norm(inputs, gain_vector):
    row_mean = jnp.mean(inputs, axis=-1, keepdims=True)
    centred = inputs - row_mean
    variance = jnp.mean(centred * centred, axis=-1, keepdims=True)
    return centred * lax.rsqrt(variance + EPSILON) * gain_vector


def one_hot(mask):
    return jnp.where(mask, 1.0, 0.0).astype(BF16)


def call(kernel, out_shape, limit, flops, moved, **extra):
    return pl.pallas_call(
        kernel,
        out_shape=out_shape,
        compiler_params=pltpu.CompilerParams(vmem_limit_bytes=limit * MIB),
        cost_estimate=pl.CostEstimate(flops=flops, bytes_accessed=moved, transcendentals=0),
        **extra,
    )


def faces_kernel(unit, core_ref, features_ref, rows_ref, own_ref, other_ref, *face_refs):
    points, width = features_ref.shape
    half = width // 2
    place = lax.broadcasted_iota(jnp.int32, (width, width), 1)
    within = lax.rem(place, half)
    source = (within // unit) * (2 * unit) + (place // half) * unit + lax.rem(place, unit)
    channel = lax.broadcasted_iota(jnp.int32, (width, width), 0)
    ordered = dot(features_ref[...], one_hot(channel == source)).astype(BF16)
    first, second = ordered[:, :half], ordered[:, half:]
    even = core_ref[0] == 0
    own_ref[...] = jnp.where(even, first, second)
    other_ref[...] = jnp.where(even, second, first)
    row_ids = lax.broadcasted_iota(jnp.int32, (rows_ref.shape[0], points), 1)
    rows = dot(one_hot(rows_ref[...] == row_ids), ordered).astype(BF16)
    taken = 0
    for ref in face_refs:
        ref[...] = rows[taken : taken + ref.shape[0]]
        taken += ref.shape[0]


def received_kernel(flags_ref, side_ref, behind_ref, ahead_ref, own_ref, other_ref):
    size = behind_ref.shape[0] // 2
    half = own_ref.shape[1]
    lower, even = flags_ref[0] == 1, flags_ref[1] == 0
    across = [ahead_ref[size:], side_ref[size : 2 * size], behind_ref[size:]]
    along = [ahead_ref[:size], behind_ref[:size]]
    for at, (low, high) in enumerate(zip(across + along, along + across)):
        rows = jnp.where(lower, low, high)
        first, second = rows[:, :half], rows[:, half:]
        own_ref[at * size : (at + 1) * size] = jnp.where(even, first, second)
        other_ref[at * size : (at + 1) * size] = jnp.where(even, second, first)


def gather_kernel(taps, start_ref, rows_ref, table_ref, *refs):
    out_ref = refs[-1]
    height, half = table_ref.shape
    lane = lax.broadcasted_iota(jnp.int32, rows_ref.shape, 1)
    row_ids = (lax.broadcasted_iota(jnp.int32, (1, height), 1) + start_ref[0]).astype(F32)
    for at in range(taps):
        chosen = lane == taps * pl.program_id(0) + at
        column = jnp.sum(jnp.where(chosen, rows_ref[...], 0.0), axis=1, keepdims=True)
        taken = dot(one_hot(column == row_ids), table_ref[...])
        place = slice(at * half, (at + 1) * half)
        if len(refs) > 1:
            taken += refs[0][:, place].astype(F32)
        out_ref[:, place] = taken.astype(BF16)


def gather_part(start, rows, table, before=None):
    points, lanes = rows.shape
    height, half = table.shape
    taps = 3
    whole = lambda step: (0, 0)
    block = pl.BlockSpec((points, taps * half), lambda step: (0, step))
    extra = [] if before is None else [before]
    return call(
        functools.partial(gather_kernel, taps),
        jax.ShapeDtypeStruct((points, TAPS * half), BF16),
        60,
        2 * TAPS * points * height * half,
        2 * TAPS * points * half * (1 + len(extra)),
        grid=(TAPS // taps,),
        in_specs=[
            pl.BlockSpec(memory_space=pltpu.SMEM),
            pl.BlockSpec((points, lanes), whole),
            pl.BlockSpec((height, half), whole),
        ]
        + [block] * len(extra),
        out_specs=block,
        input_output_aliases={3: 0} if extra else {},
    )(start, rows, table, *extra)


def conv_kernel(slots, blocks, first, places_ref, *refs):
    stacked, refs = refs[:blocks], refs[blocks:]
    pieces, refs = refs[: sum(slots)], refs[sum(slots) :]
    before = [] if first else refs[:blocks]
    outs, (lhs, held, sems) = refs[-3 - blocks : -3], refs[-3:]
    length = held.shape[1]
    copies, taken = [], 0
    for at, count in enumerate(slots):
        column = pl.multiple_of(places_ref[2 * at], 128)
        row = pl.multiple_of(places_ref[2 * at + 1], 16)
        copies.append([])
        for block in range(blocks):
            copy = pltpu.make_async_copy(
                stacked[block].at[:, pl.ds(column, length)], lhs.at[at, block], sems.at[at, block]
            )
            copy.start()
            copies[-1].append(copy)
        short = count * pieces[taken].shape[0]
        edge = length - short
        if edge:
            held[at, :edge] = jnp.zeros((edge, held.shape[2]), BF16)
            held[at, length - edge :] = jnp.zeros((edge, held.shape[2]), BF16)
        for part in range(count):
            piece = pieces[taken]
            size = piece.shape[0]
            copy = pltpu.make_async_copy(
                piece, held.at[at, pl.ds(row + part * size, size)], sems.at[at, 2 + part]
            )
            copy.start()
            copies[-1].append(copy)
            taken += 1
    for at in range(len(slots)):
        for copy in copies[at]:
            copy.wait()
        for block, ref in enumerate(outs):
            product = dot(lhs[at, block], held[at])
            if at > 0:
                ref[...] += product
            elif first:
                ref[...] = product
            else:
                ref[...] = before[block][...] + product


def conv_part(stacked, places, pieces, before, length):
    points, depth = stacked[0].shape
    width = pieces[0][0].shape[1]
    slots = [len(parts) for parts in pieces]
    flat = [piece for parts in pieces for piece in parts]
    blocks = len(stacked)
    held = 1 + blocks + len(flat)
    return call(
        functools.partial(conv_kernel, slots, blocks, before is None),
        [jax.ShapeDtypeStruct((points, width), F32)] * blocks,
        60,
        2 * blocks * points * length * width * len(slots),
        2 * length * (blocks * points + width) * len(slots),
        in_specs=[pl.BlockSpec(memory_space=pltpu.SMEM)]
        + [pl.BlockSpec(memory_space=pl.ANY)] * (held - 1)
        + ([] if before is None else [pl.BlockSpec()] * blocks),
        input_output_aliases=(
            {} if before is None else {held + block: block for block in range(blocks)}
        ),
        scratch_shapes=[
            pltpu.VMEM((len(slots), blocks, points, length), BF16),
            pltpu.VMEM((len(slots), length, width), BF16),
            pltpu.SemaphoreType.DMA((len(slots), 4)),
        ],
    )(places.reshape(-1), *stacked, *flat, *(before or ()))


def mix_kernel(own_ref, got_ref, features_ref, weight_ref, gain_ref, slot_ref, out_ref):
    convolved = (own_ref[...] + got_ref[...]).astype(BF16)
    linear = dot(convolved, weight_ref[...])
    mixed = (features_ref[...].astype(F32) + layer_norm(linear, gain_ref[...])).astype(BF16)
    slots = lax.broadcasted_iota(jnp.int32, (out_ref.shape[0], mixed.shape[0]), 0)
    out_ref[...] = dot(one_hot(slots == slot_ref[...]), mixed).astype(BF16)


def block_kernel(
    arrived_ref,
    slot_col_ref,
    slot_row_ref,
    attn_gain_ref,
    mlp_gain_ref,
    qv_hbm,
    key_hbm,
    proj_hbm,
    up_hbm,
    down_hbm,
    out_ref,
    qv_ref,
    key_ref,
    proj_ref,
    up_ref,
    down_ref,
    sems,
    serial_ref,
    qv_cols_ref,
    keys_ref,
    heads_ref,
    total_ref,
):
    sources = (key_hbm, qv_hbm, proj_hbm, up_hbm, down_hbm)
    targets = (key_ref, qv_ref, proj_ref, up_ref, down_ref)
    copies = [
        pltpu.make_async_copy(source, target, sems.at[at])
        for at, (source, target) in enumerate(zip(sources, targets))
    ]
    for copy in copies:
        copy.start()
    slots = arrived_ref.shape[0]
    points, width = serial_ref.shape
    slot_ids = lax.broadcasted_iota(jnp.int32, (points, slots), 1)
    serial = dot(one_hot(slot_col_ref[...] == slot_ids), arrived_ref[...])
    serial_ref[...] = serial
    normed = layer_norm(serial, attn_gain_ref[...]).astype(BF16)
    copies[0].wait()
    keys_ref[...] = dot(normed, key_ref[...]).astype(BF16)
    copies[1].wait()
    factor = math.log2(math.e) / math.sqrt(HD)
    contract_last = (((1,), (1,)), ((), ()))
    qv_cols_ref[:width] = (
        lax.dot_general(qv_ref[:width], normed, contract_last, preferred_element_type=F32) * factor
    ).astype(BF16)
    qv_cols_ref[width:] = lax.dot_general(
        qv_ref[width:], normed, contract_last, preferred_element_type=F32
    ).astype(BF16)
    ones = jnp.ones((HD, points), BF16)
    per_group = 128 // HD
    head_of_row = lax.broadcasted_iota(jnp.int32, (128, points), 0) // HD

    for group in range(HEADS // per_group):
        base = group * 128

        def attend(head, carry):
            group_queries = qv_cols_ref[base : base + 128]
            queries = jnp.where(head_of_row == head, group_queries.astype(F32), 0.0).astype(BF16)
            scores = dot(keys_ref[:, base : base + 128], queries)
            weights = jnp.exp2(scores - jnp.max(scores, axis=0, keepdims=True)).astype(BF16)
            at = pl.multiple_of(base + head * HD, HD)
            values = qv_cols_ref[pl.ds(width + at, HD)]
            sums = dot(jnp.concatenate([values, ones], axis=0), weights)
            heads_ref[pl.ds(at, HD)] = (sums[:HD] / sums[HD : HD + 1]).astype(BF16)
            return carry

        lax.fori_loop(0, per_group, attend, 0, unroll=4)

    for copy in copies[2:]:
        copy.wait()
    update = lax.dot_general(
        heads_ref[...], proj_ref[...], (((0,), (0,)), ((), ())), preferred_element_type=F32
    )
    attended = (serial_ref[...] + update).astype(BF16).astype(F32)
    hidden_in = layer_norm(attended, mlp_gain_ref[...]).astype(BF16)
    total_ref[...] = attended
    chunk = width
    for start in range(0, up_ref.shape[1], chunk):
        raised = dot(hidden_in, up_ref[:, start : start + chunk])
        hidden = (raised * (1.0 + lax.erf(raised * math.sqrt(0.5))) * 0.5).astype(BF16)
        total_ref[...] += dot(hidden, down_ref[start : start + chunk])
    finished = total_ref[...].astype(BF16)
    slot_rows = lax.broadcasted_iota(jnp.int32, (slots, points), 0)
    out_ref[...] = dot(one_hot(slot_rows == slot_row_ref[...]), finished).astype(BF16)


def return_kernel(arrived_ref, slot_ref, out_ref):
    slot_ids = lax.broadcasted_iota(jnp.int32, (out_ref.shape[0], arrived_ref.shape[0]), 1)
    out_ref[...] = dot(one_hot(slot_ref[...] == slot_ids), arrived_ref[...]).astype(BF16)


def face_pairs(devices, dx, dy):
    return [
        (source, source + dx * GY + dy)
        for source in range(devices)
        if 0 <= source // GY + dx < devices // GY and 0 <= source % GY + dy < GY
    ]


def way_round(devices, rows, length):
    chips = devices // 2
    cycle = list(range(0, chips, 2)) + list(range(chips - 1, 0, -2))
    back, on = [], []
    places = [None] * devices
    for place, chip in enumerate(cycle):
        for core in range(2):
            me = 2 * chip + core
            back.append((me, 2 * cycle[(place + 1) % chips] + core))
            on.append((me, 2 * cycle[place - 1] + core))
            order = [0]
            for step in range(1, chips // 2):
                order += [-step, step]
            order.append(chips // 2)
            places[me] = []
            for offset in order:
                start = cycle[(place + offset) % chips] * rows
                column = min(start // 128 * 128, chips * rows - length)
                places[me].append((column, start - column))
    return back, on, places


def padded_taps(neighbours):
    points = neighbours.shape[0]
    own = jnp.arange(points, dtype=jnp.int32)[:, None]
    rest = jnp.zeros((points, 128 - TAPS), jnp.int32)
    middle = TAPS // 2
    return jnp.concatenate(
        [neighbours[:, :middle], own, neighbours[:, middle:], rest], axis=1
    ).astype(F32)


def body(
    features,
    conv_weight,
    cpe_weight,
    cpe_gain,
    attn_gain,
    qkv_weight,
    proj_weight,
    mlp_gain,
    up_weight,
    down_weight,
    face_rows,
    neighbours,
    serial_rank,
    serial_order,
):
    points, width = features.shape
    half = width // 2
    devices = lax.axis_size("blocks")
    index = lax.axis_index("blocks")
    core = lax.rem(index, 2)
    partner = [(source, source ^ 1) for source in range(devices)]
    capacity = 2 * points // devices
    slots = devices * capacity

    unit = conv_weight.shape[0] // TAPS
    units = conv_weight.reshape(TAPS, unit, width)
    kept, sent = units[0::2], units[1::2]
    got = lax.ppermute(sent, "blocks", partner)
    mine = jnp.where(
        core == 0, jnp.concatenate([kept, got]), jnp.concatenate([got, kept])
    ).reshape(TAPS * unit, width)
    round_trip = devices == 2 * GY
    lower = index < GY
    if round_trip:
        across = jnp.where(lower, face_rows[0, 5:], face_rows[0, :3])
        face_list = jnp.concatenate([across, face_rows[0, 3:5]]).reshape(-1, 1)
        counts = (3, 1, 1)
    else:
        face_list = face_rows.reshape(-1, 1)
        counts = (1,) * 8
    size = face_rows.shape[2]
    own_local, other_half, *faces = call(
        functools.partial(faces_kernel, unit),
        [jax.ShapeDtypeStruct((points, half), BF16)] * 2
        + [jax.ShapeDtypeStruct((count * size, width), BF16) for count in counts],
        60,
        4 * points * width * width,
        8 * points * width,
        in_specs=[pl.BlockSpec(memory_space=pltpu.SMEM)] + [pl.BlockSpec()] * 2,
    )(core.reshape(1), features, face_list)
    other_local = lax.ppermute(other_half, "blocks", partner)
    other_neighbours = lax.ppermute(neighbours, "blocks", partner)

    rows = mine.shape[0]
    length = -(-(rows + 127) // 128) * 128 if round_trip else rows * (devices // 2)
    back_pairs, on_pairs, places = way_round(devices, rows, length)
    back, on = [mine], [mine]

    def pass_on(*beside):
        if not round_trip:
            return beside
        tied = lax.optimization_barrier((back[-1], on[-1], *beside))
        first, second = tied[:2]
        back[-1], on[-1] = first, second
        if len(back) == devices // 4:
            first, second = first[: rows // 2], second[rows // 2 :]
        back.append(lax.ppermute(first, "blocks", back_pairs))
        on.append(lax.ppermute(second, "blocks", on_pairs))
        return tied[2:]

    if round_trip:
        lists, back_list, on_list = faces
        side = face_pairs(devices, 1, 0) + face_pairs(devices, -1, 0)
        lists = lax.ppermute(lists, "blocks", side)
        other_local, other_neighbours = pass_on(other_local, other_neighbours)
    own_rows, other_rows = padded_taps(neighbours), padded_taps(other_neighbours)
    nothing = jnp.zeros((1,), jnp.int32)
    own_stacked = gather_part(nothing, own_rows, own_local)
    other_stacked = gather_part(nothing, other_rows, other_local)
    if round_trip:
        own_stacked, lists = lax.optimization_barrier((own_stacked, lists))
        to_on = jnp.concatenate([on_list, lists[2 * size :]])
        to_back = jnp.concatenate([back_list, lists[:size]])
        behind = lax.ppermute(to_on, "blocks", face_pairs(devices, 0, 1))
        ahead = lax.ppermute(to_back, "blocks", face_pairs(devices, 0, -1))
        own_stacked, other_stacked, lists, behind, ahead = pass_on(
            own_stacked, other_stacked, lists, behind, ahead
        )
        own_remote, other_half = call(
            received_kernel,
            [jax.ShapeDtypeStruct((5 * size, half), BF16)] * 2,
            32,
            0,
            20 * size * width,
            in_specs=[pl.BlockSpec(memory_space=pltpu.SMEM)] + [pl.BlockSpec()] * 3,
        )(jnp.stack([lower.astype(jnp.int32), core]), lists, behind, ahead)
        start = jnp.where(lower, points, points + 3 * size).reshape(1)
    else:
        received = jnp.concatenate(
            [
                lax.ppermute(faces[k], "blocks", face_pairs(devices, STEPS_X[k], STEPS_Y[k]))
                for k in range(8)
            ]
        )
        own_remote = lax.dynamic_slice(received, (0, core * half), (8 * size, half))
        other_half = lax.dynamic_slice(received, (0, (1 - core) * half), (8 * size, half))
        start = nothing + points
    other_remote = lax.ppermute(other_half, "blocks", partner)
    own_stacked = gather_part(start, own_rows, own_remote, own_stacked)
    other_stacked = gather_part(start, other_rows, other_remote, other_stacked)
    stacked = pass_on(other_stacked, own_stacked)
    if round_trip:
        places = jnp.array(places, jnp.int32)[index]
        early = [[mine], [back[1]], [on[1]], [back[2]], [on[2]]]
        sums = conv_part(stacked, places[:5], early, None, length)
        sums = pass_on(*sums)
        sums = conv_part(stacked, places[5:7], [[back[3]], [on[3]]], sums, length)
        last = [[back[4], on[4]]]
        (for_partner,) = conv_part(stacked[:1], places[7:], last, sums[:1], length)
        (own_part,) = conv_part(stacked[1:], places[7:], last, sums[1:], length)
    else:
        groups = [list(range(first, devices, 2)) for first in range(2)]
        weight = lax.all_gather(mine, "blocks", axis=0, tiled=True, axis_index_groups=groups)
        nowhere = jnp.zeros((1, 2), jnp.int32)
        for_partner, own_part = conv_part(stacked, nowhere, [[weight]], None, length)

    positions = jnp.arange(points, dtype=jnp.int32)
    target = serial_rank // points
    earlier = (target[None, :] == target[:, None]) & (serial_rank[None, :] < serial_rank[:, None])
    out_slot = target * capacity + jnp.sum(earlier.astype(jnp.int32), axis=1)
    anchor = serial_order // points
    before = (anchor[None, :] == anchor[:, None]) & (positions[None, :] < positions[:, None])
    in_slot = anchor * capacity + jnp.sum(before.astype(jnp.int32), axis=1)

    from_partner = lax.ppermute(for_partner, "blocks", partner)

    outgoing = call(
        mix_kernel,
        jax.ShapeDtypeStruct((slots, width), BF16),
        60,
        2 * points * width * (width + slots),
        8 * points * width,
    )(
        own_part,
        from_partner,
        features,
        cpe_weight,
        cpe_gain.reshape(1, width),
        out_slot.reshape(1, points),
    )
    arrived = lax.all_to_all(
        outgoing.reshape(devices, capacity, width), "blocks", split_axis=0, concat_axis=0, tiled=True
    ).reshape(slots, width)

    key_weight = qkv_weight[:, width : 2 * width]
    qv_weight = jnp.concatenate([qkv_weight[:, :width], qkv_weight[:, 2 * width :]], axis=1).T
    weights = (qv_weight, key_weight, proj_weight, up_weight, down_weight)
    back = call(
        block_kernel,
        jax.ShapeDtypeStruct((slots, width), BF16),
        60,
        20 * points * width * width,
        16 * width * width,
        in_specs=[pl.BlockSpec()] * 5 + [pl.BlockSpec(memory_space=pl.ANY)] * len(weights),
        scratch_shapes=[pltpu.VMEM(weight.shape, BF16) for weight in weights]
        + [
            pltpu.SemaphoreType.DMA((len(weights),)),
            pltpu.VMEM((points, width), F32),
            pltpu.VMEM((2 * width, points), BF16),
            pltpu.VMEM((points, width), BF16),
            pltpu.VMEM((width, points), BF16),
            pltpu.VMEM((points, width), F32),
        ],
    )(
        arrived,
        in_slot.reshape(points, 1),
        in_slot.reshape(1, points),
        attn_gain.reshape(1, width),
        mlp_gain.reshape(1, width),
        *weights,
    )
    returned = lax.all_to_all(
        back.reshape(devices, capacity, width), "blocks", split_axis=0, concat_axis=0, tiled=True
    ).reshape(slots, width)
    return call(
        return_kernel,
        jax.ShapeDtypeStruct((points, width), BF16),
        32,
        2 * points * slots * width,
        6 * points * width,
    )(returned, out_slot.reshape(points, 1))


def solution(mesh):
    placed = (
        P(("groups", "blocks"), None),
        P("blocks", None),
        P(),
        P(),
        P(),
        P(),
        P(),
        P(),
        P(),
        P(),
        P(("groups", "blocks"), None, None),
        P(("groups", "blocks"), None),
        P(("groups", "blocks")),
        P(("groups", "blocks")),
    )
    return jax.shard_map(
        body, mesh=mesh, in_specs=placed, out_specs=P(("groups", "blocks"), None), check_vma=False
    )
```

```python
import functools
import math

import jax
import jax.numpy as jnp
from jax import lax
from jax.experimental import pallas as pl
from jax.experimental.pallas import tpu as pltpu
from jax.sharding import PartitionSpec as P

HEADS = 32
GY = 8
HD = 16
TAPS = 27
EPSILON = 1e-05
STEPS_X = (-1, -1, -1, 0, 0, 1, 1, 1)
STEPS_Y = (-1, 0, 1, -1, 1, -1, 0, 1)
F32 = jnp.float32
BF16 = jnp.bfloat16
MIB = 1 << 20


def dot(left, right):
    return jnp.dot(left, right, preferred_element_type=F32)


def layer_norm(inputs, gain_vector):
    row_mean = jnp.mean(inputs, axis=-1, keepdims=True)
    centred = inputs - row_mean
    variance = jnp.mean(centred * centred, axis=-1, keepdims=True)
    return centred * lax.rsqrt(variance + EPSILON) * gain_vector


def one_hot(mask):
    return jnp.where(mask, 1.0, 0.0).astype(BF16)


def call(kernel, out_shape, limit, flops, moved, **extra):
    return pl.pallas_call(
        kernel,
        out_shape=out_shape,
        compiler_params=pltpu.CompilerParams(vmem_limit_bytes=limit * MIB),
        cost_estimate=pl.CostEstimate(flops=flops, bytes_accessed=moved, transcendentals=0),
        **extra,
    )


def faces_kernel(unit, core_ref, features_ref, rows_ref, own_ref, other_ref, *face_refs):
    points, width = features_ref.shape
    half = width // 2
    place = lax.broadcasted_iota(jnp.int32, (width, width), 1)
    within = lax.rem(place, half)
    source = (within // unit) * (2 * unit) + (place // half) * unit + lax.rem(place, unit)
    channel = lax.broadcasted_iota(jnp.int32, (width, width), 0)
    ordered = dot(features_ref[...], one_hot(channel == source)).astype(BF16)
    first, second = ordered[:, :half], ordered[:, half:]
    even = core_ref[0] == 0
    own_ref[...] = jnp.where(even, first, second)
    other_ref[...] = jnp.where(even, second, first)
    row_ids = lax.broadcasted_iota(jnp.int32, (rows_ref.shape[0], points), 1)
    rows = dot(one_hot(rows_ref[...] == row_ids), ordered).astype(BF16)
    taken = 0
    for ref in face_refs:
        ref[...] = rows[taken : taken + ref.shape[0]]
        taken += ref.shape[0]


def received_kernel(flags_ref, side_ref, behind_ref, ahead_ref, own_ref, other_ref):
    size = behind_ref.shape[0] // 2
    half = own_ref.shape[1]
    lower, even = flags_ref[0] == 1, flags_ref[1] == 0
    across = [ahead_ref[size:], side_ref[size : 2 * size], behind_ref[size:]]
    along = [ahead_ref[:size], behind_ref[:size]]
    for at, (low, high) in enumerate(zip(across + along, along + across)):
        rows = jnp.where(lower, low, high)
        first, second = rows[:, :half], rows[:, half:]
        own_ref[at * size : (at + 1) * size] = jnp.where(even, first, second)
        other_ref[at * size : (at + 1) * size] = jnp.where(even, second, first)
    rest = jnp.zeros((size, half), BF16)
    own_ref[5 * size :] = rest
    other_ref[5 * size :] = rest


def gather_kernel(taps, start_ref, rows_ref, own_ref, got_ref, out_ref):
    half = own_ref.shape[1]
    part = lax.rem(lax.broadcasted_iota(jnp.int32, (rows_ref.shape[1], 128), 0), 128)
    lane = lax.broadcasted_iota(jnp.int32, (1, 128), 1)
    for at in range(taps):
        chosen = one_hot(part == taps * pl.program_id(0) + at)
        index = dot(rows_ref[...], chosen)
        taken = None
        for table, start in ((own_ref, 0), (got_ref, start_ref[0])):
            hits = [
                one_hot(index == (lane + (start + first)).astype(F32))
                for first in range(0, table.shape[0], 128)
            ]
            product = dot(jnp.concatenate(hits, axis=1), table[...])
            taken = product if taken is None else taken + product
        out_ref[:, at * half : (at + 1) * half] = taken.astype(BF16)


def gather_block(start, rows, own, got):
    points, lanes = rows.shape
    half = own.shape[1]
    height = own.shape[0] + got.shape[0]
    taps = 3
    whole = lambda step: (0, 0)
    return call(
        functools.partial(gather_kernel, taps),
        jax.ShapeDtypeStruct((points, TAPS * half), BF16),
        60,
        2 * TAPS * points * height * half,
        2 * TAPS * points * half,
        grid=(TAPS // taps,),
        in_specs=[
            pl.BlockSpec(memory_space=pltpu.SMEM),
            pl.BlockSpec((points, lanes), whole),
            pl.BlockSpec(own.shape, whole),
            pl.BlockSpec(got.shape, whole),
        ],
        out_specs=pl.BlockSpec((points, taps * half), lambda step: (0, step)),
    )(start, rows, own, got)


def conv_kernel(slots, blocks, first, places_ref, *refs):
    stacked, refs = refs[:blocks], refs[blocks:]
    pieces, refs = refs[: sum(slots)], refs[sum(slots) :]
    before = [] if first else refs[:blocks]
    outs, (lhs, held, sems) = refs[-3 - blocks : -3], refs[-3:]
    length = held.shape[1]
    copies, taken = [], 0
    for at, count in enumerate(slots):
        column = pl.multiple_of(places_ref[2 * at], 128)
        row = pl.multiple_of(places_ref[2 * at + 1], 16)
        copies.append([])
        for block in range(blocks):
            copy = pltpu.make_async_copy(
                stacked[block].at[:, pl.ds(column, length)], lhs.at[at, block], sems.at[at, block]
            )
            copy.start()
            copies[-1].append(copy)
        short = count * pieces[taken].shape[0]
        edge = length - short
        if edge:
            held[at, :edge] = jnp.zeros((edge, held.shape[2]), BF16)
            held[at, length - edge :] = jnp.zeros((edge, held.shape[2]), BF16)
        for part in range(count):
            piece = pieces[taken]
            size = piece.shape[0]
            copy = pltpu.make_async_copy(
                piece, held.at[at, pl.ds(row + part * size, size)], sems.at[at, 2 + part]
            )
            copy.start()
            copies[-1].append(copy)
            taken += 1
    for at in range(len(slots)):
        for copy in copies[at]:
            copy.wait()
        for block, ref in enumerate(outs):
            product = dot(lhs[at, block], held[at])
            if at > 0:
                ref[...] += product
            elif first:
                ref[...] = product
            else:
                ref[...] = before[block][...] + product


def conv_part(stacked, places, pieces, before, length):
    points, depth = stacked[0].shape
    width = pieces[0][0].shape[1]
    slots = [len(parts) for parts in pieces]
    flat = [piece for parts in pieces for piece in parts]
    blocks = len(stacked)
    held = 1 + blocks + len(flat)
    return call(
        functools.partial(conv_kernel, slots, blocks, before is None),
        [jax.ShapeDtypeStruct((points, width), F32)] * blocks,
        60,
        2 * blocks * points * length * width * len(slots),
        2 * length * (blocks * points + width) * len(slots),
        in_specs=[pl.BlockSpec(memory_space=pltpu.SMEM)]
        + [pl.BlockSpec(memory_space=pl.ANY)] * (held - 1)
        + ([] if before is None else [pl.BlockSpec()] * blocks),
        input_output_aliases=(
            {} if before is None else {held + block: block for block in range(blocks)}
        ),
        scratch_shapes=[
            pltpu.VMEM((len(slots), blocks, points, length), BF16),
            pltpu.VMEM((len(slots), length, width), BF16),
            pltpu.SemaphoreType.DMA((len(slots), 4)),
        ],
    )(places.reshape(-1), *stacked, *flat, *(before or ()))


def mix_kernel(own_ref, got_ref, features_ref, weight_ref, gain_ref, slot_ref, out_ref):
    convolved = (own_ref[...] + got_ref[...]).astype(BF16)
    linear = dot(convolved, weight_ref[...])
    mixed = (features_ref[...].astype(F32) + layer_norm(linear, gain_ref[...])).astype(BF16)
    slots = lax.broadcasted_iota(jnp.int32, (out_ref.shape[0], mixed.shape[0]), 0)
    out_ref[...] = dot(one_hot(slots == slot_ref[...]), mixed).astype(BF16)


def block_kernel(
    arrived_ref,
    slot_col_ref,
    slot_row_ref,
    attn_gain_ref,
    mlp_gain_ref,
    qv_hbm,
    key_hbm,
    proj_hbm,
    up_hbm,
    down_hbm,
    out_ref,
    qv_ref,
    key_ref,
    proj_ref,
    up_ref,
    down_ref,
    sems,
    serial_ref,
    qv_cols_ref,
    keys_ref,
    heads_ref,
    total_ref,
):
    sources = (key_hbm, qv_hbm, proj_hbm, up_hbm, down_hbm)
    targets = (key_ref, qv_ref, proj_ref, up_ref, down_ref)
    copies = [
        pltpu.make_async_copy(source, target, sems.at[at])
        for at, (source, target) in enumerate(zip(sources, targets))
    ]
    for copy in copies:
        copy.start()
    slots = arrived_ref.shape[0]
    points, width = serial_ref.shape
    slot_ids = lax.broadcasted_iota(jnp.int32, (points, slots), 1)
    serial = dot(one_hot(slot_col_ref[...] == slot_ids), arrived_ref[...])
    serial_ref[...] = serial
    normed = layer_norm(serial, attn_gain_ref[...]).astype(BF16)
    copies[0].wait()
    keys_ref[...] = dot(normed, key_ref[...]).astype(BF16)
    copies[1].wait()
    factor = math.log2(math.e) / math.sqrt(HD)
    contract_last = (((1,), (1,)), ((), ()))
    qv_cols_ref[:width] = (
        lax.dot_general(qv_ref[:width], normed, contract_last, preferred_element_type=F32) * factor
    ).astype(BF16)
    qv_cols_ref[width:] = lax.dot_general(
        qv_ref[width:], normed, contract_last, preferred_element_type=F32
    ).astype(BF16)
    ones = jnp.ones((HD, points), BF16)
    per_group = 128 // HD
    head_of_row = lax.broadcasted_iota(jnp.int32, (128, points), 0) // HD

    for group in range(HEADS // per_group):
        base = group * 128

        def attend(head, carry):
            group_queries = qv_cols_ref[base : base + 128]
            queries = jnp.where(head_of_row == head, group_queries.astype(F32), 0.0).astype(BF16)
            scores = dot(keys_ref[:, base : base + 128], queries)
            weights = jnp.exp2(scores - jnp.max(scores, axis=0, keepdims=True)).astype(BF16)
            at = pl.multiple_of(base + head * HD, HD)
            values = qv_cols_ref[pl.ds(width + at, HD)]
            sums = dot(jnp.concatenate([values, ones], axis=0), weights)
            heads_ref[pl.ds(at, HD)] = (sums[:HD] / sums[HD : HD + 1]).astype(BF16)
            return carry

        lax.fori_loop(0, per_group, attend, 0, unroll=4)

    for copy in copies[2:]:
        copy.wait()
    update = lax.dot_general(
        heads_ref[...], proj_ref[...], (((0,), (0,)), ((), ())), preferred_element_type=F32
    )
    attended = (serial_ref[...] + update).astype(BF16).astype(F32)
    hidden_in = layer_norm(attended, mlp_gain_ref[...]).astype(BF16)
    total_ref[...] = attended
    chunk = width
    for start in range(0, up_ref.shape[1], chunk):
        raised = dot(hidden_in, up_ref[:, start : start + chunk])
        hidden = (raised * (1.0 + lax.erf(raised * math.sqrt(0.5))) * 0.5).astype(BF16)
        total_ref[...] += dot(hidden, down_ref[start : start + chunk])
    finished = total_ref[...].astype(BF16)
    slot_rows = lax.broadcasted_iota(jnp.int32, (slots, points), 0)
    out_ref[...] = dot(one_hot(slot_rows == slot_row_ref[...]), finished).astype(BF16)


def return_kernel(arrived_ref, slot_ref, out_ref):
    slot_ids = lax.broadcasted_iota(jnp.int32, (out_ref.shape[0], arrived_ref.shape[0]), 1)
    out_ref[...] = dot(one_hot(slot_ref[...] == slot_ids), arrived_ref[...]).astype(BF16)


def face_pairs(devices, dx, dy):
    return [
        (source, source + dx * GY + dy)
        for source in range(devices)
        if 0 <= source // GY + dx < devices // GY and 0 <= source % GY + dy < GY
    ]


def way_round(devices, rows, length):
    chips = devices // 2
    cycle = list(range(0, chips, 2)) + list(range(chips - 1, 0, -2))
    back, on = [], []
    places = [None] * devices
    for place, chip in enumerate(cycle):
        for core in range(2):
            me = 2 * chip + core
            back.append((me, 2 * cycle[(place + 1) % chips] + core))
            on.append((me, 2 * cycle[place - 1] + core))
            order = [0]
            for step in range(1, chips // 2):
                order += [-step, step]
            order.append(chips // 2)
            places[me] = []
            for offset in order:
                start = cycle[(place + offset) % chips] * rows
                column = min(start // 128 * 128, chips * rows - length)
                places[me].append((column, start - column))
    return back, on, places


def padded_taps(neighbours):
    points = neighbours.shape[0]
    own = jnp.arange(points, dtype=jnp.int32)[:, None]
    rest = jnp.zeros((points, 128 - TAPS), jnp.int32)
    middle = TAPS // 2
    rows = jnp.concatenate([neighbours[:, :middle], own, neighbours[:, middle:], rest], axis=1)
    fine = rows % 32
    return jnp.concatenate([rows - fine, fine], axis=1).astype(BF16)


def body(
    features,
    conv_weight,
    cpe_weight,
    cpe_gain,
    attn_gain,
    qkv_weight,
    proj_weight,
    mlp_gain,
    up_weight,
    down_weight,
    face_rows,
    neighbours,
    serial_rank,
    serial_order,
):
    points, width = features.shape
    half = width // 2
    devices = lax.axis_size("blocks")
    index = lax.axis_index("blocks")
    core = lax.rem(index, 2)
    partner = [(source, source ^ 1) for source in range(devices)]
    capacity = 2 * points // devices
    slots = devices * capacity

    unit = conv_weight.shape[0] // TAPS
    units = conv_weight.reshape(TAPS, unit, width)
    kept, sent = units[0::2], units[1::2]
    got = lax.ppermute(sent, "blocks", partner)
    mine = jnp.where(
        core == 0, jnp.concatenate([kept, got]), jnp.concatenate([got, kept])
    ).reshape(TAPS * unit, width)
    round_trip = devices == 2 * GY
    lower = index < GY
    if round_trip:
        across = jnp.where(lower, face_rows[0, 5:], face_rows[0, :3])
        face_list = jnp.concatenate([across, face_rows[0, 3:5]]).reshape(-1, 1)
        counts = (3, 1, 1)
    else:
        face_list = face_rows.reshape(-1, 1)
        counts = (1,) * 8
    size = face_rows.shape[2]
    own_local, other_half, *faces = call(
        functools.partial(faces_kernel, unit),
        [jax.ShapeDtypeStruct((points, half), BF16)] * 2
        + [jax.ShapeDtypeStruct((count * size, width), BF16) for count in counts],
        60,
        4 * points * width * width,
        8 * points * width,
        in_specs=[pl.BlockSpec(memory_space=pltpu.SMEM)] + [pl.BlockSpec()] * 2,
    )(core.reshape(1), features, face_list)
    other_local = lax.ppermute(other_half, "blocks", partner)
    other_neighbours = lax.ppermute(neighbours, "blocks", partner)

    rows = mine.shape[0]
    length = -(-(rows + 127) // 128) * 128 if round_trip else rows * (devices // 2)
    back_pairs, on_pairs, places = way_round(devices, rows, length)
    back, on = [mine], [mine]

    def pass_on(*beside):
        if not round_trip:
            return beside
        tied = lax.optimization_barrier((back[-1], on[-1], *beside))
        first, second = tied[:2]
        back[-1], on[-1] = first, second
        if len(back) == devices // 4:
            first, second = first[: rows // 2], second[rows // 2 :]
        back.append(lax.ppermute(first, "blocks", back_pairs))
        on.append(lax.ppermute(second, "blocks", on_pairs))
        return tied[2:]

    if round_trip:
        lists, back_list, on_list = faces
        side = face_pairs(devices, 1, 0) + face_pairs(devices, -1, 0)
        lists, other_local, other_neighbours = pass_on(lists, other_local, other_neighbours)
        lists = lax.ppermute(lists, "blocks", side)
    own_rows, other_rows = padded_taps(neighbours), padded_taps(other_neighbours)
    if round_trip:
        to_on = jnp.concatenate([on_list, lists[2 * size :]])
        to_back = jnp.concatenate([back_list, lists[:size]])
        behind = lax.ppermute(to_on, "blocks", face_pairs(devices, 0, 1))
        ahead = lax.ppermute(to_back, "blocks", face_pairs(devices, 0, -1))
        lists, behind, ahead = pass_on(lists, behind, ahead)
        own_remote, other_half = call(
            received_kernel,
            [jax.ShapeDtypeStruct((6 * size, half), BF16)] * 2,
            32,
            0,
            20 * size * width,
            in_specs=[pl.BlockSpec(memory_space=pltpu.SMEM)] + [pl.BlockSpec()] * 3,
        )(jnp.stack([lower.astype(jnp.int32), core]), lists, behind, ahead)
        start = jnp.where(lower, points, points + 3 * size).reshape(1)
    else:
        received = jnp.concatenate(
            [
                lax.ppermute(faces[k], "blocks", face_pairs(devices, STEPS_X[k], STEPS_Y[k]))
                for k in range(8)
            ]
        )
        own_remote = lax.dynamic_slice(received, (0, core * half), (8 * size, half))
        other_half = lax.dynamic_slice(received, (0, (1 - core) * half), (8 * size, half))
        start = jnp.full((1,), points, jnp.int32)
    other_remote = lax.ppermute(other_half, "blocks", partner)
    own_stacked = gather_block(start, own_rows, own_local, own_remote)
    other_stacked = gather_block(start, other_rows, other_local, other_remote)
    stacked = pass_on(other_stacked, own_stacked)
    if round_trip:
        places = jnp.array(places, jnp.int32)[index]
        early = [[mine], [back[1]], [on[1]], [back[2]], [on[2]]]
        sums = conv_part(stacked, places[:5], early, None, length)
        sums = pass_on(*sums)
        sums = conv_part(stacked, places[5:7], [[back[3]], [on[3]]], sums, length)
        last = [[back[4], on[4]]]
        (for_partner,) = conv_part(stacked[:1], places[7:], last, sums[:1], length)
        (own_part,) = conv_part(stacked[1:], places[7:], last, sums[1:], length)
    else:
        groups = [list(range(first, devices, 2)) for first in range(2)]
        weight = lax.all_gather(mine, "blocks", axis=0, tiled=True, axis_index_groups=groups)
        nowhere = jnp.zeros((1, 2), jnp.int32)
        for_partner, own_part = conv_part(stacked, nowhere, [[weight]], None, length)

    positions = jnp.arange(points, dtype=jnp.int32)
    target = serial_rank // points
    earlier = (target[None, :] == target[:, None]) & (serial_rank[None, :] < serial_rank[:, None])
    out_slot = target * capacity + jnp.sum(earlier.astype(jnp.int32), axis=1)
    anchor = serial_order // points
    before = (anchor[None, :] == anchor[:, None]) & (positions[None, :] < positions[:, None])
    in_slot = anchor * capacity + jnp.sum(before.astype(jnp.int32), axis=1)

    from_partner = lax.ppermute(for_partner, "blocks", partner)

    outgoing = call(
        mix_kernel,
        jax.ShapeDtypeStruct((slots, width), BF16),
        32,
        2 * points * width * (width + slots),
        8 * points * width,
    )(
        own_part,
        from_partner,
        features,
        cpe_weight,
        cpe_gain.reshape(1, width),
        out_slot.reshape(1, points),
    )
    arrived = lax.all_to_all(
        outgoing.reshape(devices, capacity, width), "blocks", split_axis=0, concat_axis=0, tiled=True
    ).reshape(slots, width)

    key_weight = qkv_weight[:, width : 2 * width]
    qv_weight = jnp.concatenate([qkv_weight[:, :width], qkv_weight[:, 2 * width :]], axis=1).T
    weights = (qv_weight, key_weight, proj_weight, up_weight, down_weight)
    back = call(
        block_kernel,
        jax.ShapeDtypeStruct((slots, width), BF16),
        60,
        20 * points * width * width,
        16 * width * width,
        in_specs=[pl.BlockSpec()] * 5 + [pl.BlockSpec(memory_space=pl.ANY)] * len(weights),
        scratch_shapes=[pltpu.VMEM(weight.shape, BF16) for weight in weights]
        + [
            pltpu.SemaphoreType.DMA((len(weights),)),
            pltpu.VMEM((points, width), F32),
            pltpu.VMEM((2 * width, points), BF16),
            pltpu.VMEM((points, width), BF16),
            pltpu.VMEM((width, points), BF16),
            pltpu.VMEM((points, width), F32),
        ],
    )(
        arrived,
        in_slot.reshape(points, 1),
        in_slot.reshape(1, points),
        attn_gain.reshape(1, width),
        mlp_gain.reshape(1, width),
        *weights,
    )
    returned = lax.all_to_all(
        back.reshape(devices, capacity, width), "blocks", split_axis=0, concat_axis=0, tiled=True
    ).reshape(slots, width)
    return call(
        return_kernel,
        jax.ShapeDtypeStruct((points, width), BF16),
        32,
        2 * points * slots * width,
        6 * points * width,
    )(returned, out_slot.reshape(points, 1))


def solution(mesh):
    placed = (
        P(("groups", "blocks"), None),
        P("blocks", None),
        P(),
        P(),
        P(),
        P(),
        P(),
        P(),
        P(),
        P(),
        P(("groups", "blocks"), None, None),
        P(("groups", "blocks"), None),
        P(("groups", "blocks")),
        P(("groups", "blocks")),
    )
    return jax.shard_map(
        body, mesh=mesh, in_specs=placed, out_specs=P(("groups", "blocks"), None), check_vma=False
    )
```

```python
import functools
import math

import jax
import jax.numpy as jnp
from jax import lax
from jax.experimental import pallas as pl
from jax.experimental.pallas import tpu as pltpu
from jax.sharding import PartitionSpec as P

HEADS = 32
GY = 8
HD = 16
TAPS = 27
EPSILON = 1e-05
STEPS_X = (-1, -1, -1, 0, 0, 1, 1, 1)
STEPS_Y = (-1, 0, 1, -1, 1, -1, 0, 1)
F32 = jnp.float32
BF16 = jnp.bfloat16
MIB = 1 << 20


def dot(left, right):
    return jnp.dot(left, right, preferred_element_type=F32)


def layer_norm(inputs, gain_vector):
    row_mean = jnp.mean(inputs, axis=-1, keepdims=True)
    centred = inputs - row_mean
    variance = jnp.mean(centred * centred, axis=-1, keepdims=True)
    return centred * lax.rsqrt(variance + EPSILON) * gain_vector


def one_hot(mask):
    return jnp.where(mask, 1.0, 0.0).astype(BF16)


def call(kernel, out_shape, limit, flops, moved, **extra):
    return pl.pallas_call(
        kernel,
        out_shape=out_shape,
        compiler_params=pltpu.CompilerParams(vmem_limit_bytes=limit * MIB),
        cost_estimate=pl.CostEstimate(flops=flops, bytes_accessed=moved, transcendentals=0),
        **extra,
    )


def faces_kernel(unit, core_ref, features_ref, rows_ref, own_ref, other_ref, *face_refs):
    points, width = features_ref.shape
    half = width // 2
    place = lax.broadcasted_iota(jnp.int32, (width, width), 1)
    within = lax.rem(place, half)
    source = (within // unit) * (2 * unit) + (place // half) * unit + lax.rem(place, unit)
    channel = lax.broadcasted_iota(jnp.int32, (width, width), 0)
    ordered = dot(features_ref[...], one_hot(channel == source)).astype(BF16)
    first, second = ordered[:, :half], ordered[:, half:]
    even = core_ref[0] == 0
    own_ref[...] = jnp.where(even, first, second)
    other_ref[...] = jnp.where(even, second, first)
    row_ids = lax.broadcasted_iota(jnp.int32, (rows_ref.shape[0], points), 1)
    rows = dot(one_hot(rows_ref[...] == row_ids), ordered).astype(BF16)
    taken = 0
    for ref in face_refs:
        ref[...] = rows[taken : taken + ref.shape[0]]
        taken += ref.shape[0]


def received_kernel(flags_ref, side_ref, behind_ref, ahead_ref, own_ref, other_ref):
    size = behind_ref.shape[0] // 2
    half = own_ref.shape[1]
    lower, even = flags_ref[0] == 1, flags_ref[1] == 0
    across = [ahead_ref[size:], side_ref[size : 2 * size], behind_ref[size:]]
    along = [ahead_ref[:size], behind_ref[:size]]
    for at, (low, high) in enumerate(zip(across + along, along + across)):
        rows = jnp.where(lower, low, high)
        first, second = rows[:, :half], rows[:, half:]
        own_ref[at * size : (at + 1) * size] = jnp.where(even, first, second)
        other_ref[at * size : (at + 1) * size] = jnp.where(even, second, first)
    rest = jnp.zeros((size, half), BF16)
    own_ref[5 * size :] = rest
    other_ref[5 * size :] = rest


def gather_kernel(taps, start_ref, rows_ref, own_ref, got_ref, out_ref):
    half = own_ref.shape[1]
    lane = lax.broadcasted_iota(jnp.int32, rows_ref.shape, 1)
    parts = []
    for table, start in ((own_ref, 0), (got_ref, start_ref[0])):
        ids = lax.broadcasted_iota(jnp.int32, (1, table.shape[0]), 1) + start
        parts.append((table, ids.astype(F32)))
    for at in range(taps):
        chosen = lane == taps * pl.program_id(0) + at
        column = jnp.sum(jnp.where(chosen, rows_ref[...], 0.0), axis=1, keepdims=True)
        hits = [one_hot(column == ids) for _, ids in parts]
        products = [dot(hit, table[...]) for hit, (table, _) in zip(hits, parts)]
        out_ref[:, at * half : (at + 1) * half] = (products[0] + products[1]).astype(BF16)


def gather_block(start, rows, own, got):
    points, lanes = rows.shape
    half = own.shape[1]
    height = own.shape[0] + got.shape[0]
    taps = 9
    whole = lambda step: (0, 0)
    return call(
        functools.partial(gather_kernel, taps),
        jax.ShapeDtypeStruct((points, TAPS * half), BF16),
        60,
        2 * TAPS * points * height * half,
        2 * TAPS * points * half,
        grid=(TAPS // taps,),
        in_specs=[
            pl.BlockSpec(memory_space=pltpu.SMEM),
            pl.BlockSpec((points, lanes), whole),
            pl.BlockSpec(own.shape, whole),
            pl.BlockSpec(got.shape, whole),
        ],
        out_specs=pl.BlockSpec((points, taps * half), lambda step: (0, step)),
    )(start, rows, own, got)


def conv_kernel(slots, blocks, first, places_ref, *refs):
    stacked, refs = refs[:blocks], refs[blocks:]
    pieces, refs = refs[: sum(slots)], refs[sum(slots) :]
    before = [] if first else refs[:blocks]
    outs, (lhs, held, sems) = refs[-3 - blocks : -3], refs[-3:]
    length = held.shape[1]
    copies, taken = [], 0
    for at, count in enumerate(slots):
        column = pl.multiple_of(places_ref[2 * at], 128)
        row = pl.multiple_of(places_ref[2 * at + 1], 16)
        copies.append([])
        for block in range(blocks):
            copy = pltpu.make_async_copy(
                stacked[block].at[:, pl.ds(column, length)], lhs.at[at, block], sems.at[at, block]
            )
            copy.start()
            copies[-1].append(copy)
        short = count * pieces[taken].shape[0]
        edge = length - short
        if edge:
            held[at, :edge] = jnp.zeros((edge, held.shape[2]), BF16)
            held[at, length - edge :] = jnp.zeros((edge, held.shape[2]), BF16)
        for part in range(count):
            piece = pieces[taken]
            size = piece.shape[0]
            copy = pltpu.make_async_copy(
                piece, held.at[at, pl.ds(row + part * size, size)], sems.at[at, 2 + part]
            )
            copy.start()
            copies[-1].append(copy)
            taken += 1
    for at in range(len(slots)):
        for copy in copies[at]:
            copy.wait()
        for block, ref in enumerate(outs):
            product = dot(lhs[at, block], held[at])
            if at > 0:
                ref[...] += product
            elif first:
                ref[...] = product
            else:
                ref[...] = before[block][...] + product


def conv_part(stacked, places, pieces, before, length):
    points, depth = stacked[0].shape
    width = pieces[0][0].shape[1]
    slots = [len(parts) for parts in pieces]
    flat = [piece for parts in pieces for piece in parts]
    blocks = len(stacked)
    held = 1 + blocks + len(flat)
    return call(
        functools.partial(conv_kernel, slots, blocks, before is None),
        [jax.ShapeDtypeStruct((points, width), F32)] * blocks,
        60,
        2 * blocks * points * length * width * len(slots),
        2 * length * (blocks * points + width) * len(slots),
        in_specs=[pl.BlockSpec(memory_space=pltpu.SMEM)]
        + [pl.BlockSpec(memory_space=pl.ANY)] * (held - 1)
        + ([] if before is None else [pl.BlockSpec()] * blocks),
        input_output_aliases=(
            {} if before is None else {held + block: block for block in range(blocks)}
        ),
        scratch_shapes=[
            pltpu.VMEM((len(slots), blocks, points, length), BF16),
            pltpu.VMEM((len(slots), length, width), BF16),
            pltpu.SemaphoreType.DMA((len(slots), 4)),
        ],
    )(places.reshape(-1), *stacked, *flat, *(before or ()))


def mix_kernel(
    count,
    places_ref,
    own_ref,
    got_ref,
    features_ref,
    weight_ref,
    gain_ref,
    slot_ref,
    *refs,
):
    out_ref, own_held = refs[-5], refs[-4]
    if count:
        conv_kernel(
            [count], 1, False, places_ref, *refs[: 1 + count], own_ref, own_held, *refs[-3:]
        )
        own = own_held[...]
    else:
        own = own_ref[...]
    convolved = (own + got_ref[...]).astype(BF16)
    linear = dot(convolved, weight_ref[...])
    mixed = (features_ref[...].astype(F32) + layer_norm(linear, gain_ref[...])).astype(BF16)
    slots = lax.broadcasted_iota(jnp.int32, (out_ref.shape[0], mixed.shape[0]), 0)
    out_ref[...] = dot(one_hot(slots == slot_ref[...]), mixed).astype(BF16)


def block_kernel(
    arrived_ref,
    slot_col_ref,
    slot_row_ref,
    attn_gain_ref,
    mlp_gain_ref,
    qv_hbm,
    key_hbm,
    proj_hbm,
    up_hbm,
    down_hbm,
    out_ref,
    qv_ref,
    key_ref,
    proj_ref,
    up_ref,
    down_ref,
    sems,
    serial_ref,
    qv_cols_ref,
    keys_ref,
    heads_ref,
    total_ref,
):
    sources = (key_hbm, qv_hbm, proj_hbm, up_hbm, down_hbm)
    targets = (key_ref, qv_ref, proj_ref, up_ref, down_ref)
    copies = [
        pltpu.make_async_copy(source, target, sems.at[at])
        for at, (source, target) in enumerate(zip(sources, targets))
    ]
    for copy in copies:
        copy.start()
    slots = arrived_ref.shape[0]
    points, width = serial_ref.shape
    slot_ids = lax.broadcasted_iota(jnp.int32, (points, slots), 1)
    serial = dot(one_hot(slot_col_ref[...] == slot_ids), arrived_ref[...])
    serial_ref[...] = serial
    normed = layer_norm(serial, attn_gain_ref[...]).astype(BF16)
    copies[0].wait()
    keys_ref[...] = dot(normed, key_ref[...]).astype(BF16)
    copies[1].wait()
    factor = math.log2(math.e) / math.sqrt(HD)
    contract_last = (((1,), (1,)), ((), ()))
    qv_cols_ref[:width] = (
        lax.dot_general(qv_ref[:width], normed, contract_last, preferred_element_type=F32) * factor
    ).astype(BF16)
    qv_cols_ref[width:] = lax.dot_general(
        qv_ref[width:], normed, contract_last, preferred_element_type=F32
    ).astype(BF16)
    ones = jnp.ones((HD, points), BF16)
    per_group = 128 // HD
    head_of_row = lax.broadcasted_iota(jnp.int32, (128, points), 0) // HD

    for group in range(HEADS // per_group):
        base = group * 128

        def attend(head, carry):
            group_queries = qv_cols_ref[base : base + 128]
            queries = jnp.where(head_of_row == head, group_queries.astype(F32), 0.0).astype(BF16)
            scores = dot(keys_ref[:, base : base + 128], queries)
            weights = jnp.exp2(scores - jnp.max(scores, axis=0, keepdims=True)).astype(BF16)
            at = pl.multiple_of(base + head * HD, HD)
            values = qv_cols_ref[pl.ds(width + at, HD)]
            sums = dot(jnp.concatenate([values, ones], axis=0), weights)
            heads_ref[pl.ds(at, HD)] = (sums[:HD] / sums[HD : HD + 1]).astype(BF16)
            return carry

        lax.fori_loop(0, per_group, attend, 0, unroll=4)

    for copy in copies[2:]:
        copy.wait()
    update = lax.dot_general(
        heads_ref[...], proj_ref[...], (((0,), (0,)), ((), ())), preferred_element_type=F32
    )
    attended = (serial_ref[...] + update).astype(BF16).astype(F32)
    hidden_in = layer_norm(attended, mlp_gain_ref[...]).astype(BF16)
    total_ref[...] = attended
    chunk = width
    for start in range(0, up_ref.shape[1], chunk):
        raised = dot(hidden_in, up_ref[:, start : start + chunk])
        hidden = (raised * (1.0 + lax.erf(raised * math.sqrt(0.5))) * 0.5).astype(BF16)
        total_ref[...] += dot(hidden, down_ref[start : start + chunk])
    finished = total_ref[...].astype(BF16)
    slot_rows = lax.broadcasted_iota(jnp.int32, (slots, points), 0)
    out_ref[...] = dot(one_hot(slot_rows == slot_row_ref[...]), finished).astype(BF16)


def return_kernel(arrived_ref, slot_ref, out_ref):
    slot_ids = lax.broadcasted_iota(jnp.int32, (out_ref.shape[0], arrived_ref.shape[0]), 1)
    out_ref[...] = dot(one_hot(slot_ref[...] == slot_ids), arrived_ref[...]).astype(BF16)


def face_pairs(devices, dx, dy):
    return [
        (source, source + dx * GY + dy)
        for source in range(devices)
        if 0 <= source // GY + dx < devices // GY and 0 <= source % GY + dy < GY
    ]


def way_round(devices, rows, length):
    chips = devices // 2
    cycle = list(range(0, chips, 2)) + list(range(chips - 1, 0, -2))
    back, on = [], []
    places = [None] * devices
    for place, chip in enumerate(cycle):
        for core in range(2):
            me = 2 * chip + core
            back.append((me, 2 * cycle[(place + 1) % chips] + core))
            on.append((me, 2 * cycle[place - 1] + core))
            order = [0]
            for step in range(1, chips // 2):
                order += [-step, step]
            order.append(chips // 2)
            places[me] = []
            for offset in order:
                start = cycle[(place + offset) % chips] * rows
                column = min(start // 128 * 128, chips * rows - length)
                places[me].append((column, start - column))
    return back, on, places


def padded_taps(neighbours):
    points = neighbours.shape[0]
    own = jnp.arange(points, dtype=jnp.int32)[:, None]
    rest = jnp.zeros((points, 128 - TAPS), jnp.int32)
    middle = TAPS // 2
    rows = jnp.concatenate([neighbours[:, :middle], own, neighbours[:, middle:], rest], axis=1)
    return rows.astype(F32)


def body(
    features,
    conv_weight,
    cpe_weight,
    cpe_gain,
    attn_gain,
    qkv_weight,
    proj_weight,
    mlp_gain,
    up_weight,
    down_weight,
    face_rows,
    neighbours,
    serial_rank,
    serial_order,
):
    points, width = features.shape
    half = width // 2
    devices = lax.axis_size("blocks")
    index = lax.axis_index("blocks")
    core = lax.rem(index, 2)
    partner = [(source, source ^ 1) for source in range(devices)]
    capacity = 2 * points // devices
    slots = devices * capacity

    unit = conv_weight.shape[0] // TAPS
    units = conv_weight.reshape(TAPS, unit, width)
    kept, sent = units[0::2], units[1::2]
    got = lax.ppermute(sent, "blocks", partner)
    mine = jnp.where(
        core == 0, jnp.concatenate([kept, got]), jnp.concatenate([got, kept])
    ).reshape(TAPS * unit, width)
    round_trip = devices == 2 * GY
    lower = index < GY
    if round_trip:
        across = jnp.where(lower, face_rows[0, 5:], face_rows[0, :3])
        face_list = jnp.concatenate([across, face_rows[0, 3:5]]).reshape(-1, 1)
        counts = (3, 1, 1)
    else:
        face_list = face_rows.reshape(-1, 1)
        counts = (1,) * 8
    size = face_rows.shape[2]
    own_local, other_half, *faces = call(
        functools.partial(faces_kernel, unit),
        [jax.ShapeDtypeStruct((points, half), BF16)] * 2
        + [jax.ShapeDtypeStruct((count * size, width), BF16) for count in counts],
        60,
        4 * points * width * width,
        8 * points * width,
        in_specs=[pl.BlockSpec(memory_space=pltpu.SMEM)] + [pl.BlockSpec()] * 2,
    )(core.reshape(1), features, face_list)
    other_local = lax.ppermute(other_half, "blocks", partner)
    other_neighbours = lax.ppermute(neighbours, "blocks", partner)

    rows = mine.shape[0]
    length = -(-(rows + 127) // 128) * 128 if round_trip else rows * (devices // 2)
    back_pairs, on_pairs, places = way_round(devices, rows, length)
    back, on = [mine], [mine]

    def pass_on(*beside):
        if not round_trip:
            return beside
        tied = lax.optimization_barrier((back[-1], on[-1], *beside))
        first, second = tied[:2]
        back[-1], on[-1] = first, second
        if len(back) == devices // 4:
            first, second = first[: rows // 2], second[rows // 2 :]
        back.append(lax.ppermute(first, "blocks", back_pairs))
        on.append(lax.ppermute(second, "blocks", on_pairs))
        return tied[2:]

    if round_trip:
        lists, back_list, on_list = faces
        side = face_pairs(devices, 1, 0) + face_pairs(devices, -1, 0)
        lists, other_local, other_neighbours = pass_on(lists, other_local, other_neighbours)
        lists = lax.ppermute(lists, "blocks", side)
    own_rows, other_rows = padded_taps(neighbours), padded_taps(other_neighbours)
    if round_trip:
        to_on = jnp.concatenate([on_list, lists[2 * size :]])
        to_back = jnp.concatenate([back_list, lists[:size]])
        behind = lax.ppermute(to_on, "blocks", face_pairs(devices, 0, 1))
        ahead = lax.ppermute(to_back, "blocks", face_pairs(devices, 0, -1))
        lists, behind, ahead = pass_on(lists, behind, ahead)
        own_remote, other_half = call(
            received_kernel,
            [jax.ShapeDtypeStruct((6 * size, half), BF16)] * 2,
            32,
            0,
            20 * size * width,
            in_specs=[pl.BlockSpec(memory_space=pltpu.SMEM)] + [pl.BlockSpec()] * 3,
        )(jnp.stack([lower.astype(jnp.int32), core]), lists, behind, ahead)
        start = jnp.where(lower, points, points + 3 * size).reshape(1)
    else:
        received = jnp.concatenate(
            [
                lax.ppermute(faces[k], "blocks", face_pairs(devices, STEPS_X[k], STEPS_Y[k]))
                for k in range(8)
            ]
        )
        own_remote = lax.dynamic_slice(received, (0, core * half), (8 * size, half))
        other_half = lax.dynamic_slice(received, (0, (1 - core) * half), (8 * size, half))
        start = jnp.full((1,), points, jnp.int32)
    other_remote = lax.ppermute(other_half, "blocks", partner)
    own_stacked = gather_block(start, own_rows, own_local, own_remote)
    other_stacked = gather_block(start, other_rows, other_local, other_remote)
    stacked = pass_on(other_stacked, own_stacked)
    if round_trip:
        places = jnp.array(places, jnp.int32)[index]
        early = [[mine], [back[1]], [on[1]], [back[2]], [on[2]]]
        sums = conv_part(stacked, places[:5], early, None, length)
        sums = pass_on(*sums)
        sums = conv_part(stacked, places[5:7], [[back[3]], [on[3]]], sums, length)
        last = [[back[4], on[4]]]
        (for_partner,) = conv_part(stacked[:1], places[7:], last, sums[:1], length)
        own_part = sums[1]
        rest = [stacked[1], *last[0]]
        places = places[7]
    else:
        groups = [list(range(first, devices, 2)) for first in range(2)]
        weight = lax.all_gather(mine, "blocks", axis=0, tiled=True, axis_index_groups=groups)
        nowhere = jnp.zeros((1, 2), jnp.int32)
        for_partner, own_part = conv_part(stacked, nowhere, [[weight]], None, length)
        places, rest = nowhere[0], []

    positions = jnp.arange(points, dtype=jnp.int32)
    target = serial_rank // points
    earlier = (target[None, :] == target[:, None]) & (serial_rank[None, :] < serial_rank[:, None])
    out_slot = target * capacity + jnp.sum(earlier.astype(jnp.int32), axis=1)
    anchor = serial_order // points
    before = (anchor[None, :] == anchor[:, None]) & (positions[None, :] < positions[:, None])
    in_slot = anchor * capacity + jnp.sum(before.astype(jnp.int32), axis=1)

    from_partner = lax.ppermute(for_partner, "blocks", partner)

    outgoing = call(
        functools.partial(mix_kernel, len(rest) - 1 if rest else 0),
        jax.ShapeDtypeStruct((slots, width), BF16),
        48,
        2 * points * width * (width + slots + length),
        8 * points * width,
        in_specs=[pl.BlockSpec(memory_space=pltpu.SMEM)]
        + [pl.BlockSpec()] * 6
        + [pl.BlockSpec(memory_space=pl.ANY)] * len(rest),
        scratch_shapes=[
            pltpu.VMEM((points, width), F32),
            pltpu.VMEM((1, 1, points, length if rest else 128), BF16),
            pltpu.VMEM((1, length if rest else 128, width), BF16),
            pltpu.SemaphoreType.DMA((1, 4)),
        ],
    )(
        places,
        own_part,
        from_partner,
        features,
        cpe_weight,
        cpe_gain.reshape(1, width),
        out_slot.reshape(1, points),
        *rest,
    )
    arrived = lax.all_to_all(
        outgoing.reshape(devices, capacity, width), "blocks", split_axis=0, concat_axis=0, tiled=True
    ).reshape(slots, width)

    key_weight = qkv_weight[:, width : 2 * width]
    qv_weight = jnp.concatenate([qkv_weight[:, :width], qkv_weight[:, 2 * width :]], axis=1).T
    weights = (qv_weight, key_weight, proj_weight, up_weight, down_weight)
    back = call(
        block_kernel,
        jax.ShapeDtypeStruct((slots, width), BF16),
        60,
        20 * points * width * width,
        16 * width * width,
        in_specs=[pl.BlockSpec()] * 5 + [pl.BlockSpec(memory_space=pl.ANY)] * len(weights),
        scratch_shapes=[pltpu.VMEM(weight.shape, BF16) for weight in weights]
        + [
            pltpu.SemaphoreType.DMA((len(weights),)),
            pltpu.VMEM((points, width), F32),
            pltpu.VMEM((2 * width, points), BF16),
            pltpu.VMEM((points, width), BF16),
            pltpu.VMEM((width, points), BF16),
            pltpu.VMEM((points, width), F32),
        ],
    )(
        arrived,
        in_slot.reshape(points, 1),
        in_slot.reshape(1, points),
        attn_gain.reshape(1, width),
        mlp_gain.reshape(1, width),
        *weights,
    )
    returned = lax.all_to_all(
        back.reshape(devices, capacity, width), "blocks", split_axis=0, concat_axis=0, tiled=True
    ).reshape(slots, width)
    return call(
        return_kernel,
        jax.ShapeDtypeStruct((points, width), BF16),
        32,
        2 * points * slots * width,
        6 * points * width,
    )(returned, out_slot.reshape(points, 1))


def solution(mesh):
    placed = (
        P(("groups", "blocks"), None),
        P("blocks", None),
        P(),
        P(),
        P(),
        P(),
        P(),
        P(),
        P(),
        P(),
        P(("groups", "blocks"), None, None),
        P(("groups", "blocks"), None),
        P(("groups", "blocks")),
        P(("groups", "blocks")),
    )
    return jax.shard_map(
        body, mesh=mesh, in_specs=placed, out_specs=P(("groups", "blocks"), None), check_vma=False
    )
```

```python
import functools
import math

import jax
import jax.numpy as jnp
from jax import lax
from jax.experimental import pallas as pl
from jax.experimental.pallas import tpu as pltpu
from jax.sharding import PartitionSpec as P

HEADS = 32
GY = 8
HD = 16
TAPS = 27
EPSILON = 1e-05
STEPS_X = (-1, -1, -1, 0, 0, 1, 1, 1)
STEPS_Y = (-1, 0, 1, -1, 1, -1, 0, 1)
F32 = jnp.float32
BF16 = jnp.bfloat16
MIB = 1 << 20


def dot(left, right):
    return jnp.dot(left, right, preferred_element_type=F32)


def layer_norm(inputs, gain_vector):
    row_mean = jnp.mean(inputs, axis=-1, keepdims=True)
    centred = inputs - row_mean
    variance = jnp.mean(centred * centred, axis=-1, keepdims=True)
    return centred * lax.rsqrt(variance + EPSILON) * gain_vector


def one_hot(mask):
    return jnp.where(mask, 1.0, 0.0).astype(BF16)


def call(kernel, out_shape, limit, flops, moved, **extra):
    return pl.pallas_call(
        kernel,
        out_shape=out_shape,
        compiler_params=pltpu.CompilerParams(vmem_limit_bytes=limit * MIB),
        cost_estimate=pl.CostEstimate(flops=flops, bytes_accessed=moved, transcendentals=0),
        **extra,
    )


def faces_kernel(unit, core_ref, features_ref, rows_ref, own_ref, other_ref, *face_refs):
    points, width = features_ref.shape
    half = width // 2
    place = lax.broadcasted_iota(jnp.int32, (width, width), 1)
    within = lax.rem(place, half)
    source = (within // unit) * (2 * unit) + (place // half) * unit + lax.rem(place, unit)
    channel = lax.broadcasted_iota(jnp.int32, (width, width), 0)
    ordered = dot(features_ref[...], one_hot(channel == source)).astype(BF16)
    first, second = ordered[:, :half], ordered[:, half:]
    even = core_ref[0] == 0
    own_ref[...] = jnp.where(even, first, second)
    other_ref[...] = jnp.where(even, second, first)
    row_ids = lax.broadcasted_iota(jnp.int32, (rows_ref.shape[0], points), 1)
    rows = dot(one_hot(rows_ref[...] == row_ids), ordered).astype(BF16)
    taken = 0
    for ref in face_refs:
        ref[...] = rows[taken : taken + ref.shape[0]]
        taken += ref.shape[0]


def received_kernel(flags_ref, side_ref, behind_ref, ahead_ref, own_ref, other_ref):
    size = behind_ref.shape[0] // 2
    half = own_ref.shape[1]
    lower, even = flags_ref[0] == 1, flags_ref[1] == 0
    across = [ahead_ref[size:], side_ref[size : 2 * size], behind_ref[size:]]
    along = [ahead_ref[:size], behind_ref[:size]]
    for at, (low, high) in enumerate(zip(across + along, along + across)):
        rows = jnp.where(lower, low, high)
        first, second = rows[:, :half], rows[:, half:]
        own_ref[at * size : (at + 1) * size] = jnp.where(even, first, second)
        other_ref[at * size : (at + 1) * size] = jnp.where(even, second, first)
    rest = jnp.zeros((size, half), BF16)
    own_ref[5 * size :] = rest
    other_ref[5 * size :] = rest


def gather_kernel(taps, start_ref, rows_ref, own_ref, got_ref, out_ref):
    half = own_ref.shape[1]
    lane = lax.broadcasted_iota(jnp.int32, rows_ref.shape, 1)
    parts = []
    for table, start in ((own_ref, 0), (got_ref, start_ref[0])):
        ids = lax.broadcasted_iota(jnp.int32, (1, table.shape[0]), 1) + start
        parts.append((table, ids.astype(F32)))
    for at in range(taps):
        chosen = lane == taps * pl.program_id(0) + at
        column = jnp.sum(jnp.where(chosen, rows_ref[...], 0.0), axis=1, keepdims=True)
        hits = [one_hot(column == ids) for _, ids in parts]
        products = [dot(hit, table[...]) for hit, (table, _) in zip(hits, parts)]
        out_ref[:, at * half : (at + 1) * half] = (products[0] + products[1]).astype(BF16)


def gather_block(start, rows, own, got):
    points, lanes = rows.shape
    half = own.shape[1]
    height = own.shape[0] + got.shape[0]
    taps = 9
    whole = lambda step: (0, 0)
    return call(
        functools.partial(gather_kernel, taps),
        jax.ShapeDtypeStruct((points, TAPS * half), BF16),
        60,
        2 * TAPS * points * height * half,
        2 * TAPS * points * half,
        grid=(TAPS // taps,),
        in_specs=[
            pl.BlockSpec(memory_space=pltpu.SMEM),
            pl.BlockSpec((points, lanes), whole),
            pl.BlockSpec(own.shape, whole),
            pl.BlockSpec(got.shape, whole),
        ],
        out_specs=pl.BlockSpec((points, taps * half), lambda step: (0, step)),
    )(start, rows, own, got)


def conv_kernel(slots, blocks, first, places_ref, *refs):
    stacked, refs = refs[:blocks], refs[blocks:]
    pieces, refs = refs[: sum(slots)], refs[sum(slots) :]
    before = [] if first else refs[:blocks]
    outs, (lhs, held, sems) = refs[-3 - blocks : -3], refs[-3:]
    length = held.shape[1]
    copies, taken = [], 0
    for at, count in enumerate(slots):
        column = pl.multiple_of(places_ref[2 * at], 128)
        row = pl.multiple_of(places_ref[2 * at + 1], 16)
        copies.append([])
        for block in range(blocks):
            copy = pltpu.make_async_copy(
                stacked[block].at[:, pl.ds(column, length)], lhs.at[at, block], sems.at[at, block]
            )
            copy.start()
            copies[-1].append(copy)
        short = count * pieces[taken].shape[0]
        edge = length - short
        if edge:
            held[at, :edge] = jnp.zeros((edge, held.shape[2]), BF16)
            held[at, length - edge :] = jnp.zeros((edge, held.shape[2]), BF16)
        for part in range(count):
            piece = pieces[taken]
            size = piece.shape[0]
            copy = pltpu.make_async_copy(
                piece, held.at[at, pl.ds(row + part * size, size)], sems.at[at, 2 + part]
            )
            copy.start()
            copies[-1].append(copy)
            taken += 1
    for at in range(len(slots)):
        for copy in copies[at]:
            copy.wait()
        for block, ref in enumerate(outs):
            product = dot(lhs[at, block], held[at])
            if at > 0:
                ref[...] += product
            elif first:
                ref[...] = product
            else:
                ref[...] = (before[block][...] + product).astype(ref.dtype)


def conv_part(stacked, places, pieces, before, length, dtype=F32):
    points, depth = stacked[0].shape
    width = pieces[0][0].shape[1]
    slots = [len(parts) for parts in pieces]
    flat = [piece for parts in pieces for piece in parts]
    blocks = len(stacked)
    held = 1 + blocks + len(flat)
    return call(
        functools.partial(conv_kernel, slots, blocks, before is None),
        [jax.ShapeDtypeStruct((points, width), dtype)] * blocks,
        60,
        2 * blocks * points * length * width * len(slots),
        2 * length * (blocks * points + width) * len(slots),
        in_specs=[pl.BlockSpec(memory_space=pltpu.SMEM)]
        + [pl.BlockSpec(memory_space=pl.ANY)] * (held - 1)
        + ([] if before is None else [pl.BlockSpec()] * blocks),
        input_output_aliases=(
            {}
            if before is None or dtype != F32
            else {held + block: block for block in range(blocks)}
        ),
        scratch_shapes=[
            pltpu.VMEM((len(slots), blocks, points, length), BF16),
            pltpu.VMEM((len(slots), length, width), BF16),
            pltpu.SemaphoreType.DMA((len(slots), 4)),
        ],
    )(places.reshape(-1), *stacked, *flat, *(before or ()))


def mix_kernel(
    count, places_ref, got_ref, gain_ref, slot_ref, own_hbm, features_hbm, weight_hbm, *refs
):
    out_ref, own_ref, features_ref, weight_ref, own_held, load_sems = refs[-9:-3]
    loads = [
        pltpu.make_async_copy(source, target, load_sems.at[at])
        for at, (source, target) in enumerate(
            ((own_hbm, own_ref), (features_hbm, features_ref), (weight_hbm, weight_ref))
        )
    ]
    for load in loads:
        load.start()
    if count:
        conv_kernel(
            [count], 1, True, places_ref, *refs[: 1 + count], own_held, *refs[-3:]
        )
    else:
        own_held[...] = jnp.zeros_like(own_held)
    for load in loads:
        load.wait()
    convolved = (own_ref[...] + own_held[...] + got_ref[...].astype(F32)).astype(BF16)
    linear = dot(convolved, weight_ref[...])
    mixed = (features_ref[...].astype(F32) + layer_norm(linear, gain_ref[...])).astype(BF16)
    slots = lax.broadcasted_iota(jnp.int32, (out_ref.shape[0], mixed.shape[0]), 0)
    out_ref[...] = dot(one_hot(slots == slot_ref[...]), mixed).astype(BF16)


def block_kernel(
    arrived_ref,
    slot_col_ref,
    slot_row_ref,
    attn_gain_ref,
    mlp_gain_ref,
    qv_hbm,
    key_hbm,
    proj_hbm,
    up_hbm,
    down_hbm,
    out_ref,
    qv_ref,
    key_ref,
    proj_ref,
    up_ref,
    down_ref,
    sems,
    serial_ref,
    qv_cols_ref,
    keys_ref,
    heads_ref,
    total_ref,
    scores_ref,
    weights_ref,
):
    sources = (key_hbm, qv_hbm, proj_hbm, up_hbm, down_hbm)
    targets = (key_ref, qv_ref, proj_ref, up_ref, down_ref)
    copies = [
        pltpu.make_async_copy(source, target, sems.at[at])
        for at, (source, target) in enumerate(zip(sources, targets))
    ]
    for copy in copies:
        copy.start()
    slots = arrived_ref.shape[0]
    points, width = serial_ref.shape
    slot_ids = lax.broadcasted_iota(jnp.int32, (points, slots), 1)
    serial = dot(one_hot(slot_col_ref[...] == slot_ids), arrived_ref[...])
    serial_ref[...] = serial
    normed = layer_norm(serial, attn_gain_ref[...]).astype(BF16)
    copies[0].wait()
    keys_ref[...] = dot(normed, key_ref[...]).astype(BF16)
    copies[1].wait()
    factor = math.log2(math.e) / math.sqrt(HD)
    contract_last = (((1,), (1,)), ((), ()))
    qv_cols_ref[:width] = (
        lax.dot_general(qv_ref[:width], normed, contract_last, preferred_element_type=F32) * factor
    ).astype(BF16)
    qv_cols_ref[width:] = lax.dot_general(
        qv_ref[width:], normed, contract_last, preferred_element_type=F32
    ).astype(BF16)
    ones = jnp.ones((HD, points), BF16)
    per_group = 128 // HD
    head_of_row = lax.broadcasted_iota(jnp.int32, (128, points), 0) // HD

    def score(head, slot):
        base = pl.multiple_of(head // per_group * 128, 128)
        group_queries = qv_cols_ref[pl.ds(base, 128)].astype(F32)
        chosen = head_of_row == lax.rem(head, per_group)
        queries = jnp.where(chosen, group_queries, 0.0).astype(BF16)
        scores_ref[slot] = dot(keys_ref[:, pl.ds(base, 128)], queries)

    def weigh(slot):
        scores = scores_ref[slot]
        weights_ref[slot] = jnp.exp2(scores - jnp.max(scores, axis=0, keepdims=True)).astype(BF16)

    def gather(head, slot):
        at = pl.multiple_of(head * HD, HD)
        values = jnp.concatenate([qv_cols_ref[pl.ds(width + at, HD)], ones], axis=0)
        sums = dot(values, weights_ref[slot])
        heads_ref[pl.ds(at, HD)] = (sums[:HD] / sums[HD : HD + 1]).astype(BF16)

    score(0, 0)
    score(1, 1)
    weigh(0)

    def two_heads(pair, carry):
        head = 2 * pair + 1
        for slot in (1, 0):
            score(head + 1, 1 - slot)
            weigh(slot)
            gather(head - 1, 1 - slot)
            head += 1
        return carry

    lax.fori_loop(0, HEADS // 2 - 1, two_heads, 0)
    weigh(1)
    gather(HEADS - 2, 0)
    gather(HEADS - 1, 1)

    for copy in copies[2:]:
        copy.wait()
    update = lax.dot_general(
        heads_ref[...], proj_ref[...], (((0,), (0,)), ((), ())), preferred_element_type=F32
    )
    attended = (serial_ref[...] + update).astype(BF16).astype(F32)
    hidden_in = layer_norm(attended, mlp_gain_ref[...]).astype(BF16)
    total_ref[...] = attended
    chunk = width
    for start in range(0, up_ref.shape[1], chunk):
        raised = dot(hidden_in, up_ref[:, start : start + chunk])
        hidden = (raised * (1.0 + lax.erf(raised * math.sqrt(0.5))) * 0.5).astype(BF16)
        total_ref[...] += dot(hidden, down_ref[start : start + chunk])
    finished = total_ref[...].astype(BF16)
    slot_rows = lax.broadcasted_iota(jnp.int32, (slots, points), 0)
    out_ref[...] = dot(one_hot(slot_rows == slot_row_ref[...]), finished).astype(BF16)


def return_kernel(arrived_ref, slot_ref, out_ref):
    slot_ids = lax.broadcasted_iota(jnp.int32, (out_ref.shape[0], arrived_ref.shape[0]), 1)
    out_ref[...] = dot(one_hot(slot_ref[...] == slot_ids), arrived_ref[...]).astype(BF16)


def face_pairs(devices, dx, dy):
    return [
        (source, source + dx * GY + dy)
        for source in range(devices)
        if 0 <= source // GY + dx < devices // GY and 0 <= source % GY + dy < GY
    ]


def way_round(devices, rows, length):
    chips = devices // 2
    cycle = list(range(0, chips, 2)) + list(range(chips - 1, 0, -2))
    back, on = [], []
    places = [None] * devices
    for place, chip in enumerate(cycle):
        for core in range(2):
            me = 2 * chip + core
            back.append((me, 2 * cycle[(place + 1) % chips] + core))
            on.append((me, 2 * cycle[place - 1] + core))
            order = [0]
            for step in range(1, chips // 2):
                order += [-step, step]
            order.append(chips // 2)
            places[me] = []
            for offset in order:
                start = cycle[(place + offset) % chips] * rows
                column = min(start // 128 * 128, chips * rows - length)
                places[me].append((column, start - column))
    return back, on, places


def padded_taps(neighbours):
    points = neighbours.shape[0]
    own = jnp.arange(points, dtype=jnp.int32)[:, None]
    rest = jnp.zeros((points, 128 - TAPS), jnp.int32)
    middle = TAPS // 2
    rows = jnp.concatenate([neighbours[:, :middle], own, neighbours[:, middle:], rest], axis=1)
    return rows.astype(F32)


def body(
    features,
    conv_weight,
    cpe_weight,
    cpe_gain,
    attn_gain,
    qkv_weight,
    proj_weight,
    mlp_gain,
    up_weight,
    down_weight,
    face_rows,
    neighbours,
    serial_rank,
    serial_order,
):
    points, width = features.shape
    half = width // 2
    devices = lax.axis_size("blocks")
    index = lax.axis_index("blocks")
    core = lax.rem(index, 2)
    partner = [(source, source ^ 1) for source in range(devices)]
    capacity = 2 * points // devices
    slots = devices * capacity

    unit = conv_weight.shape[0] // TAPS
    units = conv_weight.reshape(TAPS, unit, width)
    kept, sent = units[0::2], units[1::2]
    got = lax.ppermute(sent, "blocks", partner)
    mine = jnp.where(
        core == 0, jnp.concatenate([kept, got]), jnp.concatenate([got, kept])
    ).reshape(TAPS * unit, width)
    round_trip = devices == 2 * GY
    lower = index < GY
    if round_trip:
        across = jnp.where(lower, face_rows[0, 5:], face_rows[0, :3])
        face_list = jnp.concatenate([across, face_rows[0, 3:5]]).reshape(-1, 1)
        counts = (3, 1, 1)
    else:
        face_list = face_rows.reshape(-1, 1)
        counts = (1,) * 8
    size = face_rows.shape[2]
    own_local, other_half, *faces = call(
        functools.partial(faces_kernel, unit),
        [jax.ShapeDtypeStruct((points, half), BF16)] * 2
        + [jax.ShapeDtypeStruct((count * size, width), BF16) for count in counts],
        60,
        4 * points * width * width,
        8 * points * width,
        in_specs=[pl.BlockSpec(memory_space=pltpu.SMEM)] + [pl.BlockSpec()] * 2,
    )(core.reshape(1), features, face_list)
    other_local = lax.ppermute(other_half, "blocks", partner)
    other_neighbours = lax.ppermute(neighbours, "blocks", partner)

    rows = mine.shape[0]
    length = -(-(rows + 127) // 128) * 128 if round_trip else rows * (devices // 2)
    back_pairs, on_pairs, places = way_round(devices, rows, length)
    back, on = [mine], [mine]

    def pass_on(*beside):
        if not round_trip:
            return beside
        tied = lax.optimization_barrier((back[-1], on[-1], *beside))
        first, second = tied[:2]
        back[-1], on[-1] = first, second
        if len(back) == devices // 4:
            first, second = first[: rows // 2], second[rows // 2 :]
        back.append(lax.ppermute(first, "blocks", back_pairs))
        on.append(lax.ppermute(second, "blocks", on_pairs))
        return tied[2:]

    if round_trip:
        lists, back_list, on_list = faces
        side = face_pairs(devices, 1, 0) + face_pairs(devices, -1, 0)
        lists, other_local, other_neighbours = pass_on(lists, other_local, other_neighbours)
        lists = lax.ppermute(lists, "blocks", side)
    own_rows, other_rows = padded_taps(neighbours), padded_taps(other_neighbours)
    if round_trip:
        to_on = jnp.concatenate([on_list, lists[2 * size :]])
        to_back = jnp.concatenate([back_list, lists[:size]])
        behind = lax.ppermute(to_on, "blocks", face_pairs(devices, 0, 1))
        ahead = lax.ppermute(to_back, "blocks", face_pairs(devices, 0, -1))
        lists, behind, ahead = pass_on(lists, behind, ahead)
        own_remote, other_half = call(
            received_kernel,
            [jax.ShapeDtypeStruct((6 * size, half), BF16)] * 2,
            32,
            0,
            20 * size * width,
            in_specs=[pl.BlockSpec(memory_space=pltpu.SMEM)] + [pl.BlockSpec()] * 3,
        )(jnp.stack([lower.astype(jnp.int32), core]), lists, behind, ahead)
        start = jnp.where(lower, points, points + 3 * size).reshape(1)
    else:
        received = jnp.concatenate(
            [
                lax.ppermute(faces[k], "blocks", face_pairs(devices, STEPS_X[k], STEPS_Y[k]))
                for k in range(8)
            ]
        )
        own_remote = lax.dynamic_slice(received, (0, core * half), (8 * size, half))
        other_half = lax.dynamic_slice(received, (0, (1 - core) * half), (8 * size, half))
        start = jnp.full((1,), points, jnp.int32)
    other_remote = lax.ppermute(other_half, "blocks", partner)
    own_stacked = gather_block(start, own_rows, own_local, own_remote)
    other_stacked = gather_block(start, other_rows, other_local, other_remote)
    stacked = pass_on(other_stacked, own_stacked)
    if round_trip:
        places = jnp.array(places, jnp.int32)[index]
        early = [[mine], [back[1]], [on[1]], [back[2]], [on[2]]]
        sums = conv_part(stacked, places[:5], early, None, length)
        sums = pass_on(*sums)
        sums = conv_part(stacked, places[5:7], [[back[3]], [on[3]]], sums, length)
        last = [[back[4], on[4]]]
        (for_partner,) = conv_part(stacked[:1], places[7:], last, sums[:1], length, BF16)
        own_part = sums[1]
        rest = [stacked[1], *last[0]]
        places = places[7]
    else:
        groups = [list(range(first, devices, 2)) for first in range(2)]
        weight = lax.all_gather(mine, "blocks", axis=0, tiled=True, axis_index_groups=groups)
        nowhere = jnp.zeros((1, 2), jnp.int32)
        for_partner, own_part = conv_part(stacked, nowhere, [[weight]], None, length)
        places, rest = nowhere[0], []

    positions = jnp.arange(points, dtype=jnp.int32)
    target = serial_rank // points
    earlier = (target[None, :] == target[:, None]) & (serial_rank[None, :] < serial_rank[:, None])
    out_slot = target * capacity + jnp.sum(earlier.astype(jnp.int32), axis=1)
    anchor = serial_order // points
    before = (anchor[None, :] == anchor[:, None]) & (positions[None, :] < positions[:, None])
    in_slot = anchor * capacity + jnp.sum(before.astype(jnp.int32), axis=1)

    from_partner = lax.ppermute(for_partner, "blocks", partner)

    outgoing = call(
        functools.partial(mix_kernel, len(rest) - 1 if rest else 0),
        jax.ShapeDtypeStruct((slots, width), BF16),
        60,
        2 * points * width * (width + slots + length),
        8 * points * width,
        in_specs=[pl.BlockSpec(memory_space=pltpu.SMEM)]
        + [pl.BlockSpec()] * 3
        + [pl.BlockSpec(memory_space=pl.ANY)] * (3 + len(rest)),
        scratch_shapes=[
            pltpu.VMEM((points, width), F32),
            pltpu.VMEM((points, width), BF16),
            pltpu.VMEM((width, width), BF16),
            pltpu.VMEM((points, width), F32),
            pltpu.SemaphoreType.DMA((3,)),
            pltpu.VMEM((1, 1, points, length if rest else 128), BF16),
            pltpu.VMEM((1, length if rest else 128, width), BF16),
            pltpu.SemaphoreType.DMA((1, 4)),
        ],
    )(
        places,
        from_partner,
        cpe_gain.reshape(1, width),
        out_slot.reshape(1, points),
        own_part,
        features,
        cpe_weight,
        *rest,
    )
    arrived = lax.all_to_all(
        outgoing.reshape(devices, capacity, width), "blocks", split_axis=0, concat_axis=0, tiled=True
    ).reshape(slots, width)

    key_weight = qkv_weight[:, width : 2 * width]
    qv_weight = jnp.concatenate([qkv_weight[:, :width], qkv_weight[:, 2 * width :]], axis=1).T
    weights = (qv_weight, key_weight, proj_weight, up_weight, down_weight)
    back = call(
        block_kernel,
        jax.ShapeDtypeStruct((slots, width), BF16),
        60,
        20 * points * width * width,
        16 * width * width,
        in_specs=[pl.BlockSpec()] * 5 + [pl.BlockSpec(memory_space=pl.ANY)] * len(weights),
        scratch_shapes=[pltpu.VMEM(weight.shape, BF16) for weight in weights]
        + [
            pltpu.SemaphoreType.DMA((len(weights),)),
            pltpu.VMEM((points, width), F32),
            pltpu.VMEM((2 * width, points), BF16),
            pltpu.VMEM((points, width), BF16),
            pltpu.VMEM((width, points), BF16),
            pltpu.VMEM((points, width), F32),
            pltpu.VMEM((2, points, points), F32),
            pltpu.VMEM((2, points, points), BF16),
        ],
    )(
        arrived,
        in_slot.reshape(points, 1),
        in_slot.reshape(1, points),
        attn_gain.reshape(1, width),
        mlp_gain.reshape(1, width),
        *weights,
    )
    returned = lax.all_to_all(
        back.reshape(devices, capacity, width), "blocks", split_axis=0, concat_axis=0, tiled=True
    ).reshape(slots, width)
    return call(
        return_kernel,
        jax.ShapeDtypeStruct((points, width), BF16),
        32,
        2 * points * slots * width,
        6 * points * width,
    )(returned, out_slot.reshape(points, 1))


def solution(mesh):
    placed = (
        P(("groups", "blocks"), None),
        P("blocks", None),
        P(),
        P(),
        P(),
        P(),
        P(),
        P(),
        P(),
        P(),
        P(("groups", "blocks"), None, None),
        P(("groups", "blocks"), None),
        P(("groups", "blocks")),
        P(("groups", "blocks")),
    )
    return jax.shard_map(
        body, mesh=mesh, in_specs=placed, out_specs=P(("groups", "blocks"), None), check_vma=False
    )
```

```python
import functools
import math

import jax
import jax.numpy as jnp
from jax import lax
from jax.experimental import pallas as pl
from jax.experimental.pallas import tpu as pltpu
from jax.sharding import PartitionSpec as P

HEADS = 32
GY = 8
HD = 16
TAPS = 27
EPSILON = 1e-05
STEPS_X = (-1, -1, -1, 0, 0, 1, 1, 1)
STEPS_Y = (-1, 0, 1, -1, 1, -1, 0, 1)
F32 = jnp.float32
BF16 = jnp.bfloat16
MIB = 1 << 20
CONV_LIMITS = (24, 40)


def dot(left, right):
    return jnp.dot(left, right, preferred_element_type=F32)


def layer_norm(inputs, gain_vector):
    row_mean = jnp.mean(inputs, axis=-1, keepdims=True)
    centred = inputs - row_mean
    variance = jnp.mean(centred * centred, axis=-1, keepdims=True)
    return centred * lax.rsqrt(variance + EPSILON) * gain_vector


def one_hot(mask):
    return jnp.where(mask, 1.0, 0.0).astype(BF16)


def call(kernel, out_shape, limit, flops, moved, **extra):
    return pl.pallas_call(
        kernel,
        out_shape=out_shape,
        compiler_params=pltpu.CompilerParams(vmem_limit_bytes=limit * MIB),
        cost_estimate=pl.CostEstimate(flops=flops, bytes_accessed=moved, transcendentals=0),
        **extra,
    )


def faces_kernel(unit, core_ref, features_ref, rows_ref, own_ref, other_ref, *face_refs):
    points, width = features_ref.shape
    half = width // 2
    place = lax.broadcasted_iota(jnp.int32, (width, width), 1)
    within = lax.rem(place, half)
    source = (within // unit) * (2 * unit) + (place // half) * unit + lax.rem(place, unit)
    channel = lax.broadcasted_iota(jnp.int32, (width, width), 0)
    ordered = dot(features_ref[...], one_hot(channel == source)).astype(BF16)
    first, second = ordered[:, :half], ordered[:, half:]
    even = core_ref[0] == 0
    own_ref[...] = jnp.where(even, first, second)
    other_ref[...] = jnp.where(even, second, first)
    row_ids = lax.broadcasted_iota(jnp.int32, (rows_ref.shape[0], points), 1)
    rows = dot(one_hot(rows_ref[...] == row_ids), ordered).astype(BF16)
    taken = 0
    for ref in face_refs:
        ref[...] = rows[taken : taken + ref.shape[0]]
        taken += ref.shape[0]


def received_kernel(flags_ref, side_ref, behind_ref, ahead_ref, own_ref, other_ref):
    size = behind_ref.shape[0] // 2
    half = own_ref.shape[1]
    lower, even = flags_ref[0] == 1, flags_ref[1] == 0
    across = [ahead_ref[size:], side_ref[size : 2 * size], behind_ref[size:]]
    along = [ahead_ref[:size], behind_ref[:size]]
    for at, (low, high) in enumerate(zip(across + along, along + across)):
        rows = jnp.where(lower, low, high)
        first, second = rows[:, :half], rows[:, half:]
        own_ref[at * size : (at + 1) * size] = jnp.where(even, first, second)
        other_ref[at * size : (at + 1) * size] = jnp.where(even, second, first)
    rest = jnp.zeros((size, half), BF16)
    own_ref[5 * size :] = rest
    other_ref[5 * size :] = rest


def gather_kernel(taps, start_ref, rows_ref, own_ref, got_ref, out_ref):
    half = own_ref.shape[1]
    lane = lax.broadcasted_iota(jnp.int32, rows_ref.shape, 1)
    parts = []
    for table, start in ((own_ref, 0), (got_ref, start_ref[0])):
        ids = lax.broadcasted_iota(jnp.int32, (1, table.shape[0]), 1) + start
        parts.append((table, ids.astype(F32)))
    for at in range(taps):
        chosen = lane == taps * pl.program_id(0) + at
        column = jnp.sum(jnp.where(chosen, rows_ref[...], 0.0), axis=1, keepdims=True)
        hits = [one_hot(column == ids) for _, ids in parts]
        products = [dot(hit, table[...]) for hit, (table, _) in zip(hits, parts)]
        out_ref[:, at * half : (at + 1) * half] = (products[0] + products[1]).astype(BF16)


def gather_block(start, rows, own, got):
    points, lanes = rows.shape
    half = own.shape[1]
    height = own.shape[0] + got.shape[0]
    taps = 9
    whole = lambda step: (0, 0)
    return call(
        functools.partial(gather_kernel, taps),
        jax.ShapeDtypeStruct((points, TAPS * half), BF16),
        60,
        2 * TAPS * points * height * half,
        2 * TAPS * points * half,
        grid=(TAPS // taps,),
        in_specs=[
            pl.BlockSpec(memory_space=pltpu.SMEM),
            pl.BlockSpec((points, lanes), whole),
            pl.BlockSpec(own.shape, whole),
            pl.BlockSpec(got.shape, whole),
        ],
        out_specs=pl.BlockSpec((points, taps * half), lambda step: (0, step)),
    )(start, rows, own, got)


def conv_kernel(slots, blocks, first, places_ref, *refs):
    stacked, refs = refs[:blocks], refs[blocks:]
    pieces, refs = refs[: sum(slots)], refs[sum(slots) :]
    before = [] if first else refs[:blocks]
    outs, (lhs, held, sems) = refs[-3 - blocks : -3], refs[-3:]
    length = held.shape[1]
    copies, taken = [], 0
    for at, count in enumerate(slots):
        column = pl.multiple_of(places_ref[2 * at], 128)
        row = pl.multiple_of(places_ref[2 * at + 1], 16)
        copies.append([])
        for block in range(blocks):
            copy = pltpu.make_async_copy(
                stacked[block].at[:, pl.ds(column, length)], lhs.at[at, block], sems.at[at, block]
            )
            copy.start()
            copies[-1].append(copy)
        short = count * pieces[taken].shape[0]
        edge = length - short
        if edge:
            held[at, :edge] = jnp.zeros((edge, held.shape[2]), BF16)
            held[at, length - edge :] = jnp.zeros((edge, held.shape[2]), BF16)
        for part in range(count):
            piece = pieces[taken]
            size = piece.shape[0]
            copy = pltpu.make_async_copy(
                piece, held.at[at, pl.ds(row + part * size, size)], sems.at[at, 2 + part]
            )
            copy.start()
            copies[-1].append(copy)
            taken += 1
    for at in range(len(slots)):
        for copy in copies[at]:
            copy.wait()
        for block, ref in enumerate(outs):
            product = dot(lhs[at, block], held[at])
            if at > 0:
                ref[...] += product
            elif first:
                ref[...] = product
            else:
                ref[...] = (before[block][...] + product).astype(ref.dtype)


def conv_part(stacked, places, pieces, before, length, dtype=F32):
    points, depth = stacked[0].shape
    width = pieces[0][0].shape[1]
    slots = [len(parts) for parts in pieces]
    flat = [piece for parts in pieces for piece in parts]
    blocks = len(stacked)
    held = 1 + blocks + len(flat)
    kept = [] if before is None else [block for block in range(blocks) if block or dtype == F32]
    return call(
        functools.partial(conv_kernel, slots, blocks, before is None),
        [
            jax.ShapeDtypeStruct((points, width), dtype if block == 0 else F32)
            for block in range(blocks)
        ],
        CONV_LIMITS[len(slots) > 2],
        2 * blocks * points * length * width * len(slots),
        2 * length * (blocks * points + width) * len(slots),
        in_specs=[pl.BlockSpec(memory_space=pltpu.SMEM)]
        + [pl.BlockSpec(memory_space=pl.ANY)] * (held - 1)
        + ([] if before is None else [pl.BlockSpec()] * blocks),
        input_output_aliases={held + block: block for block in kept},
        scratch_shapes=[
            pltpu.VMEM((len(slots), blocks, points, length), BF16),
            pltpu.VMEM((len(slots), length, width), BF16),
            pltpu.SemaphoreType.DMA((len(slots), 4)),
        ],
    )(places.reshape(-1), *stacked, *flat, *(before or ()))


def mix_kernel(own_ref, got_ref, features_ref, weight_ref, gain_ref, slot_ref, out_ref):
    convolved = (own_ref[...] + got_ref[...].astype(F32)).astype(BF16)
    linear = dot(convolved, weight_ref[...])
    mixed = (features_ref[...].astype(F32) + layer_norm(linear, gain_ref[...])).astype(BF16)
    slots = lax.broadcasted_iota(jnp.int32, (out_ref.shape[0], mixed.shape[0]), 0)
    out_ref[...] = dot(one_hot(slots == slot_ref[...]), mixed).astype(BF16)


def block_kernel(
    arrived_ref,
    slot_col_ref,
    slot_row_ref,
    attn_gain_ref,
    mlp_gain_ref,
    qv_hbm,
    key_hbm,
    proj_hbm,
    up_hbm,
    down_hbm,
    out_ref,
    qv_ref,
    key_ref,
    proj_ref,
    up_ref,
    down_ref,
    sems,
    serial_ref,
    qv_cols_ref,
    keys_ref,
    heads_ref,
    total_ref,
    scores_ref,
    weights_ref,
):
    sources = (key_hbm, qv_hbm, proj_hbm, up_hbm, down_hbm)
    targets = (key_ref, qv_ref, proj_ref, up_ref, down_ref)
    copies = [
        pltpu.make_async_copy(source, target, sems.at[at])
        for at, (source, target) in enumerate(zip(sources, targets))
    ]
    for copy in copies:
        copy.start()
    slots = arrived_ref.shape[0]
    points, width = serial_ref.shape
    slot_ids = lax.broadcasted_iota(jnp.int32, (points, slots), 1)
    serial = dot(one_hot(slot_col_ref[...] == slot_ids), arrived_ref[...])
    serial_ref[...] = serial
    normed = layer_norm(serial, attn_gain_ref[...]).astype(BF16)
    copies[0].wait()
    keys_ref[...] = dot(normed, key_ref[...]).astype(BF16)
    copies[1].wait()
    factor = math.log2(math.e) / math.sqrt(HD)
    contract_last = (((1,), (1,)), ((), ()))
    qv_cols_ref[:width] = (
        lax.dot_general(qv_ref[:width], normed, contract_last, preferred_element_type=F32) * factor
    ).astype(BF16)
    qv_cols_ref[width:] = lax.dot_general(
        qv_ref[width:], normed, contract_last, preferred_element_type=F32
    ).astype(BF16)
    ones = jnp.ones((HD, points), BF16)
    per_group = 128 // HD
    head_of_row = lax.broadcasted_iota(jnp.int32, (128, points), 0) // HD

    def score(head, slot):
        base = pl.multiple_of(head // per_group * 128, 128)
        group_queries = qv_cols_ref[pl.ds(base, 128)].astype(F32)
        chosen = head_of_row == lax.rem(head, per_group)
        queries = jnp.where(chosen, group_queries, 0.0).astype(BF16)
        scores_ref[slot] = dot(keys_ref[:, pl.ds(base, 128)], queries)

    def weigh(slot):
        scores = scores_ref[slot]
        weights_ref[slot] = jnp.exp2(scores - jnp.max(scores, axis=0, keepdims=True)).astype(BF16)

    def gather(head, slot):
        at = pl.multiple_of(head * HD, HD)
        values = jnp.concatenate([qv_cols_ref[pl.ds(width + at, HD)], ones], axis=0)
        sums = dot(values, weights_ref[slot])
        heads_ref[pl.ds(at, HD)] = (sums[:HD] / sums[HD : HD + 1]).astype(BF16)

    score(0, 0)
    score(1, 1)
    weigh(0)

    def two_heads(pair, carry):
        head = 2 * pair + 1
        for slot in (1, 0):
            score(head + 1, 1 - slot)
            weigh(slot)
            gather(head - 1, 1 - slot)
            head += 1
        return carry

    lax.fori_loop(0, HEADS // 2 - 1, two_heads, 0)
    weigh(1)
    gather(HEADS - 2, 0)
    gather(HEADS - 1, 1)

    for copy in copies[2:]:
        copy.wait()
    update = lax.dot_general(
        heads_ref[...], proj_ref[...], (((0,), (0,)), ((), ())), preferred_element_type=F32
    )
    attended = (serial_ref[...] + update).astype(BF16).astype(F32)
    hidden_in = layer_norm(attended, mlp_gain_ref[...]).astype(BF16)
    total_ref[...] = attended
    chunk = width
    for start in range(0, up_ref.shape[1], chunk):
        raised = dot(hidden_in, up_ref[:, start : start + chunk])
        hidden = (raised * (1.0 + lax.erf(raised * math.sqrt(0.5))) * 0.5).astype(BF16)
        total_ref[...] += dot(hidden, down_ref[start : start + chunk])
    finished = total_ref[...].astype(BF16)
    slot_rows = lax.broadcasted_iota(jnp.int32, (slots, points), 0)
    out_ref[...] = dot(one_hot(slot_rows == slot_row_ref[...]), finished).astype(BF16)


def return_kernel(arrived_ref, slot_ref, out_ref):
    slot_ids = lax.broadcasted_iota(jnp.int32, (out_ref.shape[0], arrived_ref.shape[0]), 1)
    out_ref[...] = dot(one_hot(slot_ref[...] == slot_ids), arrived_ref[...]).astype(BF16)


def face_pairs(devices, dx, dy):
    return [
        (source, source + dx * GY + dy)
        for source in range(devices)
        if 0 <= source // GY + dx < devices // GY and 0 <= source % GY + dy < GY
    ]


def way_round(devices, rows, length):
    chips = devices // 2
    cycle = list(range(0, chips, 2)) + list(range(chips - 1, 0, -2))
    back, on = [], []
    places = [None] * devices
    for place, chip in enumerate(cycle):
        for core in range(2):
            me = 2 * chip + core
            back.append((me, 2 * cycle[(place + 1) % chips] + core))
            on.append((me, 2 * cycle[place - 1] + core))
            order = [0]
            for step in range(1, chips // 2):
                order += [-step, step]
            order.append(chips // 2)
            places[me] = []
            for offset in order:
                start = cycle[(place + offset) % chips] * rows
                column = min(start // 128 * 128, chips * rows - length)
                places[me].append((column, start - column))
    return back, on, places


def padded_taps(neighbours):
    points = neighbours.shape[0]
    own = jnp.arange(points, dtype=jnp.int32)[:, None]
    rest = jnp.zeros((points, 128 - TAPS), jnp.int32)
    middle = TAPS // 2
    rows = jnp.concatenate([neighbours[:, :middle], own, neighbours[:, middle:], rest], axis=1)
    return rows.astype(F32)


def body(
    features,
    conv_weight,
    cpe_weight,
    cpe_gain,
    attn_gain,
    qkv_weight,
    proj_weight,
    mlp_gain,
    up_weight,
    down_weight,
    face_rows,
    neighbours,
    serial_rank,
    serial_order,
):
    points, width = features.shape
    half = width // 2
    devices = lax.axis_size("blocks")
    index = lax.axis_index("blocks")
    core = lax.rem(index, 2)
    partner = [(source, source ^ 1) for source in range(devices)]
    capacity = 2 * points // devices
    slots = devices * capacity

    unit = conv_weight.shape[0] // TAPS
    units = conv_weight.reshape(TAPS, unit, width)
    kept, sent = units[0::2], units[1::2]
    got = lax.ppermute(sent, "blocks", partner)
    mine = jnp.where(
        core == 0, jnp.concatenate([kept, got]), jnp.concatenate([got, kept])
    ).reshape(TAPS * unit, width)
    round_trip = devices == 2 * GY
    lower = index < GY
    if round_trip:
        across = jnp.where(lower, face_rows[0, 5:], face_rows[0, :3])
        face_list = jnp.concatenate([across, face_rows[0, 3:5]]).reshape(-1, 1)
        counts = (3, 1, 1)
    else:
        face_list = face_rows.reshape(-1, 1)
        counts = (1,) * 8
    size = face_rows.shape[2]
    own_local, other_half, *faces = call(
        functools.partial(faces_kernel, unit),
        [jax.ShapeDtypeStruct((points, half), BF16)] * 2
        + [jax.ShapeDtypeStruct((count * size, width), BF16) for count in counts],
        60,
        4 * points * width * width,
        8 * points * width,
        in_specs=[pl.BlockSpec(memory_space=pltpu.SMEM)] + [pl.BlockSpec()] * 2,
    )(core.reshape(1), features, face_list)
    other_local = lax.ppermute(other_half, "blocks", partner)
    other_neighbours = lax.ppermute(neighbours, "blocks", partner)

    rows = mine.shape[0]
    length = -(-(rows + 127) // 128) * 128 if round_trip else rows * (devices // 2)
    back_pairs, on_pairs, places = way_round(devices, rows, length)
    back, on = [mine], [mine]

    def pass_on(*beside):
        if not round_trip:
            return beside
        tied = lax.optimization_barrier((back[-1], on[-1], *beside))
        first, second = tied[:2]
        back[-1], on[-1] = first, second
        if len(back) == devices // 4:
            first, second = first[: rows // 2], second[rows // 2 :]
        back.append(lax.ppermute(first, "blocks", back_pairs))
        on.append(lax.ppermute(second, "blocks", on_pairs))
        return tied[2:]

    if round_trip:
        lists, back_list, on_list = faces
        side = face_pairs(devices, 1, 0) + face_pairs(devices, -1, 0)
        lists, other_local, other_neighbours = pass_on(lists, other_local, other_neighbours)
        lists = lax.ppermute(lists, "blocks", side)
    own_rows, other_rows = padded_taps(neighbours), padded_taps(other_neighbours)
    if round_trip:
        to_on = jnp.concatenate([on_list, lists[2 * size :]])
        to_back = jnp.concatenate([back_list, lists[:size]])
        behind = lax.ppermute(to_on, "blocks", face_pairs(devices, 0, 1))
        ahead = lax.ppermute(to_back, "blocks", face_pairs(devices, 0, -1))
        lists, behind, ahead = pass_on(lists, behind, ahead)
        own_remote, other_half = call(
            received_kernel,
            [jax.ShapeDtypeStruct((6 * size, half), BF16)] * 2,
            32,
            0,
            20 * size * width,
            in_specs=[pl.BlockSpec(memory_space=pltpu.SMEM)] + [pl.BlockSpec()] * 3,
        )(jnp.stack([lower.astype(jnp.int32), core]), lists, behind, ahead)
        start = jnp.where(lower, points, points + 3 * size).reshape(1)
    else:
        received = jnp.concatenate(
            [
                lax.ppermute(faces[k], "blocks", face_pairs(devices, STEPS_X[k], STEPS_Y[k]))
                for k in range(8)
            ]
        )
        own_remote = lax.dynamic_slice(received, (0, core * half), (8 * size, half))
        other_half = lax.dynamic_slice(received, (0, (1 - core) * half), (8 * size, half))
        start = jnp.full((1,), points, jnp.int32)
    other_remote = lax.ppermute(other_half, "blocks", partner)
    own_stacked = gather_block(start, own_rows, own_local, own_remote)
    other_stacked = gather_block(start, other_rows, other_local, other_remote)
    stacked = pass_on(other_stacked, own_stacked)
    if round_trip:
        places = jnp.array(places, jnp.int32)[index]
        early = [[mine], [back[1]], [on[1]], [back[2]], [on[2]]]
        sums = conv_part(stacked, places[:5], early, None, length)
        sums = pass_on(*sums)
        sums = conv_part(stacked, places[5:7], [[back[3]], [on[3]]], sums, length)
        last = [[back[4], on[4]]]
        for_partner, own_part = conv_part(stacked, places[7:], last, sums, length, BF16)
    else:
        groups = [list(range(first, devices, 2)) for first in range(2)]
        weight = lax.all_gather(mine, "blocks", axis=0, tiled=True, axis_index_groups=groups)
        nowhere = jnp.zeros((1, 2), jnp.int32)
        for_partner, own_part = conv_part(stacked, nowhere, [[weight]], None, length)

    positions = jnp.arange(points, dtype=jnp.int32)
    target = serial_rank // points
    earlier = (target[None, :] == target[:, None]) & (serial_rank[None, :] < serial_rank[:, None])
    out_slot = target * capacity + jnp.sum(earlier.astype(jnp.int32), axis=1)
    anchor = serial_order // points
    before = (anchor[None, :] == anchor[:, None]) & (positions[None, :] < positions[:, None])
    in_slot = anchor * capacity + jnp.sum(before.astype(jnp.int32), axis=1)

    from_partner = lax.ppermute(for_partner, "blocks", partner)

    outgoing = call(
        mix_kernel,
        jax.ShapeDtypeStruct((slots, width), BF16),
        32,
        2 * points * width * (width + slots),
        8 * points * width,
    )(
        own_part,
        from_partner,
        features,
        cpe_weight,
        cpe_gain.reshape(1, width),
        out_slot.reshape(1, points),
    )
    arrived = lax.all_to_all(
        outgoing.reshape(devices, capacity, width), "blocks", split_axis=0, concat_axis=0, tiled=True
    ).reshape(slots, width)

    key_weight = qkv_weight[:, width : 2 * width]
    qv_weight = jnp.concatenate([qkv_weight[:, :width], qkv_weight[:, 2 * width :]], axis=1).T
    weights = (qv_weight, key_weight, proj_weight, up_weight, down_weight)
    back = call(
        block_kernel,
        jax.ShapeDtypeStruct((slots, width), BF16),
        60,
        20 * points * width * width,
        16 * width * width,
        in_specs=[pl.BlockSpec()] * 5 + [pl.BlockSpec(memory_space=pl.ANY)] * len(weights),
        scratch_shapes=[pltpu.VMEM(weight.shape, BF16) for weight in weights]
        + [
            pltpu.SemaphoreType.DMA((len(weights),)),
            pltpu.VMEM((points, width), F32),
            pltpu.VMEM((2 * width, points), BF16),
            pltpu.VMEM((points, width), BF16),
            pltpu.VMEM((width, points), BF16),
            pltpu.VMEM((points, width), F32),
            pltpu.VMEM((2, points, points), F32),
            pltpu.VMEM((2, points, points), BF16),
        ],
    )(
        arrived,
        in_slot.reshape(points, 1),
        in_slot.reshape(1, points),
        attn_gain.reshape(1, width),
        mlp_gain.reshape(1, width),
        *weights,
    )
    returned = lax.all_to_all(
        back.reshape(devices, capacity, width), "blocks", split_axis=0, concat_axis=0, tiled=True
    ).reshape(slots, width)
    return call(
        return_kernel,
        jax.ShapeDtypeStruct((points, width), BF16),
        32,
        2 * points * slots * width,
        6 * points * width,
    )(returned, out_slot.reshape(points, 1))


def solution(mesh):
    placed = (
        P(("groups", "blocks"), None),
        P("blocks", None),
        P(),
        P(),
        P(),
        P(),
        P(),
        P(),
        P(),
        P(),
        P(("groups", "blocks"), None, None),
        P(("groups", "blocks"), None),
        P(("groups", "blocks")),
        P(("groups", "blocks")),
    )
    return jax.shard_map(
        body, mesh=mesh, in_specs=placed, out_specs=P(("groups", "blocks"), None), check_vma=False
    )
```

```python
import functools
import math

import jax
import jax.numpy as jnp
from jax import lax
from jax.experimental import pallas as pl
from jax.experimental.pallas import tpu as pltpu
from jax.sharding import PartitionSpec as P

HEADS = 32
GY = 8
HD = 16
TAPS = 27
EPSILON = 1e-05
STEPS_X = (-1, -1, -1, 0, 0, 1, 1, 1)
STEPS_Y = (-1, 0, 1, -1, 1, -1, 0, 1)
F32 = jnp.float32
BF16 = jnp.bfloat16
MIB = 1 << 20


def dot(left, right):
    return jnp.dot(left, right, preferred_element_type=F32)


def layer_norm(inputs, gain_vector):
    row_mean = jnp.mean(inputs, axis=-1, keepdims=True)
    centred = inputs - row_mean
    variance = jnp.mean(centred * centred, axis=-1, keepdims=True)
    return centred * lax.rsqrt(variance + EPSILON) * gain_vector


def one_hot(mask):
    return jnp.where(mask, 1.0, 0.0).astype(BF16)


def call(kernel, out_shape, limit, flops, moved, **extra):
    return pl.pallas_call(
        kernel,
        out_shape=out_shape,
        compiler_params=pltpu.CompilerParams(vmem_limit_bytes=limit * MIB),
        cost_estimate=pl.CostEstimate(flops=flops, bytes_accessed=moved, transcendentals=0),
        **extra,
    )


def faces_kernel(unit, core_ref, features_ref, rows_ref, own_ref, other_ref, *face_refs):
    points, width = features_ref.shape
    half = width // 2
    place = lax.broadcasted_iota(jnp.int32, (width, width), 1)
    within = lax.rem(place, half)
    source = (within // unit) * (2 * unit) + (place // half) * unit + lax.rem(place, unit)
    channel = lax.broadcasted_iota(jnp.int32, (width, width), 0)
    ordered = dot(features_ref[...], one_hot(channel == source)).astype(BF16)
    first, second = ordered[:, :half], ordered[:, half:]
    even = core_ref[0] == 0
    own_ref[...] = jnp.where(even, first, second)
    other_ref[...] = jnp.where(even, second, first)
    row_ids = lax.broadcasted_iota(jnp.int32, (rows_ref.shape[0], points), 1)
    rows = dot(one_hot(rows_ref[...] == row_ids), ordered).astype(BF16)
    taken = 0
    for ref in face_refs:
        ref[...] = rows[taken : taken + ref.shape[0]]
        taken += ref.shape[0]


def received_kernel(flags_ref, side_ref, behind_ref, ahead_ref, own_ref, other_ref):
    size = behind_ref.shape[0] // 2
    half = own_ref.shape[1]
    lower, even = flags_ref[0] == 1, flags_ref[1] == 0
    across = [ahead_ref[size:], side_ref[size : 2 * size], behind_ref[size:]]
    along = [ahead_ref[:size], behind_ref[:size]]
    for at, (low, high) in enumerate(zip(across + along, along + across)):
        rows = jnp.where(lower, low, high)
        first, second = rows[:, :half], rows[:, half:]
        own_ref[at * size : (at + 1) * size] = jnp.where(even, first, second)
        other_ref[at * size : (at + 1) * size] = jnp.where(even, second, first)
    rest = jnp.zeros((size, half), BF16)
    own_ref[5 * size :] = rest
    other_ref[5 * size :] = rest


def gather_kernel(taps, start_ref, rows_ref, own_ref, got_ref, out_ref):
    half = own_ref.shape[1]
    lane = lax.broadcasted_iota(jnp.int32, rows_ref.shape, 1)
    parts = []
    for table, start in ((own_ref, 0), (got_ref, start_ref[0])):
        ids = lax.broadcasted_iota(jnp.int32, (1, table.shape[0]), 1) + start
        parts.append((table, ids.astype(F32)))
    for at in range(taps):
        chosen = lane == taps * pl.program_id(0) + at
        column = jnp.sum(jnp.where(chosen, rows_ref[...], 0.0), axis=1, keepdims=True)
        hits = [one_hot(column == ids) for _, ids in parts]
        products = [dot(hit, table[...]) for hit, (table, _) in zip(hits, parts)]
        out_ref[:, at * half : (at + 1) * half] = (products[0] + products[1]).astype(BF16)


def gather_block(start, rows, own, got):
    points, lanes = rows.shape
    half = own.shape[1]
    height = own.shape[0] + got.shape[0]
    taps = 9
    whole = lambda step: (0, 0)
    return call(
        functools.partial(gather_kernel, taps),
        jax.ShapeDtypeStruct((points, TAPS * half), BF16),
        60,
        2 * TAPS * points * height * half,
        2 * TAPS * points * half,
        grid=(TAPS // taps,),
        in_specs=[
            pl.BlockSpec(memory_space=pltpu.SMEM),
            pl.BlockSpec((points, lanes), whole),
            pl.BlockSpec(own.shape, whole),
            pl.BlockSpec(got.shape, whole),
        ],
        out_specs=pl.BlockSpec((points, taps * half), lambda step: (0, step)),
    )(start, rows, own, got)


def conv_kernel(slots, later, ready, first, places_ref, *refs):
    refs = list(refs)

    def take(count):
        taken = refs[:count]
        del refs[:count]
        return taken

    sources = take(1 if ready else 2)
    pieces = take(sum(slots))
    before = [] if first else take(2)
    outs = take(2)
    kept = take(len(later))
    (lhs,) = sources if ready else take(1)
    held, sems = take(2)
    length = held.shape[1]

    def stretch(slot, target, sem):
        column = pl.multiple_of(places_ref[2 * slot], 128)
        copies = [
            pltpu.make_async_copy(
                stacked.at[:, pl.ds(column, length)], target.at[block], sem.at[block]
            )
            for block, stacked in enumerate(sources)
        ]
        for copy in copies:
            copy.start()
        return copies

    copies, taken = [], 0
    for at, count in enumerate(slots):
        row = pl.multiple_of(places_ref[2 * at + 1], 16)
        copies.append([] if ready else stretch(at, lhs.at[at], sems.at[at]))
        short = count * pieces[taken].shape[0]
        edge = length - short
        if edge:
            held[at, :edge] = jnp.zeros((edge, held.shape[2]), BF16)
            held[at, length - edge :] = jnp.zeros((edge, held.shape[2]), BF16)
        for part in range(count):
            piece = pieces[taken]
            size = piece.shape[0]
            copy = pltpu.make_async_copy(
                piece, held.at[at, pl.ds(row + part * size, size)], sems.at[at, 2 + part]
            )
            copy.start()
            copies[-1].append(copy)
            taken += 1
    extra, slot = [], len(slots)
    for group, count in enumerate(later):
        for place in range(count):
            extra += stretch(slot, kept[group].at[place], sems.at[slot])
            slot += 1
    for at in range(len(slots)):
        for copy in copies[at]:
            copy.wait()
        for block, ref in enumerate(outs):
            product = dot(lhs[at, block], held[at])
            if at > 0:
                ref[...] += product
            elif first:
                ref[...] = product
            else:
                ref[...] = (before[block][...] + product).astype(ref.dtype)
    for copy in extra:
        copy.wait()


def conv_part(sources, places, pieces, before, length, later=(), dtype=F32):
    ready = len(sources) == 1
    points = sources[0].shape[2] if ready else sources[0].shape[0]
    width = pieces[0][0].shape[1]
    slots = [len(parts) for parts in pieces]
    flat = [piece for parts in pieces for piece in parts]
    held = 1 + len(sources) + len(flat)
    kept = [] if before is None else [block for block in range(2) if block or dtype == F32]
    spec = pl.BlockSpec(memory_space=pl.ANY)
    return call(
        functools.partial(conv_kernel, slots, later, ready, before is None),
        [
            jax.ShapeDtypeStruct((points, width), dtype),
            jax.ShapeDtypeStruct((points, width), F32),
        ]
        + [jax.ShapeDtypeStruct((count, 2, points, length), BF16) for count in later],
        24 if ready else 36,
        4 * points * length * width * len(slots),
        2 * length * (2 * points + width) * len(slots),
        in_specs=[pl.BlockSpec(memory_space=pltpu.SMEM)]
        + [pl.BlockSpec() if ready else spec] * len(sources)
        + [spec] * len(flat)
        + ([] if before is None else [pl.BlockSpec()] * 2),
        input_output_aliases={held + block: block for block in kept},
        scratch_shapes=([] if ready else [pltpu.VMEM((len(slots), 2, points, length), BF16)])
        + [
            pltpu.VMEM((len(slots), length, width), BF16),
            pltpu.SemaphoreType.DMA((len(slots) + sum(later), 4)),
        ],
    )(places.reshape(-1), *sources, *flat, *(before or ()))


def mix_kernel(own_ref, got_ref, features_ref, weight_ref, gain_ref, slot_ref, out_ref):
    convolved = (own_ref[...] + got_ref[...].astype(F32)).astype(BF16)
    linear = dot(convolved, weight_ref[...])
    mixed = (features_ref[...].astype(F32) + layer_norm(linear, gain_ref[...])).astype(BF16)
    slots = lax.broadcasted_iota(jnp.int32, (out_ref.shape[0], mixed.shape[0]), 0)
    out_ref[...] = dot(one_hot(slots == slot_ref[...]), mixed).astype(BF16)


def block_kernel(
    arrived_ref,
    slot_col_ref,
    slot_row_ref,
    attn_gain_ref,
    mlp_gain_ref,
    qv_hbm,
    key_hbm,
    proj_hbm,
    up_hbm,
    down_hbm,
    out_ref,
    qv_ref,
    key_ref,
    proj_ref,
    up_ref,
    down_ref,
    sems,
    serial_ref,
    qv_cols_ref,
    keys_ref,
    heads_ref,
    total_ref,
    scores_ref,
    weights_ref,
):
    sources = (key_hbm, qv_hbm, proj_hbm, up_hbm, down_hbm)
    targets = (key_ref, qv_ref, proj_ref, up_ref, down_ref)
    copies = [
        pltpu.make_async_copy(source, target, sems.at[at])
        for at, (source, target) in enumerate(zip(sources, targets))
    ]
    for copy in copies:
        copy.start()
    slots = arrived_ref.shape[0]
    points, width = serial_ref.shape
    slot_ids = lax.broadcasted_iota(jnp.int32, (points, slots), 1)
    serial = dot(one_hot(slot_col_ref[...] == slot_ids), arrived_ref[...])
    serial_ref[...] = serial
    normed = layer_norm(serial, attn_gain_ref[...]).astype(BF16)
    copies[0].wait()
    keys_ref[...] = dot(normed, key_ref[...]).astype(BF16)
    copies[1].wait()
    factor = math.log2(math.e) / math.sqrt(HD)
    contract_last = (((1,), (1,)), ((), ()))
    qv_cols_ref[:width] = (
        lax.dot_general(qv_ref[:width], normed, contract_last, preferred_element_type=F32) * factor
    ).astype(BF16)
    qv_cols_ref[width:] = lax.dot_general(
        qv_ref[width:], normed, contract_last, preferred_element_type=F32
    ).astype(BF16)
    ones = jnp.ones((HD, points), BF16)
    per_group = 128 // HD
    head_of_row = lax.broadcasted_iota(jnp.int32, (128, points), 0) // HD

    def score(head, slot):
        base = pl.multiple_of(head // per_group * 128, 128)
        group_queries = qv_cols_ref[pl.ds(base, 128)].astype(F32)
        chosen = head_of_row == lax.rem(head, per_group)
        queries = jnp.where(chosen, group_queries, 0.0).astype(BF16)
        scores_ref[slot] = dot(keys_ref[:, pl.ds(base, 128)], queries)

    def weigh(slot):
        scores = scores_ref[slot]
        weights_ref[slot] = jnp.exp2(scores - jnp.max(scores, axis=0, keepdims=True)).astype(BF16)

    def gather(head, slot):
        at = pl.multiple_of(head * HD, HD)
        values = jnp.concatenate([qv_cols_ref[pl.ds(width + at, HD)], ones], axis=0)
        sums = dot(values, weights_ref[slot])
        heads_ref[pl.ds(at, HD)] = (sums[:HD] / sums[HD : HD + 1]).astype(BF16)

    score(0, 0)
    score(1, 1)
    weigh(0)

    def two_heads(pair, carry):
        head = 2 * pair + 1
        for slot in (1, 0):
            score(head + 1, 1 - slot)
            weigh(slot)
            gather(head - 1, 1 - slot)
            head += 1
        return carry

    lax.fori_loop(0, HEADS // 2 - 1, two_heads, 0)
    weigh(1)
    gather(HEADS - 2, 0)
    gather(HEADS - 1, 1)

    for copy in copies[2:]:
        copy.wait()
    update = lax.dot_general(
        heads_ref[...], proj_ref[...], (((0,), (0,)), ((), ())), preferred_element_type=F32
    )
    attended = (serial_ref[...] + update).astype(BF16).astype(F32)
    hidden_in = layer_norm(attended, mlp_gain_ref[...]).astype(BF16)
    total_ref[...] = attended
    chunk = width
    for start in range(0, up_ref.shape[1], chunk):
        raised = dot(hidden_in, up_ref[:, start : start + chunk])
        hidden = (raised * (1.0 + lax.erf(raised * math.sqrt(0.5))) * 0.5).astype(BF16)
        total_ref[...] += dot(hidden, down_ref[start : start + chunk])
    finished = total_ref[...].astype(BF16)
    slot_rows = lax.broadcasted_iota(jnp.int32, (slots, points), 0)
    out_ref[...] = dot(one_hot(slot_rows == slot_row_ref[...]), finished).astype(BF16)


def return_kernel(arrived_ref, slot_ref, out_ref):
    slot_ids = lax.broadcasted_iota(jnp.int32, (out_ref.shape[0], arrived_ref.shape[0]), 1)
    out_ref[...] = dot(one_hot(slot_ref[...] == slot_ids), arrived_ref[...]).astype(BF16)


def face_pairs(devices, dx, dy):
    return [
        (source, source + dx * GY + dy)
        for source in range(devices)
        if 0 <= source // GY + dx < devices // GY and 0 <= source % GY + dy < GY
    ]


def way_round(devices, rows, length):
    chips = devices // 2
    cycle = list(range(0, chips, 2)) + list(range(chips - 1, 0, -2))
    back, on = [], []
    places = [None] * devices
    for place, chip in enumerate(cycle):
        for core in range(2):
            me = 2 * chip + core
            back.append((me, 2 * cycle[(place + 1) % chips] + core))
            on.append((me, 2 * cycle[place - 1] + core))
            order = [0]
            for step in range(1, chips // 2):
                order += [-step, step]
            order.append(chips // 2)
            places[me] = []
            for offset in order:
                start = cycle[(place + offset) % chips] * rows
                column = min(start // 128 * 128, chips * rows - length)
                places[me].append((column, start - column))
    return back, on, places


def padded_taps(neighbours):
    points = neighbours.shape[0]
    own = jnp.arange(points, dtype=jnp.int32)[:, None]
    rest = jnp.zeros((points, 128 - TAPS), jnp.int32)
    middle = TAPS // 2
    rows = jnp.concatenate([neighbours[:, :middle], own, neighbours[:, middle:], rest], axis=1)
    return rows.astype(F32)


def body(
    features,
    conv_weight,
    cpe_weight,
    cpe_gain,
    attn_gain,
    qkv_weight,
    proj_weight,
    mlp_gain,
    up_weight,
    down_weight,
    face_rows,
    neighbours,
    serial_rank,
    serial_order,
):
    points, width = features.shape
    half = width // 2
    devices = lax.axis_size("blocks")
    index = lax.axis_index("blocks")
    core = lax.rem(index, 2)
    partner = [(source, source ^ 1) for source in range(devices)]
    capacity = 2 * points // devices
    slots = devices * capacity

    unit = conv_weight.shape[0] // TAPS
    units = conv_weight.reshape(TAPS, unit, width)
    kept, sent = units[0::2], units[1::2]
    got = lax.ppermute(sent, "blocks", partner)
    mine = jnp.where(
        core == 0, jnp.concatenate([kept, got]), jnp.concatenate([got, kept])
    ).reshape(TAPS * unit, width)
    round_trip = devices == 2 * GY
    lower = index < GY
    if round_trip:
        across = jnp.where(lower, face_rows[0, 5:], face_rows[0, :3])
        face_list = jnp.concatenate([across, face_rows[0, 3:5]]).reshape(-1, 1)
        counts = (3, 1, 1)
    else:
        face_list = face_rows.reshape(-1, 1)
        counts = (1,) * 8
    size = face_rows.shape[2]
    own_local, other_half, *faces = call(
        functools.partial(faces_kernel, unit),
        [jax.ShapeDtypeStruct((points, half), BF16)] * 2
        + [jax.ShapeDtypeStruct((count * size, width), BF16) for count in counts],
        60,
        4 * points * width * width,
        8 * points * width,
        in_specs=[pl.BlockSpec(memory_space=pltpu.SMEM)] + [pl.BlockSpec()] * 2,
    )(core.reshape(1), features, face_list)
    other_local = lax.ppermute(other_half, "blocks", partner)
    other_neighbours = lax.ppermute(neighbours, "blocks", partner)

    rows = mine.shape[0]
    length = -(-(rows + 127) // 128) * 128 if round_trip else rows * (devices // 2)
    back_pairs, on_pairs, places = way_round(devices, rows, length)
    back, on = [mine], [mine]

    def pass_on(*beside):
        if not round_trip:
            return beside
        tied = lax.optimization_barrier((back[-1], on[-1], *beside))
        first, second = tied[:2]
        back[-1], on[-1] = first, second
        if len(back) == devices // 4:
            first, second = first[: rows // 2], second[rows // 2 :]
        back.append(lax.ppermute(first, "blocks", back_pairs))
        on.append(lax.ppermute(second, "blocks", on_pairs))
        return tied[2:]

    if round_trip:
        lists, back_list, on_list = faces
        side = face_pairs(devices, 1, 0) + face_pairs(devices, -1, 0)
        lists, other_local, other_neighbours = pass_on(lists, other_local, other_neighbours)
        lists = lax.ppermute(lists, "blocks", side)
    own_rows, other_rows = padded_taps(neighbours), padded_taps(other_neighbours)
    if round_trip:
        to_on = jnp.concatenate([on_list, lists[2 * size :]])
        to_back = jnp.concatenate([back_list, lists[:size]])
        behind = lax.ppermute(to_on, "blocks", face_pairs(devices, 0, 1))
        ahead = lax.ppermute(to_back, "blocks", face_pairs(devices, 0, -1))
        lists, behind, ahead = pass_on(lists, behind, ahead)
        own_remote, other_half = call(
            received_kernel,
            [jax.ShapeDtypeStruct((6 * size, half), BF16)] * 2,
            32,
            0,
            20 * size * width,
            in_specs=[pl.BlockSpec(memory_space=pltpu.SMEM)] + [pl.BlockSpec()] * 3,
        )(jnp.stack([lower.astype(jnp.int32), core]), lists, behind, ahead)
        start = jnp.where(lower, points, points + 3 * size).reshape(1)
    else:
        received = jnp.concatenate(
            [
                lax.ppermute(faces[k], "blocks", face_pairs(devices, STEPS_X[k], STEPS_Y[k]))
                for k in range(8)
            ]
        )
        own_remote = lax.dynamic_slice(received, (0, core * half), (8 * size, half))
        other_half = lax.dynamic_slice(received, (0, (1 - core) * half), (8 * size, half))
        start = jnp.full((1,), points, jnp.int32)
    other_remote = lax.ppermute(other_half, "blocks", partner)
    own_stacked = gather_block(start, own_rows, own_local, own_remote)
    other_stacked = gather_block(start, other_rows, other_local, other_remote)
    stacked = pass_on(other_stacked, own_stacked)
    if round_trip:
        places = jnp.array(places, jnp.int32)[index]
        early = [[mine], [back[1]], [on[1]], [back[2]], [on[2]]]
        *sums, next_lhs, last_lhs = conv_part(stacked, places, early, None, length, (2, 1))
        sums = pass_on(*sums)
        late = [[back[3]], [on[3]]]
        sums = conv_part([next_lhs], places[5:7], late, sums, length)
        last = [[back[4], on[4]]]
        for_partner, own_part = conv_part(
            [last_lhs], places[7:], last, sums, length, dtype=BF16
        )
    else:
        groups = [list(range(first, devices, 2)) for first in range(2)]
        weight = lax.all_gather(mine, "blocks", axis=0, tiled=True, axis_index_groups=groups)
        nowhere = jnp.zeros((1, 2), jnp.int32)
        for_partner, own_part = conv_part(stacked, nowhere, [[weight]], None, length)

    positions = jnp.arange(points, dtype=jnp.int32)
    target = serial_rank // points
    earlier = (target[None, :] == target[:, None]) & (serial_rank[None, :] < serial_rank[:, None])
    out_slot = target * capacity + jnp.sum(earlier.astype(jnp.int32), axis=1)
    anchor = serial_order // points
    before = (anchor[None, :] == anchor[:, None]) & (positions[None, :] < positions[:, None])
    in_slot = anchor * capacity + jnp.sum(before.astype(jnp.int32), axis=1)

    from_partner = lax.ppermute(for_partner, "blocks", partner)

    outgoing = call(
        mix_kernel,
        jax.ShapeDtypeStruct((slots, width), BF16),
        32,
        2 * points * width * (width + slots),
        8 * points * width,
    )(
        own_part,
        from_partner,
        features,
        cpe_weight,
        cpe_gain.reshape(1, width),
        out_slot.reshape(1, points),
    )
    arrived = lax.all_to_all(
        outgoing.reshape(devices, capacity, width), "blocks", split_axis=0, concat_axis=0, tiled=True
    ).reshape(slots, width)

    key_weight = qkv_weight[:, width : 2 * width]
    qv_weight = jnp.concatenate([qkv_weight[:, :width], qkv_weight[:, 2 * width :]], axis=1).T
    weights = (qv_weight, key_weight, proj_weight, up_weight, down_weight)
    back = call(
        block_kernel,
        jax.ShapeDtypeStruct((slots, width), BF16),
        60,
        20 * points * width * width,
        16 * width * width,
        in_specs=[pl.BlockSpec()] * 5 + [pl.BlockSpec(memory_space=pl.ANY)] * len(weights),
        scratch_shapes=[pltpu.VMEM(weight.shape, BF16) for weight in weights]
        + [
            pltpu.SemaphoreType.DMA((len(weights),)),
            pltpu.VMEM((points, width), F32),
            pltpu.VMEM((2 * width, points), BF16),
            pltpu.VMEM((points, width), BF16),
            pltpu.VMEM((width, points), BF16),
            pltpu.VMEM((points, width), F32),
            pltpu.VMEM((2, points, points), F32),
            pltpu.VMEM((2, points, points), BF16),
        ],
    )(
        arrived,
        in_slot.reshape(points, 1),
        in_slot.reshape(1, points),
        attn_gain.reshape(1, width),
        mlp_gain.reshape(1, width),
        *weights,
    )
    returned = lax.all_to_all(
        back.reshape(devices, capacity, width), "blocks", split_axis=0, concat_axis=0, tiled=True
    ).reshape(slots, width)
    return call(
        return_kernel,
        jax.ShapeDtypeStruct((points, width), BF16),
        32,
        2 * points * slots * width,
        6 * points * width,
    )(returned, out_slot.reshape(points, 1))


def solution(mesh):
    placed = (
        P(("groups", "blocks"), None),
        P("blocks", None),
        P(),
        P(),
        P(),
        P(),
        P(),
        P(),
        P(),
        P(),
        P(("groups", "blocks"), None, None),
        P(("groups", "blocks"), None),
        P(("groups", "blocks")),
        P(("groups", "blocks")),
    )
    return jax.shard_map(
        body, mesh=mesh, in_specs=placed, out_specs=P(("groups", "blocks"), None), check_vma=False
    )
```

```python
import functools
import math

import jax
import jax.numpy as jnp
from jax import lax
from jax.experimental import pallas as pl
from jax.experimental.pallas import tpu as pltpu
from jax.sharding import PartitionSpec as P

HEADS = 32
GY = 8
HD = 16
TAPS = 27
EPSILON = 1e-05
STEPS_X = (-1, -1, -1, 0, 0, 1, 1, 1)
STEPS_Y = (-1, 0, 1, -1, 1, -1, 0, 1)
F32 = jnp.float32
BF16 = jnp.bfloat16
MIB = 1 << 20


def dot(left, right):
    return jnp.dot(left, right, preferred_element_type=F32)


def layer_norm(inputs, gain_vector):
    row_mean = jnp.mean(inputs, axis=-1, keepdims=True)
    centred = inputs - row_mean
    variance = jnp.mean(centred * centred, axis=-1, keepdims=True)
    return centred * lax.rsqrt(variance + EPSILON) * gain_vector


def one_hot(mask):
    return jnp.where(mask, 1.0, 0.0).astype(BF16)


def call(kernel, out_shape, limit, flops, moved, **extra):
    return pl.pallas_call(
        kernel,
        out_shape=out_shape,
        compiler_params=pltpu.CompilerParams(vmem_limit_bytes=limit * MIB),
        cost_estimate=pl.CostEstimate(flops=flops, bytes_accessed=moved, transcendentals=0),
        **extra,
    )


def faces_kernel(unit, core_ref, features_ref, rows_ref, own_ref, other_ref, *face_refs):
    points, width = features_ref.shape
    half = width // 2
    place = lax.broadcasted_iota(jnp.int32, (width, width), 1)
    within = lax.rem(place, half)
    source = (within // unit) * (2 * unit) + (place // half) * unit + lax.rem(place, unit)
    channel = lax.broadcasted_iota(jnp.int32, (width, width), 0)
    ordered = dot(features_ref[...], one_hot(channel == source)).astype(BF16)
    first, second = ordered[:, :half], ordered[:, half:]
    even = core_ref[0] == 0
    own_ref[...] = jnp.where(even, first, second)
    other_ref[...] = jnp.where(even, second, first)
    row_ids = lax.broadcasted_iota(jnp.int32, (rows_ref.shape[0], points), 1)
    rows = dot(one_hot(rows_ref[...] == row_ids), ordered).astype(BF16)
    taken = 0
    for ref in face_refs:
        ref[...] = rows[taken : taken + ref.shape[0]]
        taken += ref.shape[0]


def received_kernel(flags_ref, side_ref, behind_ref, ahead_ref, own_ref, other_ref):
    size = behind_ref.shape[0] // 2
    half = own_ref.shape[1]
    lower, even = flags_ref[0] == 1, flags_ref[1] == 0
    across = [ahead_ref[size:], side_ref[size : 2 * size], behind_ref[size:]]
    along = [ahead_ref[:size], behind_ref[:size]]
    for at, (low, high) in enumerate(zip(across + along, along + across)):
        rows = jnp.where(lower, low, high)
        first, second = rows[:, :half], rows[:, half:]
        own_ref[at * size : (at + 1) * size] = jnp.where(even, first, second)
        other_ref[at * size : (at + 1) * size] = jnp.where(even, second, first)
    rest = jnp.zeros((size, half), BF16)
    own_ref[5 * size :] = rest
    other_ref[5 * size :] = rest


def gather_kernel(taps, start_ref, rows_ref, own_ref, got_ref, out_ref):
    half = own_ref.shape[1]
    lane = lax.broadcasted_iota(jnp.int32, rows_ref.shape, 1)
    parts = []
    for table, start in ((own_ref, 0), (got_ref, start_ref[0])):
        ids = lax.broadcasted_iota(jnp.int32, (1, table.shape[0]), 1) + start
        parts.append((table, ids.astype(F32)))
    for at in range(taps):
        chosen = lane == taps * pl.program_id(0) + at
        column = jnp.sum(jnp.where(chosen, rows_ref[...], 0.0), axis=1, keepdims=True)
        hits = [one_hot(column == ids) for _, ids in parts]
        products = [dot(hit, table[...]) for hit, (table, _) in zip(hits, parts)]
        out_ref[:, at * half : (at + 1) * half] = (products[0] + products[1]).astype(BF16)


def gather_block(start, rows, own, got):
    points, lanes = rows.shape
    half = own.shape[1]
    height = own.shape[0] + got.shape[0]
    taps = 9
    whole = lambda step: (0, 0)
    return call(
        functools.partial(gather_kernel, taps),
        jax.ShapeDtypeStruct((points, TAPS * half), BF16),
        60,
        2 * TAPS * points * height * half,
        2 * TAPS * points * half,
        grid=(TAPS // taps,),
        in_specs=[
            pl.BlockSpec(memory_space=pltpu.SMEM),
            pl.BlockSpec((points, lanes), whole),
            pl.BlockSpec(own.shape, whole),
            pl.BlockSpec(got.shape, whole),
        ],
        out_specs=pl.BlockSpec((points, taps * half), lambda step: (0, step)),
    )(start, rows, own, got)


def conv_kernel(slots, later, ready, first, places_ref, shifts_ref, *refs):
    refs = list(refs)

    def take(count):
        taken = refs[:count]
        del refs[:count]
        return taken

    sources = take(1 if ready else 2)
    pieces = take(sum(len(parts) for parts in slots))
    before = [] if first else take(2)
    outs = take(2)
    kept = take(len(later))
    (lhs,) = sources if ready else take(1)
    held, sems = take(2)
    length = held.shape[1]

    def stretch(slot, target, sem):
        column = pl.multiple_of(places_ref[2 * slot], 128)
        copies = [
            pltpu.make_async_copy(
                stacked.at[:, pl.ds(column, length)], target.at[block], sem.at[block]
            )
            for block, stacked in enumerate(sources)
        ]
        for copy in copies:
            copy.start()
        return copies

    copies = []
    for at, parts in enumerate(slots):
        row = pl.multiple_of(places_ref[2 * at + 1], 16)
        copies.append([] if ready else stretch(at, lhs.at[at], sems.at[at]))
        edge = length - sum(size for _, size, _ in parts)
        if edge:
            held[at, :edge] = jnp.zeros((edge, held.shape[2]), BF16)
            held[at, length - edge :] = jnp.zeros((edge, held.shape[2]), BF16)
        for part, (start, size, kind) in enumerate(parts):
            place = row if kind is None else pl.multiple_of(row + shifts_ref[kind], 16)
            (piece,) = pieces[:1]
            del pieces[:1]
            copy = pltpu.make_async_copy(
                piece.at[pl.ds(start, size)], held.at[at, pl.ds(place, size)], sems.at[at, 2 + part]
            )
            copy.start()
            copies[-1].append(copy)
    extra, slot = [], len(slots)
    for group, count in enumerate(later):
        for place in range(count):
            extra += stretch(slot, kept[group].at[place], sems.at[slot])
            slot += 1
    for at in range(len(slots)):
        for copy in copies[at]:
            copy.wait()
        for block, ref in enumerate(outs):
            product = dot(lhs[at, block], held[at])
            if at > 0:
                ref[...] += product
            elif first:
                ref[...] = product
            else:
                ref[...] = (before[block][...] + product).astype(ref.dtype)
    for copy in extra:
        copy.wait()


def conv_part(sources, places, shifts, pieces, before, length, later=(), dtype=F32):
    ready = len(sources) == 1
    points = sources[0].shape[2] if ready else sources[0].shape[0]
    width = pieces[0][0][0].shape[1]
    slots = [[part[1:] for part in parts] for parts in pieces]
    flat = [part[0] for parts in pieces for part in parts]
    held = 2 + len(sources) + len(flat)
    kept = [] if before is None else [block for block in range(2) if block or dtype == F32]
    spec = pl.BlockSpec(memory_space=pl.ANY)
    return call(
        functools.partial(conv_kernel, slots, later, ready, before is None),
        [
            jax.ShapeDtypeStruct((points, width), dtype),
            jax.ShapeDtypeStruct((points, width), F32),
        ]
        + [jax.ShapeDtypeStruct((count, 2, points, length), BF16) for count in later],
        24 if ready else 36,
        4 * points * length * width * len(slots),
        2 * length * (2 * points + width) * len(slots),
        in_specs=[pl.BlockSpec(memory_space=pltpu.SMEM)] * 2
        + [pl.BlockSpec() if ready else spec] * len(sources)
        + [spec] * len(flat)
        + ([] if before is None else [pl.BlockSpec()] * 2),
        input_output_aliases={held + block: block for block in kept},
        scratch_shapes=([] if ready else [pltpu.VMEM((len(slots), 2, points, length), BF16)])
        + [
            pltpu.VMEM((len(slots), length, width), BF16),
            pltpu.SemaphoreType.DMA((len(slots) + sum(later), 4)),
        ],
    )(places.reshape(-1), shifts, *sources, *flat, *(before or ()))


def mix_kernel(own_ref, got_ref, features_ref, weight_ref, gain_ref, slot_ref, out_ref):
    convolved = (own_ref[...] + got_ref[...].astype(F32)).astype(BF16)
    linear = dot(convolved, weight_ref[...])
    mixed = (features_ref[...].astype(F32) + layer_norm(linear, gain_ref[...])).astype(BF16)
    slots = lax.broadcasted_iota(jnp.int32, (out_ref.shape[0], mixed.shape[0]), 0)
    out_ref[...] = dot(one_hot(slots == slot_ref[...]), mixed).astype(BF16)


def block_kernel(
    arrived_ref,
    slot_col_ref,
    slot_row_ref,
    attn_gain_ref,
    mlp_gain_ref,
    qv_hbm,
    key_hbm,
    proj_hbm,
    up_hbm,
    down_hbm,
    out_ref,
    qv_ref,
    key_ref,
    proj_ref,
    up_ref,
    down_ref,
    sems,
    serial_ref,
    qv_cols_ref,
    keys_ref,
    heads_ref,
    total_ref,
    scores_ref,
    weights_ref,
):
    sources = (key_hbm, qv_hbm, proj_hbm, up_hbm, down_hbm)
    targets = (key_ref, qv_ref, proj_ref, up_ref, down_ref)
    copies = [
        pltpu.make_async_copy(source, target, sems.at[at])
        for at, (source, target) in enumerate(zip(sources, targets))
    ]
    for copy in copies:
        copy.start()
    slots = arrived_ref.shape[0]
    points, width = serial_ref.shape
    slot_ids = lax.broadcasted_iota(jnp.int32, (points, slots), 1)
    serial = dot(one_hot(slot_col_ref[...] == slot_ids), arrived_ref[...])
    serial_ref[...] = serial
    normed = layer_norm(serial, attn_gain_ref[...]).astype(BF16)
    copies[0].wait()
    keys_ref[...] = dot(normed, key_ref[...]).astype(BF16)
    copies[1].wait()
    factor = math.log2(math.e) / math.sqrt(HD)
    contract_last = (((1,), (1,)), ((), ()))
    qv_cols_ref[:width] = (
        lax.dot_general(qv_ref[:width], normed, contract_last, preferred_element_type=F32) * factor
    ).astype(BF16)
    qv_cols_ref[width:] = lax.dot_general(
        qv_ref[width:], normed, contract_last, preferred_element_type=F32
    ).astype(BF16)
    ones = jnp.ones((HD, points), BF16)
    per_group = 128 // HD
    head_of_row = lax.broadcasted_iota(jnp.int32, (128, points), 0) // HD

    def score(head, slot):
        base = pl.multiple_of(head // per_group * 128, 128)
        group_queries = qv_cols_ref[pl.ds(base, 128)].astype(F32)
        chosen = head_of_row == lax.rem(head, per_group)
        queries = jnp.where(chosen, group_queries, 0.0).astype(BF16)
        scores_ref[slot] = dot(keys_ref[:, pl.ds(base, 128)], queries)

    def weigh(slot):
        scores = scores_ref[slot]
        weights_ref[slot] = jnp.exp2(scores - jnp.max(scores, axis=0, keepdims=True)).astype(BF16)

    def gather(head, slot):
        at = pl.multiple_of(head * HD, HD)
        values = jnp.concatenate([qv_cols_ref[pl.ds(width + at, HD)], ones], axis=0)
        sums = dot(values, weights_ref[slot])
        heads_ref[pl.ds(at, HD)] = (sums[:HD] / sums[HD : HD + 1]).astype(BF16)

    score(0, 0)
    score(1, 1)
    weigh(0)

    def two_heads(pair, carry):
        head = 2 * pair + 1
        for slot in (1, 0):
            score(head + 1, 1 - slot)
            weigh(slot)
            gather(head - 1, 1 - slot)
            head += 1
        return carry

    lax.fori_loop(0, HEADS // 2 - 1, two_heads, 0)
    weigh(1)
    gather(HEADS - 2, 0)
    gather(HEADS - 1, 1)

    for copy in copies[2:]:
        copy.wait()
    update = lax.dot_general(
        heads_ref[...], proj_ref[...], (((0,), (0,)), ((), ())), preferred_element_type=F32
    )
    attended = (serial_ref[...] + update).astype(BF16).astype(F32)
    hidden_in = layer_norm(attended, mlp_gain_ref[...]).astype(BF16)
    total_ref[...] = attended
    chunk = width
    for start in range(0, up_ref.shape[1], chunk):
        raised = dot(hidden_in, up_ref[:, start : start + chunk])
        hidden = (raised * (1.0 + lax.erf(raised * math.sqrt(0.5))) * 0.5).astype(BF16)
        total_ref[...] += dot(hidden, down_ref[start : start + chunk])
    finished = total_ref[...].astype(BF16)
    slot_rows = lax.broadcasted_iota(jnp.int32, (slots, points), 0)
    out_ref[...] = dot(one_hot(slot_rows == slot_row_ref[...]), finished).astype(BF16)


def return_kernel(arrived_ref, slot_ref, out_ref):
    slot_ids = lax.broadcasted_iota(jnp.int32, (out_ref.shape[0], arrived_ref.shape[0]), 1)
    out_ref[...] = dot(one_hot(slot_ref[...] == slot_ids), arrived_ref[...]).astype(BF16)


def face_pairs(devices, dx, dy):
    return [
        (source, source + dx * GY + dy)
        for source in range(devices)
        if 0 <= source // GY + dx < devices // GY and 0 <= source % GY + dy < GY
    ]


def way_round(devices, rows, length):
    chips = devices // 2
    cycle = list(range(0, chips, 2)) + list(range(chips - 1, 0, -2))
    chains = [], []
    places = [None] * devices
    for place, chip in enumerate(cycle):
        for core, way in ((0, 1), (1, -1)):
            me = 2 * chip + core
            for chain, step in zip(chains, (way, -way)):
                chain.append((me, 2 * cycle[(place + step) % chips] + core))
            order = [0]
            for step in range(1, chips // 2):
                order += [-step * way, step * way]
            order.append(chips // 2)
            places[me] = []
            for offset in order:
                start = cycle[(place + offset) % chips] * rows
                column = min(start // 128 * 128, chips * rows - length)
                places[me].append((column, start - column))
    return *chains, places


def padded_taps(neighbours):
    points = neighbours.shape[0]
    own = jnp.arange(points, dtype=jnp.int32)[:, None]
    rest = jnp.zeros((points, 128 - TAPS), jnp.int32)
    middle = TAPS // 2
    rows = jnp.concatenate([neighbours[:, :middle], own, neighbours[:, middle:], rest], axis=1)
    return rows.astype(F32)


def body(
    features,
    conv_weight,
    cpe_weight,
    cpe_gain,
    attn_gain,
    qkv_weight,
    proj_weight,
    mlp_gain,
    up_weight,
    down_weight,
    face_rows,
    neighbours,
    serial_rank,
    serial_order,
):
    points, width = features.shape
    half = width // 2
    devices = lax.axis_size("blocks")
    index = lax.axis_index("blocks")
    core = lax.rem(index, 2)
    partner = [(source, source ^ 1) for source in range(devices)]
    capacity = 2 * points // devices
    slots = devices * capacity

    unit = conv_weight.shape[0] // TAPS
    units = conv_weight.reshape(TAPS, unit, width)
    kept, sent = units[0::2], units[1::2]
    got = lax.ppermute(sent, "blocks", partner)
    mine = jnp.where(
        core == 0, jnp.concatenate([kept, got]), jnp.concatenate([got, kept])
    ).reshape(TAPS * unit, width)
    round_trip = devices == 2 * GY
    lower = index < GY
    if round_trip:
        across = jnp.where(lower, face_rows[0, 5:], face_rows[0, :3])
        face_list = jnp.concatenate([across, face_rows[0, 3:5]]).reshape(-1, 1)
        counts = (3, 1, 1)
    else:
        face_list = face_rows.reshape(-1, 1)
        counts = (1,) * 8
    size = face_rows.shape[2]
    own_local, other_half, *faces = call(
        functools.partial(faces_kernel, unit),
        [jax.ShapeDtypeStruct((points, half), BF16)] * 2
        + [jax.ShapeDtypeStruct((count * size, width), BF16) for count in counts],
        32,
        4 * points * width * width,
        8 * points * width,
        in_specs=[pl.BlockSpec(memory_space=pltpu.SMEM)] + [pl.BlockSpec()] * 2,
    )(core.reshape(1), features, face_list)
    other_local = lax.ppermute(other_half, "blocks", partner)
    other_neighbours = lax.ppermute(neighbours, "blocks", partner)

    rows = mine.shape[0]
    length = -(-(rows + 127) // 128) * 128 if round_trip else rows * (devices // 2)
    first_pairs, second_pairs, places = way_round(devices, rows, length)
    side = lax.axis_index("groups")
    missing = -(-rows // 64) * 16
    passed = rows - missing
    shifts = jnp.stack([side * missing, (1 - side) * passed]).astype(jnp.int32)
    begun = lax.dynamic_slice(mine, (side * missing, 0), (passed, width))
    first, second = [begun], [begun]

    def pass_on(*beside):
        if not round_trip:
            return beside
        tied = lax.optimization_barrier((first[-1], second[-1], *beside))
        first[-1], second[-1] = tied[:2]
        last = len(first) == devices // 4
        first.append(lax.ppermute(first[-1], "blocks", first_pairs))
        if not last:
            second.append(lax.ppermute(second[-1], "blocks", second_pairs))
        return tied[2:]

    def complete(*arrived):
        lent = [
            lax.dynamic_slice(piece, (side * (passed - missing), 0), (missing, width))
            for piece in arrived
        ]
        got = lax.ppermute(jnp.concatenate(lent), "groups", [(0, 1), (1, 0)])
        return [
            [(piece, 0, passed, 0), (got, at * missing, missing, 1)]
            for at, piece in enumerate(arrived)
        ]

    if round_trip:
        lists, back_list, on_list = faces
        across = face_pairs(devices, 1, 0) + face_pairs(devices, -1, 0)
        lists, other_local, other_neighbours = pass_on(lists, other_local, other_neighbours)
        lists = lax.ppermute(lists, "blocks", across)
    own_rows, other_rows = padded_taps(neighbours), padded_taps(other_neighbours)
    if round_trip:
        to_on = jnp.concatenate([on_list, lists[2 * size :]])
        to_back = jnp.concatenate([back_list, lists[:size]])
        behind = lax.ppermute(to_on, "blocks", face_pairs(devices, 0, 1))
        ahead = lax.ppermute(to_back, "blocks", face_pairs(devices, 0, -1))
        lists, behind, ahead = pass_on(lists, behind, ahead)
        near = complete(first[1], second[1])
        own_remote, other_half = call(
            received_kernel,
            [jax.ShapeDtypeStruct((6 * size, half), BF16)] * 2,
            32,
            0,
            20 * size * width,
            in_specs=[pl.BlockSpec(memory_space=pltpu.SMEM)] + [pl.BlockSpec()] * 3,
        )(jnp.stack([lower.astype(jnp.int32), core]), lists, behind, ahead)
        start = jnp.where(lower, points, points + 3 * size).reshape(1)
    else:
        received = jnp.concatenate(
            [
                lax.ppermute(faces[k], "blocks", face_pairs(devices, STEPS_X[k], STEPS_Y[k]))
                for k in range(8)
            ]
        )
        own_remote = lax.dynamic_slice(received, (0, core * half), (8 * size, half))
        other_half = lax.dynamic_slice(received, (0, (1 - core) * half), (8 * size, half))
        start = jnp.full((1,), points, jnp.int32)
    other_remote = lax.ppermute(other_half, "blocks", partner)
    own_stacked = gather_block(start, own_rows, own_local, own_remote)
    own_stacked, other_rows, other_remote = pass_on(own_stacked, other_rows, other_remote)
    if round_trip:
        middle = complete(first[2], second[2])
    other_stacked = gather_block(start, other_rows, other_local, other_remote)
    if round_trip:
        other_stacked, own_stacked, middle_got = pass_on(other_stacked, own_stacked, middle[0][1][0])
        middle = [[parts[0], (middle_got, *parts[1][1:])] for parts in middle]
    stacked = other_stacked, own_stacked
    if round_trip:
        far = complete(first[3], second[3])
        opposite = complete(first[4])
        places = jnp.array(places, jnp.int32)[index]
        early = [[(mine, 0, rows, None)]] + near
        *sums, middle_lhs, far_lhs, last_lhs = conv_part(
            stacked, places, shifts, early, None, length, (2, 2, 1)
        )
        sums = conv_part([middle_lhs], places[3:5], shifts, middle, sums, length)
        sums = conv_part([far_lhs], places[5:7], shifts, far, sums, length)
        for_partner, own_part = conv_part(
            [last_lhs], places[7:], shifts, opposite, sums, length, dtype=BF16
        )
    else:
        groups = [list(range(core, devices, 2)) for core in range(2)]
        weight = lax.all_gather(mine, "blocks", axis=0, tiled=True, axis_index_groups=groups)
        nowhere = jnp.zeros((1, 2), jnp.int32)
        whole = [[(weight, 0, weight.shape[0], None)]]
        for_partner, own_part = conv_part(stacked, nowhere, shifts, whole, None, length)

    positions = jnp.arange(points, dtype=jnp.int32)
    target = serial_rank // points
    earlier = (target[None, :] == target[:, None]) & (serial_rank[None, :] < serial_rank[:, None])
    out_slot = target * capacity + jnp.sum(earlier.astype(jnp.int32), axis=1)
    anchor = serial_order // points
    before = (anchor[None, :] == anchor[:, None]) & (positions[None, :] < positions[:, None])
    in_slot = anchor * capacity + jnp.sum(before.astype(jnp.int32), axis=1)

    from_partner = lax.ppermute(for_partner, "blocks", partner)

    outgoing = call(
        mix_kernel,
        jax.ShapeDtypeStruct((slots, width), BF16),
        32,
        2 * points * width * (width + slots),
        8 * points * width,
    )(
        own_part,
        from_partner,
        features,
        cpe_weight,
        cpe_gain.reshape(1, width),
        out_slot.reshape(1, points),
    )
    arrived = lax.all_to_all(
        outgoing.reshape(devices, capacity, width), "blocks", split_axis=0, concat_axis=0, tiled=True
    ).reshape(slots, width)

    key_weight = qkv_weight[:, width : 2 * width]
    qv_weight = jnp.concatenate([qkv_weight[:, :width], qkv_weight[:, 2 * width :]], axis=1).T
    weights = (qv_weight, key_weight, proj_weight, up_weight, down_weight)
    back = call(
        block_kernel,
        jax.ShapeDtypeStruct((slots, width), BF16),
        60,
        20 * points * width * width,
        16 * width * width,
        in_specs=[pl.BlockSpec()] * 5 + [pl.BlockSpec(memory_space=pl.ANY)] * len(weights),
        scratch_shapes=[pltpu.VMEM(weight.shape, BF16) for weight in weights]
        + [
            pltpu.SemaphoreType.DMA((len(weights),)),
            pltpu.VMEM((points, width), F32),
            pltpu.VMEM((2 * width, points), BF16),
            pltpu.VMEM((points, width), BF16),
            pltpu.VMEM((width, points), BF16),
            pltpu.VMEM((points, width), F32),
            pltpu.VMEM((2, points, points), F32),
            pltpu.VMEM((2, points, points), BF16),
        ],
    )(
        arrived,
        in_slot.reshape(points, 1),
        in_slot.reshape(1, points),
        attn_gain.reshape(1, width),
        mlp_gain.reshape(1, width),
        *weights,
    )
    returned = lax.all_to_all(
        back.reshape(devices, capacity, width), "blocks", split_axis=0, concat_axis=0, tiled=True
    ).reshape(slots, width)
    return call(
        return_kernel,
        jax.ShapeDtypeStruct((points, width), BF16),
        32,
        2 * points * slots * width,
        6 * points * width,
    )(returned, out_slot.reshape(points, 1))


def solution(mesh):
    placed = (
        P(("groups", "blocks"), None),
        P("blocks", None),
        P(),
        P(),
        P(),
        P(),
        P(),
        P(),
        P(),
        P(),
        P(("groups", "blocks"), None, None),
        P(("groups", "blocks"), None),
        P(("groups", "blocks")),
        P(("groups", "blocks")),
    )
    return jax.shard_map(
        body, mesh=mesh, in_specs=placed, out_specs=P(("groups", "blocks"), None), check_vma=False
    )
```

```python
import functools
import math

import jax
import jax.numpy as jnp
from jax import lax
from jax.experimental import pallas as pl
from jax.experimental.pallas import tpu as pltpu
from jax.sharding import PartitionSpec as P

HEADS = 32
GY = 8
HD = 16
TAPS = 27
EPSILON = 1e-05
STEPS_X = (-1, -1, -1, 0, 0, 1, 1, 1)
STEPS_Y = (-1, 0, 1, -1, 1, -1, 0, 1)
F32 = jnp.float32
BF16 = jnp.bfloat16
MIB = 1 << 20


def dot(left, right):
    return jnp.dot(left, right, preferred_element_type=F32)


def layer_norm(inputs, gain_vector):
    row_mean = jnp.mean(inputs, axis=-1, keepdims=True)
    centred = inputs - row_mean
    variance = jnp.mean(centred * centred, axis=-1, keepdims=True)
    return centred * lax.rsqrt(variance + EPSILON) * gain_vector


def one_hot(mask):
    return jnp.where(mask, 1.0, 0.0).astype(BF16)


def call(kernel, out_shape, limit, flops, moved, **extra):
    return pl.pallas_call(
        kernel,
        out_shape=out_shape,
        compiler_params=pltpu.CompilerParams(vmem_limit_bytes=limit * MIB),
        cost_estimate=pl.CostEstimate(flops=flops, bytes_accessed=moved, transcendentals=0),
        **extra,
    )


def rows_kernel(flags_ref, units_ref, got_ref, mine_ref, begun_ref):
    count, unit, _ = units_ref.shape
    missing = mine_ref.shape[0] - begun_ref.shape[0]
    kept = [units_ref.at[at] for at in range(0, count, 2)]
    got = [got_ref.at[at] for at in range(count // 2)]
    for core, order in enumerate((kept + got, got + kept)):

        @pl.when(flags_ref[0] == core)
        def _():
            for at, source in enumerate(order):
                mine_ref[at * unit : (at + 1) * unit] = source[...]

    start = pl.multiple_of(flags_ref[1] * missing, 16)
    begun_ref[...] = mine_ref[pl.ds(start, begun_ref.shape[0])]


def faces_kernel(unit, core_ref, features_ref, rows_ref, own_ref, other_ref, *face_refs):
    points, width = features_ref.shape
    half = width // 2
    place = lax.broadcasted_iota(jnp.int32, (width, width), 1)
    within = lax.rem(place, half)
    source = (within // unit) * (2 * unit) + (place // half) * unit + lax.rem(place, unit)
    channel = lax.broadcasted_iota(jnp.int32, (width, width), 0)
    ordered = dot(features_ref[...], one_hot(channel == source)).astype(BF16)
    first, second = ordered[:, :half], ordered[:, half:]
    even = core_ref[0] == 0
    own_ref[...] = jnp.where(even, first, second)
    other_ref[...] = jnp.where(even, second, first)
    row_ids = lax.broadcasted_iota(jnp.int32, (rows_ref.shape[0], points), 1)
    rows = dot(one_hot(rows_ref[...] == row_ids), ordered).astype(BF16)
    taken = 0
    for ref in face_refs:
        ref[...] = rows[taken : taken + ref.shape[0]]
        taken += ref.shape[0]


def table_kernel(
    flags_ref, own_rows, other_rows, side_ref, behind_ref, ahead_ref, own_ref, other_ref
):
    size = behind_ref.shape[0] // 2
    points, half = own_rows.shape
    lower, even = flags_ref[0] == 1, flags_ref[1] == 0
    own_ref[:points] = own_rows[...]
    other_ref[:points] = other_rows[...]
    across = [ahead_ref[size:], side_ref[size : 2 * size], behind_ref[size:]]
    along = [ahead_ref[:size], behind_ref[:size]]
    for at, (low, high) in enumerate(zip(across + along, along + across)):
        rows = jnp.where(lower, low, high)
        first, second = rows[:, :half], rows[:, half:]
        start = points + at * size
        own_ref[start : start + size] = jnp.where(even, first, second)
        other_ref[start : start + size] = jnp.where(even, second, first)
    rest = jnp.zeros((size, half), BF16)
    own_ref[points + 5 * size :] = rest
    other_ref[points + 5 * size :] = rest


def gather_kernel(taps, start_ref, rows_ref, table_ref, out_ref):
    points, lanes = rows_ref.shape
    height, half = table_ref.shape
    lane = lax.broadcasted_iota(jnp.int32, (points, lanes), 1)
    segments = []
    for first in range(0, height, 256):
        start = first if first < points else first - points + start_ref[0]
        segments.append(
            (first, min(height, first + 256), jnp.asarray(start, jnp.int32).astype(F32))
        )
    places = lax.broadcasted_iota(jnp.int32, (1, 256), 1).astype(F32).astype(BF16)
    one, zero = jnp.ones((), BF16), jnp.zeros((), BF16)
    for at in range(taps):
        chosen = lane == taps * pl.program_id(0) + at
        column = jnp.sum(jnp.where(chosen, rows_ref[...], 0.0), axis=1, keepdims=True)
        taken = None
        for first, end, start in segments:
            place = jnp.clip(column - start, -1.0, 256.0).astype(BF16)
            hits = jnp.where(place == places[:, : end - first], one, zero)
            product = dot(hits, table_ref[first:end])
            taken = product if taken is None else taken + product
        out_ref[:, at * half : (at + 1) * half] = taken.astype(BF16)


def gather_block(start, rows, table):
    points, lanes = rows.shape
    height, half = table.shape
    taps = 9
    whole = lambda step: (0, 0)
    return call(
        functools.partial(gather_kernel, taps),
        jax.ShapeDtypeStruct((points, TAPS * half), BF16),
        60,
        2 * TAPS * points * height * half,
        2 * TAPS * points * half,
        grid=(TAPS // taps,),
        in_specs=[
            pl.BlockSpec(memory_space=pltpu.SMEM),
            pl.BlockSpec((points, lanes), whole),
            pl.BlockSpec((height, half), whole),
        ],
        out_specs=pl.BlockSpec((points, taps * half), lambda step: (0, step)),
    )(start, rows, table)


def conv_kernel(slots, later, ready, first, places_ref, shifts_ref, *refs):
    refs = list(refs)

    def take(count):
        taken = refs[:count]
        del refs[:count]
        return taken

    sources = take(1 if ready else 2)
    pieces = take(sum(len(parts) for parts in slots))
    before = [] if first else take(2)
    outs = take(2)
    kept = take(len(later))
    (lhs,) = sources if ready else take(1)
    held, sems = take(2)
    length = held.shape[1]

    def stretch(slot, target, sem):
        column = pl.multiple_of(places_ref[2 * slot], 128)
        copies = [
            pltpu.make_async_copy(
                stacked.at[:, pl.ds(column, length)], target.at[block], sem.at[block]
            )
            for block, stacked in enumerate(sources)
        ]
        for copy in copies:
            copy.start()
        return copies

    copies = []
    for at, parts in enumerate(slots):
        row = pl.multiple_of(places_ref[2 * at + 1], 16)
        copies.append([] if ready else stretch(at, lhs.at[at], sems.at[at]))
        edge = length - sum(size for _, size, _ in parts)
        if edge:
            held[at, :edge] = jnp.zeros((edge, held.shape[2]), BF16)
            held[at, length - edge :] = jnp.zeros((edge, held.shape[2]), BF16)
        for part, (start, size, kind) in enumerate(parts):
            place = row if kind is None else pl.multiple_of(row + shifts_ref[kind], 16)
            (piece,) = pieces[:1]
            del pieces[:1]
            copy = pltpu.make_async_copy(
                piece.at[pl.ds(start, size)], held.at[at, pl.ds(place, size)], sems.at[at, 2 + part]
            )
            copy.start()
            copies[-1].append(copy)
    extra, slot = [], len(slots)
    for group, count in enumerate(later):
        for place in range(count):
            extra += stretch(slot, kept[group].at[place], sems.at[slot])
            slot += 1
    for at in range(len(slots)):
        for copy in copies[at]:
            copy.wait()
        for block, ref in enumerate(outs):
            product = dot(lhs[at, block], held[at])
            if at > 0:
                ref[...] += product
            elif first:
                ref[...] = product
            else:
                ref[...] = (before[block][...] + product).astype(ref.dtype)
    for copy in extra:
        copy.wait()


def conv_part(sources, places, shifts, pieces, before, length, later=(), dtype=F32):
    ready = len(sources) == 1
    points = sources[0].shape[2] if ready else sources[0].shape[0]
    width = pieces[0][0][0].shape[1]
    slots = [[part[1:] for part in parts] for parts in pieces]
    flat = [part[0] for parts in pieces for part in parts]
    held = 2 + len(sources) + len(flat)
    kept = [] if before is None else [block for block in range(2) if block or dtype == F32]
    spec = pl.BlockSpec(memory_space=pl.ANY)
    return call(
        functools.partial(conv_kernel, slots, later, ready, before is None),
        [
            jax.ShapeDtypeStruct((points, width), dtype),
            jax.ShapeDtypeStruct((points, width), F32),
        ]
        + [jax.ShapeDtypeStruct((count, 2, points, length), BF16) for count in later],
        24 if ready else 36,
        4 * points * length * width * len(slots),
        2 * length * (2 * points + width) * len(slots),
        in_specs=[pl.BlockSpec(memory_space=pltpu.SMEM)] * 2
        + [pl.BlockSpec() if ready else spec] * len(sources)
        + [spec] * len(flat)
        + ([] if before is None else [pl.BlockSpec()] * 2),
        input_output_aliases={held + block: block for block in kept},
        scratch_shapes=([] if ready else [pltpu.VMEM((len(slots), 2, points, length), BF16)])
        + [
            pltpu.VMEM((len(slots), length, width), BF16),
            pltpu.SemaphoreType.DMA((len(slots) + sum(later), 4)),
        ],
    )(places.reshape(-1), shifts, *sources, *flat, *(before or ()))


def mix_kernel(own_ref, got_ref, features_ref, weight_ref, gain_ref, slot_ref, out_ref):
    convolved = (own_ref[...] + got_ref[...].astype(F32)).astype(BF16)
    linear = dot(convolved, weight_ref[...])
    mixed = (features_ref[...].astype(F32) + layer_norm(linear, gain_ref[...])).astype(BF16)
    slots = lax.broadcasted_iota(jnp.int32, (out_ref.shape[0], mixed.shape[0]), 0)
    out_ref[...] = dot(one_hot(slots == slot_ref[...]), mixed).astype(BF16)


def block_kernel(
    arrived_ref,
    slot_col_ref,
    slot_row_ref,
    attn_gain_ref,
    mlp_gain_ref,
    qv_hbm,
    key_hbm,
    proj_hbm,
    up_hbm,
    down_hbm,
    out_ref,
    qv_ref,
    key_ref,
    proj_ref,
    up_ref,
    down_ref,
    sems,
    serial_ref,
    qv_cols_ref,
    keys_ref,
    heads_ref,
    total_ref,
    scores_ref,
    weights_ref,
):
    sources = (key_hbm, qv_hbm, proj_hbm, up_hbm, down_hbm)
    targets = (key_ref, qv_ref, proj_ref, up_ref, down_ref)
    copies = [
        pltpu.make_async_copy(source, target, sems.at[at])
        for at, (source, target) in enumerate(zip(sources, targets))
    ]
    for copy in copies:
        copy.start()
    slots = arrived_ref.shape[0]
    points, width = serial_ref.shape
    slot_ids = lax.broadcasted_iota(jnp.int32, (points, slots), 1)
    serial = dot(one_hot(slot_col_ref[...] == slot_ids), arrived_ref[...])
    serial_ref[...] = serial
    normed = layer_norm(serial, attn_gain_ref[...]).astype(BF16)
    copies[0].wait()
    keys_ref[...] = dot(normed, key_ref[...]).astype(BF16)
    copies[1].wait()
    factor = math.log2(math.e) / math.sqrt(HD)
    contract_last = (((1,), (1,)), ((), ()))
    qv_cols_ref[:width] = (
        lax.dot_general(qv_ref[:width], normed, contract_last, preferred_element_type=F32) * factor
    ).astype(BF16)
    qv_cols_ref[width:] = lax.dot_general(
        qv_ref[width:], normed, contract_last, preferred_element_type=F32
    ).astype(BF16)
    ones = jnp.ones((HD, points), BF16)
    per_group = 128 // HD
    head_of_row = lax.broadcasted_iota(jnp.int32, (128, points), 0) // HD

    def score(head, slot):
        base = pl.multiple_of(head // per_group * 128, 128)
        group_queries = qv_cols_ref[pl.ds(base, 128)].astype(F32)
        chosen = head_of_row == lax.rem(head, per_group)
        queries = jnp.where(chosen, group_queries, 0.0).astype(BF16)
        scores_ref[slot] = dot(keys_ref[:, pl.ds(base, 128)], queries)

    def weigh(slot):
        scores = scores_ref[slot]
        weights_ref[slot] = jnp.exp2(scores - jnp.max(scores, axis=0, keepdims=True)).astype(BF16)

    def gather(head, slot):
        at = pl.multiple_of(head * HD, HD)
        values = jnp.concatenate([qv_cols_ref[pl.ds(width + at, HD)], ones], axis=0)
        sums = dot(values, weights_ref[slot])
        heads_ref[pl.ds(at, HD)] = (sums[:HD] / sums[HD : HD + 1]).astype(BF16)

    score(0, 0)
    score(1, 1)
    weigh(0)

    def two_heads(pair, carry):
        head = 2 * pair + 1
        for slot in (1, 0):
            score(head + 1, 1 - slot)
            weigh(slot)
            gather(head - 1, 1 - slot)
            head += 1
        return carry

    lax.fori_loop(0, HEADS // 2 - 1, two_heads, 0)
    weigh(1)
    gather(HEADS - 2, 0)
    gather(HEADS - 1, 1)

    for copy in copies[2:]:
        copy.wait()
    update = lax.dot_general(
        heads_ref[...], proj_ref[...], (((0,), (0,)), ((), ())), preferred_element_type=F32
    )
    attended = (serial_ref[...] + update).astype(BF16).astype(F32)
    hidden_in = layer_norm(attended, mlp_gain_ref[...]).astype(BF16)
    total_ref[...] = attended
    chunk = width
    for start in range(0, up_ref.shape[1], chunk):
        raised = dot(hidden_in, up_ref[:, start : start + chunk])
        hidden = (raised * (1.0 + lax.erf(raised * math.sqrt(0.5))) * 0.5).astype(BF16)
        total_ref[...] += dot(hidden, down_ref[start : start + chunk])
    finished = total_ref[...].astype(BF16)
    slot_rows = lax.broadcasted_iota(jnp.int32, (slots, points), 0)
    out_ref[...] = dot(one_hot(slot_rows == slot_row_ref[...]), finished).astype(BF16)


def return_kernel(arrived_ref, slot_ref, out_ref):
    slot_ids = lax.broadcasted_iota(jnp.int32, (out_ref.shape[0], arrived_ref.shape[0]), 1)
    out_ref[...] = dot(one_hot(slot_ref[...] == slot_ids), arrived_ref[...]).astype(BF16)


def face_pairs(devices, dx, dy):
    return [
        (source, source + dx * GY + dy)
        for source in range(devices)
        if 0 <= source // GY + dx < devices // GY and 0 <= source % GY + dy < GY
    ]


def way_round(devices, rows, length):
    chips = devices // 2
    cycle = list(range(0, chips, 2)) + list(range(chips - 1, 0, -2))
    chains = [], []
    places = [None] * devices
    for place, chip in enumerate(cycle):
        for core, way in ((0, 1), (1, -1)):
            me = 2 * chip + core
            for chain, step in zip(chains, (way, -way)):
                chain.append((me, 2 * cycle[(place + step) % chips] + core))
            order = [0]
            for step in range(1, chips // 2):
                order += [-step * way, step * way]
            order.append(chips // 2)
            places[me] = []
            for offset in order:
                start = cycle[(place + offset) % chips] * rows
                column = min(start // 128 * 128, chips * rows - length)
                places[me].append((column, start - column))
    return *chains, places


def padded_taps(neighbours):
    points = neighbours.shape[0]
    own = jnp.arange(points, dtype=jnp.int32)[:, None]
    rest = jnp.zeros((points, 128 - TAPS), jnp.int32)
    middle = TAPS // 2
    rows = jnp.concatenate([neighbours[:, :middle], own, neighbours[:, middle:], rest], axis=1)
    return rows.astype(F32)


def body(
    features,
    conv_weight,
    cpe_weight,
    cpe_gain,
    attn_gain,
    qkv_weight,
    proj_weight,
    mlp_gain,
    up_weight,
    down_weight,
    face_rows,
    neighbours,
    serial_rank,
    serial_order,
):
    points, width = features.shape
    half = width // 2
    devices = lax.axis_size("blocks")
    index = lax.axis_index("blocks")
    core = lax.rem(index, 2)
    partner = [(source, source ^ 1) for source in range(devices)]
    capacity = 2 * points // devices
    slots = devices * capacity

    unit = conv_weight.shape[0] // TAPS
    units = conv_weight.reshape(TAPS, unit, width)
    got = lax.ppermute(units[1::2], "blocks", partner)
    rows = TAPS * unit
    side = lax.axis_index("groups")
    missing = -(-rows // 64) * 16
    passed = rows - missing
    if devices == 2 * GY:
        mine, begun = call(
            rows_kernel,
            [
                jax.ShapeDtypeStruct((rows, width), BF16),
                jax.ShapeDtypeStruct((passed, width), BF16),
            ],
            24,
            0,
            8 * rows * width,
            in_specs=[pl.BlockSpec(memory_space=pltpu.SMEM)] + [pl.BlockSpec()] * 2,
        )(jnp.stack([core, side]).astype(jnp.int32), units, got)
    else:
        kept = units[0::2]
        mine = begun = jnp.where(
            core == 0, jnp.concatenate([kept, got]), jnp.concatenate([got, kept])
        ).reshape(rows, width)

    round_trip = devices == 2 * GY
    lower = index < GY
    if round_trip:
        across = jnp.where(lower, face_rows[0, 5:], face_rows[0, :3])
        face_list = jnp.concatenate([across, face_rows[0, 3:5]]).reshape(-1, 1)
        counts = (3, 1, 1)
    else:
        face_list = face_rows.reshape(-1, 1)
        counts = (1,) * 8
    size = face_rows.shape[2]
    own_local, other_local, *faces = call(
        functools.partial(faces_kernel, unit),
        [jax.ShapeDtypeStruct((points, half), BF16)] * 2
        + [jax.ShapeDtypeStruct((count * size, width), BF16) for count in counts],
        32,
        4 * points * width * width,
        8 * points * width,
        in_specs=[pl.BlockSpec(memory_space=pltpu.SMEM)] + [pl.BlockSpec()] * 2,
    )(core.reshape(1), features, face_list)
    length = -(-(rows + 127) // 128) * 128 if round_trip else rows * (devices // 2)
    first_pairs, second_pairs, places = way_round(devices, rows, length)
    shifts = jnp.stack([side * missing, (1 - side) * passed]).astype(jnp.int32)
    first, second = [begun], [begun]

    def pass_on(*beside):
        if not round_trip:
            return beside
        tied = lax.optimization_barrier((first[-1], second[-1], *beside))
        first[-1], second[-1] = tied[:2]
        last = len(first) == devices // 4
        first.append(lax.ppermute(first[-1], "blocks", first_pairs))
        if not last:
            second.append(lax.ppermute(second[-1], "blocks", second_pairs))
        return tied[2:]

    def lend(*arrived):
        return jnp.concatenate(
            [
                lax.dynamic_slice(piece, (side * (passed - missing), 0), (missing, width))
                for piece in arrived
            ]
        )

    def complete(lent, *arrived):
        got = lax.ppermute(lent, "groups", [(0, 1), (1, 0)])
        return [
            [(piece, 0, passed, 0), (got, at * missing, missing, 1)]
            for at, piece in enumerate(arrived)
        ]

    if round_trip:
        lists, back_list, on_list = faces
        across = face_pairs(devices, 1, 0) + face_pairs(devices, -1, 0)
        (lists,) = pass_on(lists)
        lists = lax.ppermute(lists, "blocks", across)
        to_on = jnp.concatenate([on_list, lists[2 * size :]])
        to_back = jnp.concatenate([back_list, lists[:size]])
        behind = lax.ppermute(to_on, "blocks", face_pairs(devices, 0, 1))
        ahead = lax.ppermute(to_back, "blocks", face_pairs(devices, 0, -1))
        sent_neighbours, lists, behind, ahead = pass_on(neighbours, lists, behind, ahead)
        near = complete(lend(first[1], second[1]), first[1], second[1])
        own_table, other_half = call(
            table_kernel,
            [jax.ShapeDtypeStruct((points + 6 * size, half), BF16)] * 2,
            32,
            0,
            20 * size * width,
            in_specs=[pl.BlockSpec(memory_space=pltpu.SMEM)] + [pl.BlockSpec()] * 5,
        )(
            jnp.stack([lower.astype(jnp.int32), core]),
            own_local,
            other_local,
            lists,
            behind,
            ahead,
        )
        start = jnp.where(lower, points, points + 3 * size).reshape(1)
    else:
        sent_neighbours = neighbours
        received = jnp.concatenate(
            [
                lax.ppermute(faces[k], "blocks", face_pairs(devices, STEPS_X[k], STEPS_Y[k]))
                for k in range(8)
            ]
        )
        shape = (received.shape[0], half)
        own_table = jnp.concatenate(
            [own_local, lax.dynamic_slice(received, (0, core * half), shape)]
        )
        other_half = jnp.concatenate(
            [other_local, lax.dynamic_slice(received, (0, (1 - core) * half), shape)]
        )
        start = jnp.full((1,), points, jnp.int32)
    other_table = lax.ppermute(other_half, "blocks", partner)
    other_neighbours = lax.ppermute(sent_neighbours, "blocks", partner)
    own_stacked = gather_block(start, padded_taps(neighbours), own_table)
    other_rows = padded_taps(other_neighbours)
    own_stacked, other_rows, other_table = pass_on(own_stacked, other_rows, other_table)
    if round_trip:
        middle = complete(lend(first[2], second[2]), first[2], second[2])
    other_stacked = gather_block(start, other_rows, other_table)
    stacked = other_stacked, own_stacked
    if round_trip:
        places = jnp.array(places, jnp.int32)[index]
        early = [[(mine, 0, rows, None)]] + near
        *sums, middle_lhs, far_lhs, last_lhs = conv_part(
            stacked, places, shifts, early, None, length, (2, 2, 1)
        )
        *sums, middle_got, lent = pass_on(*sums, middle[0][1][0], lend(first[3], second[3]))
        middle = [[parts[0], (middle_got, *parts[1][1:])] for parts in middle]
        far = complete(lent, first[3], second[3])
        opposite = complete(lend(first[4]), first[4])
        sums = conv_part([middle_lhs], places[3:5], shifts, middle, sums, length)
        sums = conv_part([far_lhs], places[5:7], shifts, far, sums, length)
        for_partner, own_part = conv_part(
            [last_lhs], places[7:], shifts, opposite, sums, length, dtype=BF16
        )
    else:
        groups = [list(range(core, devices, 2)) for core in range(2)]
        weight = lax.all_gather(mine, "blocks", axis=0, tiled=True, axis_index_groups=groups)
        nowhere = jnp.zeros((1, 2), jnp.int32)
        whole = [[(weight, 0, weight.shape[0], None)]]
        for_partner, own_part = conv_part(stacked, nowhere, shifts, whole, None, length)

    positions = jnp.arange(points, dtype=jnp.int32)
    target = serial_rank // points
    earlier = (target[None, :] == target[:, None]) & (serial_rank[None, :] < serial_rank[:, None])
    out_slot = target * capacity + jnp.sum(earlier.astype(jnp.int32), axis=1)
    anchor = serial_order // points
    before = (anchor[None, :] == anchor[:, None]) & (positions[None, :] < positions[:, None])
    in_slot = anchor * capacity + jnp.sum(before.astype(jnp.int32), axis=1)

    from_partner = lax.ppermute(for_partner, "blocks", partner)

    outgoing = call(
        mix_kernel,
        jax.ShapeDtypeStruct((slots, width), BF16),
        32,
        2 * points * width * (width + slots),
        8 * points * width,
    )(
        own_part,
        from_partner,
        features,
        cpe_weight,
        cpe_gain.reshape(1, width),
        out_slot.reshape(1, points),
    )
    arrived = lax.all_to_all(
        outgoing.reshape(devices, capacity, width), "blocks", split_axis=0, concat_axis=0, tiled=True
    ).reshape(slots, width)

    key_weight = qkv_weight[:, width : 2 * width]
    qv_weight = jnp.concatenate([qkv_weight[:, :width], qkv_weight[:, 2 * width :]], axis=1).T
    weights = (qv_weight, key_weight, proj_weight, up_weight, down_weight)
    back = call(
        block_kernel,
        jax.ShapeDtypeStruct((slots, width), BF16),
        60,
        20 * points * width * width,
        16 * width * width,
        in_specs=[pl.BlockSpec()] * 5 + [pl.BlockSpec(memory_space=pl.ANY)] * len(weights),
        scratch_shapes=[pltpu.VMEM(weight.shape, BF16) for weight in weights]
        + [
            pltpu.SemaphoreType.DMA((len(weights),)),
            pltpu.VMEM((points, width), F32),
            pltpu.VMEM((2 * width, points), BF16),
            pltpu.VMEM((points, width), BF16),
            pltpu.VMEM((width, points), BF16),
            pltpu.VMEM((points, width), F32),
            pltpu.VMEM((2, points, points), F32),
            pltpu.VMEM((2, points, points), BF16),
        ],
    )(
        arrived,
        in_slot.reshape(points, 1),
        in_slot.reshape(1, points),
        attn_gain.reshape(1, width),
        mlp_gain.reshape(1, width),
        *weights,
    )
    returned = lax.all_to_all(
        back.reshape(devices, capacity, width), "blocks", split_axis=0, concat_axis=0, tiled=True
    ).reshape(slots, width)
    return call(
        return_kernel,
        jax.ShapeDtypeStruct((points, width), BF16),
        32,
        2 * points * slots * width,
        6 * points * width,
    )(returned, out_slot.reshape(points, 1))


def solution(mesh):
    placed = (
        P(("groups", "blocks"), None),
        P("blocks", None),
        P(),
        P(),
        P(),
        P(),
        P(),
        P(),
        P(),
        P(),
        P(("groups", "blocks"), None, None),
        P(("groups", "blocks"), None),
        P(("groups", "blocks")),
        P(("groups", "blocks")),
    )
    return jax.shard_map(
        body, mesh=mesh, in_specs=placed, out_specs=P(("groups", "blocks"), None), check_vma=False
    )
```

```python
import functools
import math

import jax
import jax.numpy as jnp
from jax import lax
from jax.experimental import pallas as pl
from jax.experimental.pallas import tpu as pltpu
from jax.sharding import PartitionSpec as P

HEADS = 32
GY = 8
HD = 16
TAPS = 27
EPSILON = 1e-05
STEPS_X = (-1, -1, -1, 0, 0, 1, 1, 1)
STEPS_Y = (-1, 0, 1, -1, 1, -1, 0, 1)
F32 = jnp.float32
BF16 = jnp.bfloat16
MIB = 1 << 20


def dot(left, right):
    return jnp.dot(left, right, preferred_element_type=F32)


def layer_norm(inputs, gain_vector):
    row_mean = jnp.mean(inputs, axis=-1, keepdims=True)
    centred = inputs - row_mean
    variance = jnp.mean(centred * centred, axis=-1, keepdims=True)
    return centred * lax.rsqrt(variance + EPSILON) * gain_vector


def one_hot(mask):
    return jnp.where(mask, 1.0, 0.0).astype(BF16)


def call(kernel, out_shape, limit, flops, moved, **extra):
    return pl.pallas_call(
        kernel,
        out_shape=out_shape,
        compiler_params=pltpu.CompilerParams(vmem_limit_bytes=limit * MIB),
        cost_estimate=pl.CostEstimate(flops=flops, bytes_accessed=moved, transcendentals=0),
        **extra,
    )


def rows_kernel(flags_ref, units_ref, got_ref, mine_ref, begun_ref):
    count, unit, _ = units_ref.shape
    missing = mine_ref.shape[0] - begun_ref.shape[0]
    kept = [units_ref.at[at] for at in range(0, count, 2)]
    got = [got_ref.at[at] for at in range(count // 2)]
    for core, order in enumerate((kept + got, got + kept)):

        @pl.when(flags_ref[0] == core)
        def _():
            for at, source in enumerate(order):
                mine_ref[at * unit : (at + 1) * unit] = source[...]

    start = pl.multiple_of(flags_ref[1] * missing, 16)
    begun_ref[...] = mine_ref[pl.ds(start, begun_ref.shape[0])]


def faces_kernel(unit, core_ref, features_ref, rows_ref, own_ref, other_ref, *face_refs):
    points, width = features_ref.shape
    half = width // 2
    place = lax.broadcasted_iota(jnp.int32, (width, width), 1)
    within = lax.rem(place, half)
    source = (within // unit) * (2 * unit) + (place // half) * unit + lax.rem(place, unit)
    channel = lax.broadcasted_iota(jnp.int32, (width, width), 0)
    ordered = dot(features_ref[...], one_hot(channel == source)).astype(BF16)
    first, second = ordered[:, :half], ordered[:, half:]
    even = core_ref[0] == 0
    own_ref[...] = jnp.where(even, first, second)
    other_ref[...] = jnp.where(even, second, first)
    row_ids = lax.broadcasted_iota(jnp.int32, (rows_ref.shape[0], points), 1)
    rows = dot(one_hot(rows_ref[...] == row_ids), ordered).astype(BF16)
    taken = 0
    for ref in face_refs:
        ref[...] = rows[taken : taken + ref.shape[0]]
        taken += ref.shape[0]


def table_kernel(
    flags_ref, own_rows, other_rows, side_ref, behind_ref, ahead_ref, own_ref, other_ref
):
    size = behind_ref.shape[0] // 2
    points, half = own_rows.shape
    lower, even = flags_ref[0] == 1, flags_ref[1] == 0
    own_ref[:points] = own_rows[...]
    other_ref[:points] = other_rows[...]
    across = [ahead_ref[size:], side_ref[size : 2 * size], behind_ref[size:]]
    along = [ahead_ref[:size], behind_ref[:size]]
    for at, (low, high) in enumerate(zip(across + along, along + across)):
        rows = jnp.where(lower, low, high)
        first, second = rows[:, :half], rows[:, half:]
        start = points + at * size
        own_ref[start : start + size] = jnp.where(even, first, second)
        other_ref[start : start + size] = jnp.where(even, second, first)
    rest = jnp.zeros((size, half), BF16)
    own_ref[points + 5 * size :] = rest
    other_ref[points + 5 * size :] = rest


def gather_kernel(taps, start_ref, rows_ref, table_ref, out_ref):
    points, lanes = rows_ref.shape
    height, half = table_ref.shape
    lane = lax.broadcasted_iota(jnp.int32, (points, lanes), 1)
    segments = []
    for first in range(0, height, 256):
        start = first if first < points else first - points + start_ref[0]
        segments.append(
            (first, min(height, first + 256), jnp.asarray(start, jnp.int32).astype(F32))
        )
    places = lax.broadcasted_iota(jnp.int32, (1, 256), 1).astype(F32).astype(BF16)
    one, zero = jnp.ones((), BF16), jnp.zeros((), BF16)
    for at in range(taps):
        chosen = lane == taps * pl.program_id(0) + at
        column = jnp.sum(jnp.where(chosen, rows_ref[...], 0.0), axis=1, keepdims=True)
        taken = None
        for first, end, start in segments:
            place = jnp.clip(column - start, -1.0, 256.0).astype(BF16)
            hits = jnp.where(place == places[:, : end - first], one, zero)
            product = dot(hits, table_ref[first:end])
            taken = product if taken is None else taken + product
        out_ref[:, at * half : (at + 1) * half] = taken.astype(BF16)


def gather_block(start, rows, table):
    points, lanes = rows.shape
    height, half = table.shape
    taps = 9
    whole = lambda step: (0, 0)
    return call(
        functools.partial(gather_kernel, taps),
        jax.ShapeDtypeStruct((points, TAPS * half), BF16),
        60,
        2 * TAPS * points * height * half,
        2 * TAPS * points * half,
        grid=(TAPS // taps,),
        in_specs=[
            pl.BlockSpec(memory_space=pltpu.SMEM),
            pl.BlockSpec((points, lanes), whole),
            pl.BlockSpec((height, half), whole),
        ],
        out_specs=pl.BlockSpec((points, taps * half), lambda step: (0, step)),
    )(start, rows, table)


def conv_kernel(slots, later, ready, first, places_ref, shifts_ref, *refs):
    refs = list(refs)

    def take(count):
        taken = refs[:count]
        del refs[:count]
        return taken

    sources = take(1 if ready else 2)
    pieces = take(sum(len(parts) for parts in slots))
    before = [] if first else take(2)
    outs = take(2)
    kept = take(len(later))
    (lhs,) = sources if ready else take(1)
    held, sems = take(2)
    length = held.shape[1]

    def stretch(slot, target, sem):
        column = pl.multiple_of(places_ref[2 * slot], 128)
        copies = [
            pltpu.make_async_copy(
                stacked.at[:, pl.ds(column, length)], target.at[block], sem.at[block]
            )
            for block, stacked in enumerate(sources)
        ]
        for copy in copies:
            copy.start()
        return copies

    copies = []
    for at, parts in enumerate(slots):
        row = pl.multiple_of(places_ref[2 * at + 1], 16)
        copies.append([] if ready else stretch(at, lhs.at[at], sems.at[at]))
        edge = length - sum(size for _, size, _ in parts)
        if edge:
            held[at, :edge] = jnp.zeros((edge, held.shape[2]), BF16)
            held[at, length - edge :] = jnp.zeros((edge, held.shape[2]), BF16)
        for part, (start, size, kind) in enumerate(parts):
            place = row if kind is None else pl.multiple_of(row + shifts_ref[kind], 16)
            (piece,) = pieces[:1]
            del pieces[:1]
            copy = pltpu.make_async_copy(
                piece.at[pl.ds(start, size)], held.at[at, pl.ds(place, size)], sems.at[at, 2 + part]
            )
            copy.start()
            copies[-1].append(copy)
    extra, slot = [], len(slots)
    for group, count in enumerate(later):
        for place in range(count):
            extra += stretch(slot, kept[group].at[place], sems.at[slot])
            slot += 1
    for at in range(len(slots)):
        for copy in copies[at]:
            copy.wait()
        for block, ref in enumerate(outs):
            product = dot(lhs[at, block], held[at])
            if at > 0:
                ref[...] += product
            elif first:
                ref[...] = product
            else:
                ref[...] = (before[block][...] + product).astype(ref.dtype)
    for copy in extra:
        copy.wait()


def conv_part(sources, places, shifts, pieces, before, length, later=(), dtype=F32):
    ready = len(sources) == 1
    points = sources[0].shape[2] if ready else sources[0].shape[0]
    width = pieces[0][0][0].shape[1]
    slots = [[part[1:] for part in parts] for parts in pieces]
    flat = [part[0] for parts in pieces for part in parts]
    held = 2 + len(sources) + len(flat)
    kept = [] if before is None else [block for block in range(2) if block or dtype == F32]
    spec = pl.BlockSpec(memory_space=pl.ANY)
    return call(
        functools.partial(conv_kernel, slots, later, ready, before is None),
        [
            jax.ShapeDtypeStruct((points, width), dtype),
            jax.ShapeDtypeStruct((points, width), F32),
        ]
        + [jax.ShapeDtypeStruct((count, 2, points, length), BF16) for count in later],
        24 if ready else 36,
        4 * points * length * width * len(slots),
        2 * length * (2 * points + width) * len(slots),
        in_specs=[pl.BlockSpec(memory_space=pltpu.SMEM)] * 2
        + [pl.BlockSpec() if ready else spec] * len(sources)
        + [spec] * len(flat)
        + ([] if before is None else [pl.BlockSpec()] * 2),
        input_output_aliases={held + block: block for block in kept},
        scratch_shapes=([] if ready else [pltpu.VMEM((len(slots), 2, points, length), BF16)])
        + [
            pltpu.VMEM((len(slots), length, width), BF16),
            pltpu.SemaphoreType.DMA((len(slots) + sum(later), 4)),
        ],
    )(places.reshape(-1), shifts, *sources, *flat, *(before or ()))


def mix_kernel(own_ref, got_ref, features_ref, weight_ref, gain_ref, slot_ref, out_ref):
    convolved = (own_ref[...] + got_ref[...].astype(F32)).astype(BF16)
    linear = dot(convolved, weight_ref[...])
    mixed = (features_ref[...].astype(F32) + layer_norm(linear, gain_ref[...])).astype(BF16)
    slots = lax.broadcasted_iota(jnp.int32, (out_ref.shape[0], mixed.shape[0]), 0)
    out_ref[...] = dot(one_hot(slots == slot_ref[...]), mixed).astype(BF16)


def block_kernel(
    arrived_ref,
    slot_col_ref,
    slot_row_ref,
    attn_gain_ref,
    mlp_gain_ref,
    qv_hbm,
    key_hbm,
    proj_hbm,
    up_hbm,
    down_hbm,
    out_ref,
    qv_ref,
    key_ref,
    proj_ref,
    up_ref,
    down_ref,
    sems,
    serial_ref,
    qv_cols_ref,
    keys_ref,
    heads_ref,
    total_ref,
    scores_ref,
    weights_ref,
):
    sources = (key_hbm, qv_hbm, proj_hbm, up_hbm, down_hbm)
    targets = (key_ref, qv_ref, proj_ref, up_ref, down_ref)
    copies = [
        pltpu.make_async_copy(source, target, sems.at[at])
        for at, (source, target) in enumerate(zip(sources, targets))
    ]
    for copy in copies:
        copy.start()
    slots = arrived_ref.shape[0]
    points, width = serial_ref.shape
    slot_ids = lax.broadcasted_iota(jnp.int32, (points, slots), 1)
    serial = dot(one_hot(slot_col_ref[...] == slot_ids), arrived_ref[...])
    serial_ref[...] = serial
    normed = layer_norm(serial, attn_gain_ref[...]).astype(BF16)
    copies[0].wait()
    keys_ref[...] = dot(normed, key_ref[...]).astype(BF16)
    copies[1].wait()
    factor = math.log2(math.e) / math.sqrt(HD)
    contract_last = (((1,), (1,)), ((), ()))
    qv_cols_ref[:width] = (
        lax.dot_general(qv_ref[:width], normed, contract_last, preferred_element_type=F32) * factor
    ).astype(BF16)
    qv_cols_ref[width:] = lax.dot_general(
        qv_ref[width:], normed, contract_last, preferred_element_type=F32
    ).astype(BF16)
    ones = jnp.ones((HD, points), BF16)
    per_group = 128 // HD
    head_of_row = lax.broadcasted_iota(jnp.int32, (128, points), 0) // HD

    def score(head, slot):
        base = pl.multiple_of(head // per_group * 128, 128)
        group_queries = qv_cols_ref[pl.ds(base, 128)].astype(F32)
        chosen = head_of_row == lax.rem(head, per_group)
        queries = jnp.where(chosen, group_queries, 0.0).astype(BF16)
        scores_ref[slot] = dot(keys_ref[:, pl.ds(base, 128)], queries)

    def weigh(slot):
        scores = scores_ref[slot]
        weights_ref[slot] = jnp.exp2(scores - jnp.max(scores, axis=0, keepdims=True)).astype(BF16)

    def gather(head, slot):
        at = pl.multiple_of(head * HD, HD)
        values = jnp.concatenate([qv_cols_ref[pl.ds(width + at, HD)], ones], axis=0)
        sums = dot(values, weights_ref[slot])
        heads_ref[pl.ds(at, HD)] = (sums[:HD] / sums[HD : HD + 1]).astype(BF16)

    score(0, 0)
    score(1, 1)
    weigh(0)

    def two_heads(pair, carry):
        head = 2 * pair + 1
        for slot in (1, 0):
            score(head + 1, 1 - slot)
            weigh(slot)
            gather(head - 1, 1 - slot)
            head += 1
        return carry

    lax.fori_loop(0, HEADS // 2 - 1, two_heads, 0)
    weigh(1)
    gather(HEADS - 2, 0)
    gather(HEADS - 1, 1)

    for copy in copies[2:]:
        copy.wait()
    update = lax.dot_general(
        heads_ref[...], proj_ref[...], (((0,), (0,)), ((), ())), preferred_element_type=F32
    )
    attended = (serial_ref[...] + update).astype(BF16).astype(F32)
    hidden_in = layer_norm(attended, mlp_gain_ref[...]).astype(BF16)
    total_ref[...] = attended
    chunk = width
    for start in range(0, up_ref.shape[1], chunk):
        raised = dot(hidden_in, up_ref[:, start : start + chunk])
        hidden = (raised * (1.0 + lax.erf(raised * math.sqrt(0.5))) * 0.5).astype(BF16)
        total_ref[...] += dot(hidden, down_ref[start : start + chunk])
    finished = total_ref[...].astype(BF16)
    slot_rows = lax.broadcasted_iota(jnp.int32, (slots, points), 0)
    out_ref[...] = dot(one_hot(slot_rows == slot_row_ref[...]), finished).astype(BF16)


def return_kernel(arrived_ref, slot_ref, out_ref):
    slot_ids = lax.broadcasted_iota(jnp.int32, (out_ref.shape[0], arrived_ref.shape[0]), 1)
    out_ref[...] = dot(one_hot(slot_ref[...] == slot_ids), arrived_ref[...]).astype(BF16)


def face_pairs(devices, dx, dy):
    return [
        (source, source + dx * GY + dy)
        for source in range(devices)
        if 0 <= source // GY + dx < devices // GY and 0 <= source % GY + dy < GY
    ]


def way_round(devices, rows, length):
    chips = devices // 2
    cycle = list(range(0, chips, 2)) + list(range(chips - 1, 0, -2))
    chains = [], []
    places = [None] * devices
    for place, chip in enumerate(cycle):
        for core, way in ((0, 1), (1, -1)):
            me = 2 * chip + core
            for chain, step in zip(chains, (way, -way)):
                chain.append((me, 2 * cycle[(place + step) % chips] + core))
            order = [0]
            for step in range(1, chips // 2):
                order += [-step * way, step * way]
            order.append(chips // 2)
            places[me] = []
            for offset in order:
                start = cycle[(place + offset) % chips] * rows
                column = min(start // 128 * 128, chips * rows - length)
                places[me].append((column, start - column))
    return *chains, places


def padded_taps(neighbours):
    points = neighbours.shape[0]
    own = jnp.arange(points, dtype=jnp.int32)[:, None]
    rest = jnp.zeros((points, 128 - TAPS), jnp.int32)
    middle = TAPS // 2
    rows = jnp.concatenate([neighbours[:, :middle], own, neighbours[:, middle:], rest], axis=1)
    return rows.astype(F32)


def body(
    features,
    conv_weight,
    cpe_weight,
    cpe_gain,
    attn_gain,
    qkv_weight,
    proj_weight,
    mlp_gain,
    up_weight,
    down_weight,
    face_rows,
    neighbours,
    serial_rank,
    serial_order,
):
    points, width = features.shape
    half = width // 2
    devices = lax.axis_size("blocks")
    index = lax.axis_index("blocks")
    core = lax.rem(index, 2)
    partner = [(source, source ^ 1) for source in range(devices)]
    capacity = 2 * points // devices
    slots = devices * capacity

    unit = conv_weight.shape[0] // TAPS
    units = conv_weight.reshape(TAPS, unit, width)
    got = lax.ppermute(units[1::2], "blocks", partner)
    rows = TAPS * unit
    side = lax.axis_index("groups")
    missing = -(-rows // 64) * 16
    passed = rows - missing
    if devices == 2 * GY:
        mine, begun = call(
            rows_kernel,
            [
                jax.ShapeDtypeStruct((rows, width), BF16),
                jax.ShapeDtypeStruct((passed, width), BF16),
            ],
            24,
            0,
            8 * rows * width,
            in_specs=[pl.BlockSpec(memory_space=pltpu.SMEM)] + [pl.BlockSpec()] * 2,
        )(jnp.stack([core, side]).astype(jnp.int32), units, got)
    else:
        kept = units[0::2]
        mine = begun = jnp.where(
            core == 0, jnp.concatenate([kept, got]), jnp.concatenate([got, kept])
        ).reshape(rows, width)

    round_trip = devices == 2 * GY
    lower = index < GY
    if round_trip:
        across = jnp.where(lower, face_rows[0, 5:], face_rows[0, :3])
        face_list = jnp.concatenate([across, face_rows[0, 3:5]]).reshape(-1, 1)
        counts = (3, 1, 1)
    else:
        face_list = face_rows.reshape(-1, 1)
        counts = (1,) * 8
    size = face_rows.shape[2]
    own_local, other_local, *faces = call(
        functools.partial(faces_kernel, unit),
        [jax.ShapeDtypeStruct((points, half), BF16)] * 2
        + [jax.ShapeDtypeStruct((count * size, width), BF16) for count in counts],
        32,
        4 * points * width * width,
        8 * points * width,
        in_specs=[pl.BlockSpec(memory_space=pltpu.SMEM)] + [pl.BlockSpec()] * 2,
    )(core.reshape(1), features, face_list)
    length = -(-(rows + 127) // 128) * 128 if round_trip else rows * (devices // 2)
    first_pairs, second_pairs, places = way_round(devices, rows, length)
    shifts = jnp.stack([side * missing, (1 - side) * passed]).astype(jnp.int32)
    first, second = [begun], [begun]

    def pass_on(*beside):
        if not round_trip:
            return beside
        tied = lax.optimization_barrier((first[-1], second[-1], *beside))
        first[-1], second[-1] = tied[:2]
        last = len(first) == devices // 4
        first.append(lax.ppermute(first[-1], "blocks", first_pairs))
        if not last:
            second.append(lax.ppermute(second[-1], "blocks", second_pairs))
        return tied[2:]

    def lend(*arrived):
        return jnp.concatenate(
            [
                lax.dynamic_slice(piece, (side * (passed - missing), 0), (missing, width))
                for piece in arrived
            ]
        )

    def complete(lent, *arrived):
        got = lax.ppermute(lent, "groups", [(0, 1), (1, 0)])
        return [
            [(piece, 0, passed, 0), (got, at * missing, missing, 1)]
            for at, piece in enumerate(arrived)
        ]

    if round_trip:
        lists, back_list, on_list = faces
        across = face_pairs(devices, 1, 0) + face_pairs(devices, -1, 0)
        (lists,) = pass_on(lists)
        lists = lax.ppermute(lists, "blocks", across)
        to_on = jnp.concatenate([on_list, lists[2 * size :]])
        to_back = jnp.concatenate([back_list, lists[:size]])
        behind = lax.ppermute(to_on, "blocks", face_pairs(devices, 0, 1))
        ahead = lax.ppermute(to_back, "blocks", face_pairs(devices, 0, -1))
        sent_neighbours, lists, behind, ahead = pass_on(neighbours, lists, behind, ahead)
        near = complete(lend(first[1], second[1]), first[1], second[1])
        own_table, other_half = call(
            table_kernel,
            [jax.ShapeDtypeStruct((points + 6 * size, half), BF16)] * 2,
            32,
            0,
            20 * size * width,
            in_specs=[pl.BlockSpec(memory_space=pltpu.SMEM)] + [pl.BlockSpec()] * 5,
        )(
            jnp.stack([lower.astype(jnp.int32), core]),
            own_local,
            other_local,
            lists,
            behind,
            ahead,
        )
        start = jnp.where(lower, points, points + 3 * size).reshape(1)
    else:
        sent_neighbours = neighbours
        received = jnp.concatenate(
            [
                lax.ppermute(faces[k], "blocks", face_pairs(devices, STEPS_X[k], STEPS_Y[k]))
                for k in range(8)
            ]
        )
        shape = (received.shape[0], half)
        own_table = jnp.concatenate(
            [own_local, lax.dynamic_slice(received, (0, core * half), shape)]
        )
        other_half = jnp.concatenate(
            [other_local, lax.dynamic_slice(received, (0, (1 - core) * half), shape)]
        )
        start = jnp.full((1,), points, jnp.int32)
    other_table = lax.ppermute(other_half, "blocks", partner)
    other_neighbours = lax.ppermute(sent_neighbours, "blocks", partner)
    own_stacked = gather_block(start, padded_taps(neighbours), own_table)
    other_rows = padded_taps(other_neighbours)
    own_stacked, other_rows, other_table = pass_on(own_stacked, other_rows, other_table)
    if round_trip:
        middle = complete(lend(first[2], second[2]), first[2], second[2])
    other_stacked = gather_block(start, other_rows, other_table)
    stacked = other_stacked, own_stacked
    if round_trip:
        *stacked, middle_got, lent = pass_on(
            *stacked, middle[0][1][0], lend(first[3], second[3])
        )
        middle = [[parts[0], (middle_got, *parts[1][1:])] for parts in middle]
        places = jnp.array(places, jnp.int32)[index]
        early = [[(mine, 0, rows, None)]] + near
        *sums, middle_lhs, far_lhs, last_lhs = conv_part(
            stacked, places, shifts, early, None, length, (2, 2, 1)
        )
        far = complete(lent, first[3], second[3])
        opposite = complete(lend(first[4]), first[4])
        sums = conv_part([middle_lhs], places[3:5], shifts, middle, sums, length)
        sums = conv_part([far_lhs], places[5:7], shifts, far, sums, length)
        for_partner, own_part = conv_part(
            [last_lhs], places[7:], shifts, opposite, sums, length, dtype=BF16
        )
    else:
        groups = [list(range(core, devices, 2)) for core in range(2)]
        weight = lax.all_gather(mine, "blocks", axis=0, tiled=True, axis_index_groups=groups)
        nowhere = jnp.zeros((1, 2), jnp.int32)
        whole = [[(weight, 0, weight.shape[0], None)]]
        for_partner, own_part = conv_part(stacked, nowhere, shifts, whole, None, length)

    positions = jnp.arange(points, dtype=jnp.int32)
    target = serial_rank // points
    earlier = (target[None, :] == target[:, None]) & (serial_rank[None, :] < serial_rank[:, None])
    out_slot = target * capacity + jnp.sum(earlier.astype(jnp.int32), axis=1)
    anchor = serial_order // points
    before = (anchor[None, :] == anchor[:, None]) & (positions[None, :] < positions[:, None])
    in_slot = anchor * capacity + jnp.sum(before.astype(jnp.int32), axis=1)

    from_partner = lax.ppermute(for_partner, "blocks", partner)

    outgoing = call(
        mix_kernel,
        jax.ShapeDtypeStruct((slots, width), BF16),
        32,
        2 * points * width * (width + slots),
        8 * points * width,
    )(
        own_part,
        from_partner,
        features,
        cpe_weight,
        cpe_gain.reshape(1, width),
        out_slot.reshape(1, points),
    )
    arrived = lax.all_to_all(
        outgoing.reshape(devices, capacity, width), "blocks", split_axis=0, concat_axis=0, tiled=True
    ).reshape(slots, width)

    key_weight = qkv_weight[:, width : 2 * width]
    qv_weight = jnp.concatenate([qkv_weight[:, :width], qkv_weight[:, 2 * width :]], axis=1).T
    weights = (qv_weight, key_weight, proj_weight, up_weight, down_weight)
    back = call(
        block_kernel,
        jax.ShapeDtypeStruct((slots, width), BF16),
        60,
        20 * points * width * width,
        16 * width * width,
        in_specs=[pl.BlockSpec()] * 5 + [pl.BlockSpec(memory_space=pl.ANY)] * len(weights),
        scratch_shapes=[pltpu.VMEM(weight.shape, BF16) for weight in weights]
        + [
            pltpu.SemaphoreType.DMA((len(weights),)),
            pltpu.VMEM((points, width), F32),
            pltpu.VMEM((2 * width, points), BF16),
            pltpu.VMEM((points, width), BF16),
            pltpu.VMEM((width, points), BF16),
            pltpu.VMEM((points, width), F32),
            pltpu.VMEM((2, points, points), F32),
            pltpu.VMEM((2, points, points), BF16),
        ],
    )(
        arrived,
        in_slot.reshape(points, 1),
        in_slot.reshape(1, points),
        attn_gain.reshape(1, width),
        mlp_gain.reshape(1, width),
        *weights,
    )
    returned = lax.all_to_all(
        back.reshape(devices, capacity, width), "blocks", split_axis=0, concat_axis=0, tiled=True
    ).reshape(slots, width)
    return call(
        return_kernel,
        jax.ShapeDtypeStruct((points, width), BF16),
        32,
        2 * points * slots * width,
        6 * points * width,
    )(returned, out_slot.reshape(points, 1))


def solution(mesh):
    placed = (
        P(("groups", "blocks"), None),
        P("blocks", None),
        P(),
        P(),
        P(),
        P(),
        P(),
        P(),
        P(),
        P(),
        P(("groups", "blocks"), None, None),
        P(("groups", "blocks"), None),
        P(("groups", "blocks")),
        P(("groups", "blocks")),
    )
    return jax.shard_map(
        body, mesh=mesh, in_specs=placed, out_specs=P(("groups", "blocks"), None), check_vma=False
    )
```

```python
import functools
import math

import jax
import jax.numpy as jnp
from jax import lax
from jax.experimental import pallas as pl
from jax.experimental.pallas import tpu as pltpu
from jax.sharding import PartitionSpec as P

HEADS = 32
GY = 8
HD = 16
TAPS = 27
EPSILON = 1e-05
STEPS_X = (-1, -1, -1, 0, 0, 1, 1, 1)
STEPS_Y = (-1, 0, 1, -1, 1, -1, 0, 1)
F32 = jnp.float32
BF16 = jnp.bfloat16
MIB = 1 << 20


def dot(left, right):
    return jnp.dot(left, right, preferred_element_type=F32)


def layer_norm(inputs, gain_vector):
    row_mean = jnp.mean(inputs, axis=-1, keepdims=True)
    centred = inputs - row_mean
    variance = jnp.mean(centred * centred, axis=-1, keepdims=True)
    return centred * lax.rsqrt(variance + EPSILON) * gain_vector


def one_hot(mask):
    return jnp.where(mask, 1.0, 0.0).astype(BF16)


def call(kernel, out_shape, limit, flops, moved, **extra):
    return pl.pallas_call(
        kernel,
        out_shape=out_shape,
        compiler_params=pltpu.CompilerParams(vmem_limit_bytes=limit * MIB),
        cost_estimate=pl.CostEstimate(flops=flops, bytes_accessed=moved, transcendentals=0),
        **extra,
    )


def rows_kernel(flags_ref, units_ref, got_ref, mine_ref, begun_ref):
    count, unit, _ = units_ref.shape
    missing = mine_ref.shape[0] - begun_ref.shape[0]
    kept = [units_ref.at[at] for at in range(0, count, 2)]
    got = [got_ref.at[at] for at in range(count // 2)]
    for core, order in enumerate((kept + got, got + kept)):

        @pl.when(flags_ref[0] == core)
        def _():
            for at, source in enumerate(order):
                mine_ref[at * unit : (at + 1) * unit] = source[...]

    passed = begun_ref.shape[0]
    lent = pl.multiple_of(flags_ref[1] * passed, 16)
    begun_ref[:missing] = mine_ref[pl.ds(lent, missing)]
    begun_ref[missing:] = mine_ref[missing:passed]


def faces_kernel(unit, core_ref, features_ref, rows_ref, own_ref, other_ref, *face_refs):
    points, width = features_ref.shape
    half = width // 2
    place = lax.broadcasted_iota(jnp.int32, (width, width), 1)
    within = lax.rem(place, half)
    source = (within // unit) * (2 * unit) + (place // half) * unit + lax.rem(place, unit)
    channel = lax.broadcasted_iota(jnp.int32, (width, width), 0)
    ordered = dot(features_ref[...], one_hot(channel == source)).astype(BF16)
    first, second = ordered[:, :half], ordered[:, half:]
    even = core_ref[0] == 0
    own_ref[...] = jnp.where(even, first, second)
    other_ref[...] = jnp.where(even, second, first)
    row_ids = lax.broadcasted_iota(jnp.int32, (rows_ref.shape[0], points), 1)
    rows = dot(one_hot(rows_ref[...] == row_ids), ordered).astype(BF16)
    taken = 0
    for ref in face_refs:
        ref[...] = rows[taken : taken + ref.shape[0]]
        taken += ref.shape[0]


def table_kernel(
    flags_ref, own_rows, other_rows, side_ref, behind_ref, ahead_ref, own_ref, other_ref
):
    size = behind_ref.shape[0] // 2
    points, half = own_rows.shape
    lower, even = flags_ref[0] == 1, flags_ref[1] == 0
    own_ref[:points] = own_rows[...]
    other_ref[:points] = other_rows[...]
    across = [ahead_ref[size:], side_ref[size : 2 * size], behind_ref[size:]]
    along = [ahead_ref[:size], behind_ref[:size]]
    for at, (low, high) in enumerate(zip(across + along, along + across)):
        rows = jnp.where(lower, low, high)
        first, second = rows[:, :half], rows[:, half:]
        start = points + at * size
        own_ref[start : start + size] = jnp.where(even, first, second)
        other_ref[start : start + size] = jnp.where(even, second, first)
    rest = jnp.zeros((size, half), BF16)
    own_ref[points + 5 * size :] = rest
    other_ref[points + 5 * size :] = rest


def gather_kernel(taps, start_ref, rows_ref, table_ref, out_ref):
    points, lanes = rows_ref.shape
    height, half = table_ref.shape
    lane = lax.broadcasted_iota(jnp.int32, (points, lanes), 1)
    segments = []
    for first in range(0, height, 256):
        start = first if first < points else first - points + start_ref[0]
        segments.append(
            (first, min(height, first + 256), jnp.asarray(start, jnp.int32).astype(F32))
        )
    places = lax.broadcasted_iota(jnp.int32, (1, 256), 1).astype(F32).astype(BF16)
    one, zero = jnp.ones((), BF16), jnp.zeros((), BF16)
    for at in range(taps):
        chosen = lane == taps * pl.program_id(0) + at
        column = jnp.sum(jnp.where(chosen, rows_ref[...], 0.0), axis=1, keepdims=True)
        taken = None
        for first, end, start in segments:
            place = jnp.clip(column - start, -1.0, 256.0).astype(BF16)
            hits = jnp.where(place == places[:, : end - first], one, zero)
            product = dot(hits, table_ref[first:end])
            taken = product if taken is None else taken + product
        out_ref[:, at * half : (at + 1) * half] = taken.astype(BF16)


def gather_block(start, rows, table):
    points, lanes = rows.shape
    height, half = table.shape
    taps = 9
    whole = lambda step: (0, 0)
    return call(
        functools.partial(gather_kernel, taps),
        jax.ShapeDtypeStruct((points, TAPS * half), BF16),
        60,
        2 * TAPS * points * height * half,
        2 * TAPS * points * half,
        grid=(TAPS // taps,),
        in_specs=[
            pl.BlockSpec(memory_space=pltpu.SMEM),
            pl.BlockSpec((points, lanes), whole),
            pl.BlockSpec((height, half), whole),
        ],
        out_specs=pl.BlockSpec((points, taps * half), lambda step: (0, step)),
    )(start, rows, table)


def conv_kernel(slots, later, ready, first, places_ref, shifts_ref, *refs):
    refs = list(refs)

    def take(count):
        taken = refs[:count]
        del refs[:count]
        return taken

    sources = take(1 if ready else 2)
    pieces = take(sum(len(parts) for parts in slots))
    before = [] if first else take(2)
    outs = take(2)
    kept = take(len(later))
    (lhs,) = sources if ready else take(1)
    held, sems = take(2)
    length = held.shape[1]

    def stretch(slot, target, sem):
        column = pl.multiple_of(places_ref[2 * slot], 128)
        copies = [
            pltpu.make_async_copy(
                stacked.at[:, pl.ds(column, length)], target.at[block], sem.at[block]
            )
            for block, stacked in enumerate(sources)
        ]
        for copy in copies:
            copy.start()
        return copies

    copies = []
    for at, parts in enumerate(slots):
        row = pl.multiple_of(places_ref[2 * at + 1], 16)
        copies.append([] if ready else stretch(at, lhs.at[at], sems.at[at]))
        edge = length - sum(size for _, size, _, _ in parts)
        if edge:
            held[at, :edge] = jnp.zeros((edge, held.shape[2]), BF16)
            held[at, length - edge :] = jnp.zeros((edge, held.shape[2]), BF16)
        for part, (start, size, offset, kind) in enumerate(parts):
            moved = row + offset if kind is None else row + shifts_ref[kind]
            place = pl.multiple_of(moved, 16)
            (piece,) = pieces[:1]
            del pieces[:1]
            copy = pltpu.make_async_copy(
                piece.at[pl.ds(start, size)], held.at[at, pl.ds(place, size)], sems.at[at, 2 + part]
            )
            copy.start()
            copies[-1].append(copy)
    extra, slot = [], len(slots)
    for group, count in enumerate(later):
        for place in range(count):
            extra += stretch(slot, kept[group].at[place], sems.at[slot])
            slot += 1
    for at in range(len(slots)):
        for copy in copies[at]:
            copy.wait()
        for block, ref in enumerate(outs):
            product = dot(lhs[at, block], held[at])
            if at > 0:
                ref[...] += product
            elif first:
                ref[...] = product
            else:
                ref[...] = (before[block][...] + product).astype(ref.dtype)
    for copy in extra:
        copy.wait()


def conv_part(sources, places, shifts, pieces, before, length, later=(), dtype=F32):
    ready = len(sources) == 1
    points = sources[0].shape[2] if ready else sources[0].shape[0]
    width = pieces[0][0][0].shape[1]
    slots = [[part[1:] for part in parts] for parts in pieces]
    flat = [part[0] for parts in pieces for part in parts]
    held = 2 + len(sources) + len(flat)
    kept = [] if before is None else [block for block in range(2) if block or dtype == F32]
    spec = pl.BlockSpec(memory_space=pl.ANY)
    return call(
        functools.partial(conv_kernel, slots, later, ready, before is None),
        [
            jax.ShapeDtypeStruct((points, width), dtype),
            jax.ShapeDtypeStruct((points, width), F32),
        ]
        + [jax.ShapeDtypeStruct((count, 2, points, length), BF16) for count in later],
        24 if ready else 36,
        4 * points * length * width * len(slots),
        2 * length * (2 * points + width) * len(slots),
        in_specs=[pl.BlockSpec(memory_space=pltpu.SMEM)] * 2
        + [pl.BlockSpec() if ready else spec] * len(sources)
        + [spec] * len(flat)
        + ([] if before is None else [pl.BlockSpec()] * 2),
        input_output_aliases={held + block: block for block in kept},
        scratch_shapes=([] if ready else [pltpu.VMEM((len(slots), 2, points, length), BF16)])
        + [
            pltpu.VMEM((len(slots), length, width), BF16),
            pltpu.SemaphoreType.DMA((len(slots) + sum(later), 5)),
        ],
    )(places, shifts, *sources, *flat, *(before or ()))


def mix_kernel(own_ref, got_ref, features_ref, weight_ref, gain_ref, slot_ref, out_ref):
    convolved = (own_ref[...] + got_ref[...].astype(F32)).astype(BF16)
    linear = dot(convolved, weight_ref[...])
    mixed = (features_ref[...].astype(F32) + layer_norm(linear, gain_ref[...])).astype(BF16)
    slots = lax.broadcasted_iota(jnp.int32, (out_ref.shape[0], mixed.shape[0]), 0)
    out_ref[...] = dot(one_hot(slots == slot_ref[...]), mixed).astype(BF16)


def block_kernel(
    arrived_ref,
    slot_col_ref,
    slot_row_ref,
    attn_gain_ref,
    mlp_gain_ref,
    qv_hbm,
    key_hbm,
    proj_hbm,
    up_hbm,
    down_hbm,
    out_ref,
    qv_ref,
    key_ref,
    proj_ref,
    up_ref,
    down_ref,
    sems,
    serial_ref,
    qv_cols_ref,
    keys_ref,
    heads_ref,
    total_ref,
    scores_ref,
    weights_ref,
):
    sources = (key_hbm, qv_hbm, proj_hbm, up_hbm, down_hbm)
    targets = (key_ref, qv_ref, proj_ref, up_ref, down_ref)
    copies = [
        pltpu.make_async_copy(source, target, sems.at[at])
        for at, (source, target) in enumerate(zip(sources, targets))
    ]
    for copy in copies:
        copy.start()
    slots = arrived_ref.shape[0]
    points, width = serial_ref.shape
    slot_ids = lax.broadcasted_iota(jnp.int32, (points, slots), 1)
    serial = dot(one_hot(slot_col_ref[...] == slot_ids), arrived_ref[...])
    serial_ref[...] = serial
    normed = layer_norm(serial, attn_gain_ref[...]).astype(BF16)
    copies[0].wait()
    keys_ref[...] = dot(normed, key_ref[...]).astype(BF16)
    copies[1].wait()
    factor = math.log2(math.e) / math.sqrt(HD)
    contract_last = (((1,), (1,)), ((), ()))
    qv_cols_ref[:width] = (
        lax.dot_general(qv_ref[:width], normed, contract_last, preferred_element_type=F32) * factor
    ).astype(BF16)
    qv_cols_ref[width:] = lax.dot_general(
        qv_ref[width:], normed, contract_last, preferred_element_type=F32
    ).astype(BF16)
    ones = jnp.ones((HD, points), BF16)
    per_group = 128 // HD
    head_of_row = lax.broadcasted_iota(jnp.int32, (128, points), 0) // HD

    def score(head, slot):
        base = pl.multiple_of(head // per_group * 128, 128)
        group_queries = qv_cols_ref[pl.ds(base, 128)].astype(F32)
        chosen = head_of_row == lax.rem(head, per_group)
        queries = jnp.where(chosen, group_queries, 0.0).astype(BF16)
        scores_ref[slot] = dot(keys_ref[:, pl.ds(base, 128)], queries)

    def weigh(slot):
        scores = scores_ref[slot]
        weights_ref[slot] = jnp.exp2(scores - jnp.max(scores, axis=0, keepdims=True)).astype(BF16)

    def gather(head, slot):
        at = pl.multiple_of(head * HD, HD)
        values = jnp.concatenate([qv_cols_ref[pl.ds(width + at, HD)], ones], axis=0)
        sums = dot(values, weights_ref[slot])
        heads_ref[pl.ds(at, HD)] = (sums[:HD] / sums[HD : HD + 1]).astype(BF16)

    score(0, 0)
    score(1, 1)
    weigh(0)

    def two_heads(pair, carry):
        head = 2 * pair + 1
        for slot in (1, 0):
            score(head + 1, 1 - slot)
            weigh(slot)
            gather(head - 1, 1 - slot)
            head += 1
        return carry

    lax.fori_loop(0, HEADS // 2 - 1, two_heads, 0)
    weigh(1)
    gather(HEADS - 2, 0)
    gather(HEADS - 1, 1)

    for copy in copies[2:]:
        copy.wait()
    update = lax.dot_general(
        heads_ref[...], proj_ref[...], (((0,), (0,)), ((), ())), preferred_element_type=F32
    )
    attended = (serial_ref[...] + update).astype(BF16).astype(F32)
    hidden_in = layer_norm(attended, mlp_gain_ref[...]).astype(BF16)
    total_ref[...] = attended
    chunk = width
    for start in range(0, up_ref.shape[1], chunk):
        raised = dot(hidden_in, up_ref[:, start : start + chunk])
        hidden = (raised * (1.0 + lax.erf(raised * math.sqrt(0.5))) * 0.5).astype(BF16)
        total_ref[...] += dot(hidden, down_ref[start : start + chunk])
    finished = total_ref[...].astype(BF16)
    slot_rows = lax.broadcasted_iota(jnp.int32, (slots, points), 0)
    out_ref[...] = dot(one_hot(slot_rows == slot_row_ref[...]), finished).astype(BF16)


def return_kernel(arrived_ref, slot_ref, out_ref):
    slot_ids = lax.broadcasted_iota(jnp.int32, (out_ref.shape[0], arrived_ref.shape[0]), 1)
    out_ref[...] = dot(one_hot(slot_ref[...] == slot_ids), arrived_ref[...]).astype(BF16)


def face_pairs(devices, dx, dy):
    return [
        (source, source + dx * GY + dy)
        for source in range(devices)
        if 0 <= source // GY + dx < devices // GY and 0 <= source % GY + dy < GY
    ]


def way_round(devices, rows, length):
    chips = devices // 2
    cycle = list(range(0, chips, 2)) + list(range(chips - 1, 0, -2))
    chains = [], []
    places = [None] * devices
    for place, chip in enumerate(cycle):
        for core, way in ((0, 1), (1, -1)):
            me = 2 * chip + core
            for chain, step in zip(chains, (way, -way)):
                chain.append((me, 2 * cycle[(place + step) % chips] + core))
            order = [0]
            for step in range(1, chips // 2):
                order += [-step * way, step * way]
            order.append(chips // 2)
            places[me] = []
            for offset in order:
                start = cycle[(place + offset) % chips] * rows
                column = min(start // 128 * 128, chips * rows - length)
                places[me].append((column, start - column))
    return *chains, places


def padded_taps(neighbours):
    points = neighbours.shape[0]
    own = jnp.arange(points, dtype=jnp.int32)[:, None]
    rest = jnp.zeros((points, 128 - TAPS), jnp.int32)
    middle = TAPS // 2
    rows = jnp.concatenate([neighbours[:, :middle], own, neighbours[:, middle:], rest], axis=1)
    return rows.astype(F32)


def body(
    features,
    conv_weight,
    cpe_weight,
    cpe_gain,
    attn_gain,
    qkv_weight,
    proj_weight,
    mlp_gain,
    up_weight,
    down_weight,
    face_rows,
    neighbours,
    serial_rank,
    serial_order,
):
    points, width = features.shape
    half = width // 2
    devices = lax.axis_size("blocks")
    index = lax.axis_index("blocks")
    core = lax.rem(index, 2)
    partner = [(source, source ^ 1) for source in range(devices)]
    capacity = 2 * points // devices
    slots = devices * capacity

    unit = conv_weight.shape[0] // TAPS
    units = conv_weight.reshape(TAPS, unit, width)
    got = lax.ppermute(units[1::2], "blocks", partner)
    rows = TAPS * unit
    side = lax.axis_index("groups")
    missing = -(-rows // 64) * 16
    passed = rows - missing
    if devices == 2 * GY:
        mine, begun = call(
            rows_kernel,
            [
                jax.ShapeDtypeStruct((rows, width), BF16),
                jax.ShapeDtypeStruct((passed, width), BF16),
            ],
            24,
            0,
            8 * rows * width,
            in_specs=[pl.BlockSpec(memory_space=pltpu.SMEM)] + [pl.BlockSpec()] * 2,
        )(jnp.stack([core, side]).astype(jnp.int32), units, got)
    else:
        kept = units[0::2]
        mine = begun = jnp.where(
            core == 0, jnp.concatenate([kept, got]), jnp.concatenate([got, kept])
        ).reshape(rows, width)

    round_trip = devices == 2 * GY
    lower = index < GY
    if round_trip:
        across = jnp.where(lower, face_rows[0, 5:], face_rows[0, :3])
        face_list = jnp.concatenate([across, face_rows[0, 3:5]]).reshape(-1, 1)
        counts = (3, 1, 1)
    else:
        face_list = face_rows.reshape(-1, 1)
        counts = (1,) * 8
    size = face_rows.shape[2]
    own_local, other_local, *faces = call(
        functools.partial(faces_kernel, unit),
        [jax.ShapeDtypeStruct((points, half), BF16)] * 2
        + [jax.ShapeDtypeStruct((count * size, width), BF16) for count in counts],
        32,
        4 * points * width * width,
        8 * points * width,
        in_specs=[pl.BlockSpec(memory_space=pltpu.SMEM)] + [pl.BlockSpec()] * 2,
    )(core.reshape(1), features, face_list)
    length = -(-(rows + 127) // 128) * 128 if round_trip else rows * (devices // 2)
    first_pairs, second_pairs, places = way_round(devices, rows, length)
    shifts = jnp.stack([side * passed, (1 - side) * passed]).astype(jnp.int32)
    first, second = [begun], [begun]

    def pass_on(*beside):
        if not round_trip:
            return beside
        tied = lax.optimization_barrier((first[-1], second[-1], *beside))
        first[-1], second[-1] = tied[:2]
        last = len(first) == devices // 4
        first.append(lax.ppermute(first[-1], "blocks", first_pairs))
        if not last:
            second.append(lax.ppermute(second[-1], "blocks", second_pairs))
        return tied[2:]

    def complete(*arrived):
        lent = [piece[:missing] for piece in arrived]
        lent = jnp.concatenate(lent) if len(lent) > 1 else lent[0]
        got = lax.ppermute(lent, "groups", [(0, 1), (1, 0)])
        return [
            [
                (piece, 0, missing, 0, 0),
                (piece, missing, passed - missing, missing, None),
                (got, at * missing, missing, 0, 1),
            ]
            for at, piece in enumerate(arrived)
        ]

    if round_trip:
        lists, back_list, on_list = faces
        across = face_pairs(devices, 1, 0) + face_pairs(devices, -1, 0)
        (lists,) = pass_on(lists)
        lists = lax.ppermute(lists, "blocks", across)
        places = jnp.array(places, jnp.int32)[index].reshape(-1)
        lists, sent_neighbours, places = lax.optimization_barrier((lists, neighbours, places))
        other_neighbours = lax.ppermute(sent_neighbours, "blocks", partner)
        to_on = jnp.concatenate([on_list, lists[2 * size :]])
        to_back = jnp.concatenate([back_list, lists[:size]])
        behind = lax.ppermute(to_on, "blocks", face_pairs(devices, 0, 1))
        ahead = lax.ppermute(to_back, "blocks", face_pairs(devices, 0, -1))
        lists, behind, ahead = pass_on(lists, behind, ahead)
        near = complete(first[1], second[1])
        own_table, other_half = call(
            table_kernel,
            [jax.ShapeDtypeStruct((points + 6 * size, half), BF16)] * 2,
            32,
            0,
            20 * size * width,
            in_specs=[pl.BlockSpec(memory_space=pltpu.SMEM)] + [pl.BlockSpec()] * 5,
        )(
            jnp.stack([lower.astype(jnp.int32), core]),
            own_local,
            other_local,
            lists,
            behind,
            ahead,
        )
        start = jnp.where(lower, points, points + 3 * size).reshape(1)
    else:
        other_neighbours = lax.ppermute(neighbours, "blocks", partner)
        received = jnp.concatenate(
            [
                lax.ppermute(faces[k], "blocks", face_pairs(devices, STEPS_X[k], STEPS_Y[k]))
                for k in range(8)
            ]
        )
        shape = (received.shape[0], half)
        own_table = jnp.concatenate(
            [own_local, lax.dynamic_slice(received, (0, core * half), shape)]
        )
        other_half = jnp.concatenate(
            [other_local, lax.dynamic_slice(received, (0, (1 - core) * half), shape)]
        )
        start = jnp.full((1,), points, jnp.int32)
    other_table = lax.ppermute(other_half, "blocks", partner)
    own_stacked = gather_block(start, padded_taps(neighbours), own_table)
    other_rows = padded_taps(other_neighbours)
    own_stacked, other_rows, other_table = pass_on(own_stacked, other_rows, other_table)
    if round_trip:
        middle = complete(first[2], second[2])
    other_stacked = gather_block(start, other_rows, other_table)
    stacked = other_stacked, own_stacked
    if round_trip:
        *stacked, middle_got = pass_on(*stacked, middle[0][2][0])
        middle = [[*parts[:2], (middle_got, *parts[2][1:])] for parts in middle]
        early = [[(mine, 0, rows, 0, None)]] + near
        *sums, middle_lhs, far_lhs, last_lhs = conv_part(
            stacked, places, shifts, early, None, length, (2, 2, 1)
        )
        far = complete(first[3], second[3])
        opposite = complete(first[4])
        sums = conv_part([middle_lhs], places[6:10], shifts, middle, sums, length)
        sums = conv_part([far_lhs], places[10:14], shifts, far, sums, length)
        for_partner, own_part = conv_part(
            [last_lhs], places[14:], shifts, opposite, sums, length, dtype=BF16
        )
    else:
        groups = [list(range(core, devices, 2)) for core in range(2)]
        weight = lax.all_gather(mine, "blocks", axis=0, tiled=True, axis_index_groups=groups)
        nowhere = jnp.zeros((2,), jnp.int32)
        whole = [[(weight, 0, weight.shape[0], 0, None)]]
        for_partner, own_part = conv_part(stacked, nowhere, shifts, whole, None, length)

    positions = jnp.arange(points, dtype=jnp.int32)
    target = serial_rank // points
    earlier = (target[None, :] == target[:, None]) & (serial_rank[None, :] < serial_rank[:, None])
    out_slot = target * capacity + jnp.sum(earlier.astype(jnp.int32), axis=1)
    anchor = serial_order // points
    before = (anchor[None, :] == anchor[:, None]) & (positions[None, :] < positions[:, None])
    in_slot = anchor * capacity + jnp.sum(before.astype(jnp.int32), axis=1)

    from_partner = lax.ppermute(for_partner, "blocks", partner)

    outgoing = call(
        mix_kernel,
        jax.ShapeDtypeStruct((slots, width), BF16),
        32,
        2 * points * width * (width + slots),
        8 * points * width,
    )(
        own_part,
        from_partner,
        features,
        cpe_weight,
        cpe_gain.reshape(1, width),
        out_slot.reshape(1, points),
    )
    arrived = lax.all_to_all(
        outgoing.reshape(devices, capacity, width), "blocks", split_axis=0, concat_axis=0, tiled=True
    ).reshape(slots, width)

    key_weight = qkv_weight[:, width : 2 * width]
    qv_weight = jnp.concatenate([qkv_weight[:, :width], qkv_weight[:, 2 * width :]], axis=1).T
    weights = (qv_weight, key_weight, proj_weight, up_weight, down_weight)
    back = call(
        block_kernel,
        jax.ShapeDtypeStruct((slots, width), BF16),
        60,
        20 * points * width * width,
        16 * width * width,
        in_specs=[pl.BlockSpec()] * 5 + [pl.BlockSpec(memory_space=pl.ANY)] * len(weights),
        scratch_shapes=[pltpu.VMEM(weight.shape, BF16) for weight in weights]
        + [
            pltpu.SemaphoreType.DMA((len(weights),)),
            pltpu.VMEM((points, width), F32),
            pltpu.VMEM((2 * width, points), BF16),
            pltpu.VMEM((points, width), BF16),
            pltpu.VMEM((width, points), BF16),
            pltpu.VMEM((points, width), F32),
            pltpu.VMEM((2, points, points), F32),
            pltpu.VMEM((2, points, points), BF16),
        ],
    )(
        arrived,
        in_slot.reshape(points, 1),
        in_slot.reshape(1, points),
        attn_gain.reshape(1, width),
        mlp_gain.reshape(1, width),
        *weights,
    )
    returned = lax.all_to_all(
        back.reshape(devices, capacity, width), "blocks", split_axis=0, concat_axis=0, tiled=True
    ).reshape(slots, width)
    return call(
        return_kernel,
        jax.ShapeDtypeStruct((points, width), BF16),
        32,
        2 * points * slots * width,
        6 * points * width,
    )(returned, out_slot.reshape(points, 1))


def solution(mesh):
    placed = (
        P(("groups", "blocks"), None),
        P("blocks", None),
        P(),
        P(),
        P(),
        P(),
        P(),
        P(),
        P(),
        P(),
        P(("groups", "blocks"), None, None),
        P(("groups", "blocks"), None),
        P(("groups", "blocks")),
        P(("groups", "blocks")),
    )
    return jax.shard_map(
        body, mesh=mesh, in_specs=placed, out_specs=P(("groups", "blocks"), None), check_vma=False
    )
```

```python
import functools
import math

import jax
import jax.numpy as jnp
from jax import lax
from jax.experimental import pallas as pl
from jax.experimental.pallas import tpu as pltpu
from jax.sharding import PartitionSpec as P

HEADS = 32
GY = 8
HD = 16
TAPS = 27
EPSILON = 1e-05
STEPS_X = (-1, -1, -1, 0, 0, 1, 1, 1)
STEPS_Y = (-1, 0, 1, -1, 1, -1, 0, 1)
F32 = jnp.float32
BF16 = jnp.bfloat16
MIB = 1 << 20


def dot(left, right):
    return jnp.dot(left, right, preferred_element_type=F32)


def layer_norm(inputs, gain_vector):
    row_mean = jnp.mean(inputs, axis=-1, keepdims=True)
    centred = inputs - row_mean
    variance = jnp.mean(centred * centred, axis=-1, keepdims=True)
    return centred * lax.rsqrt(variance + EPSILON) * gain_vector


def one_hot(mask):
    return jnp.where(mask, 1.0, 0.0).astype(BF16)


def call(kernel, out_shape, limit, flops, moved, **extra):
    return pl.pallas_call(
        kernel,
        out_shape=out_shape,
        compiler_params=pltpu.CompilerParams(vmem_limit_bytes=limit * MIB),
        cost_estimate=pl.CostEstimate(flops=flops, bytes_accessed=moved, transcendentals=0),
        **extra,
    )


def rows_kernel(flags_ref, units_ref, got_ref, mine_ref, begun_ref):
    count, unit, _ = units_ref.shape
    missing = mine_ref.shape[0] - begun_ref.shape[0]
    kept = [units_ref.at[at] for at in range(0, count, 2)]
    got = [got_ref.at[at] for at in range(count // 2)]
    for core, order in enumerate((kept + got, got + kept)):

        @pl.when(flags_ref[0] == core)
        def _():
            for at, source in enumerate(order):
                mine_ref[at * unit : (at + 1) * unit] = source[...]

    passed = begun_ref.shape[0]
    lent = pl.multiple_of(flags_ref[1] * passed, 16)
    begun_ref[:missing] = mine_ref[pl.ds(lent, missing)]
    begun_ref[missing:] = mine_ref[missing:passed]


def faces_kernel(unit, core_ref, features_ref, rows_ref, own_ref, other_ref, *face_refs):
    points, width = features_ref.shape
    half = width // 2
    place = lax.broadcasted_iota(jnp.int32, (width, width), 1)
    within = lax.rem(place, half)
    source = (within // unit) * (2 * unit) + (place // half) * unit + lax.rem(place, unit)
    channel = lax.broadcasted_iota(jnp.int32, (width, width), 0)
    ordered = dot(features_ref[...], one_hot(channel == source)).astype(BF16)
    first, second = ordered[:, :half], ordered[:, half:]
    even = core_ref[0] == 0
    own_ref[...] = jnp.where(even, first, second)
    other_ref[...] = jnp.where(even, second, first)
    row_ids = lax.broadcasted_iota(jnp.int32, (rows_ref.shape[0], points), 1)
    rows = dot(one_hot(rows_ref[...] == row_ids), ordered).astype(BF16)
    taken = 0
    for ref in face_refs:
        ref[...] = rows[taken : taken + ref.shape[0]]
        taken += ref.shape[0]


def table_kernel(
    flags_ref, own_rows, other_rows, side_ref, behind_ref, ahead_ref, own_ref, other_ref
):
    size = behind_ref.shape[0] // 2
    points, half = own_rows.shape
    lower, even = flags_ref[0] == 1, flags_ref[1] == 0
    own_ref[:points] = own_rows[...]
    other_ref[:points] = other_rows[...]
    across = [ahead_ref[size:], side_ref[size : 2 * size], behind_ref[size:]]
    along = [ahead_ref[:size], behind_ref[:size]]
    for at, (low, high) in enumerate(zip(across + along, along + across)):
        rows = jnp.where(lower, low, high)
        first, second = rows[:, :half], rows[:, half:]
        start = points + at * size
        own_ref[start : start + size] = jnp.where(even, first, second)
        other_ref[start : start + size] = jnp.where(even, second, first)
    rest = jnp.zeros((size, half), BF16)
    own_ref[points + 5 * size :] = rest
    other_ref[points + 5 * size :] = rest


def gather_kernel(taps, start_ref, rows_ref, table_ref, out_ref):
    points, lanes = rows_ref.shape
    height, half = table_ref.shape
    lane = lax.broadcasted_iota(jnp.int32, (points, lanes), 1)
    segments = []
    for first in range(0, height, 256):
        start = first if first < points else first - points + start_ref[0]
        segments.append(
            (first, min(height, first + 256), jnp.asarray(start, jnp.int32).astype(F32))
        )
    places = lax.broadcasted_iota(jnp.int32, (1, 256), 1).astype(F32).astype(BF16)
    one, zero = jnp.ones((), BF16), jnp.zeros((), BF16)
    together = 3
    for base in range(0, taps, together):
        columns = []
        for at in range(base, base + together):
            chosen = lane == taps * pl.program_id(0) + at
            columns.append(jnp.sum(jnp.where(chosen, rows_ref[...], 0.0), axis=1, keepdims=True))
        column = jnp.concatenate(columns, axis=0)
        taken = None
        for first, end, start in segments:
            place = jnp.clip(column - start, -1.0, 256.0).astype(BF16)
            hits = jnp.where(place == places[:, : end - first], one, zero)
            product = dot(hits, table_ref[first:end])
            taken = product if taken is None else taken + product
        taken = taken.astype(BF16)
        for at in range(together):
            column_block = slice((base + at) * half, (base + at + 1) * half)
            out_ref[:, column_block] = taken[at * points : (at + 1) * points]


def gather_block(start, rows, table):
    points, lanes = rows.shape
    height, half = table.shape
    taps = 9
    whole = lambda step: (0, 0)
    return call(
        functools.partial(gather_kernel, taps),
        jax.ShapeDtypeStruct((points, TAPS * half), BF16),
        60,
        2 * TAPS * points * height * half,
        2 * TAPS * points * half,
        grid=(TAPS // taps,),
        in_specs=[
            pl.BlockSpec(memory_space=pltpu.SMEM),
            pl.BlockSpec((points, lanes), whole),
            pl.BlockSpec((height, half), whole),
        ],
        out_specs=pl.BlockSpec((points, taps * half), lambda step: (0, step)),
    )(start, rows, table)


def conv_kernel(slots, later, ready, first, places_ref, shifts_ref, *refs):
    refs = list(refs)

    def take(count):
        taken = refs[:count]
        del refs[:count]
        return taken

    sources = take(1 if ready else 2)
    pieces = take(sum(len(parts) for parts in slots))
    before = [] if first else take(2)
    outs = take(2)
    kept = take(len(later))
    (lhs,) = sources if ready else take(1)
    held, sems = take(2)
    length = held.shape[1]

    def stretch(slot, target, sem):
        column = pl.multiple_of(places_ref[2 * slot], 128)
        copies = [
            pltpu.make_async_copy(
                stacked.at[:, pl.ds(column, length)], target.at[block], sem.at[block]
            )
            for block, stacked in enumerate(sources)
        ]
        for copy in copies:
            copy.start()
        return copies

    copies = []
    for at, parts in enumerate(slots):
        row = pl.multiple_of(places_ref[2 * at + 1], 16)
        copies.append([] if ready else stretch(at, lhs.at[at], sems.at[at]))
        edge = length - sum(size for _, size, _, _ in parts)
        if edge:
            held[at, :edge] = jnp.zeros((edge, held.shape[2]), BF16)
            held[at, length - edge :] = jnp.zeros((edge, held.shape[2]), BF16)
        for part, (start, size, offset, kind) in enumerate(parts):
            moved = row + offset if kind is None else row + shifts_ref[kind]
            place = pl.multiple_of(moved, 16)
            (piece,) = pieces[:1]
            del pieces[:1]
            copy = pltpu.make_async_copy(
                piece.at[pl.ds(start, size)], held.at[at, pl.ds(place, size)], sems.at[at, 2 + part]
            )
            copy.start()
            copies[-1].append(copy)
    extra, slot = [], len(slots)
    for group, count in enumerate(later):
        for place in range(count):
            extra += stretch(slot, kept[group].at[place], sems.at[slot])
            slot += 1
    for at in range(len(slots)):
        for copy in copies[at]:
            copy.wait()
        points = lhs.shape[2]
        products = dot(lhs[at].reshape(2 * points, length), held[at])
        for block, ref in enumerate(outs):
            product = products[block * points : (block + 1) * points]
            if at > 0:
                ref[...] += product
            elif first:
                ref[...] = product
            else:
                ref[...] = (before[block][...] + product).astype(ref.dtype)
    for copy in extra:
        copy.wait()


def conv_part(sources, places, shifts, pieces, before, length, later=(), dtype=F32):
    ready = len(sources) == 1
    points = sources[0].shape[2] if ready else sources[0].shape[0]
    width = pieces[0][0][0].shape[1]
    slots = [[part[1:] for part in parts] for parts in pieces]
    flat = [part[0] for parts in pieces for part in parts]
    held = 2 + len(sources) + len(flat)
    kept = [] if before is None else [block for block in range(2) if block or dtype == F32]
    spec = pl.BlockSpec(memory_space=pl.ANY)
    return call(
        functools.partial(conv_kernel, slots, later, ready, before is None),
        [
            jax.ShapeDtypeStruct((points, width), dtype),
            jax.ShapeDtypeStruct((points, width), F32),
        ]
        + [jax.ShapeDtypeStruct((count, 2, points, length), BF16) for count in later],
        24 if ready else 36,
        4 * points * length * width * len(slots),
        2 * length * (2 * points + width) * len(slots),
        in_specs=[pl.BlockSpec(memory_space=pltpu.SMEM)] * 2
        + [pl.BlockSpec() if ready else spec] * len(sources)
        + [spec] * len(flat)
        + ([] if before is None else [pl.BlockSpec()] * 2),
        input_output_aliases={held + block: block for block in kept},
        scratch_shapes=([] if ready else [pltpu.VMEM((len(slots), 2, points, length), BF16)])
        + [
            pltpu.VMEM((len(slots), length, width), BF16),
            pltpu.SemaphoreType.DMA((len(slots) + sum(later), 5)),
        ],
    )(places, shifts, *sources, *flat, *(before or ()))


def mix_kernel(own_ref, got_ref, features_ref, weight_ref, gain_ref, slot_ref, out_ref):
    convolved = (own_ref[...] + got_ref[...].astype(F32)).astype(BF16)
    linear = dot(convolved, weight_ref[...])
    mixed = (features_ref[...].astype(F32) + layer_norm(linear, gain_ref[...])).astype(BF16)
    slots = lax.broadcasted_iota(jnp.int32, (out_ref.shape[0], mixed.shape[0]), 0)
    out_ref[...] = dot(one_hot(slots == slot_ref[...]), mixed).astype(BF16)


def block_kernel(
    arrived_ref,
    slot_col_ref,
    slot_row_ref,
    attn_gain_ref,
    mlp_gain_ref,
    qv_hbm,
    key_hbm,
    proj_hbm,
    up_hbm,
    down_hbm,
    out_ref,
    qv_ref,
    key_ref,
    proj_ref,
    up_ref,
    down_ref,
    sems,
    serial_ref,
    qv_cols_ref,
    keys_ref,
    heads_ref,
    total_ref,
    scores_ref,
    weights_ref,
):
    sources = (key_hbm, qv_hbm, proj_hbm, up_hbm, down_hbm)
    targets = (key_ref, qv_ref, proj_ref, up_ref, down_ref)
    copies = [
        pltpu.make_async_copy(source, target, sems.at[at])
        for at, (source, target) in enumerate(zip(sources, targets))
    ]
    for copy in copies:
        copy.start()
    slots = arrived_ref.shape[0]
    points, width = serial_ref.shape
    slot_ids = lax.broadcasted_iota(jnp.int32, (points, slots), 1)
    serial = dot(one_hot(slot_col_ref[...] == slot_ids), arrived_ref[...])
    serial_ref[...] = serial
    normed = layer_norm(serial, attn_gain_ref[...]).astype(BF16)
    copies[0].wait()
    keys_ref[...] = dot(normed, key_ref[...]).astype(BF16)
    copies[1].wait()
    factor = math.log2(math.e) / math.sqrt(HD)
    contract_last = (((1,), (1,)), ((), ()))
    qv_cols_ref[:width] = (
        lax.dot_general(qv_ref[:width], normed, contract_last, preferred_element_type=F32) * factor
    ).astype(BF16)
    qv_cols_ref[width:] = lax.dot_general(
        qv_ref[width:], normed, contract_last, preferred_element_type=F32
    ).astype(BF16)
    ones = jnp.ones((HD, points), BF16)
    per_group = 128 // HD
    head_of_row = lax.broadcasted_iota(jnp.int32, (128, points), 0) // HD

    def score(head, slot):
        base = pl.multiple_of(head // per_group * 128, 128)
        group_queries = qv_cols_ref[pl.ds(base, 128)].astype(F32)
        chosen = head_of_row == lax.rem(head, per_group)
        queries = jnp.where(chosen, group_queries, 0.0).astype(BF16)
        scores_ref[slot] = dot(keys_ref[:, pl.ds(base, 128)], queries)

    def weigh(slot):
        scores = scores_ref[slot]
        weights_ref[slot] = jnp.exp2(scores - jnp.max(scores, axis=0, keepdims=True)).astype(BF16)

    def gather(head, slot):
        at = pl.multiple_of(head * HD, HD)
        values = jnp.concatenate([qv_cols_ref[pl.ds(width + at, HD)], ones], axis=0)
        sums = dot(values, weights_ref[slot])
        heads_ref[pl.ds(at, HD)] = (sums[:HD] / sums[HD : HD + 1]).astype(BF16)

    score(0, 0)
    score(1, 1)
    weigh(0)

    def two_heads(pair, carry):
        head = 2 * pair + 1
        for slot in (1, 0):
            score(head + 1, 1 - slot)
            weigh(slot)
            gather(head - 1, 1 - slot)
            head += 1
        return carry

    lax.fori_loop(0, HEADS // 2 - 1, two_heads, 0)
    weigh(1)
    gather(HEADS - 2, 0)
    gather(HEADS - 1, 1)

    for copy in copies[2:]:
        copy.wait()
    update = lax.dot_general(
        heads_ref[...], proj_ref[...], (((0,), (0,)), ((), ())), preferred_element_type=F32
    )
    attended = (serial_ref[...] + update).astype(BF16).astype(F32)
    hidden_in = layer_norm(attended, mlp_gain_ref[...]).astype(BF16)
    total_ref[...] = attended
    chunk = width
    for start in range(0, up_ref.shape[1], chunk):
        raised = dot(hidden_in, up_ref[:, start : start + chunk])
        hidden = (raised * (1.0 + lax.erf(raised * math.sqrt(0.5))) * 0.5).astype(BF16)
        total_ref[...] += dot(hidden, down_ref[start : start + chunk])
    finished = total_ref[...].astype(BF16)
    slot_rows = lax.broadcasted_iota(jnp.int32, (slots, points), 0)
    out_ref[...] = dot(one_hot(slot_rows == slot_row_ref[...]), finished).astype(BF16)


def return_kernel(arrived_ref, slot_ref, out_ref):
    slot_ids = lax.broadcasted_iota(jnp.int32, (out_ref.shape[0], arrived_ref.shape[0]), 1)
    out_ref[...] = dot(one_hot(slot_ref[...] == slot_ids), arrived_ref[...]).astype(BF16)


def face_pairs(devices, dx, dy):
    return [
        (source, source + dx * GY + dy)
        for source in range(devices)
        if 0 <= source // GY + dx < devices // GY and 0 <= source % GY + dy < GY
    ]


def way_round(devices, rows, length):
    chips = devices // 2
    cycle = list(range(0, chips, 2)) + list(range(chips - 1, 0, -2))
    chains = [], []
    places = [None] * devices
    for place, chip in enumerate(cycle):
        for core, way in ((0, 1), (1, -1)):
            me = 2 * chip + core
            for chain, step in zip(chains, (way, -way)):
                chain.append((me, 2 * cycle[(place + step) % chips] + core))
            order = [0]
            for step in range(1, chips // 2):
                order += [-step * way, step * way]
            order.append(chips // 2)
            places[me] = []
            for offset in order:
                start = cycle[(place + offset) % chips] * rows
                column = min(start // 128 * 128, chips * rows - length)
                places[me].append((column, start - column))
    return *chains, places


def padded_taps(neighbours):
    points = neighbours.shape[0]
    own = jnp.arange(points, dtype=jnp.int32)[:, None]
    rest = jnp.zeros((points, 128 - TAPS), jnp.int32)
    middle = TAPS // 2
    rows = jnp.concatenate([neighbours[:, :middle], own, neighbours[:, middle:], rest], axis=1)
    return rows.astype(F32)


def body(
    features,
    conv_weight,
    cpe_weight,
    cpe_gain,
    attn_gain,
    qkv_weight,
    proj_weight,
    mlp_gain,
    up_weight,
    down_weight,
    face_rows,
    neighbours,
    serial_rank,
    serial_order,
):
    points, width = features.shape
    half = width // 2
    devices = lax.axis_size("blocks")
    index = lax.axis_index("blocks")
    core = lax.rem(index, 2)
    partner = [(source, source ^ 1) for source in range(devices)]
    capacity = 2 * points // devices
    slots = devices * capacity

    unit = conv_weight.shape[0] // TAPS
    units = conv_weight.reshape(TAPS, unit, width)
    got = lax.ppermute(units[1::2], "blocks", partner)
    rows = TAPS * unit
    side = lax.axis_index("groups")
    missing = -(-rows // 64) * 16
    passed = rows - missing
    if devices == 2 * GY:
        mine, begun = call(
            rows_kernel,
            [
                jax.ShapeDtypeStruct((rows, width), BF16),
                jax.ShapeDtypeStruct((passed, width), BF16),
            ],
            24,
            0,
            8 * rows * width,
            in_specs=[pl.BlockSpec(memory_space=pltpu.SMEM)] + [pl.BlockSpec()] * 2,
        )(jnp.stack([core, side]).astype(jnp.int32), units, got)
    else:
        kept = units[0::2]
        mine = begun = jnp.where(
            core == 0, jnp.concatenate([kept, got]), jnp.concatenate([got, kept])
        ).reshape(rows, width)

    round_trip = devices == 2 * GY
    lower = index < GY
    if round_trip:
        across = jnp.where(lower, face_rows[0, 5:], face_rows[0, :3])
        face_list = jnp.concatenate([across, face_rows[0, 3:5]]).reshape(-1, 1)
        counts = (3, 1, 1)
    else:
        face_list = face_rows.reshape(-1, 1)
        counts = (1,) * 8
    size = face_rows.shape[2]
    own_local, other_local, *faces = call(
        functools.partial(faces_kernel, unit),
        [jax.ShapeDtypeStruct((points, half), BF16)] * 2
        + [jax.ShapeDtypeStruct((count * size, width), BF16) for count in counts],
        32,
        4 * points * width * width,
        8 * points * width,
        in_specs=[pl.BlockSpec(memory_space=pltpu.SMEM)] + [pl.BlockSpec()] * 2,
    )(core.reshape(1), features, face_list)
    length = -(-(rows + 127) // 128) * 128 if round_trip else rows * (devices // 2)
    first_pairs, second_pairs, places = way_round(devices, rows, length)
    shifts = jnp.stack([side * passed, (1 - side) * passed]).astype(jnp.int32)
    first, second = [begun], [begun]

    def pass_on(*beside):
        if not round_trip:
            return beside
        tied = lax.optimization_barrier((first[-1], second[-1], *beside))
        first[-1], second[-1] = tied[:2]
        last = len(first) == devices // 4
        first.append(lax.ppermute(first[-1], "blocks", first_pairs))
        if not last:
            second.append(lax.ppermute(second[-1], "blocks", second_pairs))
        return tied[2:]

    def complete(*arrived):
        lent = [piece[:missing] for piece in arrived]
        lent = jnp.concatenate(lent) if len(lent) > 1 else lent[0]
        got = lax.ppermute(lent, "groups", [(0, 1), (1, 0)])
        return [
            [
                (piece, 0, missing, 0, 0),
                (piece, missing, passed - missing, missing, None),
                (got, at * missing, missing, 0, 1),
            ]
            for at, piece in enumerate(arrived)
        ]

    if round_trip:
        lists, back_list, on_list = faces
        across = face_pairs(devices, 1, 0) + face_pairs(devices, -1, 0)
        (lists,) = pass_on(lists)
        lists = lax.ppermute(lists, "blocks", across)
        places = jnp.array(places, jnp.int32)[index].reshape(-1)
        lists, sent_neighbours, places = lax.optimization_barrier((lists, neighbours, places))
        other_neighbours = lax.ppermute(sent_neighbours, "blocks", partner)
        to_on = jnp.concatenate([on_list, lists[2 * size :]])
        to_back = jnp.concatenate([back_list, lists[:size]])
        behind = lax.ppermute(to_on, "blocks", face_pairs(devices, 0, 1))
        ahead = lax.ppermute(to_back, "blocks", face_pairs(devices, 0, -1))
        lists, behind, ahead = pass_on(lists, behind, ahead)
        near = complete(first[1], second[1])
        own_table, other_half = call(
            table_kernel,
            [jax.ShapeDtypeStruct((points + 6 * size, half), BF16)] * 2,
            32,
            0,
            20 * size * width,
            in_specs=[pl.BlockSpec(memory_space=pltpu.SMEM)] + [pl.BlockSpec()] * 5,
        )(
            jnp.stack([lower.astype(jnp.int32), core]),
            own_local,
            other_local,
            lists,
            behind,
            ahead,
        )
        start = jnp.where(lower, points, points + 3 * size).reshape(1)
    else:
        other_neighbours = lax.ppermute(neighbours, "blocks", partner)
        received = jnp.concatenate(
            [
                lax.ppermute(faces[k], "blocks", face_pairs(devices, STEPS_X[k], STEPS_Y[k]))
                for k in range(8)
            ]
        )
        shape = (received.shape[0], half)
        own_table = jnp.concatenate(
            [own_local, lax.dynamic_slice(received, (0, core * half), shape)]
        )
        other_half = jnp.concatenate(
            [other_local, lax.dynamic_slice(received, (0, (1 - core) * half), shape)]
        )
        start = jnp.full((1,), points, jnp.int32)
    other_table = lax.ppermute(other_half, "blocks", partner)
    own_stacked = gather_block(start, padded_taps(neighbours), own_table)
    other_rows = padded_taps(other_neighbours)
    own_stacked, other_rows, other_table = pass_on(own_stacked, other_rows, other_table)
    if round_trip:
        middle = complete(first[2], second[2])
    other_stacked = gather_block(start, other_rows, other_table)
    stacked = other_stacked, own_stacked
    if round_trip:
        *stacked, middle_got = pass_on(*stacked, middle[0][2][0])
        middle = [[*parts[:2], (middle_got, *parts[2][1:])] for parts in middle]
        early = [[(mine, 0, rows, 0, None)]] + near
        *sums, middle_lhs, far_lhs, last_lhs = conv_part(
            stacked, places, shifts, early, None, length, (2, 2, 1)
        )
        far = complete(first[3], second[3])
        opposite = complete(first[4])
        sums = conv_part([middle_lhs], places[6:10], shifts, middle, sums, length)
        sums = conv_part([far_lhs], places[10:14], shifts, far, sums, length)
        for_partner, own_part = conv_part(
            [last_lhs], places[14:], shifts, opposite, sums, length, dtype=BF16
        )
    else:
        groups = [list(range(core, devices, 2)) for core in range(2)]
        weight = lax.all_gather(mine, "blocks", axis=0, tiled=True, axis_index_groups=groups)
        nowhere = jnp.zeros((2,), jnp.int32)
        whole = [[(weight, 0, weight.shape[0], 0, None)]]
        for_partner, own_part = conv_part(stacked, nowhere, shifts, whole, None, length)

    positions = jnp.arange(points, dtype=jnp.int32)
    target = serial_rank // points
    earlier = (target[None, :] == target[:, None]) & (serial_rank[None, :] < serial_rank[:, None])
    out_slot = target * capacity + jnp.sum(earlier.astype(jnp.int32), axis=1)
    anchor = serial_order // points
    before = (anchor[None, :] == anchor[:, None]) & (positions[None, :] < positions[:, None])
    in_slot = anchor * capacity + jnp.sum(before.astype(jnp.int32), axis=1)

    from_partner = lax.ppermute(for_partner, "blocks", partner)

    outgoing = call(
        mix_kernel,
        jax.ShapeDtypeStruct((slots, width), BF16),
        32,
        2 * points * width * (width + slots),
        8 * points * width,
    )(
        own_part,
        from_partner,
        features,
        cpe_weight,
        cpe_gain.reshape(1, width),
        out_slot.reshape(1, points),
    )
    arrived = lax.all_to_all(
        outgoing.reshape(devices, capacity, width), "blocks", split_axis=0, concat_axis=0, tiled=True
    ).reshape(slots, width)

    key_weight = qkv_weight[:, width : 2 * width]
    qv_weight = jnp.concatenate([qkv_weight[:, :width], qkv_weight[:, 2 * width :]], axis=1).T
    weights = (qv_weight, key_weight, proj_weight, up_weight, down_weight)
    back = call(
        block_kernel,
        jax.ShapeDtypeStruct((slots, width), BF16),
        60,
        20 * points * width * width,
        16 * width * width,
        in_specs=[pl.BlockSpec()] * 5 + [pl.BlockSpec(memory_space=pl.ANY)] * len(weights),
        scratch_shapes=[pltpu.VMEM(weight.shape, BF16) for weight in weights]
        + [
            pltpu.SemaphoreType.DMA((len(weights),)),
            pltpu.VMEM((points, width), F32),
            pltpu.VMEM((2 * width, points), BF16),
            pltpu.VMEM((points, width), BF16),
            pltpu.VMEM((width, points), BF16),
            pltpu.VMEM((points, width), F32),
            pltpu.VMEM((2, points, points), F32),
            pltpu.VMEM((2, points, points), BF16),
        ],
    )(
        arrived,
        in_slot.reshape(points, 1),
        in_slot.reshape(1, points),
        attn_gain.reshape(1, width),
        mlp_gain.reshape(1, width),
        *weights,
    )
    returned = lax.all_to_all(
        back.reshape(devices, capacity, width), "blocks", split_axis=0, concat_axis=0, tiled=True
    ).reshape(slots, width)
    return call(
        return_kernel,
        jax.ShapeDtypeStruct((points, width), BF16),
        32,
        2 * points * slots * width,
        6 * points * width,
    )(returned, out_slot.reshape(points, 1))


def solution(mesh):
    placed = (
        P(("groups", "blocks"), None),
        P("blocks", None),
        P(),
        P(),
        P(),
        P(),
        P(),
        P(),
        P(),
        P(),
        P(("groups", "blocks"), None, None),
        P(("groups", "blocks"), None),
        P(("groups", "blocks")),
        P(("groups", "blocks")),
    )
    return jax.shard_map(
        body, mesh=mesh, in_specs=placed, out_specs=P(("groups", "blocks"), None), check_vma=False
    )
```

```python
import functools
import math

import jax
import jax.numpy as jnp
from jax import lax
from jax.experimental import pallas as pl
from jax.experimental.pallas import tpu as pltpu
from jax.sharding import PartitionSpec as P

HEADS = 32
GY = 8
HD = 16
TAPS = 27
EPSILON = 1e-05
STEPS_X = (-1, -1, -1, 0, 0, 1, 1, 1)
STEPS_Y = (-1, 0, 1, -1, 1, -1, 0, 1)
F32 = jnp.float32
BF16 = jnp.bfloat16
MIB = 1 << 20
GATHER_LIMIT, CONV_LIMIT = 24, 24


def dot(left, right):
    return jnp.dot(left, right, preferred_element_type=F32)


def layer_norm(inputs, gain_vector):
    row_mean = jnp.mean(inputs, axis=-1, keepdims=True)
    centred = inputs - row_mean
    variance = jnp.mean(centred * centred, axis=-1, keepdims=True)
    return centred * lax.rsqrt(variance + EPSILON) * gain_vector


def one_hot(mask):
    return jnp.where(mask, 1.0, 0.0).astype(BF16)


def call(kernel, out_shape, limit, flops, moved, **extra):
    return pl.pallas_call(
        kernel,
        out_shape=out_shape,
        compiler_params=pltpu.CompilerParams(vmem_limit_bytes=limit * MIB),
        cost_estimate=pl.CostEstimate(flops=flops, bytes_accessed=moved, transcendentals=0),
        **extra,
    )


def rows_kernel(flags_ref, units_ref, got_ref, mine_ref, begun_ref):
    count, unit, _ = units_ref.shape
    missing = mine_ref.shape[0] - begun_ref.shape[0]
    kept = [units_ref.at[at] for at in range(0, count, 2)]
    got = [got_ref.at[at] for at in range(count // 2)]
    for core, order in enumerate((kept + got, got + kept)):

        @pl.when(flags_ref[0] == core)
        def _():
            for at, source in enumerate(order):
                mine_ref[at * unit : (at + 1) * unit] = source[...]

    passed = begun_ref.shape[0]
    lent = pl.multiple_of(flags_ref[1] * passed, 16)
    begun_ref[:missing] = mine_ref[pl.ds(lent, missing)]
    begun_ref[missing:] = mine_ref[missing:passed]


def faces_kernel(unit, core_ref, features_ref, rows_ref, own_ref, other_ref, *face_refs):
    points, width = features_ref.shape
    half = width // 2
    place = lax.broadcasted_iota(jnp.int32, (width, width), 1)
    within = lax.rem(place, half)
    source = (within // unit) * (2 * unit) + (place // half) * unit + lax.rem(place, unit)
    channel = lax.broadcasted_iota(jnp.int32, (width, width), 0)
    ordered = dot(features_ref[...], one_hot(channel == source)).astype(BF16)
    first, second = ordered[:, :half], ordered[:, half:]
    even = core_ref[0] == 0
    own_ref[...] = jnp.where(even, first, second)
    other_ref[...] = jnp.where(even, second, first)
    row_ids = lax.broadcasted_iota(jnp.int32, (rows_ref.shape[0], points), 1)
    rows = dot(one_hot(rows_ref[...] == row_ids), ordered).astype(BF16)
    taken = 0
    for ref in face_refs:
        ref[...] = rows[taken : taken + ref.shape[0]]
        taken += ref.shape[0]


def table_kernel(
    flags_ref, own_rows, other_rows, side_ref, behind_ref, ahead_ref, own_ref, other_ref
):
    size = behind_ref.shape[0] // 2
    points, half = own_rows.shape
    lower, even = flags_ref[0] == 1, flags_ref[1] == 0
    own_ref[:points] = own_rows[...]
    other_ref[:points] = other_rows[...]
    across = [ahead_ref[size:], side_ref[size : 2 * size], behind_ref[size:]]
    along = [ahead_ref[:size], behind_ref[:size]]
    for at, (low, high) in enumerate(zip(across + along, along + across)):
        rows = jnp.where(lower, low, high)
        first, second = rows[:, :half], rows[:, half:]
        start = points + at * size
        own_ref[start : start + size] = jnp.where(even, first, second)
        other_ref[start : start + size] = jnp.where(even, second, first)
    rest = jnp.zeros((size, half), BF16)
    own_ref[points + 5 * size :] = rest
    other_ref[points + 5 * size :] = rest


def gather_kernel(taps, start_ref, rows_ref, table_ref, out_ref):
    points, lanes = rows_ref.shape
    height, half = table_ref.shape
    lane = lax.broadcasted_iota(jnp.int32, (points, lanes), 1)
    segments = []
    for first in range(0, height, 256):
        start = first if first < points else first - points + start_ref[0]
        segments.append(
            (first, min(height, first + 256), jnp.asarray(start, jnp.int32).astype(F32))
        )
    places = lax.broadcasted_iota(jnp.int32, (1, 256), 1).astype(F32).astype(BF16)
    one, zero = jnp.ones((), BF16), jnp.zeros((), BF16)
    for at in range(taps):
        chosen = lane == taps * pl.program_id(0) + at
        column = jnp.sum(jnp.where(chosen, rows_ref[...], 0.0), axis=1, keepdims=True)
        taken = None
        for first, end, start in segments:
            place = jnp.clip(column - start, -1.0, 256.0).astype(BF16)
            hits = jnp.where(place == places[:, : end - first], one, zero)
            product = dot(hits, table_ref[first:end])
            taken = product if taken is None else taken + product
        out_ref[:, at * half : (at + 1) * half] = taken.astype(BF16)


def gather_block(start, rows, table):
    points, lanes = rows.shape
    height, half = table.shape
    taps = 9
    whole = lambda step: (0, 0)
    return call(
        functools.partial(gather_kernel, taps),
        jax.ShapeDtypeStruct((points, TAPS * half), BF16),
        GATHER_LIMIT,
        2 * TAPS * points * height * half,
        2 * TAPS * points * half,
        grid=(TAPS // taps,),
        in_specs=[
            pl.BlockSpec(memory_space=pltpu.SMEM),
            pl.BlockSpec((points, lanes), whole),
            pl.BlockSpec((height, half), whole),
        ],
        out_specs=pl.BlockSpec((points, taps * half), lambda step: (0, step)),
    )(start, rows, table)


def conv_kernel(slots, first, places_ref, shifts_ref, *refs):
    refs = list(refs)

    def take(count):
        taken = refs[:count]
        del refs[:count]
        return taken

    stacked = take(2)
    pieces = take(sum(len(parts) for parts in slots))
    before = [] if first else take(2)
    outs = take(2)
    held, sems = refs
    length = held.shape[1]
    copies = []
    for at, parts in enumerate(slots):
        row = pl.multiple_of(places_ref[2 * at + 1], 16)
        copies.append([])
        edge = length - sum(size for _, size, _, _ in parts)
        if edge:
            held[at, :edge] = jnp.zeros((edge, held.shape[2]), BF16)
            held[at, length - edge :] = jnp.zeros((edge, held.shape[2]), BF16)
        for part, (start, size, offset, kind) in enumerate(parts):
            moved = row + offset if kind is None else row + shifts_ref[kind]
            place = pl.multiple_of(moved, 16)
            (piece,) = pieces[:1]
            del pieces[:1]
            copy = pltpu.make_async_copy(
                piece.at[pl.ds(start, size)], held.at[at, pl.ds(place, size)], sems.at[at, part]
            )
            copy.start()
            copies[-1].append(copy)
    for at in range(len(slots)):
        for copy in copies[at]:
            copy.wait()
        column = pl.multiple_of(places_ref[2 * at], 128)
        for block, ref in enumerate(outs):
            product = dot(stacked[block][:, pl.ds(column, length)], held[at])
            if at > 0:
                ref[...] += product
            elif first:
                ref[...] = product
            else:
                ref[...] = (before[block][...] + product).astype(ref.dtype)


def conv_part(stacked, places, shifts, pieces, before, length, limit, dtype=F32):
    points = stacked[0].shape[0]
    width = pieces[0][0][0].shape[1]
    slots = [[part[1:] for part in parts] for parts in pieces]
    flat = [part[0] for parts in pieces for part in parts]
    held = 4 + len(flat)
    kept = [] if before is None else [block for block in range(2) if block or dtype == F32]
    return call(
        functools.partial(conv_kernel, slots, before is None),
        [
            jax.ShapeDtypeStruct((points, width), dtype),
            jax.ShapeDtypeStruct((points, width), F32),
        ],
        limit,
        4 * points * length * width * len(slots),
        2 * length * (2 * points + width) * len(slots),
        in_specs=[pl.BlockSpec(memory_space=pltpu.SMEM)] * 2
        + [pl.BlockSpec()] * 2
        + [pl.BlockSpec(memory_space=pl.ANY)] * len(flat)
        + ([] if before is None else [pl.BlockSpec()] * 2),
        input_output_aliases={held + block: block for block in kept},
        scratch_shapes=[
            pltpu.VMEM((len(slots), length, width), BF16),
            pltpu.SemaphoreType.DMA((len(slots), 3)),
        ],
    )(places, shifts, *stacked, *flat, *(before or ()))


def mix_kernel(own_ref, got_ref, features_ref, weight_ref, gain_ref, slot_ref, out_ref):
    convolved = (own_ref[...] + got_ref[...].astype(F32)).astype(BF16)
    linear = dot(convolved, weight_ref[...])
    mixed = (features_ref[...].astype(F32) + layer_norm(linear, gain_ref[...])).astype(BF16)
    slots = lax.broadcasted_iota(jnp.int32, (out_ref.shape[0], mixed.shape[0]), 0)
    out_ref[...] = dot(one_hot(slots == slot_ref[...]), mixed).astype(BF16)


def block_kernel(
    arrived_ref,
    slot_col_ref,
    slot_row_ref,
    attn_gain_ref,
    mlp_gain_ref,
    qv_hbm,
    key_hbm,
    proj_hbm,
    up_hbm,
    down_hbm,
    out_ref,
    qv_ref,
    key_ref,
    proj_ref,
    up_ref,
    down_ref,
    sems,
    serial_ref,
    qv_cols_ref,
    keys_ref,
    heads_ref,
    total_ref,
    scores_ref,
    weights_ref,
):
    sources = (key_hbm, qv_hbm, proj_hbm, up_hbm, down_hbm)
    targets = (key_ref, qv_ref, proj_ref, up_ref, down_ref)
    copies = [
        pltpu.make_async_copy(source, target, sems.at[at])
        for at, (source, target) in enumerate(zip(sources, targets))
    ]
    for copy in copies:
        copy.start()
    slots = arrived_ref.shape[0]
    points, width = serial_ref.shape
    slot_ids = lax.broadcasted_iota(jnp.int32, (points, slots), 1)
    serial = dot(one_hot(slot_col_ref[...] == slot_ids), arrived_ref[...])
    serial_ref[...] = serial
    normed = layer_norm(serial, attn_gain_ref[...]).astype(BF16)
    copies[0].wait()
    keys_ref[...] = dot(normed, key_ref[...]).astype(BF16)
    copies[1].wait()
    factor = math.log2(math.e) / math.sqrt(HD)
    contract_last = (((1,), (1,)), ((), ()))
    qv_cols_ref[:width] = (
        lax.dot_general(qv_ref[:width], normed, contract_last, preferred_element_type=F32) * factor
    ).astype(BF16)
    qv_cols_ref[width:] = lax.dot_general(
        qv_ref[width:], normed, contract_last, preferred_element_type=F32
    ).astype(BF16)
    ones = jnp.ones((HD, points), BF16)
    per_group = 128 // HD
    head_of_row = lax.broadcasted_iota(jnp.int32, (128, points), 0) // HD

    def score(head, slot):
        base = pl.multiple_of(head // per_group * 128, 128)
        group_queries = qv_cols_ref[pl.ds(base, 128)].astype(F32)
        chosen = head_of_row == lax.rem(head, per_group)
        queries = jnp.where(chosen, group_queries, 0.0).astype(BF16)
        scores_ref[slot] = dot(keys_ref[:, pl.ds(base, 128)], queries)

    def weigh(slot):
        scores = scores_ref[slot]
        weights_ref[slot] = jnp.exp2(scores - jnp.max(scores, axis=0, keepdims=True)).astype(BF16)

    def gather(head, slot):
        at = pl.multiple_of(head * HD, HD)
        values = jnp.concatenate([qv_cols_ref[pl.ds(width + at, HD)], ones], axis=0)
        sums = dot(values, weights_ref[slot])
        heads_ref[pl.ds(at, HD)] = (sums[:HD] / sums[HD : HD + 1]).astype(BF16)

    score(0, 0)
    score(1, 1)
    weigh(0)

    def two_heads(pair, carry):
        head = 2 * pair + 1
        for slot in (1, 0):
            score(head + 1, 1 - slot)
            weigh(slot)
            gather(head - 1, 1 - slot)
            head += 1
        return carry

    lax.fori_loop(0, HEADS // 2 - 1, two_heads, 0)
    weigh(1)
    gather(HEADS - 2, 0)
    gather(HEADS - 1, 1)

    for copy in copies[2:]:
        copy.wait()
    update = lax.dot_general(
        heads_ref[...], proj_ref[...], (((0,), (0,)), ((), ())), preferred_element_type=F32
    )
    attended = (serial_ref[...] + update).astype(BF16).astype(F32)
    hidden_in = layer_norm(attended, mlp_gain_ref[...]).astype(BF16)
    total_ref[...] = attended
    chunk = width
    for start in range(0, up_ref.shape[1], chunk):
        raised = dot(hidden_in, up_ref[:, start : start + chunk])
        hidden = (raised * (1.0 + lax.erf(raised * math.sqrt(0.5))) * 0.5).astype(BF16)
        total_ref[...] += dot(hidden, down_ref[start : start + chunk])
    finished = total_ref[...].astype(BF16)
    slot_rows = lax.broadcasted_iota(jnp.int32, (slots, points), 0)
    out_ref[...] = dot(one_hot(slot_rows == slot_row_ref[...]), finished).astype(BF16)


def return_kernel(arrived_ref, slot_ref, out_ref):
    slot_ids = lax.broadcasted_iota(jnp.int32, (out_ref.shape[0], arrived_ref.shape[0]), 1)
    out_ref[...] = dot(one_hot(slot_ref[...] == slot_ids), arrived_ref[...]).astype(BF16)


def face_pairs(devices, dx, dy):
    return [
        (source, source + dx * GY + dy)
        for source in range(devices)
        if 0 <= source // GY + dx < devices // GY and 0 <= source % GY + dy < GY
    ]


def way_round(devices, rows, length):
    chips = devices // 2
    cycle = list(range(0, chips, 2)) + list(range(chips - 1, 0, -2))
    chains = [], []
    places = [None] * devices
    for place, chip in enumerate(cycle):
        for core, way in ((0, 1), (1, -1)):
            me = 2 * chip + core
            for chain, step in zip(chains, (way, -way)):
                chain.append((me, 2 * cycle[(place + step) % chips] + core))
            order = [0]
            for step in range(1, chips // 2):
                order += [-step * way, step * way]
            order.append(chips // 2)
            places[me] = []
            for offset in order:
                start = cycle[(place + offset) % chips] * rows
                column = min(start // 128 * 128, chips * rows - length)
                places[me].append((column, start - column))
    return *chains, places


def padded_taps(neighbours):
    points = neighbours.shape[0]
    own = jnp.arange(points, dtype=jnp.int32)[:, None]
    rest = jnp.zeros((points, 128 - TAPS), jnp.int32)
    middle = TAPS // 2
    rows = jnp.concatenate([neighbours[:, :middle], own, neighbours[:, middle:], rest], axis=1)
    return rows.astype(F32)


def body(
    features,
    conv_weight,
    cpe_weight,
    cpe_gain,
    attn_gain,
    qkv_weight,
    proj_weight,
    mlp_gain,
    up_weight,
    down_weight,
    face_rows,
    neighbours,
    serial_rank,
    serial_order,
):
    points, width = features.shape
    half = width // 2
    devices = lax.axis_size("blocks")
    index = lax.axis_index("blocks")
    core = lax.rem(index, 2)
    partner = [(source, source ^ 1) for source in range(devices)]
    capacity = 2 * points // devices
    slots = devices * capacity

    unit = conv_weight.shape[0] // TAPS
    units = conv_weight.reshape(TAPS, unit, width)
    got = lax.ppermute(units[1::2], "blocks", partner)
    rows = TAPS * unit
    side = lax.axis_index("groups")
    missing = -(-rows // 64) * 16
    passed = rows - missing
    if devices == 2 * GY:
        mine, begun = call(
            rows_kernel,
            [
                jax.ShapeDtypeStruct((rows, width), BF16),
                jax.ShapeDtypeStruct((passed, width), BF16),
            ],
            24,
            0,
            8 * rows * width,
            in_specs=[pl.BlockSpec(memory_space=pltpu.SMEM)] + [pl.BlockSpec()] * 2,
        )(jnp.stack([core, side]).astype(jnp.int32), units, got)
    else:
        kept = units[0::2]
        mine = begun = jnp.where(
            core == 0, jnp.concatenate([kept, got]), jnp.concatenate([got, kept])
        ).reshape(rows, width)

    round_trip = devices == 2 * GY
    lower = index < GY
    if round_trip:
        across = jnp.where(lower, face_rows[0, 5:], face_rows[0, :3])
        face_list = jnp.concatenate([across, face_rows[0, 3:5]]).reshape(-1, 1)
        counts = (3, 1, 1)
    else:
        face_list = face_rows.reshape(-1, 1)
        counts = (1,) * 8
    size = face_rows.shape[2]
    own_local, other_local, *faces = call(
        functools.partial(faces_kernel, unit),
        [jax.ShapeDtypeStruct((points, half), BF16)] * 2
        + [jax.ShapeDtypeStruct((count * size, width), BF16) for count in counts],
        32,
        4 * points * width * width,
        8 * points * width,
        in_specs=[pl.BlockSpec(memory_space=pltpu.SMEM)] + [pl.BlockSpec()] * 2,
    )(core.reshape(1), features, face_list)
    length = -(-(rows + 127) // 128) * 128 if round_trip else rows * (devices // 2)
    first_pairs, second_pairs, places = way_round(devices, rows, length)
    shifts = jnp.stack([side * passed, (1 - side) * passed]).astype(jnp.int32)
    first, second = [begun], [begun]

    def pass_on(*beside):
        if not round_trip:
            return beside
        tied = lax.optimization_barrier((first[-1], second[-1], *beside))
        first[-1], second[-1] = tied[:2]
        last = len(first) == devices // 4
        first.append(lax.ppermute(first[-1], "blocks", first_pairs))
        if not last:
            second.append(lax.ppermute(second[-1], "blocks", second_pairs))
        return tied[2:]

    def complete(*arrived):
        lent = [piece[:missing] for piece in arrived]
        lent = jnp.concatenate(lent) if len(lent) > 1 else lent[0]
        got = lax.ppermute(lent, "groups", [(0, 1), (1, 0)])
        return [
            [
                (piece, 0, missing, 0, 0),
                (piece, missing, passed - missing, missing, None),
                (got, at * missing, missing, 0, 1),
            ]
            for at, piece in enumerate(arrived)
        ]

    if round_trip:
        lists, back_list, on_list = faces
        across = face_pairs(devices, 1, 0) + face_pairs(devices, -1, 0)
        (lists,) = pass_on(lists)
        lists = lax.ppermute(lists, "blocks", across)
        places = jnp.array(places, jnp.int32)[index].reshape(-1)
        lists, sent_neighbours, places = lax.optimization_barrier((lists, neighbours, places))
        other_neighbours = lax.ppermute(sent_neighbours, "blocks", partner)
        to_on = jnp.concatenate([on_list, lists[2 * size :]])
        to_back = jnp.concatenate([back_list, lists[:size]])
        behind = lax.ppermute(to_on, "blocks", face_pairs(devices, 0, 1))
        ahead = lax.ppermute(to_back, "blocks", face_pairs(devices, 0, -1))
        lists, behind, ahead = pass_on(lists, behind, ahead)
        near = complete(first[1], second[1])
        own_table, other_half = call(
            table_kernel,
            [jax.ShapeDtypeStruct((points + 6 * size, half), BF16)] * 2,
            32,
            0,
            20 * size * width,
            in_specs=[pl.BlockSpec(memory_space=pltpu.SMEM)] + [pl.BlockSpec()] * 5,
        )(
            jnp.stack([lower.astype(jnp.int32), core]),
            own_local,
            other_local,
            lists,
            behind,
            ahead,
        )
        start = jnp.where(lower, points, points + 3 * size).reshape(1)
    else:
        other_neighbours = lax.ppermute(neighbours, "blocks", partner)
        received = jnp.concatenate(
            [
                lax.ppermute(faces[k], "blocks", face_pairs(devices, STEPS_X[k], STEPS_Y[k]))
                for k in range(8)
            ]
        )
        shape = (received.shape[0], half)
        own_table = jnp.concatenate(
            [own_local, lax.dynamic_slice(received, (0, core * half), shape)]
        )
        other_half = jnp.concatenate(
            [other_local, lax.dynamic_slice(received, (0, (1 - core) * half), shape)]
        )
        start = jnp.full((1,), points, jnp.int32)
    other_table = lax.ppermute(other_half, "blocks", partner)
    own_stacked = gather_block(start, padded_taps(neighbours), own_table)
    other_rows = padded_taps(other_neighbours)
    own_stacked, other_rows, other_table = pass_on(own_stacked, other_rows, other_table)
    if round_trip:
        middle = complete(first[2], second[2])
    other_stacked = gather_block(start, other_rows, other_table)
    stacked = other_stacked, own_stacked
    if round_trip:
        *stacked, middle_got = pass_on(*stacked, middle[0][2][0])
        middle = [[*parts[:2], (middle_got, *parts[2][1:])] for parts in middle]
        early = [[(mine, 0, rows, 0, None)]] + near
        sums = conv_part(stacked, places[:6], shifts, early, None, length, CONV_LIMIT)
        far = complete(first[3], second[3])
        opposite = complete(first[4])
        sums = conv_part(stacked, places[6:10], shifts, middle, sums, length, CONV_LIMIT)
        sums = conv_part(stacked, places[10:14], shifts, far, sums, length, CONV_LIMIT)
        for_partner, own_part = conv_part(
            stacked, places[14:], shifts, opposite, sums, length, CONV_LIMIT, BF16
        )
    else:
        groups = [list(range(core, devices, 2)) for core in range(2)]
        weight = lax.all_gather(mine, "blocks", axis=0, tiled=True, axis_index_groups=groups)
        nowhere = jnp.zeros((2,), jnp.int32)
        whole = [[(weight, 0, weight.shape[0], 0, None)]]
        for_partner, own_part = conv_part(stacked, nowhere, shifts, whole, None, length, 48)

    positions = jnp.arange(points, dtype=jnp.int32)
    target = serial_rank // points
    earlier = (target[None, :] == target[:, None]) & (serial_rank[None, :] < serial_rank[:, None])
    out_slot = target * capacity + jnp.sum(earlier.astype(jnp.int32), axis=1)
    anchor = serial_order // points
    before = (anchor[None, :] == anchor[:, None]) & (positions[None, :] < positions[:, None])
    in_slot = anchor * capacity + jnp.sum(before.astype(jnp.int32), axis=1)

    from_partner = lax.ppermute(for_partner, "blocks", partner)

    outgoing = call(
        mix_kernel,
        jax.ShapeDtypeStruct((slots, width), BF16),
        32,
        2 * points * width * (width + slots),
        8 * points * width,
    )(
        own_part,
        from_partner,
        features,
        cpe_weight,
        cpe_gain.reshape(1, width),
        out_slot.reshape(1, points),
    )
    arrived = lax.all_to_all(
        outgoing.reshape(devices, capacity, width), "blocks", split_axis=0, concat_axis=0, tiled=True
    ).reshape(slots, width)

    key_weight = qkv_weight[:, width : 2 * width]
    qv_weight = jnp.concatenate([qkv_weight[:, :width], qkv_weight[:, 2 * width :]], axis=1).T
    weights = (qv_weight, key_weight, proj_weight, up_weight, down_weight)
    back = call(
        block_kernel,
        jax.ShapeDtypeStruct((slots, width), BF16),
        60,
        20 * points * width * width,
        16 * width * width,
        in_specs=[pl.BlockSpec()] * 5 + [pl.BlockSpec(memory_space=pl.ANY)] * len(weights),
        scratch_shapes=[pltpu.VMEM(weight.shape, BF16) for weight in weights]
        + [
            pltpu.SemaphoreType.DMA((len(weights),)),
            pltpu.VMEM((points, width), F32),
            pltpu.VMEM((2 * width, points), BF16),
            pltpu.VMEM((points, width), BF16),
            pltpu.VMEM((width, points), BF16),
            pltpu.VMEM((points, width), F32),
            pltpu.VMEM((2, points, points), F32),
            pltpu.VMEM((2, points, points), BF16),
        ],
    )(
        arrived,
        in_slot.reshape(points, 1),
        in_slot.reshape(1, points),
        attn_gain.reshape(1, width),
        mlp_gain.reshape(1, width),
        *weights,
    )
    returned = lax.all_to_all(
        back.reshape(devices, capacity, width), "blocks", split_axis=0, concat_axis=0, tiled=True
    ).reshape(slots, width)
    return call(
        return_kernel,
        jax.ShapeDtypeStruct((points, width), BF16),
        32,
        2 * points * slots * width,
        6 * points * width,
    )(returned, out_slot.reshape(points, 1))


def solution(mesh):
    placed = (
        P(("groups", "blocks"), None),
        P("blocks", None),
        P(),
        P(),
        P(),
        P(),
        P(),
        P(),
        P(),
        P(),
        P(("groups", "blocks"), None, None),
        P(("groups", "blocks"), None),
        P(("groups", "blocks")),
        P(("groups", "blocks")),
    )
    return jax.shard_map(
        body, mesh=mesh, in_specs=placed, out_specs=P(("groups", "blocks"), None), check_vma=False
    )
```

```python
import functools
import math

import jax
import jax.numpy as jnp
from jax import lax
from jax.experimental import pallas as pl
from jax.experimental.pallas import tpu as pltpu
from jax.sharding import PartitionSpec as P

HEADS = 32
GY = 8
HD = 16
TAPS = 27
EPSILON = 1e-05
STEPS_X = (-1, -1, -1, 0, 0, 1, 1, 1)
STEPS_Y = (-1, 0, 1, -1, 1, -1, 0, 1)
F32 = jnp.float32
BF16 = jnp.bfloat16
MIB = 1 << 20
GATHER_LIMIT, CONV_LIMIT = 24, 24


def dot(left, right):
    return jnp.dot(left, right, preferred_element_type=F32)


def layer_norm(inputs, gain_vector):
    row_mean = jnp.mean(inputs, axis=-1, keepdims=True)
    centred = inputs - row_mean
    variance = jnp.mean(centred * centred, axis=-1, keepdims=True)
    return centred * lax.rsqrt(variance + EPSILON) * gain_vector


def one_hot(mask):
    return jnp.where(mask, 1.0, 0.0).astype(BF16)


def call(kernel, out_shape, limit, flops, moved, **extra):
    return pl.pallas_call(
        kernel,
        out_shape=out_shape,
        compiler_params=pltpu.CompilerParams(vmem_limit_bytes=limit * MIB),
        cost_estimate=pl.CostEstimate(flops=flops, bytes_accessed=moved, transcendentals=0),
        **extra,
    )


def rows_kernel(flags_ref, units_ref, got_ref, mine_ref, begun_ref):
    count, unit, _ = units_ref.shape
    missing = mine_ref.shape[0] - begun_ref.shape[0]
    kept = [units_ref.at[at] for at in range(0, count, 2)]
    got = [got_ref.at[at] for at in range(count // 2)]
    for core, order in enumerate((kept + got, got + kept)):

        @pl.when(flags_ref[0] == core)
        def _():
            for at, source in enumerate(order):
                mine_ref[at * unit : (at + 1) * unit] = source[...]

    passed = begun_ref.shape[0]
    lent = pl.multiple_of(flags_ref[1] * passed, 16)
    begun_ref[:missing] = mine_ref[pl.ds(lent, missing)]
    begun_ref[missing:] = mine_ref[missing:passed]


def faces_kernel(unit, core_ref, features_ref, rows_ref, own_ref, other_ref, *face_refs):
    points, width = features_ref.shape
    half = width // 2
    place = lax.broadcasted_iota(jnp.int32, (width, width), 1)
    within = lax.rem(place, half)
    source = (within // unit) * (2 * unit) + (place // half) * unit + lax.rem(place, unit)
    channel = lax.broadcasted_iota(jnp.int32, (width, width), 0)
    ordered = dot(features_ref[...], one_hot(channel == source)).astype(BF16)
    first, second = ordered[:, :half], ordered[:, half:]
    even = core_ref[0] == 0
    own_ref[...] = jnp.where(even, first, second)
    other_ref[...] = jnp.where(even, second, first)
    row_ids = lax.broadcasted_iota(jnp.int32, (rows_ref.shape[0], points), 1)
    rows = dot(one_hot(rows_ref[...] == row_ids), ordered).astype(BF16)
    taken = 0
    for ref in face_refs:
        ref[...] = rows[taken : taken + ref.shape[0]]
        taken += ref.shape[0]


def table_kernel(
    flags_ref, own_rows, other_rows, side_ref, behind_ref, ahead_ref, own_ref, other_ref
):
    size = behind_ref.shape[0] // 2
    points, half = own_rows.shape
    lower, even = flags_ref[0] == 1, flags_ref[1] == 0
    own_ref[:points] = own_rows[...]
    other_ref[:points] = other_rows[...]
    across = [ahead_ref[size:], side_ref[size : 2 * size], behind_ref[size:]]
    along = [ahead_ref[:size], behind_ref[:size]]
    for at, (low, high) in enumerate(zip(across + along, along + across)):
        rows = jnp.where(lower, low, high)
        first, second = rows[:, :half], rows[:, half:]
        start = points + at * size
        own_ref[start : start + size] = jnp.where(even, first, second)
        other_ref[start : start + size] = jnp.where(even, second, first)
    rest = jnp.zeros((size, half), BF16)
    own_ref[points + 5 * size :] = rest
    other_ref[points + 5 * size :] = rest


def gather_kernel(taps, start_ref, rows_ref, table_ref, out_ref):
    points, lanes = rows_ref.shape
    height, half = table_ref.shape
    lane = lax.broadcasted_iota(jnp.int32, (points, lanes), 1)
    segments = []
    for first in range(0, height, 256):
        start = first if first < points else first - points + start_ref[0]
        segments.append(
            (first, min(height, first + 256), jnp.asarray(start, jnp.int32).astype(F32))
        )
    places = lax.broadcasted_iota(jnp.int32, (1, 256), 1).astype(F32).astype(BF16)
    one, zero = jnp.ones((), BF16), jnp.zeros((), BF16)
    for at in range(taps):
        chosen = lane == taps * pl.program_id(0) + at
        column = jnp.sum(jnp.where(chosen, rows_ref[...], 0.0), axis=1, keepdims=True)
        taken = None
        for first, end, start in segments:
            place = jnp.clip(column - start, -1.0, 256.0).astype(BF16)
            hits = jnp.where(place == places[:, : end - first], one, zero)
            product = dot(hits, table_ref[first:end])
            taken = product if taken is None else taken + product
        out_ref[:, at * half : (at + 1) * half] = taken.astype(BF16)


def gather_block(start, rows, table):
    points, lanes = rows.shape
    height, half = table.shape
    taps = 9
    whole = lambda step: (0, 0)
    return call(
        functools.partial(gather_kernel, taps),
        jax.ShapeDtypeStruct((points, TAPS * half), BF16),
        GATHER_LIMIT,
        2 * TAPS * points * height * half,
        2 * TAPS * points * half,
        grid=(TAPS // taps,),
        in_specs=[
            pl.BlockSpec(memory_space=pltpu.SMEM),
            pl.BlockSpec((points, lanes), whole),
            pl.BlockSpec((height, half), whole),
        ],
        out_specs=pl.BlockSpec((points, taps * half), lambda step: (0, step)),
    )(start, rows, table)


def conv_kernel(slots, first, places_ref, shifts_ref, *refs):
    refs = list(refs)

    def take(count):
        taken = refs[:count]
        del refs[:count]
        return taken

    stacked = take(2)
    pieces = take(sum(len(parts) for parts in slots))
    before = [] if first else take(2)
    outs = take(2)
    held, sems = refs
    length = held.shape[1]
    copies = []
    for at, parts in enumerate(slots):
        row = pl.multiple_of(places_ref[2 * at + 1], 16)
        copies.append([])
        edge = length - sum(size for _, size, _, _ in parts)
        if edge:
            held[at, :edge] = jnp.zeros((edge, held.shape[2]), BF16)
            held[at, length - edge :] = jnp.zeros((edge, held.shape[2]), BF16)
        for part, (start, size, offset, kind) in enumerate(parts):
            moved = row + offset if kind is None else row + shifts_ref[kind]
            place = pl.multiple_of(moved, 16)
            (piece,) = pieces[:1]
            del pieces[:1]
            copy = pltpu.make_async_copy(
                piece.at[pl.ds(start, size)], held.at[at, pl.ds(place, size)], sems.at[at, part]
            )
            copy.start()
            copies[-1].append(copy)
    for at in range(len(slots)):
        for copy in copies[at]:
            copy.wait()
        column = pl.multiple_of(places_ref[2 * at], 128)
        for block, ref in enumerate(outs):
            product = dot(stacked[block][:, pl.ds(column, length)], held[at])
            if at > 0:
                ref[...] += product
            elif first:
                ref[...] = product
            else:
                ref[...] = (before[block][...] + product).astype(ref.dtype)


def conv_part(stacked, places, shifts, pieces, before, length, limit, dtype=F32):
    points = stacked[0].shape[0]
    width = pieces[0][0][0].shape[1]
    slots = [[part[1:] for part in parts] for parts in pieces]
    flat = [part[0] for parts in pieces for part in parts]
    held = 4 + len(flat)
    kept = [] if before is None else [block for block in range(2) if block or dtype == F32]
    return call(
        functools.partial(conv_kernel, slots, before is None),
        [
            jax.ShapeDtypeStruct((points, width), dtype),
            jax.ShapeDtypeStruct((points, width), F32),
        ],
        limit,
        4 * points * length * width * len(slots),
        2 * length * (2 * points + width) * len(slots),
        in_specs=[pl.BlockSpec(memory_space=pltpu.SMEM)] * 2
        + [pl.BlockSpec()] * 2
        + [pl.BlockSpec(memory_space=pl.ANY)] * len(flat)
        + ([] if before is None else [pl.BlockSpec()] * 2),
        input_output_aliases={held + block: block for block in kept},
        scratch_shapes=[
            pltpu.VMEM((len(slots), length, width), BF16),
            pltpu.SemaphoreType.DMA((len(slots), 3)),
        ],
    )(places, shifts, *stacked, *flat, *(before or ()))


def mix_kernel(own_ref, got_ref, features_ref, weight_ref, gain_ref, slot_ref, out_ref):
    convolved = (own_ref[...] + got_ref[...].astype(F32)).astype(BF16)
    linear = dot(convolved, weight_ref[...])
    mixed = (features_ref[...].astype(F32) + layer_norm(linear, gain_ref[...])).astype(BF16)
    slots = lax.broadcasted_iota(jnp.int32, (out_ref.shape[0], mixed.shape[0]), 0)
    out_ref[...] = dot(one_hot(slots == slot_ref[...]), mixed).astype(BF16)


def block_kernel(
    arrived_ref,
    slot_col_ref,
    slot_row_ref,
    attn_gain_ref,
    mlp_gain_ref,
    qv_hbm,
    key_hbm,
    proj_hbm,
    up_hbm,
    down_hbm,
    out_ref,
    qv_ref,
    key_ref,
    proj_ref,
    up_ref,
    down_ref,
    sems,
    serial_ref,
    qv_cols_ref,
    keys_ref,
    heads_ref,
    total_ref,
    scores_ref,
    weights_ref,
):
    sources = (key_hbm, qv_hbm, proj_hbm, up_hbm, down_hbm)
    targets = (key_ref, qv_ref, proj_ref, up_ref, down_ref)
    copies = [
        pltpu.make_async_copy(source, target, sems.at[at])
        for at, (source, target) in enumerate(zip(sources, targets))
    ]
    for copy in copies:
        copy.start()
    slots = arrived_ref.shape[0]
    points, width = serial_ref.shape
    slot_ids = lax.broadcasted_iota(jnp.int32, (points, slots), 1)
    serial = dot(one_hot(slot_col_ref[...] == slot_ids), arrived_ref[...])
    serial_ref[...] = serial
    normed = layer_norm(serial, attn_gain_ref[...]).astype(BF16)
    copies[0].wait()
    keys_ref[...] = dot(normed, key_ref[...]).astype(BF16)
    copies[1].wait()
    factor = math.log2(math.e) / math.sqrt(HD)
    contract_last = (((1,), (1,)), ((), ()))
    qv_cols_ref[:width] = (
        lax.dot_general(qv_ref[:width], normed, contract_last, preferred_element_type=F32) * factor
    ).astype(BF16)
    qv_cols_ref[width:] = lax.dot_general(
        qv_ref[width:], normed, contract_last, preferred_element_type=F32
    ).astype(BF16)
    ones = jnp.ones((HD, points), BF16)
    per_group = 128 // HD
    head_of_row = lax.broadcasted_iota(jnp.int32, (128, points), 0) // HD

    def score(head, slot):
        base = pl.multiple_of(head // per_group * 128, 128)
        group_queries = qv_cols_ref[pl.ds(base, 128)].astype(F32)
        chosen = head_of_row == lax.rem(head, per_group)
        queries = jnp.where(chosen, group_queries, 0.0).astype(BF16)
        scores_ref[slot] = dot(keys_ref[:, pl.ds(base, 128)], queries)

    def weigh(slot):
        scores = scores_ref[slot]
        weights_ref[slot] = jnp.exp2(scores - jnp.max(scores, axis=0, keepdims=True)).astype(BF16)

    def gather(head, slot):
        at = pl.multiple_of(head * HD, HD)
        values = jnp.concatenate([qv_cols_ref[pl.ds(width + at, HD)], ones], axis=0)
        sums = dot(values, weights_ref[slot])
        heads_ref[pl.ds(at, HD)] = (sums[:HD] / sums[HD : HD + 1]).astype(BF16)

    score(0, 0)
    score(1, 1)
    weigh(0)

    def two_heads(pair, carry):
        head = 2 * pair + 1
        for slot in (1, 0):
            score(head + 1, 1 - slot)
            weigh(slot)
            gather(head - 1, 1 - slot)
            head += 1
        return carry

    lax.fori_loop(0, HEADS // 2 - 1, two_heads, 0)
    weigh(1)
    gather(HEADS - 2, 0)
    gather(HEADS - 1, 1)

    for copy in copies[2:]:
        copy.wait()
    update = lax.dot_general(
        heads_ref[...], proj_ref[...], (((0,), (0,)), ((), ())), preferred_element_type=F32
    )
    attended = (serial_ref[...] + update).astype(BF16).astype(F32)
    hidden_in = layer_norm(attended, mlp_gain_ref[...]).astype(BF16)
    total_ref[...] = attended
    chunk = width
    for start in range(0, up_ref.shape[1], chunk):
        raised = dot(hidden_in, up_ref[:, start : start + chunk])
        hidden = (raised * (1.0 + lax.erf(raised * math.sqrt(0.5))) * 0.5).astype(BF16)
        total_ref[...] += dot(hidden, down_ref[start : start + chunk])
    finished = total_ref[...].astype(BF16)
    slot_rows = lax.broadcasted_iota(jnp.int32, (slots, points), 0)
    out_ref[...] = dot(one_hot(slot_rows == slot_row_ref[...]), finished).astype(BF16)


def return_kernel(arrived_ref, slot_ref, out_ref):
    slot_ids = lax.broadcasted_iota(jnp.int32, (out_ref.shape[0], arrived_ref.shape[0]), 1)
    out_ref[...] = dot(one_hot(slot_ref[...] == slot_ids), arrived_ref[...]).astype(BF16)


def face_pairs(devices, dx, dy):
    return [
        (source, source + dx * GY + dy)
        for source in range(devices)
        if 0 <= source // GY + dx < devices // GY and 0 <= source % GY + dy < GY
    ]


def way_round(devices, rows, length):
    chips = devices // 2
    cycle = list(range(0, chips, 2)) + list(range(chips - 1, 0, -2))
    chains = [], []
    places = [None] * devices
    for place, chip in enumerate(cycle):
        for core, way in ((0, 1), (1, -1)):
            me = 2 * chip + core
            for chain, step in zip(chains, (way, -way)):
                chain.append((me, 2 * cycle[(place + step) % chips] + core))
            order = [0]
            for step in range(1, chips // 2):
                order += [-step * way, step * way]
            order.append(chips // 2)
            places[me] = []
            for offset in order:
                start = cycle[(place + offset) % chips] * rows
                column = min(start // 128 * 128, chips * rows - length)
                places[me].append((column, start - column))
    return *chains, places


def padded_taps(neighbours):
    points = neighbours.shape[0]
    own = jnp.arange(points, dtype=jnp.int32)[:, None]
    rest = jnp.zeros((points, 128 - TAPS), jnp.int32)
    middle = TAPS // 2
    rows = jnp.concatenate([neighbours[:, :middle], own, neighbours[:, middle:], rest], axis=1)
    return rows.astype(F32)


def body(
    features,
    conv_weight,
    cpe_weight,
    cpe_gain,
    attn_gain,
    qkv_weight,
    proj_weight,
    mlp_gain,
    up_weight,
    down_weight,
    face_rows,
    neighbours,
    serial_rank,
    serial_order,
):
    points, width = features.shape
    half = width // 2
    devices = lax.axis_size("blocks")
    index = lax.axis_index("blocks")
    core = lax.rem(index, 2)
    partner = [(source, source ^ 1) for source in range(devices)]
    capacity = 2 * points // devices
    slots = devices * capacity

    unit = conv_weight.shape[0] // TAPS
    units = conv_weight.reshape(TAPS, unit, width)
    got = lax.ppermute(units[1::2], "blocks", partner)
    rows = TAPS * unit
    side = lax.axis_index("groups")
    missing = -(-rows // 64) * 16
    passed = rows - missing
    if devices == 2 * GY:
        mine, begun = call(
            rows_kernel,
            [
                jax.ShapeDtypeStruct((rows, width), BF16),
                jax.ShapeDtypeStruct((passed, width), BF16),
            ],
            24,
            0,
            8 * rows * width,
            in_specs=[pl.BlockSpec(memory_space=pltpu.SMEM)] + [pl.BlockSpec()] * 2,
        )(jnp.stack([core, side]).astype(jnp.int32), units, got)
    else:
        kept = units[0::2]
        mine = begun = jnp.where(
            core == 0, jnp.concatenate([kept, got]), jnp.concatenate([got, kept])
        ).reshape(rows, width)

    round_trip = devices == 2 * GY
    lower = index < GY
    if round_trip:
        across = jnp.where(lower, face_rows[0, 5:], face_rows[0, :3])
        face_list = jnp.concatenate([across, face_rows[0, 3:5]]).reshape(-1, 1)
        counts = (3, 1, 1)
    else:
        face_list = face_rows.reshape(-1, 1)
        counts = (1,) * 8
    size = face_rows.shape[2]
    own_local, other_local, *faces = call(
        functools.partial(faces_kernel, unit),
        [jax.ShapeDtypeStruct((points, half), BF16)] * 2
        + [jax.ShapeDtypeStruct((count * size, width), BF16) for count in counts],
        32,
        4 * points * width * width,
        8 * points * width,
        in_specs=[pl.BlockSpec(memory_space=pltpu.SMEM)] + [pl.BlockSpec()] * 2,
    )(core.reshape(1), features, face_list)
    length = -(-(rows + 127) // 128) * 128 if round_trip else rows * (devices // 2)
    first_pairs, second_pairs, places = way_round(devices, rows, length)
    shifts = jnp.stack([side * passed, (1 - side) * passed]).astype(jnp.int32)
    first, second = [begun], [begun]

    def pass_on(*beside):
        if not round_trip:
            return beside
        tied = lax.optimization_barrier((first[-1], second[-1], *beside))
        first[-1], second[-1] = tied[:2]
        last = len(first) == devices // 4
        first.append(lax.ppermute(first[-1], "blocks", first_pairs))
        if not last:
            second.append(lax.ppermute(second[-1], "blocks", second_pairs))
        return tied[2:]

    def complete(*arrived):
        lent = [piece[:missing] for piece in arrived]
        lent = jnp.concatenate(lent) if len(lent) > 1 else lent[0]
        got = lax.ppermute(lent, "groups", [(0, 1), (1, 0)])
        return [
            [
                (piece, 0, missing, 0, 0),
                (piece, missing, passed - missing, missing, None),
                (got, at * missing, missing, 0, 1),
            ]
            for at, piece in enumerate(arrived)
        ]

    if round_trip:
        lists, back_list, on_list = faces
        across = face_pairs(devices, 1, 0) + face_pairs(devices, -1, 0)
        (lists,) = pass_on(lists)
        lists = lax.ppermute(lists, "blocks", across)
        to_on = jnp.concatenate([on_list, lists[2 * size :]])
        to_back = jnp.concatenate([back_list, lists[:size]])
        behind = lax.ppermute(to_on, "blocks", face_pairs(devices, 0, 1))
        ahead = lax.ppermute(to_back, "blocks", face_pairs(devices, 0, -1))
        places = jnp.array(places, jnp.int32)[index].reshape(-1)
        sent_neighbours, places, lists, behind, ahead = pass_on(
            neighbours, places, lists, behind, ahead
        )
        other_neighbours = lax.ppermute(sent_neighbours, "blocks", partner)
        near = complete(first[1], second[1])
        own_table, other_half = call(
            table_kernel,
            [jax.ShapeDtypeStruct((points + 6 * size, half), BF16)] * 2,
            32,
            0,
            20 * size * width,
            in_specs=[pl.BlockSpec(memory_space=pltpu.SMEM)] + [pl.BlockSpec()] * 5,
        )(
            jnp.stack([lower.astype(jnp.int32), core]),
            own_local,
            other_local,
            lists,
            behind,
            ahead,
        )
        start = jnp.where(lower, points, points + 3 * size).reshape(1)
    else:
        other_neighbours = lax.ppermute(neighbours, "blocks", partner)
        received = jnp.concatenate(
            [
                lax.ppermute(faces[k], "blocks", face_pairs(devices, STEPS_X[k], STEPS_Y[k]))
                for k in range(8)
            ]
        )
        shape = (received.shape[0], half)
        own_table = jnp.concatenate(
            [own_local, lax.dynamic_slice(received, (0, core * half), shape)]
        )
        other_half = jnp.concatenate(
            [other_local, lax.dynamic_slice(received, (0, (1 - core) * half), shape)]
        )
        start = jnp.full((1,), points, jnp.int32)
    other_table = lax.ppermute(other_half, "blocks", partner)
    own_stacked = gather_block(start, padded_taps(neighbours), own_table)
    other_rows = padded_taps(other_neighbours)
    own_stacked, other_rows, other_table = pass_on(own_stacked, other_rows, other_table)
    if round_trip:
        middle = complete(first[2], second[2])
    other_stacked = gather_block(start, other_rows, other_table)
    stacked = other_stacked, own_stacked
    if round_trip:
        early = [[(mine, 0, rows, 0, None)]] + near
        sums = conv_part(stacked, places[:6], shifts, early, None, length, CONV_LIMIT)
        *sums, middle_got = pass_on(*sums, middle[0][2][0])
        middle = [[*parts[:2], (middle_got, *parts[2][1:])] for parts in middle]
        far = complete(first[3], second[3])
        opposite = complete(first[4])
        sums = conv_part(stacked, places[6:10], shifts, middle, sums, length, CONV_LIMIT)
        sums = conv_part(stacked, places[10:14], shifts, far, sums, length, CONV_LIMIT)
        for_partner, own_part = conv_part(
            stacked, places[14:], shifts, opposite, sums, length, CONV_LIMIT, BF16
        )
    else:
        groups = [list(range(core, devices, 2)) for core in range(2)]
        weight = lax.all_gather(mine, "blocks", axis=0, tiled=True, axis_index_groups=groups)
        nowhere = jnp.zeros((2,), jnp.int32)
        whole = [[(weight, 0, weight.shape[0], 0, None)]]
        for_partner, own_part = conv_part(stacked, nowhere, shifts, whole, None, length, 48)

    positions = jnp.arange(points, dtype=jnp.int32)
    target = serial_rank // points
    earlier = (target[None, :] == target[:, None]) & (serial_rank[None, :] < serial_rank[:, None])
    out_slot = target * capacity + jnp.sum(earlier.astype(jnp.int32), axis=1)
    anchor = serial_order // points
    before = (anchor[None, :] == anchor[:, None]) & (positions[None, :] < positions[:, None])
    in_slot = anchor * capacity + jnp.sum(before.astype(jnp.int32), axis=1)

    from_partner = lax.ppermute(for_partner, "blocks", partner)

    outgoing = call(
        mix_kernel,
        jax.ShapeDtypeStruct((slots, width), BF16),
        32,
        2 * points * width * (width + slots),
        8 * points * width,
    )(
        own_part,
        from_partner,
        features,
        cpe_weight,
        cpe_gain.reshape(1, width),
        out_slot.reshape(1, points),
    )
    arrived = lax.all_to_all(
        outgoing.reshape(devices, capacity, width), "blocks", split_axis=0, concat_axis=0, tiled=True
    ).reshape(slots, width)

    key_weight = qkv_weight[:, width : 2 * width]
    qv_weight = jnp.concatenate([qkv_weight[:, :width], qkv_weight[:, 2 * width :]], axis=1).T
    weights = (qv_weight, key_weight, proj_weight, up_weight, down_weight)
    back = call(
        block_kernel,
        jax.ShapeDtypeStruct((slots, width), BF16),
        60,
        20 * points * width * width,
        16 * width * width,
        in_specs=[pl.BlockSpec()] * 5 + [pl.BlockSpec(memory_space=pl.ANY)] * len(weights),
        scratch_shapes=[pltpu.VMEM(weight.shape, BF16) for weight in weights]
        + [
            pltpu.SemaphoreType.DMA((len(weights),)),
            pltpu.VMEM((points, width), F32),
            pltpu.VMEM((2 * width, points), BF16),
            pltpu.VMEM((points, width), BF16),
            pltpu.VMEM((width, points), BF16),
            pltpu.VMEM((points, width), F32),
            pltpu.VMEM((2, points, points), F32),
            pltpu.VMEM((2, points, points), BF16),
        ],
    )(
        arrived,
        in_slot.reshape(points, 1),
        in_slot.reshape(1, points),
        attn_gain.reshape(1, width),
        mlp_gain.reshape(1, width),
        *weights,
    )
    returned = lax.all_to_all(
        back.reshape(devices, capacity, width), "blocks", split_axis=0, concat_axis=0, tiled=True
    ).reshape(slots, width)
    return call(
        return_kernel,
        jax.ShapeDtypeStruct((points, width), BF16),
        32,
        2 * points * slots * width,
        6 * points * width,
    )(returned, out_slot.reshape(points, 1))


def solution(mesh):
    placed = (
        P(("groups", "blocks"), None),
        P("blocks", None),
        P(),
        P(),
        P(),
        P(),
        P(),
        P(),
        P(),
        P(),
        P(("groups", "blocks"), None, None),
        P(("groups", "blocks"), None),
        P(("groups", "blocks")),
        P(("groups", "blocks")),
    )
    return jax.shard_map(
        body, mesh=mesh, in_specs=placed, out_specs=P(("groups", "blocks"), None), check_vma=False
    )
```

```python
import functools
import math

import jax
import jax.numpy as jnp
from jax import lax
from jax.experimental import pallas as pl
from jax.experimental.pallas import tpu as pltpu
from jax.sharding import PartitionSpec as P

HEADS = 32
GY = 8
HD = 16
TAPS = 27
EPSILON = 1e-05
STEPS_X = (-1, -1, -1, 0, 0, 1, 1, 1)
STEPS_Y = (-1, 0, 1, -1, 1, -1, 0, 1)
F32 = jnp.float32
BF16 = jnp.bfloat16
MIB = 1 << 20
GATHER_LIMIT, CONV_LIMIT = 20, 20


def dot(left, right):
    return jnp.dot(left, right, preferred_element_type=F32)


def layer_norm(inputs, gain_vector):
    row_mean = jnp.mean(inputs, axis=-1, keepdims=True)
    centred = inputs - row_mean
    variance = jnp.mean(centred * centred, axis=-1, keepdims=True)
    return centred * lax.rsqrt(variance + EPSILON) * gain_vector


def one_hot(mask):
    return jnp.where(mask, 1.0, 0.0).astype(BF16)


def call(kernel, out_shape, limit, flops, moved, **extra):
    return pl.pallas_call(
        kernel,
        out_shape=out_shape,
        compiler_params=pltpu.CompilerParams(vmem_limit_bytes=limit * MIB),
        cost_estimate=pl.CostEstimate(flops=flops, bytes_accessed=moved, transcendentals=0),
        **extra,
    )


def rows_kernel(flags_ref, units_ref, got_ref, mine_ref, begun_ref):
    count, unit, _ = units_ref.shape
    missing = mine_ref.shape[0] - begun_ref.shape[0]
    kept = [units_ref.at[at] for at in range(0, count, 2)]
    got = [got_ref.at[at] for at in range(count // 2)]
    for core, order in enumerate((kept + got, got + kept)):

        @pl.when(flags_ref[0] == core)
        def _():
            for at, source in enumerate(order):
                mine_ref[at * unit : (at + 1) * unit] = source[...]

    passed = begun_ref.shape[0]
    lent = pl.multiple_of(flags_ref[1] * passed, 16)
    begun_ref[:missing] = mine_ref[pl.ds(lent, missing)]
    begun_ref[missing:] = mine_ref[missing:passed]


def faces_kernel(unit, core_ref, features_ref, rows_ref, own_ref, other_ref, *face_refs):
    points, width = features_ref.shape
    half = width // 2
    place = lax.broadcasted_iota(jnp.int32, (width, width), 1)
    within = lax.rem(place, half)
    source = (within // unit) * (2 * unit) + (place // half) * unit + lax.rem(place, unit)
    channel = lax.broadcasted_iota(jnp.int32, (width, width), 0)
    ordered = dot(features_ref[...], one_hot(channel == source)).astype(BF16)
    first, second = ordered[:, :half], ordered[:, half:]
    even = core_ref[0] == 0
    own_ref[...] = jnp.where(even, first, second)
    other_ref[...] = jnp.where(even, second, first)
    row_ids = lax.broadcasted_iota(jnp.int32, (rows_ref.shape[0], points), 1)
    rows = dot(one_hot(rows_ref[...] == row_ids), ordered).astype(BF16)
    taken = 0
    for ref in face_refs:
        ref[...] = rows[taken : taken + ref.shape[0]]
        taken += ref.shape[0]


def table_kernel(
    flags_ref, own_rows, other_rows, side_ref, behind_ref, ahead_ref, own_ref, other_ref
):
    size = behind_ref.shape[0] // 2
    points, half = own_rows.shape
    lower, even = flags_ref[0] == 1, flags_ref[1] == 0
    own_ref[:points] = own_rows[...]
    other_ref[:points] = other_rows[...]
    across = [ahead_ref[size:], side_ref[size : 2 * size], behind_ref[size:]]
    along = [ahead_ref[:size], behind_ref[:size]]
    for at, (low, high) in enumerate(zip(across + along, along + across)):
        rows = jnp.where(lower, low, high)
        first, second = rows[:, :half], rows[:, half:]
        start = points + at * size
        own_ref[start : start + size] = jnp.where(even, first, second)
        other_ref[start : start + size] = jnp.where(even, second, first)
    rest = jnp.zeros((size, half), BF16)
    own_ref[points + 5 * size :] = rest
    other_ref[points + 5 * size :] = rest


def gather_kernel(taps, start_ref, rows_ref, table_ref, out_ref):
    points, lanes = rows_ref.shape
    height, half = table_ref.shape
    lane = lax.broadcasted_iota(jnp.int32, (points, lanes), 1)
    segments = []
    for first in range(0, height, 256):
        start = first if first < points else first - points + start_ref[0]
        segments.append(
            (first, min(height, first + 256), jnp.asarray(start, jnp.int32).astype(F32))
        )
    places = lax.broadcasted_iota(jnp.int32, (1, 256), 1).astype(F32).astype(BF16)
    one, zero = jnp.ones((), BF16), jnp.zeros((), BF16)
    for at in range(taps):
        chosen = lane == taps * pl.program_id(0) + at
        column = jnp.sum(jnp.where(chosen, rows_ref[...], 0.0), axis=1, keepdims=True)
        taken = None
        for first, end, start in segments:
            place = jnp.clip(column - start, -1.0, 256.0).astype(BF16)
            hits = jnp.where(place == places[:, : end - first], one, zero)
            product = dot(hits, table_ref[first:end])
            taken = product if taken is None else taken + product
        out_ref[:, at * half : (at + 1) * half] = taken.astype(BF16)


def gather_block(start, rows, table):
    points, lanes = rows.shape
    height, half = table.shape
    taps = 9
    whole = lambda step: (0, 0)
    return call(
        functools.partial(gather_kernel, taps),
        jax.ShapeDtypeStruct((points, TAPS * half), BF16),
        GATHER_LIMIT,
        2 * TAPS * points * height * half,
        2 * TAPS * points * half,
        grid=(TAPS // taps,),
        in_specs=[
            pl.BlockSpec(memory_space=pltpu.SMEM),
            pl.BlockSpec((points, lanes), whole),
            pl.BlockSpec((height, half), whole),
        ],
        out_specs=pl.BlockSpec((points, taps * half), lambda step: (0, step)),
    )(start, rows, table)


def conv_kernel(slots, first, places_ref, shifts_ref, *refs):
    refs = list(refs)

    def take(count):
        taken = refs[:count]
        del refs[:count]
        return taken

    stacked = take(2)
    pieces = take(sum(len(parts) for parts in slots))
    before = [] if first else take(2)
    outs = take(2)
    held, sems = refs
    length = held.shape[1]
    copies = []
    for at, parts in enumerate(slots):
        row = pl.multiple_of(places_ref[2 * at + 1], 16)
        copies.append([])
        edge = length - sum(size for _, size, _, _ in parts)
        if edge:
            held[at, :edge] = jnp.zeros((edge, held.shape[2]), BF16)
            held[at, length - edge :] = jnp.zeros((edge, held.shape[2]), BF16)
        for part, (start, size, offset, kind) in enumerate(parts):
            moved = row + offset if kind is None else row + shifts_ref[kind]
            place = pl.multiple_of(moved, 16)
            (piece,) = pieces[:1]
            del pieces[:1]
            copy = pltpu.make_async_copy(
                piece.at[pl.ds(start, size)], held.at[at, pl.ds(place, size)], sems.at[at, part]
            )
            copy.start()
            copies[-1].append(copy)
    for at in range(len(slots)):
        for copy in copies[at]:
            copy.wait()
        column = pl.multiple_of(places_ref[2 * at], 128)
        for block, ref in enumerate(outs):
            product = dot(stacked[block][:, pl.ds(column, length)], held[at])
            if at > 0:
                ref[...] += product
            elif first:
                ref[...] = product
            else:
                ref[...] = (before[block][...] + product).astype(ref.dtype)


def conv_part(stacked, places, shifts, pieces, before, length, limit, dtype=F32):
    points = stacked[0].shape[0]
    width = pieces[0][0][0].shape[1]
    slots = [[part[1:] for part in parts] for parts in pieces]
    flat = [part[0] for parts in pieces for part in parts]
    held = 4 + len(flat)
    kept = [] if before is None else [block for block in range(2) if block or dtype == F32]
    return call(
        functools.partial(conv_kernel, slots, before is None),
        [
            jax.ShapeDtypeStruct((points, width), dtype),
            jax.ShapeDtypeStruct((points, width), F32),
        ],
        limit,
        4 * points * length * width * len(slots),
        2 * length * (2 * points + width) * len(slots),
        in_specs=[pl.BlockSpec(memory_space=pltpu.SMEM)] * 2
        + [pl.BlockSpec()] * 2
        + [pl.BlockSpec(memory_space=pl.ANY)] * len(flat)
        + ([] if before is None else [pl.BlockSpec()] * 2),
        input_output_aliases={held + block: block for block in kept},
        scratch_shapes=[
            pltpu.VMEM((len(slots), length, width), BF16),
            pltpu.SemaphoreType.DMA((len(slots), 3)),
        ],
    )(places, shifts, *stacked, *flat, *(before or ()))


def mix_kernel(own_ref, got_ref, features_ref, weight_ref, gain_ref, slot_ref, out_ref):
    convolved = (own_ref[...] + got_ref[...].astype(F32)).astype(BF16)
    linear = dot(convolved, weight_ref[...])
    mixed = (features_ref[...].astype(F32) + layer_norm(linear, gain_ref[...])).astype(BF16)
    slots = lax.broadcasted_iota(jnp.int32, (out_ref.shape[0], mixed.shape[0]), 0)
    out_ref[...] = dot(one_hot(slots == slot_ref[...]), mixed).astype(BF16)


def block_kernel(
    arrived_ref,
    slot_col_ref,
    slot_row_ref,
    attn_gain_ref,
    mlp_gain_ref,
    qv_hbm,
    key_hbm,
    proj_hbm,
    up_hbm,
    down_hbm,
    out_ref,
    qv_ref,
    key_ref,
    proj_ref,
    up_ref,
    down_ref,
    sems,
    serial_ref,
    qv_cols_ref,
    keys_ref,
    heads_ref,
    total_ref,
    scores_ref,
    weights_ref,
):
    sources = (key_hbm, qv_hbm, proj_hbm, up_hbm, down_hbm)
    targets = (key_ref, qv_ref, proj_ref, up_ref, down_ref)
    copies = [
        pltpu.make_async_copy(source, target, sems.at[at])
        for at, (source, target) in enumerate(zip(sources, targets))
    ]
    for copy in copies:
        copy.start()
    slots = arrived_ref.shape[0]
    points, width = serial_ref.shape
    slot_ids = lax.broadcasted_iota(jnp.int32, (points, slots), 1)
    serial = dot(one_hot(slot_col_ref[...] == slot_ids), arrived_ref[...])
    serial_ref[...] = serial
    normed = layer_norm(serial, attn_gain_ref[...]).astype(BF16)
    copies[0].wait()
    keys_ref[...] = dot(normed, key_ref[...]).astype(BF16)
    copies[1].wait()
    factor = math.log2(math.e) / math.sqrt(HD)
    contract_last = (((1,), (1,)), ((), ()))
    qv_cols_ref[:width] = (
        lax.dot_general(qv_ref[:width], normed, contract_last, preferred_element_type=F32) * factor
    ).astype(BF16)
    qv_cols_ref[width:] = lax.dot_general(
        qv_ref[width:], normed, contract_last, preferred_element_type=F32
    ).astype(BF16)
    ones = jnp.ones((HD, points), BF16)
    per_group = 128 // HD
    head_of_row = lax.broadcasted_iota(jnp.int32, (128, points), 0) // HD

    def score(head, slot):
        base = pl.multiple_of(head // per_group * 128, 128)
        group_queries = qv_cols_ref[pl.ds(base, 128)].astype(F32)
        chosen = head_of_row == lax.rem(head, per_group)
        queries = jnp.where(chosen, group_queries, 0.0).astype(BF16)
        scores_ref[slot] = dot(keys_ref[:, pl.ds(base, 128)], queries)

    def weigh(slot):
        scores = scores_ref[slot]
        weights_ref[slot] = jnp.exp2(scores - jnp.max(scores, axis=0, keepdims=True)).astype(BF16)

    def gather(head, slot):
        at = pl.multiple_of(head * HD, HD)
        values = jnp.concatenate([qv_cols_ref[pl.ds(width + at, HD)], ones], axis=0)
        sums = dot(values, weights_ref[slot])
        heads_ref[pl.ds(at, HD)] = (sums[:HD] / sums[HD : HD + 1]).astype(BF16)

    score(0, 0)
    score(1, 1)
    weigh(0)

    def two_heads(pair, carry):
        head = 2 * pair + 1
        for slot in (1, 0):
            score(head + 1, 1 - slot)
            weigh(slot)
            gather(head - 1, 1 - slot)
            head += 1
        return carry

    lax.fori_loop(0, HEADS // 2 - 1, two_heads, 0)
    weigh(1)
    gather(HEADS - 2, 0)
    gather(HEADS - 1, 1)

    for copy in copies[2:]:
        copy.wait()
    update = lax.dot_general(
        heads_ref[...], proj_ref[...], (((0,), (0,)), ((), ())), preferred_element_type=F32
    )
    attended = (serial_ref[...] + update).astype(BF16).astype(F32)
    hidden_in = layer_norm(attended, mlp_gain_ref[...]).astype(BF16)
    total_ref[...] = attended
    chunk = width
    for start in range(0, up_ref.shape[1], chunk):
        raised = dot(hidden_in, up_ref[:, start : start + chunk])
        hidden = (raised * (1.0 + lax.erf(raised * math.sqrt(0.5))) * 0.5).astype(BF16)
        total_ref[...] += dot(hidden, down_ref[start : start + chunk])
    finished = total_ref[...].astype(BF16)
    slot_rows = lax.broadcasted_iota(jnp.int32, (slots, points), 0)
    out_ref[...] = dot(one_hot(slot_rows == slot_row_ref[...]), finished).astype(BF16)


def return_kernel(arrived_ref, slot_ref, out_ref):
    slot_ids = lax.broadcasted_iota(jnp.int32, (out_ref.shape[0], arrived_ref.shape[0]), 1)
    out_ref[...] = dot(one_hot(slot_ref[...] == slot_ids), arrived_ref[...]).astype(BF16)


def face_pairs(devices, dx, dy):
    return [
        (source, source + dx * GY + dy)
        for source in range(devices)
        if 0 <= source // GY + dx < devices // GY and 0 <= source % GY + dy < GY
    ]


def way_round(devices, rows, length):
    chips = devices // 2
    cycle = list(range(0, chips, 2)) + list(range(chips - 1, 0, -2))
    chains = [], []
    places = [None] * devices
    for place, chip in enumerate(cycle):
        for core, way in ((0, 1), (1, -1)):
            me = 2 * chip + core
            for chain, step in zip(chains, (way, -way)):
                chain.append((me, 2 * cycle[(place + step) % chips] + core))
            order = [0]
            for step in range(1, chips // 2):
                order += [-step * way, step * way]
            order.append(chips // 2)
            places[me] = []
            for offset in order:
                start = cycle[(place + offset) % chips] * rows
                column = min(start // 128 * 128, chips * rows - length)
                places[me].append((column, start - column))
    return *chains, places


def padded_taps(neighbours):
    points = neighbours.shape[0]
    own = jnp.arange(points, dtype=jnp.int32)[:, None]
    rest = jnp.zeros((points, 128 - TAPS), jnp.int32)
    middle = TAPS // 2
    rows = jnp.concatenate([neighbours[:, :middle], own, neighbours[:, middle:], rest], axis=1)
    return rows.astype(F32)


def body(
    features,
    conv_weight,
    cpe_weight,
    cpe_gain,
    attn_gain,
    qkv_weight,
    proj_weight,
    mlp_gain,
    up_weight,
    down_weight,
    face_rows,
    neighbours,
    serial_rank,
    serial_order,
):
    points, width = features.shape
    half = width // 2
    devices = lax.axis_size("blocks")
    index = lax.axis_index("blocks")
    core = lax.rem(index, 2)
    partner = [(source, source ^ 1) for source in range(devices)]
    capacity = 2 * points // devices
    slots = devices * capacity

    unit = conv_weight.shape[0] // TAPS
    units = conv_weight.reshape(TAPS, unit, width)
    got = lax.ppermute(units[1::2], "blocks", partner)
    rows = TAPS * unit
    side = lax.axis_index("groups")
    missing = -(-rows // 64) * 16
    passed = rows - missing
    if devices == 2 * GY:
        mine, begun = call(
            rows_kernel,
            [
                jax.ShapeDtypeStruct((rows, width), BF16),
                jax.ShapeDtypeStruct((passed, width), BF16),
            ],
            24,
            0,
            8 * rows * width,
            in_specs=[pl.BlockSpec(memory_space=pltpu.SMEM)] + [pl.BlockSpec()] * 2,
        )(jnp.stack([core, side]).astype(jnp.int32), units, got)
    else:
        kept = units[0::2]
        mine = begun = jnp.where(
            core == 0, jnp.concatenate([kept, got]), jnp.concatenate([got, kept])
        ).reshape(rows, width)

    round_trip = devices == 2 * GY
    lower = index < GY
    if round_trip:
        across = jnp.where(lower, face_rows[0, 5:], face_rows[0, :3])
        face_list = jnp.concatenate([across, face_rows[0, 3:5]]).reshape(-1, 1)
        counts = (3, 1, 1)
    else:
        face_list = face_rows.reshape(-1, 1)
        counts = (1,) * 8
    size = face_rows.shape[2]
    own_local, other_local, *faces = call(
        functools.partial(faces_kernel, unit),
        [jax.ShapeDtypeStruct((points, half), BF16)] * 2
        + [jax.ShapeDtypeStruct((count * size, width), BF16) for count in counts],
        32,
        4 * points * width * width,
        8 * points * width,
        in_specs=[pl.BlockSpec(memory_space=pltpu.SMEM)] + [pl.BlockSpec()] * 2,
    )(core.reshape(1), features, face_list)
    length = -(-(rows + 127) // 128) * 128 if round_trip else rows * (devices // 2)
    first_pairs, second_pairs, places = way_round(devices, rows, length)
    shifts = jnp.stack([side * passed, (1 - side) * passed]).astype(jnp.int32)
    first, second = [begun], [begun]

    def pass_on(*beside):
        if not round_trip:
            return beside
        tied = lax.optimization_barrier((first[-1], second[-1], *beside))
        first[-1], second[-1] = tied[:2]
        last = len(first) == devices // 4
        first.append(lax.ppermute(first[-1], "blocks", first_pairs))
        if not last:
            second.append(lax.ppermute(second[-1], "blocks", second_pairs))
        return tied[2:]

    def complete(*arrived):
        lent = [piece[:missing] for piece in arrived]
        lent = jnp.concatenate(lent) if len(lent) > 1 else lent[0]
        got = lax.ppermute(lent, "groups", [(0, 1), (1, 0)])
        return [
            [
                (piece, 0, missing, 0, 0),
                (piece, missing, passed - missing, missing, None),
                (got, at * missing, missing, 0, 1),
            ]
            for at, piece in enumerate(arrived)
        ]

    if round_trip:
        lists, back_list, on_list = faces
        across = face_pairs(devices, 1, 0) + face_pairs(devices, -1, 0)
        (lists,) = pass_on(lists)
        lists = lax.ppermute(lists, "blocks", across)
        to_on = jnp.concatenate([on_list, lists[2 * size :]])
        to_back = jnp.concatenate([back_list, lists[:size]])
        behind = lax.ppermute(to_on, "blocks", face_pairs(devices, 0, 1))
        ahead = lax.ppermute(to_back, "blocks", face_pairs(devices, 0, -1))
        places = jnp.array(places, jnp.int32)[index].reshape(-1)
        sent_neighbours, places, lists, behind, ahead = pass_on(
            neighbours, places, lists, behind, ahead
        )
        other_neighbours = lax.ppermute(sent_neighbours, "blocks", partner)
        near = complete(first[1], second[1])
        own_table, other_half = call(
            table_kernel,
            [jax.ShapeDtypeStruct((points + 6 * size, half), BF16)] * 2,
            32,
            0,
            20 * size * width,
            in_specs=[pl.BlockSpec(memory_space=pltpu.SMEM)] + [pl.BlockSpec()] * 5,
        )(
            jnp.stack([lower.astype(jnp.int32), core]),
            own_local,
            other_local,
            lists,
            behind,
            ahead,
        )
        start = jnp.where(lower, points, points + 3 * size).reshape(1)
    else:
        other_neighbours = lax.ppermute(neighbours, "blocks", partner)
        received = jnp.concatenate(
            [
                lax.ppermute(faces[k], "blocks", face_pairs(devices, STEPS_X[k], STEPS_Y[k]))
                for k in range(8)
            ]
        )
        shape = (received.shape[0], half)
        own_table = jnp.concatenate(
            [own_local, lax.dynamic_slice(received, (0, core * half), shape)]
        )
        other_half = jnp.concatenate(
            [other_local, lax.dynamic_slice(received, (0, (1 - core) * half), shape)]
        )
        start = jnp.full((1,), points, jnp.int32)
    other_table = lax.ppermute(other_half, "blocks", partner)
    own_stacked = gather_block(start, padded_taps(neighbours), own_table)
    other_rows = padded_taps(other_neighbours)
    own_stacked, other_rows, other_table = pass_on(own_stacked, other_rows, other_table)
    if round_trip:
        middle = complete(first[2], second[2])
    other_stacked = gather_block(start, other_rows, other_table)
    stacked = other_stacked, own_stacked
    if round_trip:
        *stacked, middle_got = pass_on(*stacked, middle[0][2][0])
        middle = [[*parts[:2], (middle_got, *parts[2][1:])] for parts in middle]
        early = [[(mine, 0, rows, 0, None)]] + near
        sums = conv_part(stacked, places[:6], shifts, early, None, length, CONV_LIMIT)
        far = complete(first[3], second[3])
        opposite = complete(first[4])
        sums = conv_part(stacked, places[6:10], shifts, middle, sums, length, CONV_LIMIT)
        sums = conv_part(stacked, places[10:14], shifts, far, sums, length, CONV_LIMIT)
        for_partner, own_part = conv_part(
            stacked, places[14:], shifts, opposite, sums, length, CONV_LIMIT, BF16
        )
    else:
        groups = [list(range(core, devices, 2)) for core in range(2)]
        weight = lax.all_gather(mine, "blocks", axis=0, tiled=True, axis_index_groups=groups)
        nowhere = jnp.zeros((2,), jnp.int32)
        whole = [[(weight, 0, weight.shape[0], 0, None)]]
        for_partner, own_part = conv_part(stacked, nowhere, shifts, whole, None, length, 48)

    positions = jnp.arange(points, dtype=jnp.int32)
    target = serial_rank // points
    earlier = (target[None, :] == target[:, None]) & (serial_rank[None, :] < serial_rank[:, None])
    out_slot = target * capacity + jnp.sum(earlier.astype(jnp.int32), axis=1)
    anchor = serial_order // points
    before = (anchor[None, :] == anchor[:, None]) & (positions[None, :] < positions[:, None])
    in_slot = anchor * capacity + jnp.sum(before.astype(jnp.int32), axis=1)

    from_partner = lax.ppermute(for_partner, "blocks", partner)

    outgoing = call(
        mix_kernel,
        jax.ShapeDtypeStruct((slots, width), BF16),
        32,
        2 * points * width * (width + slots),
        8 * points * width,
    )(
        own_part,
        from_partner,
        features,
        cpe_weight,
        cpe_gain.reshape(1, width),
        out_slot.reshape(1, points),
    )
    arrived = lax.all_to_all(
        outgoing.reshape(devices, capacity, width), "blocks", split_axis=0, concat_axis=0, tiled=True
    ).reshape(slots, width)

    key_weight = qkv_weight[:, width : 2 * width]
    qv_weight = jnp.concatenate([qkv_weight[:, :width], qkv_weight[:, 2 * width :]], axis=1).T
    weights = (qv_weight, key_weight, proj_weight, up_weight, down_weight)
    back = call(
        block_kernel,
        jax.ShapeDtypeStruct((slots, width), BF16),
        60,
        20 * points * width * width,
        16 * width * width,
        in_specs=[pl.BlockSpec()] * 5 + [pl.BlockSpec(memory_space=pl.ANY)] * len(weights),
        scratch_shapes=[pltpu.VMEM(weight.shape, BF16) for weight in weights]
        + [
            pltpu.SemaphoreType.DMA((len(weights),)),
            pltpu.VMEM((points, width), F32),
            pltpu.VMEM((2 * width, points), BF16),
            pltpu.VMEM((points, width), BF16),
            pltpu.VMEM((width, points), BF16),
            pltpu.VMEM((points, width), F32),
            pltpu.VMEM((2, points, points), F32),
            pltpu.VMEM((2, points, points), BF16),
        ],
    )(
        arrived,
        in_slot.reshape(points, 1),
        in_slot.reshape(1, points),
        attn_gain.reshape(1, width),
        mlp_gain.reshape(1, width),
        *weights,
    )
    returned = lax.all_to_all(
        back.reshape(devices, capacity, width), "blocks", split_axis=0, concat_axis=0, tiled=True
    ).reshape(slots, width)
    return call(
        return_kernel,
        jax.ShapeDtypeStruct((points, width), BF16),
        32,
        2 * points * slots * width,
        6 * points * width,
    )(returned, out_slot.reshape(points, 1))


def solution(mesh):
    placed = (
        P(("groups", "blocks"), None),
        P("blocks", None),
        P(),
        P(),
        P(),
        P(),
        P(),
        P(),
        P(),
        P(),
        P(("groups", "blocks"), None, None),
        P(("groups", "blocks"), None),
        P(("groups", "blocks")),
        P(("groups", "blocks")),
    )
    return jax.shard_map(
        body, mesh=mesh, in_specs=placed, out_specs=P(("groups", "blocks"), None), check_vma=False
    )
```

```python
import functools
import math

import jax
import jax.numpy as jnp
from jax import lax
from jax.experimental import pallas as pl
from jax.experimental.pallas import tpu as pltpu
from jax.sharding import PartitionSpec as P

HEADS = 32
GY = 8
HD = 16
TAPS = 27
EPSILON = 1e-05
STEPS_X = (-1, -1, -1, 0, 0, 1, 1, 1)
STEPS_Y = (-1, 0, 1, -1, 1, -1, 0, 1)
F32 = jnp.float32
BF16 = jnp.bfloat16
MIB = 1 << 20


def dot(left, right):
    return jnp.dot(left, right, preferred_element_type=F32)


def layer_norm(inputs, gain_vector):
    row_mean = jnp.mean(inputs, axis=-1, keepdims=True)
    centred = inputs - row_mean
    variance = jnp.mean(centred * centred, axis=-1, keepdims=True)
    return centred * lax.rsqrt(variance + EPSILON) * gain_vector


def one_hot(mask):
    return jnp.where(mask, 1.0, 0.0).astype(BF16)


def call(kernel, out_shape, limit, flops, moved, **extra):
    return pl.pallas_call(
        kernel,
        out_shape=out_shape,
        compiler_params=pltpu.CompilerParams(vmem_limit_bytes=limit * MIB),
        cost_estimate=pl.CostEstimate(flops=flops, bytes_accessed=moved, transcendentals=0),
        **extra,
    )


def rows_kernel(flags_ref, units_ref, got_ref, mine_ref, begun_ref):
    count, unit, _ = units_ref.shape
    missing = mine_ref.shape[0] - begun_ref.shape[0]
    kept = [units_ref.at[at] for at in range(0, count, 2)]
    got = [got_ref.at[at] for at in range(count // 2)]
    for core, order in enumerate((kept + got, got + kept)):

        @pl.when(flags_ref[0] == core)
        def _():
            for at, source in enumerate(order):
                mine_ref[at * unit : (at + 1) * unit] = source[...]

    passed = begun_ref.shape[0]
    lent = pl.multiple_of(flags_ref[1] * passed, 16)
    begun_ref[:missing] = mine_ref[pl.ds(lent, missing)]
    begun_ref[missing:] = mine_ref[missing:passed]


def faces_kernel(unit, core_ref, features_ref, rows_ref, own_ref, other_ref, *face_refs):
    points, width = features_ref.shape
    half = width // 2
    place = lax.broadcasted_iota(jnp.int32, (width, width), 1)
    within = lax.rem(place, half)
    source = (within // unit) * (2 * unit) + (place // half) * unit + lax.rem(place, unit)
    channel = lax.broadcasted_iota(jnp.int32, (width, width), 0)
    ordered = dot(features_ref[...], one_hot(channel == source)).astype(BF16)
    first, second = ordered[:, :half], ordered[:, half:]
    even = core_ref[0] == 0
    own_ref[...] = jnp.where(even, first, second)
    other_ref[...] = jnp.where(even, second, first)
    row_ids = lax.broadcasted_iota(jnp.int32, (rows_ref.shape[0], points), 1)
    rows = dot(one_hot(rows_ref[...] == row_ids), ordered).astype(BF16)
    taken = 0
    for ref in face_refs:
        ref[...] = rows[taken : taken + ref.shape[0]]
        taken += ref.shape[0]


def table_kernel(
    flags_ref, own_rows, other_rows, side_ref, behind_ref, ahead_ref, own_ref, other_ref
):
    size = behind_ref.shape[0] // 2
    points, half = own_rows.shape
    lower, even = flags_ref[0] == 1, flags_ref[1] == 0
    own_ref[:points] = own_rows[...]
    other_ref[:points] = other_rows[...]
    across = [ahead_ref[size:], side_ref[size : 2 * size], behind_ref[size:]]
    along = [ahead_ref[:size], behind_ref[:size]]
    for at, (low, high) in enumerate(zip(across + along, along + across)):
        rows = jnp.where(lower, low, high)
        first, second = rows[:, :half], rows[:, half:]
        start = points + at * size
        own_ref[start : start + size] = jnp.where(even, first, second)
        other_ref[start : start + size] = jnp.where(even, second, first)
    rest = jnp.zeros((size, half), BF16)
    own_ref[points + 5 * size :] = rest
    other_ref[points + 5 * size :] = rest


def gather_kernel(taps, start_ref, rows_ref, table_ref, out_ref):
    points, lanes = rows_ref.shape
    height, half = table_ref.shape
    lane = lax.broadcasted_iota(jnp.int32, (points, lanes), 1)
    segments = []
    for first in range(0, height, 256):
        start = first if first < points else first - points + start_ref[0]
        segments.append(
            (first, min(height, first + 256), jnp.asarray(start, jnp.int32).astype(F32))
        )
    places = lax.broadcasted_iota(jnp.int32, (1, 256), 1).astype(F32).astype(BF16)
    one, zero = jnp.ones((), BF16), jnp.zeros((), BF16)
    for at in range(taps):
        chosen = lane == taps * pl.program_id(0) + at
        column = jnp.sum(jnp.where(chosen, rows_ref[...], 0.0), axis=1, keepdims=True)
        taken = None
        for first, end, start in segments:
            place = jnp.clip(column - start, -1.0, 256.0).astype(BF16)
            hits = jnp.where(place == places[:, : end - first], one, zero)
            product = dot(hits, table_ref[first:end])
            taken = product if taken is None else taken + product
        out_ref[:, at * half : (at + 1) * half] = taken.astype(BF16)


def gather_block(start, rows, table):
    points, lanes = rows.shape
    height, half = table.shape
    taps = 9
    whole = lambda step: (0, 0)
    return call(
        functools.partial(gather_kernel, taps),
        jax.ShapeDtypeStruct((points, TAPS * half), BF16),
        60,
        2 * TAPS * points * height * half,
        2 * TAPS * points * half,
        grid=(TAPS // taps,),
        in_specs=[
            pl.BlockSpec(memory_space=pltpu.SMEM),
            pl.BlockSpec((points, lanes), whole),
            pl.BlockSpec((height, half), whole),
        ],
        out_specs=pl.BlockSpec((points, taps * half), lambda step: (0, step)),
    )(start, rows, table)


def conv_kernel(slots, later, ready, first, places_ref, shifts_ref, *refs):
    refs = list(refs)

    def take(count):
        taken = refs[:count]
        del refs[:count]
        return taken

    sources = take(1 if ready else 2)
    pieces = take(sum(len(parts) for parts in slots))
    before = [] if first else take(2)
    outs = take(2)
    kept = take(len(later))
    (lhs,) = sources if ready else take(1)
    held, sems = take(2)
    length = held.shape[1]

    def stretch(slot, target, sem):
        column = pl.multiple_of(places_ref[2 * slot], 128)
        copies = [
            pltpu.make_async_copy(
                stacked.at[:, pl.ds(column, length)], target.at[block], sem.at[block]
            )
            for block, stacked in enumerate(sources)
        ]
        for copy in copies:
            copy.start()
        return copies

    copies = []
    for at, parts in enumerate(slots):
        row = pl.multiple_of(places_ref[2 * at + 1], 16)
        copies.append([] if ready else stretch(at, lhs.at[at], sems.at[at]))
        edge = length - sum(size for _, size, _, _ in parts)
        if edge:
            held[at, :edge] = jnp.zeros((edge, held.shape[2]), BF16)
            held[at, length - edge :] = jnp.zeros((edge, held.shape[2]), BF16)
        for part, (start, size, offset, kind) in enumerate(parts):
            moved = row + offset if kind is None else row + shifts_ref[kind]
            place = pl.multiple_of(moved, 16)
            (piece,) = pieces[:1]
            del pieces[:1]
            copy = pltpu.make_async_copy(
                piece.at[pl.ds(start, size)], held.at[at, pl.ds(place, size)], sems.at[at, 2 + part]
            )
            copy.start()
            copies[-1].append(copy)
    extra, slot = [], len(slots)
    for group, count in enumerate(later):
        for place in range(count):
            extra += stretch(slot, kept[group].at[place], sems.at[slot])
            slot += 1
    for at in range(len(slots)):
        for copy in copies[at]:
            copy.wait()
        for block, ref in enumerate(outs):
            product = dot(lhs[at, block], held[at])
            if at > 0:
                ref[...] += product
            elif first:
                ref[...] = product
            else:
                ref[...] = (before[block][...] + product).astype(ref.dtype)
    for copy in extra:
        copy.wait()


def conv_part(sources, places, shifts, pieces, before, length, later=(), dtype=F32):
    ready = len(sources) == 1
    points = sources[0].shape[2] if ready else sources[0].shape[0]
    width = pieces[0][0][0].shape[1]
    slots = [[part[1:] for part in parts] for parts in pieces]
    flat = [part[0] for parts in pieces for part in parts]
    held = 2 + len(sources) + len(flat)
    kept = [] if before is None else [block for block in range(2) if block or dtype == F32]
    spec = pl.BlockSpec(memory_space=pl.ANY)
    return call(
        functools.partial(conv_kernel, slots, later, ready, before is None),
        [
            jax.ShapeDtypeStruct((points, width), dtype),
            jax.ShapeDtypeStruct((points, width), F32),
        ]
        + [jax.ShapeDtypeStruct((count, 2, points, length), BF16) for count in later],
        24 if ready else 36,
        4 * points * length * width * len(slots),
        2 * length * (2 * points + width) * len(slots),
        in_specs=[pl.BlockSpec(memory_space=pltpu.SMEM)] * 2
        + [pl.BlockSpec() if ready else spec] * len(sources)
        + [spec] * len(flat)
        + ([] if before is None else [pl.BlockSpec()] * 2),
        input_output_aliases={held + block: block for block in kept},
        scratch_shapes=([] if ready else [pltpu.VMEM((len(slots), 2, points, length), BF16)])
        + [
            pltpu.VMEM((len(slots), length, width), BF16),
            pltpu.SemaphoreType.DMA((len(slots) + sum(later), 5)),
        ],
    )(places, shifts, *sources, *flat, *(before or ()))


def mix_kernel(own_ref, got_ref, features_ref, weight_ref, gain_ref, slot_ref, out_ref):
    convolved = (own_ref[...] + got_ref[...].astype(F32)).astype(BF16)
    linear = dot(convolved, weight_ref[...])
    mixed = (features_ref[...].astype(F32) + layer_norm(linear, gain_ref[...])).astype(BF16)
    slots = lax.broadcasted_iota(jnp.int32, (out_ref.shape[0], mixed.shape[0]), 0)
    out_ref[...] = dot(one_hot(slots == slot_ref[...]), mixed).astype(BF16)


def block_kernel(
    arrived_ref,
    slot_col_ref,
    slot_row_ref,
    attn_gain_ref,
    mlp_gain_ref,
    qv_hbm,
    key_hbm,
    proj_hbm,
    up_hbm,
    down_hbm,
    out_ref,
    qv_ref,
    key_ref,
    proj_ref,
    up_ref,
    down_ref,
    sems,
    serial_ref,
    qv_cols_ref,
    keys_ref,
    heads_ref,
    total_ref,
    scores_ref,
    weights_ref,
):
    sources = (key_hbm, qv_hbm, proj_hbm, up_hbm, down_hbm)
    targets = (key_ref, qv_ref, proj_ref, up_ref, down_ref)
    copies = [
        pltpu.make_async_copy(source, target, sems.at[at])
        for at, (source, target) in enumerate(zip(sources, targets))
    ]
    for copy in copies:
        copy.start()
    slots = arrived_ref.shape[0]
    points, width = serial_ref.shape
    slot_ids = lax.broadcasted_iota(jnp.int32, (points, slots), 1)
    serial = dot(one_hot(slot_col_ref[...] == slot_ids), arrived_ref[...])
    serial_ref[...] = serial
    normed = layer_norm(serial, attn_gain_ref[...]).astype(BF16)
    copies[0].wait()
    keys_ref[...] = dot(normed, key_ref[...]).astype(BF16)
    copies[1].wait()
    factor = math.log2(math.e) / math.sqrt(HD)
    contract_last = (((1,), (1,)), ((), ()))
    qv_cols_ref[:width] = (
        lax.dot_general(qv_ref[:width], normed, contract_last, preferred_element_type=F32) * factor
    ).astype(BF16)
    qv_cols_ref[width:] = lax.dot_general(
        qv_ref[width:], normed, contract_last, preferred_element_type=F32
    ).astype(BF16)
    ones = jnp.ones((HD, points), BF16)
    per_group = 128 // HD
    head_of_row = lax.broadcasted_iota(jnp.int32, (128, points), 0) // HD

    def score(head, slot):
        base = pl.multiple_of(head // per_group * 128, 128)
        group_queries = qv_cols_ref[pl.ds(base, 128)].astype(F32)
        chosen = head_of_row == lax.rem(head, per_group)
        queries = jnp.where(chosen, group_queries, 0.0).astype(BF16)
        scores_ref[slot] = dot(keys_ref[:, pl.ds(base, 128)], queries)

    def weigh(slot):
        scores = scores_ref[slot]
        weights_ref[slot] = jnp.exp2(scores - jnp.max(scores, axis=0, keepdims=True)).astype(BF16)

    def gather(head, slot):
        at = pl.multiple_of(head * HD, HD)
        values = jnp.concatenate([qv_cols_ref[pl.ds(width + at, HD)], ones], axis=0)
        sums = dot(values, weights_ref[slot])
        heads_ref[pl.ds(at, HD)] = (sums[:HD] / sums[HD : HD + 1]).astype(BF16)

    score(0, 0)
    score(1, 1)
    weigh(0)

    def two_heads(pair, carry):
        head = 2 * pair + 1
        for slot in (1, 0):
            score(head + 1, 1 - slot)
            weigh(slot)
            gather(head - 1, 1 - slot)
            head += 1
        return carry

    lax.fori_loop(0, HEADS // 2 - 1, two_heads, 0)
    weigh(1)
    gather(HEADS - 2, 0)
    gather(HEADS - 1, 1)

    for copy in copies[2:]:
        copy.wait()
    update = lax.dot_general(
        heads_ref[...], proj_ref[...], (((0,), (0,)), ((), ())), preferred_element_type=F32
    )
    attended = (serial_ref[...] + update).astype(BF16).astype(F32)
    hidden_in = layer_norm(attended, mlp_gain_ref[...]).astype(BF16)
    total_ref[...] = attended
    chunk = width
    for start in range(0, up_ref.shape[1], chunk):
        raised = dot(hidden_in, up_ref[:, start : start + chunk])
        hidden = (raised * (1.0 + lax.erf(raised * math.sqrt(0.5))) * 0.5).astype(BF16)
        total_ref[...] += dot(hidden, down_ref[start : start + chunk])
    finished = total_ref[...].astype(BF16)
    slot_rows = lax.broadcasted_iota(jnp.int32, (slots, points), 0)
    out_ref[...] = dot(one_hot(slot_rows == slot_row_ref[...]), finished).astype(BF16)


def return_kernel(arrived_ref, slot_ref, out_ref):
    slot_ids = lax.broadcasted_iota(jnp.int32, (out_ref.shape[0], arrived_ref.shape[0]), 1)
    out_ref[...] = dot(one_hot(slot_ref[...] == slot_ids), arrived_ref[...]).astype(BF16)


def face_pairs(devices, dx, dy):
    return [
        (source, source + dx * GY + dy)
        for source in range(devices)
        if 0 <= source // GY + dx < devices // GY and 0 <= source % GY + dy < GY
    ]


def way_round(devices, rows, length):
    chips = devices // 2
    cycle = list(range(0, chips, 2)) + list(range(chips - 1, 0, -2))
    chains = [], []
    places = [None] * devices
    for place, chip in enumerate(cycle):
        for core, way in ((0, 1), (1, -1)):
            me = 2 * chip + core
            for chain, step in zip(chains, (way, -way)):
                chain.append((me, 2 * cycle[(place + step) % chips] + core))
            order = [0]
            for step in range(1, chips // 2):
                order += [-step * way, step * way]
            order.append(chips // 2)
            places[me] = []
            for offset in order:
                start = cycle[(place + offset) % chips] * rows
                column = min(start // 128 * 128, chips * rows - length)
                places[me].append((column, start - column))
    return *chains, places


def padded_taps(neighbours):
    points = neighbours.shape[0]
    own = jnp.arange(points, dtype=jnp.int32)[:, None]
    rest = jnp.zeros((points, 128 - TAPS), jnp.int32)
    middle = TAPS // 2
    rows = jnp.concatenate([neighbours[:, :middle], own, neighbours[:, middle:], rest], axis=1)
    return rows.astype(F32)


def body(
    features,
    conv_weight,
    cpe_weight,
    cpe_gain,
    attn_gain,
    qkv_weight,
    proj_weight,
    mlp_gain,
    up_weight,
    down_weight,
    face_rows,
    neighbours,
    serial_rank,
    serial_order,
):
    points, width = features.shape
    half = width // 2
    devices = lax.axis_size("blocks")
    index = lax.axis_index("blocks")
    core = lax.rem(index, 2)
    partner = [(source, source ^ 1) for source in range(devices)]
    capacity = 2 * points // devices
    slots = devices * capacity

    unit = conv_weight.shape[0] // TAPS
    units = conv_weight.reshape(TAPS, unit, width)
    got = lax.ppermute(units[1::2], "blocks", partner)
    rows = TAPS * unit
    side = lax.axis_index("groups")
    missing = -(-rows // 64) * 16
    passed = rows - missing
    if devices == 2 * GY:
        mine, begun = call(
            rows_kernel,
            [
                jax.ShapeDtypeStruct((rows, width), BF16),
                jax.ShapeDtypeStruct((passed, width), BF16),
            ],
            24,
            0,
            8 * rows * width,
            in_specs=[pl.BlockSpec(memory_space=pltpu.SMEM)] + [pl.BlockSpec()] * 2,
        )(jnp.stack([core, side]).astype(jnp.int32), units, got)
    else:
        kept = units[0::2]
        mine = begun = jnp.where(
            core == 0, jnp.concatenate([kept, got]), jnp.concatenate([got, kept])
        ).reshape(rows, width)

    round_trip = devices == 2 * GY
    lower = index < GY
    if round_trip:
        across = jnp.where(lower, face_rows[0, 5:], face_rows[0, :3])
        face_list = jnp.concatenate([across, face_rows[0, 3:5]]).reshape(-1, 1)
        counts = (3, 1, 1)
    else:
        face_list = face_rows.reshape(-1, 1)
        counts = (1,) * 8
    size = face_rows.shape[2]
    own_local, other_local, *faces = call(
        functools.partial(faces_kernel, unit),
        [jax.ShapeDtypeStruct((points, half), BF16)] * 2
        + [jax.ShapeDtypeStruct((count * size, width), BF16) for count in counts],
        32,
        4 * points * width * width,
        8 * points * width,
        in_specs=[pl.BlockSpec(memory_space=pltpu.SMEM)] + [pl.BlockSpec()] * 2,
    )(core.reshape(1), features, face_list)
    length = -(-(rows + 127) // 128) * 128 if round_trip else rows * (devices // 2)
    first_pairs, second_pairs, places = way_round(devices, rows, length)
    shifts = jnp.stack([side * passed, (1 - side) * passed]).astype(jnp.int32)
    first, second = [begun], [begun]

    def pass_on(*beside):
        if not round_trip:
            return beside
        tied = lax.optimization_barrier((first[-1], second[-1], *beside))
        first[-1], second[-1] = tied[:2]
        last = len(first) == devices // 4
        first.append(lax.ppermute(first[-1], "blocks", first_pairs))
        if not last:
            second.append(lax.ppermute(second[-1], "blocks", second_pairs))
        return tied[2:]

    def complete(*arrived):
        lent = [piece[:missing] for piece in arrived]
        lent = jnp.concatenate(lent) if len(lent) > 1 else lent[0]
        got = lax.ppermute(lent, "groups", [(0, 1), (1, 0)])
        return [
            [
                (piece, 0, missing, 0, 0),
                (piece, missing, passed - missing, missing, None),
                (got, at * missing, missing, 0, 1),
            ]
            for at, piece in enumerate(arrived)
        ]

    if round_trip:
        lists, back_list, on_list = faces
        across = face_pairs(devices, 1, 0) + face_pairs(devices, -1, 0)
        (lists,) = pass_on(lists)
        lists = lax.ppermute(lists, "blocks", across)
        places = jnp.array(places, jnp.int32)[index].reshape(-1)
        lists, sent_neighbours, places = lax.optimization_barrier((lists, neighbours, places))
        other_neighbours = lax.ppermute(sent_neighbours, "blocks", partner)
        to_on = jnp.concatenate([on_list, lists[2 * size :]])
        to_back = jnp.concatenate([back_list, lists[:size]])
        behind = lax.ppermute(to_on, "blocks", face_pairs(devices, 0, 1))
        ahead = lax.ppermute(to_back, "blocks", face_pairs(devices, 0, -1))
        lists, behind, ahead = pass_on(lists, behind, ahead)
        near = complete(first[1], second[1])
        own_table, other_half = call(
            table_kernel,
            [jax.ShapeDtypeStruct((points + 6 * size, half), BF16)] * 2,
            32,
            0,
            20 * size * width,
            in_specs=[pl.BlockSpec(memory_space=pltpu.SMEM)] + [pl.BlockSpec()] * 5,
        )(
            jnp.stack([lower.astype(jnp.int32), core]),
            own_local,
            other_local,
            lists,
            behind,
            ahead,
        )
        start = jnp.where(lower, points, points + 3 * size).reshape(1)
    else:
        other_neighbours = lax.ppermute(neighbours, "blocks", partner)
        received = jnp.concatenate(
            [
                lax.ppermute(faces[k], "blocks", face_pairs(devices, STEPS_X[k], STEPS_Y[k]))
                for k in range(8)
            ]
        )
        shape = (received.shape[0], half)
        own_table = jnp.concatenate(
            [own_local, lax.dynamic_slice(received, (0, core * half), shape)]
        )
        other_half = jnp.concatenate(
            [other_local, lax.dynamic_slice(received, (0, (1 - core) * half), shape)]
        )
        start = jnp.full((1,), points, jnp.int32)
    other_table = lax.ppermute(other_half, "blocks", partner)
    own_stacked = gather_block(start, padded_taps(neighbours), own_table)
    other_rows = padded_taps(other_neighbours)
    own_stacked, other_rows, other_table = pass_on(own_stacked, other_rows, other_table)
    if round_trip:
        middle = complete(first[2], second[2])
    other_stacked = gather_block(start, other_rows, other_table)
    stacked = other_stacked, own_stacked
    if round_trip:
        *stacked, middle_got = pass_on(*stacked, middle[0][2][0])
        middle = [[*parts[:2], (middle_got, *parts[2][1:])] for parts in middle]
        early = [[(mine, 0, rows, 0, None)]] + near
        *sums, middle_lhs, far_lhs, last_lhs = conv_part(
            stacked, places, shifts, early, None, length, (2, 2, 1)
        )
        far = complete(first[3], second[3])
        opposite = complete(first[4])
        sums = conv_part([middle_lhs], places[6:10], shifts, middle, sums, length)
        sums = conv_part([far_lhs], places[10:14], shifts, far, sums, length)
        for_partner, own_part = conv_part(
            [last_lhs], places[14:], shifts, opposite, sums, length, dtype=BF16
        )
    else:
        groups = [list(range(core, devices, 2)) for core in range(2)]
        weight = lax.all_gather(mine, "blocks", axis=0, tiled=True, axis_index_groups=groups)
        nowhere = jnp.zeros((2,), jnp.int32)
        whole = [[(weight, 0, weight.shape[0], 0, None)]]
        for_partner, own_part = conv_part(stacked, nowhere, shifts, whole, None, length)

    positions = jnp.arange(points, dtype=jnp.int32)
    target = serial_rank // points
    earlier = (target[None, :] == target[:, None]) & (serial_rank[None, :] < serial_rank[:, None])
    out_slot = target * capacity + jnp.sum(earlier.astype(jnp.int32), axis=1)
    anchor = serial_order // points
    before = (anchor[None, :] == anchor[:, None]) & (positions[None, :] < positions[:, None])
    in_slot = anchor * capacity + jnp.sum(before.astype(jnp.int32), axis=1)

    from_partner = lax.ppermute(for_partner, "blocks", partner)

    outgoing = call(
        mix_kernel,
        jax.ShapeDtypeStruct((slots, width), BF16),
        32,
        2 * points * width * (width + slots),
        8 * points * width,
    )(
        own_part,
        from_partner,
        features,
        cpe_weight,
        cpe_gain.reshape(1, width),
        out_slot.reshape(1, points),
    )
    arrived = lax.all_to_all(
        outgoing.reshape(devices, capacity, width), "blocks", split_axis=0, concat_axis=0, tiled=True
    ).reshape(slots, width)

    key_weight = qkv_weight[:, width : 2 * width]
    qv_weight = jnp.concatenate([qkv_weight[:, :width], qkv_weight[:, 2 * width :]], axis=1).T
    weights = (qv_weight, key_weight, proj_weight, up_weight, down_weight)
    back = call(
        block_kernel,
        jax.ShapeDtypeStruct((slots, width), BF16),
        50,
        20 * points * width * width,
        16 * width * width,
        in_specs=[pl.BlockSpec()] * 5 + [pl.BlockSpec(memory_space=pl.ANY)] * len(weights),
        scratch_shapes=[pltpu.VMEM(weight.shape, BF16) for weight in weights]
        + [
            pltpu.SemaphoreType.DMA((len(weights),)),
            pltpu.VMEM((points, width), F32),
            pltpu.VMEM((2 * width, points), BF16),
            pltpu.VMEM((points, width), BF16),
            pltpu.VMEM((width, points), BF16),
            pltpu.VMEM((points, width), F32),
            pltpu.VMEM((2, points, points), F32),
            pltpu.VMEM((2, points, points), BF16),
        ],
    )(
        arrived,
        in_slot.reshape(points, 1),
        in_slot.reshape(1, points),
        attn_gain.reshape(1, width),
        mlp_gain.reshape(1, width),
        *weights,
    )
    returned = lax.all_to_all(
        back.reshape(devices, capacity, width), "blocks", split_axis=0, concat_axis=0, tiled=True
    ).reshape(slots, width)
    return call(
        return_kernel,
        jax.ShapeDtypeStruct((points, width), BF16),
        32,
        2 * points * slots * width,
        6 * points * width,
    )(returned, out_slot.reshape(points, 1))


def solution(mesh):
    placed = (
        P(("groups", "blocks"), None),
        P("blocks", None),
        P(),
        P(),
        P(),
        P(),
        P(),
        P(),
        P(),
        P(),
        P(("groups", "blocks"), None, None),
        P(("groups", "blocks"), None),
        P(("groups", "blocks")),
        P(("groups", "blocks")),
    )
    return jax.shard_map(
        body, mesh=mesh, in_specs=placed, out_specs=P(("groups", "blocks"), None), check_vma=False
    )
```

```python
import functools
import math

import jax
import jax.numpy as jnp
from jax import lax
from jax.experimental import pallas as pl
from jax.experimental.pallas import tpu as pltpu
from jax.sharding import PartitionSpec as P

HEADS = 32
GY = 8
HD = 16
TAPS = 27
EPSILON = 1e-05
STEPS_X = (-1, -1, -1, 0, 0, 1, 1, 1)
STEPS_Y = (-1, 0, 1, -1, 1, -1, 0, 1)
F32 = jnp.float32
BF16 = jnp.bfloat16
MIB = 1 << 20
GATHER_LIMIT, CONV_LIMIT = 24, 24


def dot(left, right):
    return jnp.dot(left, right, preferred_element_type=F32)


def layer_norm(inputs, gain_vector):
    row_mean = jnp.mean(inputs, axis=-1, keepdims=True)
    centred = inputs - row_mean
    variance = jnp.mean(centred * centred, axis=-1, keepdims=True)
    return centred * lax.rsqrt(variance + EPSILON) * gain_vector


def one_hot(mask):
    return jnp.where(mask, 1.0, 0.0).astype(BF16)


def call(kernel, out_shape, limit, flops, moved, **extra):
    return pl.pallas_call(
        kernel,
        out_shape=out_shape,
        compiler_params=pltpu.CompilerParams(vmem_limit_bytes=limit * MIB),
        cost_estimate=pl.CostEstimate(flops=flops, bytes_accessed=moved, transcendentals=0),
        **extra,
    )


def rows_kernel(flags_ref, units_ref, got_ref, mine_ref, begun_ref):
    count, unit, _ = units_ref.shape
    missing = mine_ref.shape[0] - begun_ref.shape[0]
    kept = [units_ref.at[at] for at in range(0, count, 2)]
    got = [got_ref.at[at] for at in range(count // 2)]
    for core, order in enumerate((kept + got, got + kept)):

        @pl.when(flags_ref[0] == core)
        def _():
            for at, source in enumerate(order):
                mine_ref[at * unit : (at + 1) * unit] = source[...]

    passed = begun_ref.shape[0]
    lent = pl.multiple_of(flags_ref[1] * passed, 16)
    begun_ref[:missing] = mine_ref[pl.ds(lent, missing)]
    begun_ref[missing:] = mine_ref[missing:passed]


def faces_kernel(unit, core_ref, features_ref, rows_ref, own_ref, other_ref, *face_refs):
    points, width = features_ref.shape
    half = width // 2
    place = lax.broadcasted_iota(jnp.int32, (width, width), 1)
    within = lax.rem(place, half)
    source = (within // unit) * (2 * unit) + (place // half) * unit + lax.rem(place, unit)
    channel = lax.broadcasted_iota(jnp.int32, (width, width), 0)
    ordered = dot(features_ref[...], one_hot(channel == source)).astype(BF16)
    first, second = ordered[:, :half], ordered[:, half:]
    even = core_ref[0] == 0
    own_ref[...] = jnp.where(even, first, second)
    other_ref[...] = jnp.where(even, second, first)
    row_ids = lax.broadcasted_iota(jnp.int32, (rows_ref.shape[0], points), 1)
    rows = dot(one_hot(rows_ref[...] == row_ids), ordered).astype(BF16)
    taken = 0
    for ref in face_refs:
        ref[...] = rows[taken : taken + ref.shape[0]]
        taken += ref.shape[0]


def table_kernel(
    flags_ref, own_rows, other_rows, side_ref, behind_ref, ahead_ref, own_ref, other_ref
):
    size = behind_ref.shape[0] // 2
    points, half = own_rows.shape
    lower, even = flags_ref[0] == 1, flags_ref[1] == 0
    own_ref[:points] = own_rows[...]
    other_ref[:points] = other_rows[...]
    across = [ahead_ref[size:], side_ref[size : 2 * size], behind_ref[size:]]
    along = [ahead_ref[:size], behind_ref[:size]]
    for at, (low, high) in enumerate(zip(across + along, along + across)):
        rows = jnp.where(lower, low, high)
        first, second = rows[:, :half], rows[:, half:]
        start = points + at * size
        own_ref[start : start + size] = jnp.where(even, first, second)
        other_ref[start : start + size] = jnp.where(even, second, first)
    rest = jnp.zeros((size, half), BF16)
    own_ref[points + 5 * size :] = rest
    other_ref[points + 5 * size :] = rest


def gather_kernel(taps, start_ref, rows_ref, table_ref, out_ref):
    points, lanes = rows_ref.shape
    height, half = table_ref.shape
    lane = lax.broadcasted_iota(jnp.int32, (points, lanes), 1)
    segments = []
    for first in range(0, height, 256):
        start = first if first < points else first - points + start_ref[0]
        segments.append(
            (first, min(height, first + 256), jnp.asarray(start, jnp.int32).astype(F32))
        )
    places = lax.broadcasted_iota(jnp.int32, (1, 256), 1).astype(F32).astype(BF16)
    one, zero = jnp.ones((), BF16), jnp.zeros((), BF16)
    for at in range(taps):
        chosen = lane == taps * pl.program_id(0) + at
        column = jnp.sum(jnp.where(chosen, rows_ref[...], 0.0), axis=1, keepdims=True)
        taken = None
        for first, end, start in segments:
            place = jnp.clip(column - start, -1.0, 256.0).astype(BF16)
            hits = jnp.where(place == places[:, : end - first], one, zero)
            product = dot(hits, table_ref[first:end])
            taken = product if taken is None else taken + product
        out_ref[:, at * half : (at + 1) * half] = taken.astype(BF16)


def gather_block(start, rows, table):
    points, lanes = rows.shape
    height, half = table.shape
    taps = 9
    whole = lambda step: (0, 0)
    return call(
        functools.partial(gather_kernel, taps),
        jax.ShapeDtypeStruct((points, TAPS * half), BF16),
        GATHER_LIMIT,
        2 * TAPS * points * height * half,
        2 * TAPS * points * half,
        grid=(TAPS // taps,),
        in_specs=[
            pl.BlockSpec(memory_space=pltpu.SMEM),
            pl.BlockSpec((points, lanes), whole),
            pl.BlockSpec((height, half), whole),
        ],
        out_specs=pl.BlockSpec((points, taps * half), lambda step: (0, step)),
    )(start, rows, table)


def conv_kernel(slots, first, places_ref, shifts_ref, *refs):
    refs = list(refs)

    def take(count):
        taken = refs[:count]
        del refs[:count]
        return taken

    stacked = take(2)
    pieces = take(sum(len(parts) for parts in slots))
    before = [] if first else take(2)
    outs = take(2)
    held, sems = refs
    length = held.shape[1]
    copies = []
    for at, parts in enumerate(slots):
        row = pl.multiple_of(places_ref[2 * at + 1], 16)
        copies.append([])
        edge = length - sum(size for _, size, _, _ in parts)
        if edge:
            held[at, :edge] = jnp.zeros((edge, held.shape[2]), BF16)
            held[at, length - edge :] = jnp.zeros((edge, held.shape[2]), BF16)
        for part, (start, size, offset, kind) in enumerate(parts):
            moved = row + offset if kind is None else row + shifts_ref[kind]
            place = pl.multiple_of(moved, 16)
            (piece,) = pieces[:1]
            del pieces[:1]
            copy = pltpu.make_async_copy(
                piece.at[pl.ds(start, size)], held.at[at, pl.ds(place, size)], sems.at[at, part]
            )
            copy.start()
            copies[-1].append(copy)
    for at in range(len(slots)):
        for copy in copies[at]:
            copy.wait()
        column = pl.multiple_of(places_ref[2 * at], 128)
        for block, ref in enumerate(outs):
            product = dot(stacked[block][:, pl.ds(column, length)], held[at])
            if at > 0:
                ref[...] += product
            elif first:
                ref[...] = product
            else:
                ref[...] = (before[block][...] + product).astype(ref.dtype)


def conv_part(stacked, places, shifts, pieces, before, length, limit, dtype=F32):
    points = stacked[0].shape[0]
    width = pieces[0][0][0].shape[1]
    slots = [[part[1:] for part in parts] for parts in pieces]
    flat = [part[0] for parts in pieces for part in parts]
    held = 4 + len(flat)
    kept = [] if before is None else [block for block in range(2) if block or dtype == F32]
    return call(
        functools.partial(conv_kernel, slots, before is None),
        [
            jax.ShapeDtypeStruct((points, width), dtype),
            jax.ShapeDtypeStruct((points, width), F32),
        ],
        limit,
        4 * points * length * width * len(slots),
        2 * length * (2 * points + width) * len(slots),
        in_specs=[pl.BlockSpec(memory_space=pltpu.SMEM)] * 2
        + [pl.BlockSpec()] * 2
        + [pl.BlockSpec(memory_space=pl.ANY)] * len(flat)
        + ([] if before is None else [pl.BlockSpec()] * 2),
        input_output_aliases={held + block: block for block in kept},
        scratch_shapes=[
            pltpu.VMEM((len(slots), length, width), BF16),
            pltpu.SemaphoreType.DMA((len(slots), 3)),
        ],
    )(places, shifts, *stacked, *flat, *(before or ()))


def mix_kernel(own_ref, got_ref, features_ref, weight_ref, gain_ref, slot_ref, out_ref):
    convolved = (own_ref[...] + got_ref[...].astype(F32)).astype(BF16)
    linear = dot(convolved, weight_ref[...])
    mixed = (features_ref[...].astype(F32) + layer_norm(linear, gain_ref[...])).astype(BF16)
    slots = lax.broadcasted_iota(jnp.int32, (out_ref.shape[0], mixed.shape[0]), 0)
    out_ref[...] = dot(one_hot(slots == slot_ref[...]), mixed).astype(BF16)


def block_kernel(
    arrived_ref,
    slot_col_ref,
    slot_row_ref,
    attn_gain_ref,
    mlp_gain_ref,
    qv_hbm,
    key_hbm,
    proj_hbm,
    up_hbm,
    down_hbm,
    out_ref,
    qv_ref,
    key_ref,
    proj_ref,
    up_ref,
    down_ref,
    sems,
    serial_ref,
    qv_cols_ref,
    keys_ref,
    heads_ref,
    total_ref,
    scores_ref,
    weights_ref,
):
    sources = (key_hbm, qv_hbm, proj_hbm, up_hbm, down_hbm)
    targets = (key_ref, qv_ref, proj_ref, up_ref, down_ref)
    copies = [
        pltpu.make_async_copy(source, target, sems.at[at])
        for at, (source, target) in enumerate(zip(sources, targets))
    ]
    for copy in copies:
        copy.start()
    slots = arrived_ref.shape[0]
    points, width = serial_ref.shape
    slot_ids = lax.broadcasted_iota(jnp.int32, (points, slots), 1)
    serial = dot(one_hot(slot_col_ref[...] == slot_ids), arrived_ref[...])
    serial_ref[...] = serial
    normed = layer_norm(serial, attn_gain_ref[...]).astype(BF16)
    copies[0].wait()
    keys_ref[...] = dot(normed, key_ref[...]).astype(BF16)
    copies[1].wait()
    factor = math.log2(math.e) / math.sqrt(HD)
    contract_last = (((1,), (1,)), ((), ()))
    qv_cols_ref[:width] = (
        lax.dot_general(qv_ref[:width], normed, contract_last, preferred_element_type=F32) * factor
    ).astype(BF16)
    qv_cols_ref[width:] = lax.dot_general(
        qv_ref[width:], normed, contract_last, preferred_element_type=F32
    ).astype(BF16)
    ones = jnp.ones((HD, points), BF16)
    per_group = 128 // HD
    head_of_row = lax.broadcasted_iota(jnp.int32, (128, points), 0) // HD

    def score(head, slot):
        base = pl.multiple_of(head // per_group * 128, 128)
        group_queries = qv_cols_ref[pl.ds(base, 128)].astype(F32)
        chosen = head_of_row == lax.rem(head, per_group)
        queries = jnp.where(chosen, group_queries, 0.0).astype(BF16)
        scores_ref[slot] = dot(keys_ref[:, pl.ds(base, 128)], queries)

    def weigh(slot):
        scores = scores_ref[slot]
        weights_ref[slot] = jnp.exp2(scores - jnp.max(scores, axis=0, keepdims=True)).astype(BF16)

    def gather(head, slot):
        at = pl.multiple_of(head * HD, HD)
        values = jnp.concatenate([qv_cols_ref[pl.ds(width + at, HD)], ones], axis=0)
        sums = dot(values, weights_ref[slot])
        heads_ref[pl.ds(at, HD)] = (sums[:HD] / sums[HD : HD + 1]).astype(BF16)

    score(0, 0)
    score(1, 1)
    weigh(0)

    def two_heads(pair, carry):
        head = 2 * pair + 1
        for slot in (1, 0):
            score(head + 1, 1 - slot)
            weigh(slot)
            gather(head - 1, 1 - slot)
            head += 1
        return carry

    lax.fori_loop(0, HEADS // 2 - 1, two_heads, 0)
    weigh(1)
    gather(HEADS - 2, 0)
    gather(HEADS - 1, 1)

    for copy in copies[2:]:
        copy.wait()
    update = lax.dot_general(
        heads_ref[...], proj_ref[...], (((0,), (0,)), ((), ())), preferred_element_type=F32
    )
    attended = (serial_ref[...] + update).astype(BF16).astype(F32)
    hidden_in = layer_norm(attended, mlp_gain_ref[...]).astype(BF16)
    total_ref[...] = attended
    chunk = width
    for start in range(0, up_ref.shape[1], chunk):
        raised = dot(hidden_in, up_ref[:, start : start + chunk])
        hidden = (raised * (1.0 + lax.erf(raised * math.sqrt(0.5))) * 0.5).astype(BF16)
        total_ref[...] += dot(hidden, down_ref[start : start + chunk])
    finished = total_ref[...].astype(BF16)
    slot_rows = lax.broadcasted_iota(jnp.int32, (slots, points), 0)
    out_ref[...] = dot(one_hot(slot_rows == slot_row_ref[...]), finished).astype(BF16)


def return_kernel(arrived_ref, slot_ref, out_ref):
    slot_ids = lax.broadcasted_iota(jnp.int32, (out_ref.shape[0], arrived_ref.shape[0]), 1)
    out_ref[...] = dot(one_hot(slot_ref[...] == slot_ids), arrived_ref[...]).astype(BF16)


def face_pairs(devices, dx, dy):
    return [
        (source, source + dx * GY + dy)
        for source in range(devices)
        if 0 <= source // GY + dx < devices // GY and 0 <= source % GY + dy < GY
    ]


def way_round(devices, rows, length):
    chips = devices // 2
    cycle = list(range(0, chips, 2)) + list(range(chips - 1, 0, -2))
    chains = [], []
    places = [None] * devices
    for place, chip in enumerate(cycle):
        for core, way in ((0, 1), (1, -1)):
            me = 2 * chip + core
            for chain, step in zip(chains, (way, -way)):
                chain.append((me, 2 * cycle[(place + step) % chips] + core))
            order = [0]
            for step in range(1, chips // 2):
                order += [-step * way, step * way]
            order.append(chips // 2)
            places[me] = []
            for offset in order:
                start = cycle[(place + offset) % chips] * rows
                column = min(start // 128 * 128, chips * rows - length)
                places[me].append((column, start - column))
    return *chains, places


def padded_taps(neighbours):
    points = neighbours.shape[0]
    own = jnp.arange(points, dtype=jnp.int32)[:, None]
    rest = jnp.zeros((points, 128 - TAPS), jnp.int32)
    middle = TAPS // 2
    rows = jnp.concatenate([neighbours[:, :middle], own, neighbours[:, middle:], rest], axis=1)
    return rows.astype(F32)


def body(
    features,
    conv_weight,
    cpe_weight,
    cpe_gain,
    attn_gain,
    qkv_weight,
    proj_weight,
    mlp_gain,
    up_weight,
    down_weight,
    face_rows,
    neighbours,
    serial_rank,
    serial_order,
):
    points, width = features.shape
    half = width // 2
    devices = lax.axis_size("blocks")
    index = lax.axis_index("blocks")
    core = lax.rem(index, 2)
    partner = [(source, source ^ 1) for source in range(devices)]
    capacity = 2 * points // devices
    slots = devices * capacity

    unit = conv_weight.shape[0] // TAPS
    units = conv_weight.reshape(TAPS, unit, width)
    got = lax.ppermute(units[1::2], "blocks", partner)
    rows = TAPS * unit
    side = lax.axis_index("groups")
    missing = -(-rows // 64) * 16
    passed = rows - missing
    if devices == 2 * GY:
        mine, begun = call(
            rows_kernel,
            [
                jax.ShapeDtypeStruct((rows, width), BF16),
                jax.ShapeDtypeStruct((passed, width), BF16),
            ],
            24,
            0,
            8 * rows * width,
            in_specs=[pl.BlockSpec(memory_space=pltpu.SMEM)] + [pl.BlockSpec()] * 2,
        )(jnp.stack([core, side]).astype(jnp.int32), units, got)
    else:
        kept = units[0::2]
        mine = begun = jnp.where(
            core == 0, jnp.concatenate([kept, got]), jnp.concatenate([got, kept])
        ).reshape(rows, width)

    round_trip = devices == 2 * GY
    lower = index < GY
    if round_trip:
        across = jnp.where(lower, face_rows[0, 5:], face_rows[0, :3])
        face_list = jnp.concatenate([across, face_rows[0, 3:5]]).reshape(-1, 1)
        counts = (3, 1, 1)
    else:
        face_list = face_rows.reshape(-1, 1)
        counts = (1,) * 8
    size = face_rows.shape[2]
    own_local, other_local, *faces = call(
        functools.partial(faces_kernel, unit),
        [jax.ShapeDtypeStruct((points, half), BF16)] * 2
        + [jax.ShapeDtypeStruct((count * size, width), BF16) for count in counts],
        32,
        4 * points * width * width,
        8 * points * width,
        in_specs=[pl.BlockSpec(memory_space=pltpu.SMEM)] + [pl.BlockSpec()] * 2,
    )(core.reshape(1), features, face_list)
    length = -(-(rows + 127) // 128) * 128 if round_trip else rows * (devices // 2)
    first_pairs, second_pairs, places = way_round(devices, rows, length)
    shifts = jnp.stack([side * passed, (1 - side) * passed]).astype(jnp.int32)
    first, second = [begun], [begun]

    def pass_on(*beside):
        if not round_trip:
            return beside
        tied = lax.optimization_barrier((first[-1], second[-1], *beside))
        first[-1], second[-1] = tied[:2]
        last = len(first) == devices // 4
        first.append(lax.ppermute(first[-1], "blocks", first_pairs))
        if not last:
            second.append(lax.ppermute(second[-1], "blocks", second_pairs))
        return tied[2:]

    def complete(*arrived):
        lent = [piece[:missing] for piece in arrived]
        lent = jnp.concatenate(lent) if len(lent) > 1 else lent[0]
        got = lax.ppermute(lent, "groups", [(0, 1), (1, 0)])
        return [
            [
                (piece, 0, missing, 0, 0),
                (piece, missing, passed - missing, missing, None),
                (got, at * missing, missing, 0, 1),
            ]
            for at, piece in enumerate(arrived)
        ]

    if round_trip:
        lists, back_list, on_list = faces
        across = face_pairs(devices, 1, 0) + face_pairs(devices, -1, 0)
        (lists,) = pass_on(lists)
        lists = lax.ppermute(lists, "blocks", across)
        places = jnp.array(places, jnp.int32)[index].reshape(-1)
        lists, sent_neighbours, places = lax.optimization_barrier((lists, neighbours, places))
        other_neighbours = lax.ppermute(sent_neighbours, "blocks", partner)
        to_on = jnp.concatenate([on_list, lists[2 * size :]])
        to_back = jnp.concatenate([back_list, lists[:size]])
        behind = lax.ppermute(to_on, "blocks", face_pairs(devices, 0, 1))
        ahead = lax.ppermute(to_back, "blocks", face_pairs(devices, 0, -1))
        lists, behind, ahead = pass_on(lists, behind, ahead)
        near = complete(first[1], second[1])
        own_table, other_half = call(
            table_kernel,
            [jax.ShapeDtypeStruct((points + 6 * size, half), BF16)] * 2,
            32,
            0,
            20 * size * width,
            in_specs=[pl.BlockSpec(memory_space=pltpu.SMEM)] + [pl.BlockSpec()] * 5,
        )(
            jnp.stack([lower.astype(jnp.int32), core]),
            own_local,
            other_local,
            lists,
            behind,
            ahead,
        )
        start = jnp.where(lower, points, points + 3 * size).reshape(1)
    else:
        other_neighbours = lax.ppermute(neighbours, "blocks", partner)
        received = jnp.concatenate(
            [
                lax.ppermute(faces[k], "blocks", face_pairs(devices, STEPS_X[k], STEPS_Y[k]))
                for k in range(8)
            ]
        )
        shape = (received.shape[0], half)
        own_table = jnp.concatenate(
            [own_local, lax.dynamic_slice(received, (0, core * half), shape)]
        )
        other_half = jnp.concatenate(
            [other_local, lax.dynamic_slice(received, (0, (1 - core) * half), shape)]
        )
        start = jnp.full((1,), points, jnp.int32)
    other_table = lax.ppermute(other_half, "blocks", partner)
    own_stacked = gather_block(start, padded_taps(neighbours), own_table)
    other_rows = padded_taps(other_neighbours)
    own_stacked, other_rows, other_table = pass_on(own_stacked, other_rows, other_table)
    if round_trip:
        middle = complete(first[2], second[2])
    other_stacked = gather_block(start, other_rows, other_table)
    stacked = other_stacked, own_stacked
    if round_trip:
        *stacked, middle_got = pass_on(*stacked, middle[0][2][0])
        middle = [[*parts[:2], (middle_got, *parts[2][1:])] for parts in middle]
        early = [[(mine, 0, rows, 0, None)]] + near
        sums = conv_part(stacked, places[:6], shifts, early, None, length, CONV_LIMIT)
        far = complete(first[3], second[3])
        opposite = complete(first[4])
        sums = conv_part(stacked, places[6:10], shifts, middle, sums, length, CONV_LIMIT)
        sums = conv_part(stacked, places[10:14], shifts, far, sums, length, CONV_LIMIT)
        for_partner, own_part = conv_part(
            stacked, places[14:], shifts, opposite, sums, length, CONV_LIMIT, BF16
        )
    else:
        groups = [list(range(core, devices, 2)) for core in range(2)]
        weight = lax.all_gather(mine, "blocks", axis=0, tiled=True, axis_index_groups=groups)
        nowhere = jnp.zeros((2,), jnp.int32)
        whole = [[(weight, 0, weight.shape[0], 0, None)]]
        for_partner, own_part = conv_part(stacked, nowhere, shifts, whole, None, length, 48)

    positions = jnp.arange(points, dtype=jnp.int32)
    target = serial_rank // points
    earlier = (target[None, :] == target[:, None]) & (serial_rank[None, :] < serial_rank[:, None])
    out_slot = target * capacity + jnp.sum(earlier.astype(jnp.int32), axis=1)
    anchor = serial_order // points
    before = (anchor[None, :] == anchor[:, None]) & (positions[None, :] < positions[:, None])
    in_slot = anchor * capacity + jnp.sum(before.astype(jnp.int32), axis=1)

    from_partner = lax.ppermute(for_partner, "blocks", partner)

    outgoing = call(
        mix_kernel,
        jax.ShapeDtypeStruct((slots, width), BF16),
        32,
        2 * points * width * (width + slots),
        8 * points * width,
    )(
        own_part,
        from_partner,
        features,
        cpe_weight,
        cpe_gain.reshape(1, width),
        out_slot.reshape(1, points),
    )
    arrived = lax.all_to_all(
        outgoing.reshape(devices, capacity, width), "blocks", split_axis=0, concat_axis=0, tiled=True
    ).reshape(slots, width)

    key_weight = qkv_weight[:, width : 2 * width]
    qv_weight = jnp.concatenate([qkv_weight[:, :width], qkv_weight[:, 2 * width :]], axis=1).T
    weights = (qv_weight, key_weight, proj_weight, up_weight, down_weight)
    back = call(
        block_kernel,
        jax.ShapeDtypeStruct((slots, width), BF16),
        50,
        20 * points * width * width,
        16 * width * width,
        in_specs=[pl.BlockSpec()] * 5 + [pl.BlockSpec(memory_space=pl.ANY)] * len(weights),
        scratch_shapes=[pltpu.VMEM(weight.shape, BF16) for weight in weights]
        + [
            pltpu.SemaphoreType.DMA((len(weights),)),
            pltpu.VMEM((points, width), F32),
            pltpu.VMEM((2 * width, points), BF16),
            pltpu.VMEM((points, width), BF16),
            pltpu.VMEM((width, points), BF16),
            pltpu.VMEM((points, width), F32),
            pltpu.VMEM((2, points, points), F32),
            pltpu.VMEM((2, points, points), BF16),
        ],
    )(
        arrived,
        in_slot.reshape(points, 1),
        in_slot.reshape(1, points),
        attn_gain.reshape(1, width),
        mlp_gain.reshape(1, width),
        *weights,
    )
    returned = lax.all_to_all(
        back.reshape(devices, capacity, width), "blocks", split_axis=0, concat_axis=0, tiled=True
    ).reshape(slots, width)
    return call(
        return_kernel,
        jax.ShapeDtypeStruct((points, width), BF16),
        32,
        2 * points * slots * width,
        6 * points * width,
    )(returned, out_slot.reshape(points, 1))


def solution(mesh):
    placed = (
        P(("groups", "blocks"), None),
        P("blocks", None),
        P(),
        P(),
        P(),
        P(),
        P(),
        P(),
        P(),
        P(),
        P(("groups", "blocks"), None, None),
        P(("groups", "blocks"), None),
        P(("groups", "blocks")),
        P(("groups", "blocks")),
    )
    return jax.shard_map(
        body, mesh=mesh, in_specs=placed, out_specs=P(("groups", "blocks"), None), check_vma=False
    )
```
